32 devices in a mesh: dp: 8 (over z, x), tensor: 4 (over y, core).
Axes of the slice: x: 2, y: 2, z: 4, core: 2. Of those that a mesh axis runs over, the one named last changes fastest.
Arguments:
- tokens_in: bfloat16 [12288, 768], P('dp'), may hold values from -6 to 6
- cotangent: bfloat16 [12288, 768], P('dp'), may hold values from -6 to 6
- span_mask: int32 [12288], P('dp'), may hold values from 0 to 1, as said below
- lengths: int32 [24], P('dp'), may hold values from 128 to 512, as said below
- step: int32 [1], replicated, may hold values from 1000 to 31999
- warmup: int32 [1], replicated, may hold values from 1000 to 29999
- total: int32 [1], replicated, may hold values from 32000 to 40000
- w_qkv: float32 [768, 3, 768], P(None, None, 'tensor'), may hold values from -0.21875 to 0.21875
- w_out: float32 [768, 768], P(None, 'tensor'), may hold values from -1.25 to 1.25
- w_in: float32 [768, 3072], P(None, 'tensor'), may hold values from -0.21875 to 0.21875
- w_back: float32 [768, 3072], P(None, 'tensor'), may hold values from -0.109375 to 0.109375
- gains: float32 [2, 768], replicated, may hold values from 0.5 to 1.5
- biases: float32 [6, 768], replicated, may hold values from -3 to 3
- bias_in: float32 [3072], replicated, may hold values from -3 to 3
- mom_qkv: float32 [2, 768, 3, 768], P(None, 'dp', None, 'tensor'), as said below
- mom_out: float32 [2, 768, 768], P(None, 'dp', 'tensor'), as said below
- mom_in: float32 [2, 768, 3072], P(None, 'dp', 'tensor'), as said below
- mom_back: float32 [2, 768, 3072], P(None, 'dp', 'tensor'), as said below
- mom_gains: float32 [2, 2, 768], replicated, as said below
- mom_biases: float32 [2, 6, 768], replicated, as said below
- mom_bias_in: float32 [2, 3072], replicated, as said below
Outputs:
- normed_out: bfloat16 [12288, 768], P('dp')
- input_grad: float32 [12288, 768], P('dp')
- change_qkv: float32 [768, 3, 768], P(None, None, 'tensor')
- change_out_proj: float32 [768, 768], P(None, 'tensor')
- change_in_proj: float32 [768, 3072], P(None, 'tensor')
- change_back_proj: float32 [768, 3072], P(None, 'tensor')
- change_gains: float32 [2, 768], replicated
- change_biases: float32 [6, 768], replicated
- change_bias_in: float32 [3072], replicated
- new_mom_qkv: float32 [2, 768, 3, 768], P(None, 'dp', None, 'tensor')
- new_mom_out: float32 [2, 768, 768], P(None, 'dp', 'tensor')
- new_mom_in: float32 [2, 768, 3072], P(None, 'dp', 'tensor')
- new_mom_back: float32 [2, 768, 3072], P(None, 'dp', 'tensor')
- new_mom_gains: float32 [2, 2, 768], replicated
- new_mom_biases: float32 [2, 6, 768], replicated
- new_mom_bias_in: float32 [2, 3072], replicated
The draws below stay inside these ranges and needn't reach their ends.
Inputs may be any that keep to these rules, and one draw needn't show every extreme that they name: `span_mask`: marked positions lie below their sequence's length and form unions of spans of 1 to 10 positions; each sequence has at most 76 of them, and in every draw each of the 3 sequences of some index of dp has exactly 76. `lengths`: a sequence's real tokens stand at its start, the rest is padding. step < total. warmup < total. `mom_qkv`: index 1 of the leading dimension holds positive second moments. `mom_out`: index 1 of the leading dimension holds positive second moments. `mom_in`: index 1 of the leading dimension holds positive second moments. `mom_back`: index 1 of the leading dimension holds positive second moments. `mom_gains`: index 1 of the leading dimension holds positive second moments. `mom_biases`: index 1 of the leading dimension holds positive second moments. `mom_bias_in`: index 1 of the leading dimension holds positive second moments.
All inputs are finite; a program needn't handle non-finite values.
Results may differ from the reference program's by a relative error of at most 0.017.
The reference program's roundings to bfloat16 on the way count: a program that leaves them out, or rounds other values in their place, can miss the bound.
Values sent between devices are 32-bit elements; how exact they have to be, the bound alone decides.
A program may use at most 128 MiB of HBM per device.

```python
import jax
import jax.numpy as jnp
from jax import lax

D = 768
H = 12
HD = 64
FF = 3072
SEQ_LEN = 512
SEQ_DEV = 3
SEQS = 24
TOKENS = 12288
SPAN_MOST = 76


def sequence_lengths(key):
    length_key, full_key = jax.random.split(jax.random.fold_in(key, 11))
    drawn = jax.random.randint(length_key, (SEQS,), SEQ_LEN // 4, SEQ_LEN + 1)
    chosen = jax.random.randint(full_key, (), 0, SEQS)
    return jnp.where(jnp.arange(SEQS) == chosen, SEQ_LEN, drawn).astype(jnp.int32)


def draw_lengths(key, part):
    return sequence_lengths(key)


def draw_span_mask(key, part):
    seq_lengths = sequence_lengths(key)
    rate_key, start_key, length_key, block_key, phase_key = jax.random.split(jax.random.fold_in(key, 23), 5)
    rates = jax.random.randint(rate_key, (SEQS, 1), 25, 81)
    starts = (jax.random.randint(start_key, (SEQS, SEQ_LEN), 0, 1000) < rates).astype(jnp.int32)
    trials = (jax.random.randint(length_key, (SEQS, SEQ_LEN, 9), 0, 5) > 0).astype(jnp.int32)
    span_len = 1 + jnp.sum(jnp.cumprod(trials, axis=-1), axis=-1)
    covered = jnp.zeros((SEQS, SEQ_LEN), jnp.int32)
    for offset in range(10):
        reach = starts * (span_len > offset).astype(jnp.int32)
        shifted = jnp.pad(reach, ((0, 0), (offset, 0)))[:, :SEQ_LEN]
        covered = jnp.maximum(covered, shifted)
    positions = jnp.arange(SEQ_LEN, dtype=jnp.int32)
    full_index = jax.random.randint(block_key, (), 0, SEQS // SEQ_DEV)
    phase = jax.random.randint(phase_key, (SEQS, 1), 0, 11)
    pattern = ((positions[None, :] + phase) % 11 != 10).astype(jnp.int32)
    full_block = (jnp.arange(SEQS) // SEQ_DEV == full_index).astype(jnp.int32)[:, None]
    covered = full_block * pattern + (1 - full_block) * covered
    inside = (positions[None, :] < seq_lengths[:, None]).astype(jnp.int32)
    covered = covered * inside
    running = jnp.cumsum(covered, axis=1)
    kept = covered * (running <= SPAN_MOST).astype(jnp.int32)
    return kept.reshape(SEQS * SEQ_LEN).astype(jnp.int32)


def moment_pair(key, shape, salt):
    first_key, second_key = jax.random.split(jax.random.fold_in(key, salt))
    first = 0.5 * jax.random.normal(first_key, shape, jnp.float32)
    second = jnp.exp(jax.random.uniform(second_key, shape, jnp.float32, -6.2, -0.7))
    return jnp.stack([first, second])


def draw_mom_qkv(key, part):
    return moment_pair(key, (D, 3, D), 7)


def draw_mom_out(key, part):
    return moment_pair(key, (D, D), 8)


def draw_mom_in(key, part):
    return moment_pair(key, (D, FF), 9)


def draw_mom_back(key, part):
    return moment_pair(key, (D, FF), 10)


def draw_mom_gains(key, part):
    return moment_pair(key, (2, D), 11)


def draw_mom_biases(key, part):
    return moment_pair(key, (6, D), 12)


def draw_mom_bias_in(key, part):
    return moment_pair(key, (FF,), 13)


def block_levels(own_key, extent, cuts, least, high):
    level = 1.0
    for position, parts in cuts:
        steps = jax.random.uniform(jax.random.fold_in(jax.random.fold_in(own_key, 6), position), (parts,), jnp.float32, least / len(cuts), high / len(cuts))
        level = level * jnp.repeat(jnp.exp(steps), extent[position] // parts).reshape((-1,) + (1,) * (len(extent) - 1 - position))
    return level


def scatter_about(key, extent, width, bound, cuts=(), kind=jnp.bfloat16):
    values = jax.random.normal(key, extent, jnp.float32) * width
    if len(cuts) > 0:
        values = block_levels(key, extent, cuts, -0.22, 0.18) * values
    return jnp.clip(values, min=-bound, max=bound).astype(kind)


def setup_inputs(seed: int = 0) -> dict:
    seeds = jax.random.split(jax.random.key(seed), 22)
    return {
        "tokens_in": scatter_about(seeds[0], (TOKENS, D), 1.0, 6.0, ((0, 8),)),
        "cotangent": scatter_about(seeds[1], (TOKENS, D), 1.0, 6.0, ((0, 8),)),
        "span_mask": draw_span_mask(jax.random.fold_in(seeds[21], 71), 0),
        "lengths": draw_lengths(jax.random.fold_in(seeds[21], 71), 0),
        "step": jax.random.randint(seeds[4], (1,), 1000, 32000).astype(jnp.int32),
        "warmup": jax.random.randint(seeds[5], (1,), 1000, 30000).astype(jnp.int32),
        "total": jax.random.randint(seeds[6], (1,), 32000, 40001).astype(jnp.int32),
        "w_qkv": scatter_about(seeds[7], (D, 3, D), D ** -0.5, 0.21875, ((2, 4),), jnp.float32),
        "w_out": scatter_about(seeds[8], (D, D), (D // 32) ** -0.5, 1.25, ((1, 4),), jnp.float32),
        "w_in": scatter_about(seeds[9], (D, FF), D ** -0.5, 0.21875, ((1, 4),), jnp.float32),
        "w_back": scatter_about(seeds[10], (D, FF), FF ** -0.5, 0.109375, ((1, 4),), jnp.float32),
        "gains": jnp.clip(1.0 + 0.1 * jax.random.normal(seeds[11], (2, D), jnp.float32), 0.5, 1.5),
        "biases": scatter_about(seeds[12], (6, D), 0.5, 3.0, (), jnp.float32),
        "bias_in": scatter_about(seeds[13], (FF,), 0.5, 3.0, (), jnp.float32),
        "mom_qkv": draw_mom_qkv(jax.random.fold_in(seeds[21], 71), 0),
        "mom_out": draw_mom_out(jax.random.fold_in(seeds[21], 71), 0),
        "mom_in": draw_mom_in(jax.random.fold_in(seeds[21], 71), 0),
        "mom_back": draw_mom_back(jax.random.fold_in(seeds[21], 71), 0),
        "mom_gains": draw_mom_gains(jax.random.fold_in(seeds[21], 71), 0),
        "mom_biases": draw_mom_biases(jax.random.fold_in(seeds[21], 71), 0),
        "mom_bias_in": draw_mom_bias_in(jax.random.fold_in(seeds[21], 71), 0),
    }


@jax.custom_vjp
def low(v):
    return lax.optimization_barrier(v.astype(jnp.bfloat16)).astype(jnp.float32)

@jax.custom_vjp
def low_back(v):
    return v

def low_keep(v):
    return (low(v), None)

def low_pass(kept, grad):
    return (grad,)

def back_keep(v):
    return (v, None)

def back_low(kept, grad):
    return (low(grad),)
low.defvjp(low_keep, low_pass)
low_back.defvjp(back_keep, back_low)
NORM_EPS = 1e-12
BETA_ONE = 0.9
BETA_TWO = 0.999
ADAM_EPS = 1e-06
WEIGHT_DECAY = 0.01
seqs_per_block = 8
HIGHEST = lax.Precision.HIGHEST

def matmul(left, right):
    return jnp.dot(left, right, precision=HIGHEST, preferred_element_type=jnp.float32)

def layer_norm(values, gain, shift):
    center = values - lax.optimization_barrier(jnp.mean(values, axis=-1, keepdims=True))
    spread = lax.optimization_barrier(jnp.mean(center * center, axis=-1, keepdims=True))
    return center * lax.rsqrt(spread + NORM_EPS) * gain + shift

def forward(inputs_x, w_qkv, w_out, w_in, w_back, gains, biases, bias_in, block_len):
    row_count = inputs_x.shape[0]
    seq_count = block_len.shape[0]
    scale = 1.0 / jnp.sqrt(jnp.float32(HD))
    projected = low_back(matmul(inputs_x, low(w_qkv).reshape(D, 3 * D))).reshape(row_count, 3, D)
    shape = (seq_count, SEQ_LEN, H, HD)
    queries = low((projected[:, 0] + biases[0]) * scale).reshape(shape)
    keys = low(projected[:, 1]).reshape(shape)
    values = low(projected[:, 2] + biases[1]).reshape(shape)
    positions = jnp.arange(SEQ_LEN, dtype=jnp.int32)
    key_bias = jnp.where(positions[None, :] < block_len[:, None], 0.0, -1000000000.0).astype(jnp.float32)
    scores = jnp.einsum('sqhd,skhd->shqk', queries, keys, precision=HIGHEST)
    scores = low_back(scores + key_bias[:, None, None, :])
    probs = low(jax.nn.softmax(scores, axis=-1))
    context = jnp.einsum('shqk,skhd->sqhd', probs, values, precision=HIGHEST).reshape(row_count, D)
    context = low(low_back(context))
    attn = low_back(matmul(context, low(w_out).T)) + biases[2]
    normed = layer_norm(inputs_x + attn, gains[0], biases[3])
    pre_act = low_back(matmul(low(normed), low(w_in))) + bias_in
    act = low(jax.nn.gelu(pre_act, approximate=False))
    down = low_back(matmul(act, low(w_back).T)) + biases[4]
    return layer_norm(normed + down, gains[1], biases[5])

def adam_step(weight, grad, moments, ratio, corr_one, corr_two, decay):
    first = BETA_ONE * moments[0] + (1.0 - BETA_ONE) * grad
    second = BETA_TWO * moments[1] + (1.0 - BETA_TWO) * grad * grad
    update = first / corr_one / (jnp.sqrt(second / corr_two) + ADAM_EPS) + decay * weight
    return (-ratio * update, jnp.stack([first, second]))

def reference(tokens_in, cotangent, span_mask, lengths, step, warmup, total, w_qkv, w_out, w_in, w_back, gains, biases, bias_in, mom_qkv, mom_out, mom_in, mom_back, mom_gains, mom_biases, mom_bias_in):
    block_count = SEQS // seqs_per_block
    block_rows = seqs_per_block * SEQ_LEN
    params = (w_qkv.astype(jnp.float32), w_out.astype(jnp.float32), w_in.astype(jnp.float32), w_back.astype(jnp.float32), gains.astype(jnp.float32), biases.astype(jnp.float32), bias_in.astype(jnp.float32))
    pieces = (tokens_in.astype(jnp.float32).reshape(block_count, block_rows, D), cotangent.astype(jnp.float32).reshape(block_count, block_rows, D), span_mask.reshape(block_count, block_rows), lengths.reshape(block_count, seqs_per_block))
    positions = jnp.arange(SEQ_LEN, dtype=jnp.int32)

    def one_block(totals, block):
        block_x, block_cot, block_mask, block_len = block

        def run(inputs_x, *weights):
            return forward(inputs_x, *weights, block_len)
        block_out, pullback = jax.vjp(run, block_x, *params)
        inside = (positions[None, :] < block_len[:, None]).astype(jnp.int32).reshape(block_rows)
        live = (inside * block_mask).astype(jnp.float32)
        grads = pullback(block_cot * live[:, None])
        totals = tuple((carry + grad for carry, grad in zip(totals, grads[1:])))
        return (totals, (block_out, grads[0]))
    zeros = tuple((jnp.zeros_like(param) for param in params))
    totals, (out_blocks, grad_blocks) = lax.scan(one_block, zeros, pieces)
    normed_out = out_blocks.reshape(TOKENS, D).astype(jnp.bfloat16)
    input_grad = grad_blocks.reshape(TOKENS, D)
    clock = step[0].astype(jnp.float32)
    warm = warmup[0].astype(jnp.float32)
    horizon = total[0].astype(jnp.float32)
    ratio = jnp.minimum(clock / warm, (horizon - clock) / (horizon - warm))
    corr_one = 1.0 - jnp.power(BETA_ONE, clock)
    corr_two = 1.0 - jnp.power(BETA_TWO, clock)
    moments = (mom_qkv, mom_out, mom_in, mom_back, mom_gains, mom_biases, mom_bias_in)
    decays = (WEIGHT_DECAY, WEIGHT_DECAY, WEIGHT_DECAY, WEIGHT_DECAY, 0.0, 0.0, 0.0)
    changes = []
    new_moments = []
    for param, grad, moment, decay in zip(params, totals, moments, decays):
        change, fresh_moment = adam_step(param, grad, moment, ratio, corr_one, corr_two, decay)
        changes.append(change)
        new_moments.append(fresh_moment)
    return (normed_out, input_grad, changes[0], changes[1], changes[2], changes[3], changes[4], changes[5], changes[6], new_moments[0], new_moments[1], new_moments[2], new_moments[3], new_moments[4], new_moments[5], new_moments[6])
```

```python
import math

import jax
import jax.numpy as jnp
from jax import lax
from jax.sharding import PartitionSpec as P

HD = 64
SPAN_ROWS = 80


NORM_EPS = 1e-12
BETA_ONE = 0.9
BETA_TWO = 0.999
ADAM_EPS = 1e-06
WEIGHT_DECAY = 0.01


def layer_norm(values, gain, shift):
    center = values - jnp.mean(values, axis=-1, keepdims=True)
    spread = jnp.mean(center * center, axis=-1, keepdims=True)
    return center * lax.rsqrt(spread + NORM_EPS) * gain + shift


def exact_gelu(values):
    return jax.nn.gelu(values, approximate=False)


def outer_sum(left, right):
    return jnp.einsum("ta,tb->ab", left, right, preferred_element_type=jnp.float32)


def adam_step(weight, grad, moments, ratio, corr_one, corr_two, decay):
    first = BETA_ONE * moments[0] + (1.0 - BETA_ONE) * grad
    second = BETA_TWO * moments[1] + (1.0 - BETA_TWO) * grad * grad
    update = first / corr_one / (jnp.sqrt(second / corr_two) + ADAM_EPS) + decay * weight
    return (-ratio * update, jnp.stack([first, second]))


def on_device(
    tokens_in,
    cotangent,
    span_mask,
    lengths,
    step,
    warmup,
    total,
    w_qkv,
    w_out,
    w_in,
    w_back,
    gains,
    biases,
    bias_in,
    mom_qkv,
    mom_out,
    mom_in,
    mom_back,
    mom_gains,
    mom_biases,
    mom_bias_in,
):
    row_count, model_width = tokens_in.shape
    seq_count = lengths.shape[0]
    seq_length = row_count // seq_count
    head_cols = w_qkv.shape[2]
    hidden_cols = w_in.shape[1]
    head_size = HD
    local_heads = head_cols // head_size
    query_scale = 1.0 / math.sqrt(head_size)
    tensor_slot = lax.axis_index("tensor")
    bias_query = lax.dynamic_slice_in_dim(biases[0], tensor_slot * head_cols, head_cols)
    bias_value = lax.dynamic_slice_in_dim(biases[1], tensor_slot * head_cols, head_cols)
    bias_hidden = lax.dynamic_slice_in_dim(bias_in, tensor_slot * hidden_cols, hidden_cols)
    qkv_low = w_qkv.astype(jnp.bfloat16).reshape(model_width, 3 * head_cols)
    out_low = w_out.astype(jnp.bfloat16)
    in_low = w_in.astype(jnp.bfloat16)
    down_low = w_back.astype(jnp.bfloat16)
    projected = jnp.dot(tokens_in, qkv_low, preferred_element_type=jnp.float32).reshape(
        row_count, 3, head_cols
    )
    attn_shape = (seq_count, seq_length, local_heads, head_size)
    queries = (
        ((projected[:, 0] + bias_query) * query_scale).astype(jnp.bfloat16).reshape(attn_shape)
    )
    keys = projected[:, 1].astype(jnp.bfloat16).reshape(attn_shape)
    values = (projected[:, 2] + bias_value).astype(jnp.bfloat16).reshape(attn_shape)
    positions = jnp.arange(seq_length, dtype=jnp.int32)
    inside = positions[None, :] < lengths[:, None]
    key_bias = jnp.where(inside, 0.0, -1000000000.0).astype(jnp.float32)

    def score_block():
        raw = jnp.einsum("sqhd,skhd->shqk", queries, keys, preferred_element_type=jnp.float32)
        return raw + key_bias[:, None, None, :]

    scores = score_block()
    peak = jnp.max(scores, axis=-1, keepdims=True)
    log_total = peak + jnp.log(jnp.sum(jnp.exp(scores - peak), axis=-1, keepdims=True))
    probs_low = jnp.exp(scores - log_total).astype(jnp.bfloat16)
    context_low = (
        jnp.einsum("shqk,skhd->sqhd", probs_low, values, preferred_element_type=jnp.float32)
        .reshape(row_count, head_cols)
        .astype(jnp.bfloat16)
    )
    attn_part = jnp.einsum("tc,dc->td", context_low, out_low, preferred_element_type=jnp.float32)
    attn_sum = lax.psum(attn_part, "tensor")
    residual_one = tokens_in.astype(jnp.float32) + attn_sum + biases[2]
    normed = layer_norm(residual_one, gains[0], biases[3])
    normed_low = normed.astype(jnp.bfloat16)
    pre_act = jnp.dot(normed_low, in_low, preferred_element_type=jnp.float32) + bias_hidden
    act_low = exact_gelu(pre_act).astype(jnp.bfloat16)
    down_part = jnp.einsum("tf,df->td", act_low, down_low, preferred_element_type=jnp.float32)
    down_sum = lax.psum(down_part, "tensor")
    residual_two = normed + down_sum + biases[4]
    live = (inside.astype(jnp.int32) * span_mask.reshape(seq_count, seq_length)) > 0
    upto = (positions[:, None] <= positions[None, :]).astype(jnp.float32)
    rank = jnp.dot(live.astype(jnp.float32), upto).astype(jnp.int32) - 1
    slots = jnp.arange(SPAN_ROWS, dtype=jnp.int32)
    pick = (live[:, None, :] & (rank[:, None, :] == slots[None, :, None])).astype(jnp.float32)
    pick_low = pick.astype(jnp.bfloat16)

    def rows_of(values):
        width = values.shape[-1]
        return jnp.einsum(
            "srt,std->srd",
            pick,
            values.reshape(seq_count, seq_length, width),
            precision=lax.Precision.HIGHEST,
        ).reshape(seq_count * SPAN_ROWS, width)

    def low_rows_of(values):
        width = values.shape[-1]
        return jnp.einsum(
            "srt,std->srd",
            pick_low,
            values.reshape(seq_count, seq_length, width),
            preferred_element_type=jnp.bfloat16,
        ).reshape(seq_count * SPAN_ROWS, width)

    result = layer_norm(residual_two, gains[1], biases[5])
    normed_out = result.astype(jnp.bfloat16)
    residual_one_rows = rows_of(residual_one)
    residual_two_rows = rows_of(residual_two)
    grad_result = low_rows_of(cotangent).astype(jnp.float32)
    _, norm_two_back = jax.vjp(layer_norm, residual_two_rows, gains[1], biases[5])
    d_res_two, d_gain_two, d_shift_two = norm_two_back(grad_result)
    d_res_two_low = d_res_two.astype(jnp.bfloat16)
    normed_low_rows = low_rows_of(normed_low)
    pre_rows = jnp.dot(normed_low_rows, in_low, preferred_element_type=jnp.float32) + bias_hidden
    act_rows, gelu_back = jax.vjp(exact_gelu, pre_rows)
    grad_back = outer_sum(d_res_two_low, act_rows.astype(jnp.bfloat16))
    d_act = jnp.dot(d_res_two_low, down_low, preferred_element_type=jnp.float32)
    d_pre = gelu_back(d_act)[0]
    d_pre_low = d_pre.astype(jnp.bfloat16)
    grad_in = outer_sum(normed_low_rows, d_pre_low)
    d_normed_part = jnp.einsum("tf,df->td", d_pre_low, in_low, preferred_element_type=jnp.float32)
    d_normed = lax.psum(d_normed_part, "tensor") + d_res_two
    _, norm_one_back = jax.vjp(layer_norm, residual_one_rows, gains[0], biases[3])
    d_res_one, d_gain_one, d_shift_one = norm_one_back(d_normed)
    d_res_one_low = d_res_one.astype(jnp.bfloat16)
    grad_out_proj = outer_sum(d_res_one_low, low_rows_of(context_low))
    row_shape = (seq_count, SPAN_ROWS, local_heads, head_size)
    d_context = (
        jnp.dot(d_res_one_low, out_low, preferred_element_type=jnp.float32)
        .astype(jnp.bfloat16)
        .reshape(row_shape)
    )
    query_rows = low_rows_of(queries.reshape(row_count, head_cols)).reshape(row_shape)
    raw = jnp.einsum("sqhd,skhd->shqk", query_rows, keys, preferred_element_type=jnp.float32)
    probs = jax.nn.softmax(raw + key_bias[:, None, None, :], axis=-1)
    probs_again = probs.astype(jnp.bfloat16)
    d_probs = jnp.einsum("sqhd,skhd->shqk", d_context, values, preferred_element_type=jnp.float32)
    d_values = jnp.einsum(
        "shqk,sqhd->skhd", probs_again, d_context, preferred_element_type=jnp.float32
    ).reshape(row_count, head_cols)
    d_scores = (probs * (d_probs - jnp.sum(probs * d_probs, axis=-1, keepdims=True))).astype(
        jnp.bfloat16
    )
    d_queries = (
        jnp.einsum("shqk,skhd->sqhd", d_scores, keys, preferred_element_type=jnp.float32).reshape(
            seq_count * SPAN_ROWS, head_cols
        )
        * query_scale
    )
    d_keys = jnp.einsum(
        "shqk,sqhd->skhd", d_scores, query_rows, preferred_element_type=jnp.float32
    ).reshape(row_count, head_cols)

    def spread(row_values):
        width = row_values.shape[-1]
        return jnp.einsum(
            "srt,srd->std",
            pick,
            row_values.reshape(seq_count, SPAN_ROWS, width),
            precision=lax.Precision.HIGHEST,
        ).reshape(row_count, width)

    d_proj_low = (
        jnp.stack([spread(d_queries), d_keys, d_values], axis=1)
        .astype(jnp.bfloat16)
        .reshape(row_count, 3 * head_cols)
    )
    grad_qkv = outer_sum(tokens_in, d_proj_low).reshape(model_width, 3, head_cols)
    d_entry_part = jnp.einsum("tc,dc->td", d_proj_low, qkv_low, preferred_element_type=jnp.float32)
    input_grad = lax.psum(d_entry_part, "tensor") + spread(d_res_one)
    first_rank = (tensor_slot == 0).astype(jnp.float32)
    width_zero = jnp.zeros((model_width,), jnp.float32)

    def place_heads(partial_sum):
        return lax.dynamic_update_slice_in_dim(width_zero, partial_sum, tensor_slot * head_cols, 0)

    grad_gains = jnp.stack([d_gain_one, d_gain_two]) * first_rank
    grad_biases = jnp.stack(
        [
            place_heads(jnp.sum(d_queries, axis=0)),
            place_heads(jnp.sum(d_values, axis=0)),
            jnp.sum(d_res_one, axis=0) * first_rank,
            d_shift_one * first_rank,
            jnp.sum(d_res_two, axis=0) * first_rank,
            d_shift_two * first_rank,
        ]
    )
    grad_bias_in = lax.dynamic_update_slice_in_dim(
        jnp.zeros(bias_in.shape, jnp.float32), jnp.sum(d_pre, axis=0), tensor_slot * hidden_cols, 0
    )
    grad_gains, grad_biases, grad_bias_in = lax.psum(
        (grad_gains, grad_biases, grad_bias_in), ("dp", "tensor")
    )
    data_slot = lax.axis_index("dp")
    shard_rows = model_width // lax.axis_size("dp")
    owned = tuple(
        lax.psum_scatter(part, "dp", scatter_dimension=0, tiled=True)
        for part in (grad_qkv, grad_out_proj, grad_in, grad_back)
    )
    clock = step[0].astype(jnp.float32)
    warm = warmup[0].astype(jnp.float32)
    horizon = total[0].astype(jnp.float32)
    ratio = jnp.minimum(clock / warm, (horizon - clock) / (horizon - warm))
    corr_one = 1.0 - jnp.power(BETA_ONE, clock)
    corr_two = 1.0 - jnp.power(BETA_TWO, clock)
    change_rows = []
    fresh_moments = []
    for weight, grad_rows, moment in zip(
        (w_qkv, w_out, w_in, w_back), owned, (mom_qkv, mom_out, mom_in, mom_back)
    ):
        weight_rows = lax.dynamic_slice_in_dim(weight, data_slot * shard_rows, shard_rows, 0)
        row_change, new_moment = adam_step(
            weight_rows, grad_rows, moment, ratio, corr_one, corr_two, WEIGHT_DECAY
        )
        change_rows.append(row_change)
        fresh_moments.append(new_moment)
    change_qkv, change_out_proj, change_in_proj, change_back_proj = (
        lax.all_gather(change_rows[0], "dp", axis=0, tiled=True),
        lax.all_gather(change_rows[1], "dp", axis=0, tiled=True),
        lax.all_gather(change_rows[2], "dp", axis=0, tiled=True),
        lax.all_gather(change_rows[3], "dp", axis=0, tiled=True),
    )
    change_gains, new_mom_gains = adam_step(
        gains, grad_gains, mom_gains, ratio, corr_one, corr_two, 0.0
    )
    change_biases, new_mom_biases = adam_step(
        biases, grad_biases, mom_biases, ratio, corr_one, corr_two, 0.0
    )
    change_bias_in, new_mom_bias_in = adam_step(
        bias_in, grad_bias_in, mom_bias_in, ratio, corr_one, corr_two, 0.0
    )
    return (
        normed_out,
        input_grad,
        change_qkv,
        change_out_proj,
        change_in_proj,
        change_back_proj,
        change_gains,
        change_biases,
        change_bias_in,
        fresh_moments[0],
        fresh_moments[1],
        fresh_moments[2],
        fresh_moments[3],
        new_mom_gains,
        new_mom_biases,
        new_mom_bias_in,
    )


def solution(mesh):
    in_specs = (
        P("dp", None),
        P("dp", None),
        P("dp"),
        P("dp"),
        P(),
        P(),
        P(),
        P(None, None, "tensor"),
        P(None, "tensor"),
        P(None, "tensor"),
        P(None, "tensor"),
        P(),
        P(),
        P(),
        P(None, "dp", None, "tensor"),
        P(None, "dp", "tensor"),
        P(None, "dp", "tensor"),
        P(None, "dp", "tensor"),
        P(),
        P(),
        P(),
    )
    out_specs = (
        P("dp", None),
        P("dp", None),
        P(None, None, "tensor"),
        P(None, "tensor"),
        P(None, "tensor"),
        P(None, "tensor"),
        P(),
        P(),
        P(),
        P(None, "dp", None, "tensor"),
        P(None, "dp", "tensor"),
        P(None, "dp", "tensor"),
        P(None, "dp", "tensor"),
        P(),
        P(),
        P(),
    )
    return jax.shard_map(
        on_device, mesh=mesh, in_specs=in_specs, out_specs=out_specs, check_vma=False
    )
```

```python
import functools
import math

import jax
import jax.numpy as jnp
from jax import lax
from jax.experimental import pallas as pl
from jax.experimental.pallas import tpu as pltpu
from jax.sharding import PartitionSpec as P

HD = 64
SPAN_ROWS = 80
NORM_EPS = 1e-12
MESH = pl.DeviceIdType.MESH
F32 = jnp.float32
LOW = jnp.bfloat16


def dot(left, right, left_dim, right_dim):
    return lax.dot_general(
        left, right, (((left_dim,), (right_dim,)), ((), ())), preferred_element_type=F32
    )


def normalize(rows):
    center = rows - jnp.mean(rows, axis=-1, keepdims=True)
    scale = lax.rsqrt(jnp.mean(center * center, axis=-1, keepdims=True) + NORM_EPS)
    return center * scale, scale


def norm_back(grad, gain, unit, scale):
    weighted = grad * gain
    return scale * (
        weighted
        - jnp.mean(weighted, axis=-1, keepdims=True)
        - unit * jnp.mean(weighted * unit, axis=-1, keepdims=True)
    )


def row_sum(rows):
    return jnp.sum(rows, axis=0, keepdims=True)


class Peers:
    def __init__(self):
        self.d = lax.axis_index("dp")
        self.t = lax.axis_index("tensor")
        self.b = lax.rem(self.d, 2)
        self.c = lax.rem(self.t, 2)
        self.p = lax.div(self.t, 2)
        self.u = lax.div(self.d, 2)
        self.core = (self.d, self.t + 1 - 2 * self.c)
        self.y = (self.d, lax.rem(self.t + 2, 4))
        self.x = (self.d + 1 - 2 * self.b, self.t)


def send(src, dst, sems, k, peer):
    copy = pltpu.make_async_remote_copy(
        src_ref=src, dst_ref=dst, send_sem=sems.at[0, k], recv_sem=sems.at[1, k],
        device_id=peer, device_id_type=MESH,
    )
    copy.start()
    return copy


def local(src, dst, sem):
    copy = pltpu.make_async_copy(src, dst, sem)
    copy.start()
    return copy


def greet(peers):
    barrier = pltpu.get_barrier_semaphore()
    for peer in peers:
        pl.semaphore_signal(barrier, inc=1, device_id=peer, device_id_type=MESH)
    pl.semaphore_wait(barrier, len(peers))


def gelu_parts(pre):
    cdf = 0.5 * (1.0 + lax.erf(pre * (1.0 / math.sqrt(2.0))))
    pdf = jnp.exp(-0.5 * pre * pre) * (1.0 / math.sqrt(2.0 * math.pi))
    return pre * cdf, cdf + pre * pdf


def k1_kernel(
    lens, mask, gains, biases, bias_in, x_h, cot_h, wqkv_h, wout_h, win_h, wback_h,
    gattn, gin, gback, dproj, q_o, k_o, v_o, pick_o, dres1_o, wp_out, vec,
    x, cot, wqkv, wout, win, wback, wql, wol, wil, wbl,
    pm, xm, cotm, qm, ctxm, ctxp, ap, apc, unit1, rs1, normed, nlow, act, gp, part, rc1, h1, ry1,
    part2, rc2, h2, ry2, full2, full, dres2, d2w, d2x, nxw, nxx, dplow, dctx, hw,
    lsem, rsem,
):
    seqs, rows = 3, SPAN_ROWS
    count = x_h.shape[0]
    length = count // seqs
    total = seqs * rows
    half = total // 2
    heads = q_o.shape[1]
    n_heads = heads // HD
    width = x_h.shape[1]
    me = Peers()

    loads = [
        local(x_h, x.at[pl.ds(0, count)], lsem.at[0]),
        local(wqkv_h, wqkv, lsem.at[1]),
        local(wout_h, wout, lsem.at[2]),
        local(win_h, win, lsem.at[3]),
        local(wback_h, wback, lsem.at[4]),
        local(cot_h, cot, lsem.at[5]),
    ]
    greet((me.core, me.y, me.x))

    loads[2].wait()
    out_half = pl.ds(pl.multiple_of(me.b * (heads // 2), 8), heads // 2)
    wo_y = send(wout.at[out_half], wp_out.at[out_half], rsem, 0, me.y)
    loads[1].wait()
    wql[...] = wqkv[...].astype(LOW)
    wol[...] = wout[...].astype(LOW)

    def pick_bias(row, k=heads):
        out = jnp.zeros((1, k), F32)
        for slot in range(4):
            piece = biases[row:row + 1, slot * k:(slot + 1) * k]
            out = jnp.where(me.t == slot, piece, out)
        return out

    bias_q, bias_v = pick_bias(0), pick_bias(1)
    hidden = win.shape[1]
    lanes = 128
    bias_h = jnp.concatenate(
        [bias_in[pl.ds(me.t * (hidden // lanes) + j, 1), :] for j in range(hidden // lanes)], axis=1
    )
    upto = (
        lax.broadcasted_iota(jnp.int32, (length, length), 0)
        <= lax.broadcasted_iota(jnp.int32, (length, length), 1)
    ).astype(F32).astype(LOW)
    position = lax.broadcasted_iota(jnp.int32, (1, length), 1)
    slot_of = lax.broadcasted_iota(jnp.int32, (rows, length), 0).astype(F32)
    scale = 1.0 / math.sqrt(HD)
    loads[0].wait()

    def project(s, _):
        at = pl.ds(pl.multiple_of(s * length, length), length)
        xs = x[at, :]
        q = ((dot(xs, wql[0:heads], 1, 1) + bias_q) * scale).astype(LOW)
        k = dot(xs, wql[heads:2 * heads], 1, 1).astype(LOW)
        v = (dot(xs, wql[2 * heads:3 * heads], 1, 1) + bias_v).astype(LOW)
        q_o[at, :] = q
        k_o[at, :] = k
        v_o[at, :] = v
        parts = length // lanes
        marks = jnp.concatenate([mask[pl.ds(s * parts + j, 1), :] for j in range(parts)], axis=1)
        inside = position < lens[s]
        live = jnp.where(inside, marks, 0).astype(F32)
        rank = dot(jnp.broadcast_to(live, (8, length)).astype(LOW), upto, 1, 0)[0:1] - 1.0
        pick = jnp.where((rank == slot_of) & (live > 0.0), 1.0, 0.0).astype(LOW)
        pick_o[s] = pick
        here = pl.ds(pl.multiple_of(s * rows, rows), rows)
        xm[here, :] = dot(pick, xs, 1, 0)
        qrow = dot(pick, q, 1, 0).astype(LOW)
        qm[here, :] = qrow
        key_bias = jnp.where(inside, 0.0, -1000000000.0)
        pieces = []
        for h in range(n_heads):
            col = slice(h * HD, (h + 1) * HD)
            scores = dot(qrow[:, col], k[:, col], 1, 1) + key_bias
            e = jnp.exp(scores - jnp.max(scores, axis=-1, keepdims=True))
            prob = e / jnp.sum(e, axis=-1, keepdims=True)
            pm[s * n_heads + h] = prob
            pieces.append(dot(prob.astype(LOW), v[:, col], 1, 0))
        ctxm[here, :] = jnp.concatenate(pieces, axis=1).astype(LOW).astype(F32)
        return 0

    lax.fori_loop(0, seqs, project, 0)
    ctx_y = send(ctxm, ctxp, rsem, 1, me.y)
    wo_y.wait()
    wo_x = send(wp_out.at[out_half], wp_out.at[out_half], rsem, 2, me.x)
    part1 = dot(ctxm[...].astype(LOW), wol[...], 1, 0)
    for load in loads[3:5]:
        load.wait()
    wil[...] = win[...].astype(LOW)
    wbl[...] = wback[...].astype(LOW)
    loads[5].wait()
    for s in range(seqs):
        cotm[s * rows:(s + 1) * rows, :] = dot(pick_o[s], cot[s * length:(s + 1) * length, :], 1, 0)
    wo_x.wait()
    ctx_y.wait()
    ap[...] = part1 + dot(ctxp[...].astype(LOW), wp_out[...].astype(LOW), 1, 0)
    ap_c = send(ap, apc, rsem, 3, me.core)
    ap_c.wait()
    unit, inv = normalize(xm[...] + (ap[...] + apc[...]) + biases[2:3, :])
    unit1[...] = unit
    rs1[...] = inv
    normed[...] = unit * gains[0:1, :] + biases[3:4, :]
    nlow[...] = normed[...].astype(LOW)
    nxw[...] = nlow[...].astype(F32)
    mine = pl.ds(pl.multiple_of(me.c * half, 8), half)
    other = pl.ds(pl.multiple_of((1 - me.c) * half, 8), half)
    nx_x = send(nxw.at[mine], nxx.at[mine], rsem, 5, me.x)
    for j in range(0, hidden, 256):
        col = slice(j, j + 256)
        a, g = gelu_parts(dot(nlow[...], wil[:, col], 1, 0) + bias_h[:, col])
        act[:, col] = a.astype(LOW)
        gp[:, col] = g
    part[...] = dot(act[...], wbl[...], 1, 1)

    def all_reduce(src, rc, hs, ry, dst, base, fill):
        first = send(src.at[other], rc, rsem, base, me.core)
        first.wait()
        hs[...] = src[mine, :] + rc[...]
        second = send(hs, ry, rsem, base + 1, me.y)
        fill()
        second.wait()
        dst[mine, :] = hs[...] + ry[...]
        third = send(dst.at[mine], dst.at[mine], rsem, base + 2, me.core)
        third.wait()

    relay = []

    def fill_one():
        nx_x.wait()
        relay.append(send(nxx.at[mine], nxx.at[mine], rsem, 6, me.core))

    all_reduce(part, rc1, h1, ry1, full, 7, fill_one)
    relay[0].wait()
    unit, inv = normalize(normed[...] + full[...] + biases[4:5, :])
    grad = cotm[...]
    d_two = norm_back(grad, gains[1:2, :], unit, inv)
    dres2[...] = d_two
    vec[...] = jnp.zeros(vec.shape, F32)
    vec[1:2, :] = row_sum(grad * unit)
    vec[5:6, :] = row_sum(d_two)
    vec[6:7, :] = row_sum(grad)
    d2w[...] = d_two.astype(LOW).astype(F32)
    d2_x = send(d2w.at[mine], d2x.at[mine], rsem, 10, me.x)
    d2low = d2w[...].astype(LOW)
    for j in range(0, hidden, 256):
        col = slice(j, j + 256)
        d_pre = dot(d2low, wbl[:, col], 1, 0) * gp[:, col]
        vec[8:9, col] = row_sum(d_pre)
        dplow[0:total, col] = d_pre.astype(LOW)
    part2[...] = dot(dplow[0:total, :], wil[...], 1, 1)

    def fill_two():
        for j in range(0, hidden, 256):
            col = slice(j, j + 256)
            gin[:, col] = dot(nlow[...], dplow[0:total, col], 0, 0)
            gback[:, col] = dot(d2low, act[:, col], 0, 0)
        d2_x.wait()
        relay.append(send(d2x.at[mine], d2x.at[mine], rsem, 11, me.core))

    all_reduce(part2, rc2, h2, ry2, full2, 12, fill_two)
    d_normed = full2[...] + dres2[...]
    unit = unit1[...]
    d_one = norm_back(d_normed, gains[0:1, :], unit, rs1[...])
    dres1_o[...] = d_one
    vec[0:1, :] = row_sum(d_normed * unit)
    vec[3:4, :] = row_sum(d_one)
    vec[4:5, :] = row_sum(d_normed)
    d1low = d_one.astype(LOW)
    x[count:count + total, :] = d1low
    dctx[...] = dot(d1low, wol[...], 1, 1).astype(LOW)
    relay[1].wait()
    nlx = nxx[...].astype(LOW)
    dlx = d2x[...].astype(LOW)
    for j in range(0, hidden, 256):
        col = slice(j, j + 256)
        a, g = gelu_parts(dot(nlx, wil[:, col], 1, 0) + bias_h[:, col])
        d_pre = (dot(dlx, wbl[:, col], 1, 0) * g).astype(LOW)
        gin[:, col] += dot(nlx, d_pre, 0, 0)
        gback[:, col] += dot(dlx, a.astype(LOW), 0, 0)

    def attend(s, carry):
        dq_sum, dv_sum = carry
        at = pl.ds(pl.multiple_of(s * length, length), length)
        here = pl.ds(pl.multiple_of(s * rows, rows), rows)
        q, k, v, dc = qm[here, :], k_o[at, :], v_o[at, :], dctx[here, :]
        dqs, dks, dvs = [], [], []
        for h in range(n_heads):
            col = slice(h * HD, (h + 1) * HD)
            prob = pm[s * n_heads + h]
            d_prob = dot(dc[:, col], v[:, col], 1, 1)
            dvs.append(dot(prob.astype(LOW), dc[:, col], 0, 0))
            ds = prob * (d_prob - jnp.sum(prob * d_prob, axis=-1, keepdims=True))
            ds = ds.astype(LOW)
            dqs.append(dot(ds, k[:, col], 1, 0) * scale)
            dks.append(dot(ds, q[:, col], 0, 0))
        dq = jnp.concatenate(dqs, axis=1)
        dv = jnp.concatenate(dvs, axis=1)
        spread = dot(pick_o[s], dq.astype(LOW), 0, 0).astype(LOW)
        dproj[at, 0:3 * heads] = jnp.concatenate(
            [spread, jnp.concatenate(dks, axis=1).astype(LOW), dv.astype(LOW)], axis=1
        )
        dproj[at, 3 * heads:] = jnp.zeros((length, heads), LOW)
        return dq_sum + row_sum(dq), dv_sum + row_sum(dv)

    zero = jnp.zeros((1, heads), F32)
    dq_sum, dv_sum = lax.fori_loop(0, seqs, attend, (zero, zero))
    dproj[count:count + total, 0:3 * heads] = jnp.zeros((total, 3 * heads), LOW)
    dproj[count:count + total, 3 * heads:] = ctxm[...].astype(LOW)
    vec[2:3, :] = jnp.concatenate([dq_sum, dv_sum, jnp.zeros((1, width - 2 * heads), F32)], axis=1)
    for j in range(0, width, 256):
        col = slice(j, j + 256)
        gattn[:, col] = dot(x[...], dproj[:, col], 0, 0)


def k1_call(x, cot, mask, lens, wqkv, wout, win, wback, gains, biases, bias_in):
    count, width = x.shape
    seqs = lens.shape[0]
    heads = wout.shape[0]
    hidden = win.shape[1]
    length = count // seqs
    total = seqs * SPAN_ROWS
    half = total // 2
    any_ = pl.BlockSpec(memory_space=pl.ANY)
    vm = pl.BlockSpec(memory_space=pltpu.VMEM)
    sm = pl.BlockSpec(memory_space=pltpu.SMEM)
    sds = jax.ShapeDtypeStruct
    out_shape = (
        sds((width, width), F32), sds((width, hidden), F32), sds((width, hidden), F32),
        sds((count + total, width), LOW),
        sds((count, heads), LOW), sds((count, heads), LOW), sds((count, heads), LOW),
        sds((seqs, SPAN_ROWS, length), LOW), sds((total, width), F32),
        sds((heads, width), F32), sds((16, width), F32),
    )
    V = pltpu.VMEM
    wide = lambda r, t=F32: V((r, width), t)
    scratch = [
        wide(count + total, LOW), wide(count, LOW), wide(3 * heads), wide(heads), V((width, hidden), F32),
        V((width, hidden), F32), wide(3 * heads, LOW), wide(heads, LOW), V((width, hidden), LOW), V((width, hidden), LOW),
        V((seqs * (heads // HD), SPAN_ROWS, length), F32), wide(total), wide(total), V((total, heads), LOW),
        V((total, heads), F32), V((total, heads), F32), wide(total), wide(total), wide(total), V((total, 1), F32),
        wide(total), wide(total, LOW), V((total, hidden), LOW), V((total, hidden), F32), wide(total), wide(half), wide(half), wide(half),
        wide(total), wide(half), wide(half), wide(half), wide(total), wide(total), wide(total), wide(total), wide(total), wide(total), wide(total),
        V((total, hidden), LOW), V((total, heads), LOW), V((8, 128), F32),
        pltpu.SemaphoreType.DMA((6,)), pltpu.SemaphoreType.DMA((2, 16)),
    ]
    return pl.pallas_call(
        k1_kernel, out_shape=out_shape,
        in_specs=[sm, vm, vm, vm, vm] + [any_] * 6,
        out_specs=(vm,) * len(out_shape),
        scratch_shapes=scratch,
        compiler_params=pltpu.CompilerParams(
            collective_id=1, has_side_effects=True, vmem_limit_bytes=60 * 2**20
        ),
    )(lens, mask, gains, biases, bias_in, x, cot, wqkv, wout, win, wback)


BETA_ONE = 0.9
BETA_TWO = 0.999
ADAM_EPS = 1e-06
WEIGHT_DECAY = 0.01


def layer_norm(values, gain, shift):
    center = values - jnp.mean(values, axis=-1, keepdims=True)
    spread = jnp.mean(center * center, axis=-1, keepdims=True)
    return center * lax.rsqrt(spread + NORM_EPS) * gain + shift


def exact_gelu(values):
    return jax.nn.gelu(values, approximate=False)


def outer_sum(left, right):
    return jnp.einsum("ta,tb->ab", left, right, preferred_element_type=jnp.float32)


def adam_step(weight, grad, moments, ratio, corr_one, corr_two, decay):
    first = BETA_ONE * moments[0] + (1.0 - BETA_ONE) * grad
    second = BETA_TWO * moments[1] + (1.0 - BETA_TWO) * grad * grad
    update = first / corr_one / (jnp.sqrt(second / corr_two) + ADAM_EPS) + decay * weight
    return (-ratio * update, jnp.stack([first, second]))


def on_device(
    tokens_in,
    cotangent,
    span_mask,
    lengths,
    step,
    warmup,
    total,
    w_qkv,
    w_out,
    w_in,
    w_back,
    gains,
    biases,
    bias_in,
    mom_qkv,
    mom_out,
    mom_in,
    mom_back,
    mom_gains,
    mom_biases,
    mom_bias_in,
):
    row_count, model_width = tokens_in.shape
    seq_count = lengths.shape[0]
    seq_length = row_count // seq_count
    head_cols = w_qkv.shape[2]
    hidden_cols = w_in.shape[1]
    head_size = HD
    local_heads = head_cols // head_size
    query_scale = 1.0 / math.sqrt(head_size)
    tensor_slot = lax.axis_index("tensor")
    bias_query = lax.dynamic_slice_in_dim(biases[0], tensor_slot * head_cols, head_cols)
    bias_value = lax.dynamic_slice_in_dim(biases[1], tensor_slot * head_cols, head_cols)
    bias_hidden = lax.dynamic_slice_in_dim(bias_in, tensor_slot * hidden_cols, hidden_cols)
    qkv_low = w_qkv.astype(jnp.bfloat16).reshape(model_width, 3 * head_cols)
    out_low = w_out.astype(jnp.bfloat16)
    in_low = w_in.astype(jnp.bfloat16)
    down_low = w_back.astype(jnp.bfloat16)
    projected = jnp.dot(tokens_in, qkv_low, preferred_element_type=jnp.float32).reshape(
        row_count, 3, head_cols
    )
    attn_shape = (seq_count, seq_length, local_heads, head_size)
    queries = (
        ((projected[:, 0] + bias_query) * query_scale).astype(jnp.bfloat16).reshape(attn_shape)
    )
    keys = projected[:, 1].astype(jnp.bfloat16).reshape(attn_shape)
    values = (projected[:, 2] + bias_value).astype(jnp.bfloat16).reshape(attn_shape)
    positions = jnp.arange(seq_length, dtype=jnp.int32)
    inside = positions[None, :] < lengths[:, None]
    key_bias = jnp.where(inside, 0.0, -1000000000.0).astype(jnp.float32)

    def score_block():
        raw = jnp.einsum("sqhd,skhd->shqk", queries, keys, preferred_element_type=jnp.float32)
        return raw + key_bias[:, None, None, :]

    scores = score_block()
    peak = jnp.max(scores, axis=-1, keepdims=True)
    log_total = peak + jnp.log(jnp.sum(jnp.exp(scores - peak), axis=-1, keepdims=True))
    probs_low = jnp.exp(scores - log_total).astype(jnp.bfloat16)
    context_low = (
        jnp.einsum("shqk,skhd->sqhd", probs_low, values, preferred_element_type=jnp.float32)
        .reshape(row_count, head_cols)
        .astype(jnp.bfloat16)
    )
    attn_part = jnp.einsum("tc,dc->td", context_low, out_low, preferred_element_type=jnp.float32)
    attn_sum = lax.psum(attn_part, "tensor")
    residual_one = tokens_in.astype(jnp.float32) + attn_sum + biases[2]
    normed = layer_norm(residual_one, gains[0], biases[3])
    normed_low = normed.astype(jnp.bfloat16)
    pre_act = jnp.dot(normed_low, in_low, preferred_element_type=jnp.float32) + bias_hidden
    act_low = exact_gelu(pre_act).astype(jnp.bfloat16)
    down_part = jnp.einsum("tf,df->td", act_low, down_low, preferred_element_type=jnp.float32)
    down_sum = lax.psum(down_part, "tensor")
    residual_two = normed + down_sum + biases[4]
    live = (inside.astype(jnp.int32) * span_mask.reshape(seq_count, seq_length)) > 0
    upto = (positions[:, None] <= positions[None, :]).astype(jnp.float32)
    rank = jnp.dot(live.astype(jnp.float32), upto).astype(jnp.int32) - 1
    slots = jnp.arange(SPAN_ROWS, dtype=jnp.int32)
    pick = (live[:, None, :] & (rank[:, None, :] == slots[None, :, None])).astype(jnp.float32)
    pick_low = pick.astype(jnp.bfloat16)

    def rows_of(values):
        width = values.shape[-1]
        return jnp.einsum(
            "srt,std->srd",
            pick,
            values.reshape(seq_count, seq_length, width),
            precision=lax.Precision.HIGHEST,
        ).reshape(seq_count * SPAN_ROWS, width)

    def low_rows_of(values):
        width = values.shape[-1]
        return jnp.einsum(
            "srt,std->srd",
            pick_low,
            values.reshape(seq_count, seq_length, width),
            preferred_element_type=jnp.bfloat16,
        ).reshape(seq_count * SPAN_ROWS, width)

    result = layer_norm(residual_two, gains[1], biases[5])
    normed_out = result.astype(jnp.bfloat16)
    wqkv_t = jnp.transpose(w_qkv, (1, 2, 0)).reshape(3 * head_cols, model_width)
    (
        grad_attn, grad_in, grad_back, d_proj, _, _, _, _, d_res_one, wp_out, vec
    ) = k1_call(
        tokens_in, cotangent, span_mask.reshape(-1, 128), lengths, wqkv_t, w_out.T, w_in, w_back,
        gains, biases, bias_in.reshape(-1, 128)
    )
    grad_qkv = grad_attn[:, :3 * head_cols].reshape(model_width, 3, head_cols)
    grad_out_proj = grad_attn[:, 3 * head_cols:]

    def spread(row_values):
        width = row_values.shape[-1]
        return jnp.einsum(
            "srt,srd->std",
            pick,
            row_values.reshape(seq_count, SPAN_ROWS, width),
            precision=lax.Precision.HIGHEST,
        ).reshape(row_count, width)

    d_entry_part = jnp.einsum("tc,dc->td", d_proj[:row_count, :3 * head_cols], qkv_low, preferred_element_type=jnp.float32)
    input_grad = lax.psum(d_entry_part, "tensor") + spread(d_res_one)
    first_rank = (tensor_slot == 0).astype(jnp.float32)
    width_zero = jnp.zeros((model_width,), jnp.float32)

    def place_heads(partial_sum):
        return lax.dynamic_update_slice_in_dim(width_zero, partial_sum, tensor_slot * head_cols, 0)

    grad_gains = vec[0:2] * first_rank
    grad_biases = jnp.stack(
        [
            place_heads(vec[2, :head_cols]),
            place_heads(vec[2, head_cols:2 * head_cols]),
            vec[3] * first_rank,
            vec[4] * first_rank,
            vec[5] * first_rank,
            vec[6] * first_rank,
        ]
    )
    grad_bias_in = lax.dynamic_update_slice_in_dim(
        jnp.zeros(bias_in.shape, jnp.float32), vec[8], tensor_slot * hidden_cols, 0
    )
    grad_gains, grad_biases, grad_bias_in = lax.psum(
        (grad_gains, grad_biases, grad_bias_in), ("dp", "tensor")
    )
    data_slot = lax.axis_index("dp")
    shard_rows = model_width // lax.axis_size("dp")
    owned = tuple(
        lax.psum_scatter(part, "dp", scatter_dimension=0, tiled=True)
        for part in (grad_qkv, grad_out_proj, 0.5 * grad_in, 0.5 * grad_back)
    )
    clock = step[0].astype(jnp.float32)
    warm = warmup[0].astype(jnp.float32)
    horizon = total[0].astype(jnp.float32)
    ratio = jnp.minimum(clock / warm, (horizon - clock) / (horizon - warm))
    corr_one = 1.0 - jnp.power(BETA_ONE, clock)
    corr_two = 1.0 - jnp.power(BETA_TWO, clock)
    change_rows = []
    fresh_moments = []
    for weight, grad_rows, moment in zip(
        (w_qkv, w_out, w_in, w_back), owned, (mom_qkv, mom_out, mom_in, mom_back)
    ):
        weight_rows = lax.dynamic_slice_in_dim(weight, data_slot * shard_rows, shard_rows, 0)
        row_change, new_moment = adam_step(
            weight_rows, grad_rows, moment, ratio, corr_one, corr_two, WEIGHT_DECAY
        )
        change_rows.append(row_change)
        fresh_moments.append(new_moment)
    change_qkv, change_out_proj, change_in_proj, change_back_proj = (
        lax.all_gather(change_rows[0], "dp", axis=0, tiled=True),
        lax.all_gather(change_rows[1], "dp", axis=0, tiled=True),
        lax.all_gather(change_rows[2], "dp", axis=0, tiled=True),
        lax.all_gather(change_rows[3], "dp", axis=0, tiled=True),
    )
    change_gains, new_mom_gains = adam_step(
        gains, grad_gains, mom_gains, ratio, corr_one, corr_two, 0.0
    )
    change_biases, new_mom_biases = adam_step(
        biases, grad_biases, mom_biases, ratio, corr_one, corr_two, 0.0
    )
    change_bias_in, new_mom_bias_in = adam_step(
        bias_in, grad_bias_in, mom_bias_in, ratio, corr_one, corr_two, 0.0
    )
    return (
        normed_out,
        input_grad,
        change_qkv,
        change_out_proj,
        change_in_proj,
        change_back_proj,
        change_gains,
        change_biases,
        change_bias_in,
        fresh_moments[0],
        fresh_moments[1],
        fresh_moments[2],
        fresh_moments[3],
        new_mom_gains,
        new_mom_biases,
        new_mom_bias_in,
    )


def solution(mesh):
    in_specs = (
        P("dp", None),
        P("dp", None),
        P("dp"),
        P("dp"),
        P(),
        P(),
        P(),
        P(None, None, "tensor"),
        P(None, "tensor"),
        P(None, "tensor"),
        P(None, "tensor"),
        P(),
        P(),
        P(),
        P(None, "dp", None, "tensor"),
        P(None, "dp", "tensor"),
        P(None, "dp", "tensor"),
        P(None, "dp", "tensor"),
        P(),
        P(),
        P(),
    )
    out_specs = (
        P("dp", None),
        P("dp", None),
        P(None, None, "tensor"),
        P(None, "tensor"),
        P(None, "tensor"),
        P(None, "tensor"),
        P(),
        P(),
        P(),
        P(None, "dp", None, "tensor"),
        P(None, "dp", "tensor"),
        P(None, "dp", "tensor"),
        P(None, "dp", "tensor"),
        P(),
        P(),
        P(),
    )
    return jax.shard_map(
        on_device, mesh=mesh, in_specs=in_specs, out_specs=out_specs, check_vma=False
    )
```

```python
import math

import jax
import jax.numpy as jnp
from jax import lax
from jax.experimental import pallas as pl
from jax.experimental.pallas import tpu as pltpu
from jax.sharding import PartitionSpec as P

HD = 64
SPAN_ROWS = 80
NORM_EPS = 1e-12
MESH = pl.DeviceIdType.MESH
F32 = jnp.float32
LOW = jnp.bfloat16


def dot(left, right, left_dim, right_dim):
    return lax.dot_general(
        left, right, (((left_dim,), (right_dim,)), ((), ())), preferred_element_type=F32
    )


def normalize(rows):
    center = rows - jnp.mean(rows, axis=-1, keepdims=True)
    scale = lax.rsqrt(jnp.mean(center * center, axis=-1, keepdims=True) + NORM_EPS)
    return center * scale, scale


def norm_back(grad, gain, unit, scale):
    weighted = grad * gain
    return scale * (
        weighted
        - jnp.mean(weighted, axis=-1, keepdims=True)
        - unit * jnp.mean(weighted * unit, axis=-1, keepdims=True)
    )


def row_sum(rows):
    return jnp.sum(rows, axis=0, keepdims=True)


class Peers:
    def __init__(self):
        self.d = lax.axis_index("dp")
        self.t = lax.axis_index("tensor")
        self.b = lax.rem(self.d, 2)
        self.c = lax.rem(self.t, 2)
        self.p = lax.div(self.t, 2)
        self.u = lax.div(self.d, 2)
        self.core = (self.d, self.t + 1 - 2 * self.c)
        self.y = (self.d, lax.rem(self.t + 2, 4))
        self.x = (self.d + 1 - 2 * self.b, self.t)


def send(src, dst, sems, k, peer):
    copy = pltpu.make_async_remote_copy(
        src_ref=src, dst_ref=dst, send_sem=sems.at[0, k], recv_sem=sems.at[1, k],
        device_id=peer, device_id_type=MESH,
    )
    copy.start()
    return copy


def local(src, dst, sem):
    copy = pltpu.make_async_copy(src, dst, sem)
    copy.start()
    return copy


def greet(peers):
    barrier = pltpu.get_barrier_semaphore()
    for peer in peers:
        pl.semaphore_signal(barrier, inc=1, device_id=peer, device_id_type=MESH)
    pl.semaphore_wait(barrier, len(peers))


def gelu_parts(pre):
    cdf = 0.5 * (1.0 + lax.erf(pre * (1.0 / math.sqrt(2.0))))
    pdf = jnp.exp(-0.5 * pre * pre) * (1.0 / math.sqrt(2.0 * math.pi))
    return pre * cdf, cdf + pre * pdf


def k1_kernel(
    lens, mask, gains, biases, bias_in, x_h, cot_h, wqkv_h, wout_h, win_h, wback_h,
    gattn, gin, gback, dproj, ctx_o, pick_o, dres1_o, wal, wpl, wil, wbl, pil, pbl, vec,
    x, cot, wqkv, wout, win, wback, wp_qkv, wp_out, pwin, pwback, q_o, k_o, v_o,
    pm, xm, cotm, qm, ctxm, ctxp, ap, apc, unit1, rs1, normed, nlow, act, gp, part, rc1, h1, ry1,
    part2, rc2, h2, ry2, full2, full, dres2, d2w, d2x, nxw, nxx, dplow, dctx,
    lsem, rsem,
):
    seqs, rows = 3, SPAN_ROWS
    count = x_h.shape[0]
    length = count // seqs
    total = seqs * rows
    half = total // 2
    heads = ctx_o.shape[1]
    n_heads = heads // HD
    width = x_h.shape[1]
    me = Peers()

    loads = [
        local(x_h, x.at[pl.ds(0, count)], lsem.at[0]),
        local(wqkv_h, wqkv, lsem.at[1]),
        local(wout_h, wout, lsem.at[2]),
        local(win_h, win, lsem.at[3]),
        local(wback_h, wback, lsem.at[4]),
        local(cot_h, cot, lsem.at[5]),
    ]
    greet((me.core, me.y, me.x))

    loads[2].wait()
    out_half = pl.ds(pl.multiple_of(me.b * (heads // 2), 8), heads // 2)
    wo_y = send(wout.at[out_half], wp_out.at[out_half], rsem, 0, me.y)
    loads[1].wait()
    wal[0:3 * heads, :] = wqkv[...].astype(LOW)
    wal[3 * heads:, :] = wout[...].astype(LOW)

    def pick_bias(row, k=heads):
        out = jnp.zeros((1, k), F32)
        for slot in range(4):
            piece = biases[row:row + 1, slot * k:(slot + 1) * k]
            out = jnp.where(me.t == slot, piece, out)
        return out

    bias_q, bias_v = pick_bias(0), pick_bias(1)
    hidden = win.shape[1]
    lanes = 128
    bias_h = jnp.concatenate(
        [bias_in[pl.ds(me.t * (hidden // lanes) + j, 1), :] for j in range(hidden // lanes)], axis=1
    )
    upto = (
        lax.broadcasted_iota(jnp.int32, (length, length), 0)
        <= lax.broadcasted_iota(jnp.int32, (length, length), 1)
    ).astype(F32).astype(LOW)
    position = lax.broadcasted_iota(jnp.int32, (1, length), 1)
    slot_of = lax.broadcasted_iota(jnp.int32, (rows, length), 0).astype(F32)
    scale = 1.0 / math.sqrt(HD)
    loads[0].wait()

    def project(s, _):
        at = pl.ds(pl.multiple_of(s * length, length), length)
        xs = x[at, :]
        q = ((dot(xs, wal[0:heads, :], 1, 1) + bias_q) * scale).astype(LOW)
        k = dot(xs, wal[heads:2 * heads, :], 1, 1).astype(LOW)
        v = (dot(xs, wal[2 * heads:3 * heads, :], 1, 1) + bias_v).astype(LOW)
        q_o[at, :] = q
        k_o[at, :] = k
        v_o[at, :] = v
        parts = length // lanes
        marks = jnp.concatenate([mask[pl.ds(s * parts + j, 1), :] for j in range(parts)], axis=1)
        inside = position < lens[s]
        live = jnp.where(inside, marks, 0).astype(F32)
        rank = dot(jnp.broadcast_to(live, (8, length)).astype(LOW), upto, 1, 0)[0:1] - 1.0
        pick = jnp.where((rank == slot_of) & (live > 0.0), 1.0, 0.0).astype(LOW)
        pick_o[s] = pick
        here = pl.ds(pl.multiple_of(s * rows, rows), rows)
        xm[here, :] = dot(pick, xs, 1, 0)
        qrow = dot(pick, q, 1, 0).astype(LOW)
        qm[here, :] = qrow
        key_bias = jnp.where(inside, 0.0, -1000000000.0)
        pieces = []
        for h in range(n_heads):
            col = slice(h * HD, (h + 1) * HD)
            scores = dot(qrow[:, col], k[:, col], 1, 1) + key_bias
            e = jnp.exp(scores - jnp.max(scores, axis=-1, keepdims=True))
            prob = e / jnp.sum(e, axis=-1, keepdims=True)
            pm[s * n_heads + h] = prob
            pieces.append(dot(prob.astype(LOW), v[:, col], 1, 0))
        ctxm[here, :] = jnp.concatenate(pieces, axis=1).astype(LOW).astype(F32)
        return 0

    lax.fori_loop(0, seqs, project, 0)
    ctx_y = send(ctxm, ctxp, rsem, 1, me.y)
    wo_y.wait()
    wo_x = send(wp_out.at[out_half], wp_out.at[out_half], rsem, 2, me.x)
    third = heads // 2

    def qkv_part(k):
        return pl.ds(pl.multiple_of(me.b * (3 * third) + k * third, 8), third)

    def fetch(k):
        return send(wqkv.at[qkv_part(k)], wp_qkv.at[qkv_part(k)], rsem, 16 + k, me.y)

    def swap(k):
        return send(wp_qkv.at[qkv_part(k)], wp_qkv.at[qkv_part(k)], rsem, 19 + k, me.x)

    def attend_all(s):
        at = slice(s * length, (s + 1) * length)
        key_bias = jnp.where(position < lens[s], 0.0, -1000000000.0)
        pieces = []
        for h in range(n_heads):
            col = slice(h * HD, (h + 1) * HD)
            scores = dot(q_o[at, col], k_o[at, col], 1, 1) + key_bias
            e = jnp.exp(scores - jnp.max(scores, axis=-1, keepdims=True))
            prob = (e / jnp.sum(e, axis=-1, keepdims=True)).astype(LOW)
            pieces.append(dot(prob, v_o[at, col], 1, 0))
        ctx_o[at, :] = jnp.concatenate(pieces, axis=1).astype(LOW)

    part1 = dot(ctxm[...].astype(LOW), wal[3 * heads:, :], 1, 0)
    for load in loads[3:5]:
        load.wait()
    wil[...] = win[...].astype(LOW)
    wbl[...] = wback[...].astype(LOW)
    loads[5].wait()
    for s in range(seqs):
        cotm[s * rows:(s + 1) * rows, :] = dot(pick_o[s], cot[s * length:(s + 1) * length, :], 1, 0)
    wo_x.wait()
    ctx_y.wait()
    ap[...] = part1 + dot(ctxp[...].astype(LOW), wp_out[...].astype(LOW), 1, 0)
    ap_c = send(ap, apc, rsem, 3, me.core)
    wq_y = [fetch(0)]
    ap_c.wait()
    unit, inv = normalize(xm[...] + (ap[...] + apc[...]) + biases[2:3, :])
    unit1[...] = unit
    rs1[...] = inv
    normed[...] = unit * gains[0:1, :] + biases[3:4, :]
    nlow[...] = normed[...].astype(LOW)
    nxw[...] = nlow[...].astype(F32)
    mine = pl.ds(pl.multiple_of(me.c * half, 8), half)
    other = pl.ds(pl.multiple_of((1 - me.c) * half, 8), half)
    nx_x = send(nxw.at[mine], nxx.at[mine], rsem, 5, me.x)
    for j in range(0, hidden, 256):
        col = slice(j, j + 256)
        a, g = gelu_parts(dot(nlow[...], wil[:, col], 1, 0) + bias_h[:, col])
        act[:, col] = a.astype(LOW)
        gp[:, col] = g
    part[...] = dot(act[...], wbl[...], 1, 1)

    def all_reduce(src, rc, hs, ry, dst, base, fill):
        first = send(src.at[other], rc, rsem, base, me.core)
        first.wait()
        hs[...] = src[mine, :] + rc[...]
        second = send(hs, ry, rsem, base + 1, me.y)
        fill()
        second.wait()
        dst[mine, :] = hs[...] + ry[...]
        third = send(dst.at[mine], dst.at[mine], rsem, base + 2, me.core)
        third.wait()

    relay = []

    swaps = []

    def fill_one():
        wide.append(send(win, pwin, rsem, 22, me.core))
        attend_all(0)
        attend_all(1)
        nx_x.wait()
        relay.append(send(nxx.at[mine], nxx.at[mine], rsem, 6, me.core))

    wide = []
    all_reduce(part, rc1, h1, ry1, full, 7, fill_one)
    wq_y.append(fetch(1))
    wq_y[0].wait()
    relay[0].wait()
    unit, inv = normalize(normed[...] + full[...] + biases[4:5, :])
    grad = cotm[...]
    d_two = norm_back(grad, gains[1:2, :], unit, inv)
    dres2[...] = d_two
    vec[...] = jnp.zeros(vec.shape, F32)
    vec[1:2, :] = row_sum(grad * unit)
    vec[5:6, :] = row_sum(d_two)
    vec[6:7, :] = row_sum(grad)
    d2w[...] = d_two.astype(LOW).astype(F32)
    d2_x = send(d2w.at[mine], d2x.at[mine], rsem, 10, me.x)
    swaps.append(swap(0))
    d2low = d2w[...].astype(LOW)
    for j in range(0, hidden, 256):
        col = slice(j, j + 256)
        d_pre = dot(d2low, wbl[:, col], 1, 0) * gp[:, col]
        vec[8:9, col] = row_sum(d_pre)
        dplow[0:total, col] = d_pre.astype(LOW)
    part2[...] = dot(dplow[0:total, :], wil[...], 1, 1)

    def fill_two():
        wide.append(send(wback, pwback, rsem, 23, me.core))
        attend_all(2)
        for j in range(0, hidden, 256):
            col = slice(j, j + 256)
            gin[:, col] = dot(nlow[...], dplow[0:total, col], 0, 0)
            gback[:, col] = dot(d2low, act[:, col], 0, 0)
        d2_x.wait()
        relay.append(send(d2x.at[mine], d2x.at[mine], rsem, 11, me.core))

    all_reduce(part2, rc2, h2, ry2, full2, 12, fill_two)
    wq_y.append(fetch(2))
    wq_y[1].wait()
    swaps.append(swap(1))
    d_normed = full2[...] + dres2[...]
    unit = unit1[...]
    d_one = norm_back(d_normed, gains[0:1, :], unit, rs1[...])
    dres1_o[...] = d_one
    vec[0:1, :] = row_sum(d_normed * unit)
    vec[3:4, :] = row_sum(d_one)
    vec[4:5, :] = row_sum(d_normed)
    d1low = d_one.astype(LOW)
    x[count:count + total, :] = d1low
    dctx[...] = dot(d1low, wal[3 * heads:, :], 1, 1).astype(LOW)
    relay[1].wait()
    nlx = nxx[...].astype(LOW)
    dlx = d2x[...].astype(LOW)
    for j in range(0, hidden, 256):
        col = slice(j, j + 256)
        a, g = gelu_parts(dot(nlx, wil[:, col], 1, 0) + bias_h[:, col])
        d_pre = (dot(dlx, wbl[:, col], 1, 0) * g).astype(LOW)
        gin[:, col] += dot(nlx, d_pre, 0, 0)
        gback[:, col] += dot(dlx, a.astype(LOW), 0, 0)

    def attend(s, carry):
        dq_sum, dv_sum = carry
        at = pl.ds(pl.multiple_of(s * length, length), length)
        here = pl.ds(pl.multiple_of(s * rows, rows), rows)
        q, k, v, dc = qm[here, :], k_o[at, :], v_o[at, :], dctx[here, :]
        dqs, dks, dvs = [], [], []
        for h in range(n_heads):
            col = slice(h * HD, (h + 1) * HD)
            prob = pm[s * n_heads + h]
            d_prob = dot(dc[:, col], v[:, col], 1, 1)
            dvs.append(dot(prob.astype(LOW), dc[:, col], 0, 0))
            ds = prob * (d_prob - jnp.sum(prob * d_prob, axis=-1, keepdims=True))
            ds = ds.astype(LOW)
            dqs.append(dot(ds, k[:, col], 1, 0) * scale)
            dks.append(dot(ds, q[:, col], 0, 0))
        dq = jnp.concatenate(dqs, axis=1)
        dv = jnp.concatenate(dvs, axis=1)
        spread = dot(pick_o[s], dq.astype(LOW), 0, 0).astype(LOW)
        dproj[at, 0:3 * heads] = jnp.concatenate(
            [spread, jnp.concatenate(dks, axis=1).astype(LOW), dv.astype(LOW)], axis=1
        )
        dproj[at, 3 * heads:] = jnp.zeros((length, heads), LOW)
        return dq_sum + row_sum(dq), dv_sum + row_sum(dv)

    zero = jnp.zeros((1, heads), F32)
    dq_sum, dv_sum = lax.fori_loop(0, seqs, attend, (zero, zero))
    dproj[count:count + total, 0:3 * heads] = jnp.zeros((total, 3 * heads), LOW)
    dproj[count:count + total, 3 * heads:] = ctxm[...].astype(LOW)
    vec[2:3, :] = jnp.concatenate([dq_sum, dv_sum, jnp.zeros((1, width - 2 * heads), F32)], axis=1)
    for j in range(0, width, 256):
        col = slice(j, j + 256)
        gattn[:, col] = dot(x[...], dproj[:, col], 0, 0)
    wq_y[2].wait()
    swaps.append(swap(2))
    for copy in wide + swaps:
        copy.wait()
    pil[...] = pwin[...].astype(LOW)
    pbl[...] = pwback[...].astype(LOW)
    wpl[0:3 * heads, :] = wp_qkv[...].astype(LOW)
    wpl[3 * heads:, :] = wp_out[...].astype(LOW)


def k1_call(x, cot, mask, lens, wqkv, wout, win, wback, gains, biases, bias_in):
    count, width = x.shape
    seqs = lens.shape[0]
    heads = wout.shape[0]
    hidden = win.shape[1]
    length = count // seqs
    total = seqs * SPAN_ROWS
    half = total // 2
    any_ = pl.BlockSpec(memory_space=pl.ANY)
    vm = pl.BlockSpec(memory_space=pltpu.VMEM)
    sm = pl.BlockSpec(memory_space=pltpu.SMEM)
    sds = jax.ShapeDtypeStruct
    out_shape = (
        sds((width, width), F32), sds((width, hidden), F32), sds((width, hidden), F32),
        sds((count + total, width), LOW),
        sds((count, heads), LOW), sds((seqs, SPAN_ROWS, length), LOW), sds((total, width), F32),
        sds((4 * heads, width), LOW), sds((4 * heads, width), LOW), sds((width, hidden), LOW), sds((width, hidden), LOW),
        sds((width, hidden), LOW), sds((width, hidden), LOW), sds((16, width), F32),
    )
    V = pltpu.VMEM
    wide = lambda r, t=F32: V((r, width), t)
    scratch = [
        wide(count + total, LOW), wide(count, LOW), wide(3 * heads), wide(heads), V((width, hidden), F32),
        V((width, hidden), F32), wide(3 * heads), wide(heads), V((width, hidden), F32), V((width, hidden), F32),
        V((count, heads), LOW), V((count, heads), LOW), V((count, heads), LOW),
        V((seqs * (heads // HD), SPAN_ROWS, length), F32), wide(total), wide(total), V((total, heads), LOW),
        V((total, heads), F32), V((total, heads), F32), wide(total), wide(total), wide(total), V((total, 1), F32),
        wide(total), wide(total, LOW), V((total, hidden), LOW), V((total, hidden), F32), wide(total), wide(half), wide(half), wide(half),
        wide(total), wide(half), wide(half), wide(half), wide(total), wide(total), wide(total), wide(total), wide(total), wide(total), wide(total),
        V((total, hidden), LOW), V((total, heads), LOW),
        pltpu.SemaphoreType.DMA((6,)), pltpu.SemaphoreType.DMA((2, 24)),
    ]
    return pl.pallas_call(
        k1_kernel, out_shape=out_shape,
        in_specs=[sm, vm, vm, vm, vm] + [any_] * 6,
        out_specs=(vm,) * len(out_shape),
        scratch_shapes=scratch,
        compiler_params=pltpu.CompilerParams(
            collective_id=1, has_side_effects=True, vmem_limit_bytes=60 * 2**20
        ),
    )(lens, mask, gains, biases, bias_in, x, cot, wqkv, wout, win, wback)


BETA_ONE = 0.9
BETA_TWO = 0.999
ADAM_EPS = 1e-06
WEIGHT_DECAY = 0.01


def adam(weight, grad, first, second, ratio, corr_one, corr_two, decay):
    first = BETA_ONE * first + (1.0 - BETA_ONE) * grad
    second = BETA_TWO * second + (1.0 - BETA_TWO) * grad * grad
    update = first / corr_one / (jnp.sqrt(second / corr_two) + ADAM_EPS) + decay * weight
    return -ratio * update, first, second


class Net:
    def __init__(self):
        self.sent = []

    def start(self, make, when=None):
        self.sent.append((make, when))
        self.run(lambda: make().start(), when)

    @staticmethod
    def run(do, when):
        if when is None:
            do()
        else:
            pl.when(when)(do)

    def drain(self):
        for make, when in self.sent:
            self.run(lambda make=make: make().wait_send(), when)


def k2_kernel(
    lens, step, warmup, horizon, gains, biases, bias_in, mom_g, mom_b, mom_h, vec,
    x_h, gattn_h, gin_h, gback_h, dproj_h, ctx_h, pick_h, dres_h, wal_h, wpl_h, wil_h, wbl_h, pil_h, pbl_h,
    wqkv_h, wout_h, win_h, wback_h, mq_h, mo_h, mi_h, mb_h,
    out_h, grad_h, cq_h, co_h, ci_h, cb_h, nmq_h, nmo_h, nmi_h, nmb_h,
    ch_g, ch_b, ch_h, nm_g, nm_b, nm_h,
    x, ga, gi, gb, dproj, ctx, pick, dres, wal, wpl, wil, wbl, pil, pbl,
    wrow_i, wrow_b, wrow_a, mq, mo, mi, mb, turned, flip,
    qp, kp, vp, ctxp, dpp, sbuf, rbuf, nrm, dsc, rdn, fin, rig,
    ring, xr, ca, own, v1, vx, vz, vt,
    lsem, rs_s, rs_r, ag_s, ag_r, ax_s, ax_r, xs_s, xs_r, vs_s, vs_r, sd_s, sd_r, osem,
):
    me = Peers()
    n_u = ring.shape[2] + 1
    seqs = sbuf.shape[0]
    count, width = x.shape
    length = count // seqs
    rows = SPAN_ROWS
    heads = ctx.shape[1]
    n_heads = heads // HD
    shard = gi.shape[1]
    hidden = wil.shape[1]
    half = length // 2
    quarter = length // 4
    net = Net()
    z, b = me.u, me.b
    right = (me.d + 2, me.t)
    left = (me.d - 2, me.t)
    diag = (me.d, 3 - me.t)

    def remote(src, dst, ss, rr, peer):
        return pltpu.make_async_remote_copy(
            src_ref=src, dst_ref=dst, send_sem=ss, recv_sem=rr, device_id=peer, device_id_type=MESH
        )

    pend = {}
    order = iter(range(64))

    def fetch(name, src, dst):
        copy = pltpu.make_async_copy(src, dst, lsem.at[next(order)])
        copy.start()
        pend.setdefault(name, []).append(copy)

    def ready(*names):
        for name in names:
            for copy in pend.pop(name, []):
                copy.wait()

    for u in range(n_u):
        fetch("gi", gin_h.at[2 * u + b], gi.at[u])
    fetch("ga", gattn_h, ga)
    fetch("x", x_h, x)
    fetch("wpl", wpl_h, wpl)
    fetch("wal", wal_h, wal)
    fetch("ctx", ctx_h, ctx)
    fetch("pick", pick_h, pick)
    fetch("dres", dres_h, dres)
    for u in range(n_u):
        fetch("gb", gback_h.at[2 * u + b], gb.at[u])
    fetch("low", wil_h, wil)
    fetch("low", wbl_h, wbl)
    fetch("low", pil_h, pil)
    fetch("low", pbl_h, pbl)
    fetch("dproj", dproj_h, dproj)
    mine = pl.ds(pl.multiple_of(me.d * shard, 8), shard)
    fetch("mi", win_h.at[mine], wrow_i)
    fetch("mi", mi_h, mi)
    fetch("mb", wback_h.at[mine], wrow_b)
    fetch("mb", mb_h, mb)
    fetch("ma", wqkv_h, turned.at[pl.ds(0, 3 * heads)])
    fetch("ma", wout_h, turned.at[pl.ds(3 * heads, heads)])
    fetch("ma", mq_h, mq)
    fetch("ma", mo_h, mo)

    others = [(2 * lax.rem(z + k, n_u) + b, me.t) for k in range(1, n_u)]
    greet([me.core, me.y, diag, me.x] + others)

    g_of = {0: gi, 1: gb}

    def g_at(ch, u):
        return ga.at[2 * u + b] if ch == 2 else g_of[ch].at[u]

    def ring_copy(ch, way, s, src):
        peer = right if way == 0 else left
        return remote(src, ring.at[ch, way, s], rs_s.at[ch, way, s], rs_r.at[ch, way, s], peer)

    def reduce_step(ch, s):
        for way, place in ((0, z), (1, n_u - 1 - z)):
            active = place <= s
            d = (n_u - 1 - s + z) if way == 0 else (s - (n_u - 1 - z))
            if s > 0:
                def gather_in(way=way, d=d):
                    ring_copy(ch, way, s - 1, ring.at[ch, way, s - 1]).wait_recv()
                    g_at(ch, d)[...] += ring[ch, way, s - 1]
                pl.when(active & (place > 0))(gather_in)
            net.start(lambda way=way, d=d: ring_copy(ch, way, s, g_at(ch, d)), active)

    def reduce_end(ch):
        last = n_u - 2
        for way, place in ((0, z), (1, n_u - 1 - z)):
            def gather_in(way=way):
                ring_copy(ch, way, last, ring.at[ch, way, last]).wait_recv()
                g_at(ch, z)[...] += ring[ch, way, last]
            pl.when(place > 0)(gather_in)

    clock = jnp.full((1, 128), step[0].astype(F32))
    warm = jnp.full((1, 128), warmup[0].astype(F32))
    far = jnp.full((1, 128), horizon[0].astype(F32))
    ratio = jnp.minimum(clock / warm, (far - clock) / (far - warm))[:, 0:1]
    corr_one = (1.0 - jnp.exp(clock * math.log(0.9)))[:, 0:1]
    corr_two = (1.0 - jnp.exp(clock * math.log(0.999)))[:, 0:1]

    def target(ch, d):
        return ca.at[d] if ch == 2 else (ci_h, cb_h)[ch].at[d]

    def update(ch):
        if ch < 2:
            w, m = ((wrow_i, mi), (wrow_b, mb))[ch]
            change, first, second = adam(
                w[...], g_at(ch, z)[...], m[0], m[1], ratio, corr_one, corr_two, WEIGHT_DECAY
            )
            own[ch] = change
            m[0], m[1] = first, second
            fetch("out", m, (nmi_h, nmb_h)[ch])
            fetch("out", own.at[ch], target(ch, me.d))
        else:
            for k in range(4):
                col = slice(k * heads, (k + 1) * heads)
                old = (mq[0, k], mq[1, k]) if k < 3 else (mo[0], mo[1])
                change, first, second = adam(
                    wrow_a[:, col], ga[me.d][:, col], *old, ratio, corr_one, corr_two, WEIGHT_DECAY
                )
                own[2, :, col] = change
                if k < 3:
                    mq[0, k], mq[1, k] = first, second
                else:
                    mo[0], mo[1] = first, second
            ca[me.d] = own[2]
            fetch("out", mq, nmq_h)
            fetch("out", mo, nmo_h)

    def ag_copy(ch, way, s, src, u):
        peer = right if way == 0 else left
        return remote(src, target(ch, 2 * u + b), ag_s.at[ch, way, s], ag_r.at[ch, way, s], peer)

    def ax_copy(ch, k, src, u, parity):
        return remote(src, target(ch, 2 * u + parity), ax_s.at[ch, k], ax_r.at[ch, k], me.x)

    def gather_step(ch, s):
        for way in (0, 1):
            u = z - s if way == 0 else z + s
            edge = z < n_u - 1 if way == 0 else z > 0
            if s == 0:
                net.start(lambda way=way: ag_copy(ch, way, 0, own.at[ch], z), edge)
                continue
            here = u >= 0 if way == 0 else u <= n_u - 1
            pl.when(here)(lambda way=way, u=u: ag_copy(ch, way, s - 1, target(ch, 2 * u + b), u).wait_recv())
            if s <= n_u - 2:
                net.start(lambda way=way, u=u: ag_copy(ch, way, s, target(ch, 2 * u + b), u), here & edge)
            k = s if way == 0 else n_u - 1 + s
            net.start(lambda k=k, u=u: ax_copy(ch, k, target(ch, 2 * u + b), u, b), here)
        if s == 0:
            net.start(lambda: ax_copy(ch, 0, own.at[ch], z, b))

    def gather_end(ch):
        ax_copy(ch, 0, own.at[ch], z, 1 - b).wait_recv()
        for s in range(1, n_u):
            for k, u, here in ((s, z - s, z >= s), (n_u - 1 + s, z + s, z + s <= n_u - 1)):
                pl.when(here)(lambda k=k, u=u: ax_copy(ch, k, target(ch, 2 * u + 1 - b), u, 1 - b).wait_recv())

    def xswap(u):
        return remote(ga.at[2 * u + 1 - b], xr.at[u], xs_s.at[u], xs_r.at[u], me.x)

    def xswap_end():
        for u in range(n_u):
            xswap(u).wait_recv()
            ga[2 * u + b] += xr[u]

    def vec_x():
        return remote(vec, vx, vs_s.at[0], vs_r.at[0], me.x)

    def vec_z(k):
        peer = (2 * lax.rem(z + k, n_u) + b, me.t)
        return remote(v1, vz.at[z], vs_s.at[k], vs_r.at[k], peer)

    def vec_t(k, peer):
        return remote(v1, vt.at[me.t], vs_s.at[n_u + k], vs_r.at[n_u + k], peer)

    trio = (me.core, me.y, diag)

    def vectors_one():
        vec_x().wait_recv()
        v1[...] = vec[...] + vx[...]
        vz[z] = v1[...]
        for k in range(1, n_u):
            vec_z(k).start()

    def vectors_two():
        for k in range(1, n_u):
            vec_z(k).wait()
        total = vz[0]
        for u in range(1, n_u):
            total = total + vz[u]
        v1[...] = total
        vt[me.t] = total
        for k, peer in enumerate(trio):
            vec_t(k, peer).start()

    def vectors_three():
        for k, peer in enumerate(trio):
            vec_t(k, peer).wait()
        common = vt[0]
        put = (ratio, corr_one, corr_two, 0.0)
        ch_g[...], nm_g[0], nm_g[1] = adam(gains[...], common[0:2], mom_g[0], mom_g[1], *put)
        query = jnp.concatenate([vt[k][2:3, 0:heads] for k in range(4)], axis=1)
        value = jnp.concatenate([vt[k][2:3, heads:2 * heads] for k in range(4)], axis=1)
        grad = jnp.concatenate([query, value, common[3:7]], axis=0)
        ch_b[...], nm_b[0], nm_b[1] = adam(biases[...], grad, mom_b[0], mom_b[1], *put)
        grad = jnp.concatenate([vt[k][8:9, :] for k in range(4)], axis=0)
        bias = jnp.concatenate([hidden_bias(k) for k in range(4)], axis=0)
        ch_h[...], nm_h[0], nm_h[1] = adam(bias, grad, mom_h[0], mom_h[1], *put)

    lanes = 128

    def hidden_bias(slot):
        parts = hidden // lanes
        return jnp.concatenate([bias_in[pl.ds(slot * parts + j, 1), :] for j in range(parts)], axis=1)

    twin = lax.rem(me.t + 2, 4)

    def pick_bias(row):
        out = jnp.zeros((1, heads), F32)
        for slot in range(4):
            out = jnp.where(twin == slot, biases[row:row + 1, slot * heads:(slot + 1) * heads], out)
        return out

    scale = 1.0 / math.sqrt(HD)
    position = lax.broadcasted_iota(jnp.int32, (1, length), 1)
    my_half = pl.ds(pl.multiple_of(me.c * half, 8), half)
    its_half = pl.ds(pl.multiple_of((1 - me.c) * half, 8), half)
    my_quarter = pl.ds(pl.multiple_of(me.p * quarter, 8), quarter)
    its_quarter = pl.ds(pl.multiple_of((1 - me.p) * quarter, 8), quarter)

    def at(s, start=0, size=None):
        return pl.ds(pl.multiple_of(s * length + start, 8), size or length)

    def key_bias(s):
        return jnp.where(position < lens[s], 0.0, -1000000000.0)

    def project(s):
        xs = x[at(s), :]
        qp[...] = ((dot(xs, wpl[0:heads, :], 1, 1) + pick_bias(0)) * scale).astype(LOW)
        kp[...] = dot(xs, wpl[heads:2 * heads, :], 1, 1).astype(LOW)
        vp[...] = (dot(xs, wpl[2 * heads:3 * heads, :], 1, 1) + pick_bias(1)).astype(LOW)

    def attend_all(s):
        pieces = []
        for h in range(n_heads):
            col = slice(h * HD, (h + 1) * HD)
            e = dot(qp[:, col], kp[:, col], 1, 1) + key_bias(s)
            e = jnp.exp(e - jnp.max(e, axis=-1, keepdims=True))
            prob = (e / jnp.sum(e, axis=-1, keepdims=True)).astype(LOW)
            pieces.append(dot(prob, vp[:, col], 1, 0))
        ctxp[...] = jnp.concatenate(pieces, axis=1).astype(LOW)

    def mix_copy(s):
        return remote(sbuf.at[s], rbuf.at[s], sd_s.at[s], sd_r.at[s], me.core)

    def mix(s):
        for where, into in ((its_half, sbuf), (my_half, nrm)):
            base = at(s, where.start, half)
            into[s] = dot(ctx[base, :], wal[3 * heads:, :], 1, 0) + dot(ctxp[where, :], wpl[3 * heads:, :], 1, 0)
        mix_copy(s).start()

    def down_copy(s):
        return remote(dsc.at[s, its_quarter], rdn.at[s], sd_s.at[seqs + s], sd_r.at[seqs + s], me.y)

    def feed(s):
        mix_copy(s).wait()
        base = at(s, me.c * half, half)
        unit, _ = normalize(x[base, :].astype(F32) + (nrm[s] + rbuf[s]) + biases[2:3, :])
        normed = unit * gains[0:1, :] + biases[3:4, :]
        nrm[s] = normed
        low = normed.astype(LOW)
        total = jnp.zeros((half, width), F32)
        for w_in, w_back, slot in ((wil, wbl, me.t), (pil, pbl, me.t + 1 - 2 * me.c)):
            bias = hidden_bias(slot)
            for j in range(0, hidden, 256):
                col = slice(j, j + 256)
                pre = dot(low, w_in[:, col], 1, 0) + bias[:, col]
                act = pre * (0.5 * (1.0 + lax.erf(pre * (1.0 / math.sqrt(2.0)))))
                total = total + dot(act.astype(LOW), w_back[:, col], 1, 1)
        dsc[s] = total
        down_copy(s).start()

    def out_rows(s, p):
        return at(s, me.c * half + p * quarter, quarter)

    def out_copy(s, k, p, peer):
        src = fin.at[s] if k < 2 else out_h.at[out_rows(s, p)]
        return remote(src, out_h.at[out_rows(s, me.p if k < 2 else p)], sd_s.at[(2 + k) * seqs + s], sd_r.at[(2 + k) * seqs + s], peer)

    def finish(s):
        down_copy(s).wait()
        res = nrm[s, my_quarter] + (dsc[s, my_quarter] + rdn[s]) + biases[4:5, :]
        unit, _ = normalize(res)
        fin[s] = (unit * gains[1:2, :] + biases[5:6, :]).astype(LOW).astype(F32)
        fetch("out", fin.at[s], out_h.at[out_rows(s, me.p)])
        out_copy(s, 0, me.p, me.y).start()
        out_copy(s, 1, me.p, me.core).start()

    def relay(s):
        out_copy(s, 0, me.p, me.y).wait()
        out_copy(s, 2, 1 - me.p, me.core).start()

    def relay_end(s):
        out_copy(s, 1, me.p, me.core).wait()
        out_copy(s, 2, 1 - me.p, me.core).wait()

    def back(s):
        here = pl.ds(s * rows, rows)
        q = dot(pick[s], qp[...], 1, 0).astype(LOW)
        dc = dot(dres[here, :].astype(LOW), wpl[3 * heads:, :], 1, 1).astype(LOW)
        dqs, dks, dvs = [], [], []
        for h in range(n_heads):
            col = slice(h * HD, (h + 1) * HD)
            scores = dot(q[:, col], kp[:, col], 1, 1) + key_bias(s)
            e = jnp.exp(scores - jnp.max(scores, axis=-1, keepdims=True))
            prob = e / jnp.sum(e, axis=-1, keepdims=True)
            d_prob = dot(dc[:, col], vp[:, col], 1, 1)
            dvs.append(dot(prob.astype(LOW), dc[:, col], 0, 0))
            ds = (prob * (d_prob - jnp.sum(prob * d_prob, axis=-1, keepdims=True))).astype(LOW)
            dqs.append(dot(ds, kp[:, col], 1, 0) * scale)
            dks.append(dot(ds, q[:, col], 0, 0))
        spread = dot(pick[s], jnp.concatenate(dqs, axis=1).astype(LOW), 0, 0).astype(LOW)
        dpp[...] = jnp.concatenate(
            [spread, jnp.concatenate(dks, axis=1).astype(LOW), jnp.concatenate(dvs, axis=1).astype(LOW)], axis=1
        )

    def entry_copy(s):
        return remote(sbuf.at[s], rig.at[s], sd_s.at[5 * seqs + s], sd_r.at[5 * seqs + s], me.core)

    def entry(s):
        for where, into in ((its_half, sbuf), (my_half, rbuf)):
            base = at(s, where.start, half)
            product = lambda a, w: dot(a, w[0:3 * heads, :], 1, 0)

            def add(low, high, s=s, into=into):
                into[s] = product(*low) + product(*high)

            own_part = lambda base=base: (dproj[base, 0:3 * heads], wal)
            twin_part = lambda where=where: (dpp[where, :], wpl)
            pl.when(me.p == 0)(lambda add=add, a=own_part, b=twin_part: add(a(), b()))
            pl.when(me.p == 1)(lambda add=add, a=own_part, b=twin_part: add(b(), a()))
        entry_copy(s).start()

    def grad_rows(s):
        return at(s, me.c * half, half)

    def grad_copy(s):
        return remote(rbuf.at[s], grad_h.at[grad_rows(s)], sd_s.at[6 * seqs + s], sd_r.at[6 * seqs + s], me.core)

    def entry_end(s):
        entry_copy(s).wait()
        d_one = dres[pl.ds(s * rows, rows), :]
        high = d_one.astype(LOW)
        rest = (d_one - high.astype(F32)).astype(LOW)
        some = pick[s, :, pl.ds(pl.multiple_of(me.c * half, lanes), half)]
        rbuf[s] = (rbuf[s] + rig[s]) + (dot(some, high, 0, 0) + dot(some, rest, 0, 0))
        fetch("out", rbuf.at[s], grad_h.at[grad_rows(s)])
        grad_copy(s).start()

    def turn_weights():
        for j in range(0, width, lanes):
            flip[...] = turned[j:j + lanes, :].T
            wrow_a[:, j:j + lanes] = flip[mine, :]

    ready("gi")
    reduce_step(0, 0)
    ready("ga")
    for u in range(n_u):
        net.start(lambda u=u: xswap(u))
    net.start(vec_x)
    ready("x", "wpl", "wal", "ctx")
    project(0)
    attend_all(0)
    mix(0)
    reduce_step(0, 1)
    ready("pick", "dres")
    back(0)
    ready("low")
    feed(0)
    reduce_step(0, 2)
    vectors_one()
    ready("dproj")
    entry(0)
    project(1)
    ready("mi", "gb")
    reduce_end(0)
    update(0)
    gather_step(0, 0)
    reduce_step(1, 0)
    attend_all(1)
    mix(1)
    finish(0)
    back(1)
    reduce_step(1, 1)
    gather_step(0, 1)
    feed(1)
    entry(1)
    vectors_two()
    reduce_step(1, 2)
    gather_step(0, 2)
    relay(0)
    project(2)
    attend_all(2)
    mix(2)
    finish(1)
    xswap_end()
    ready("mb")
    reduce_end(1)
    update(1)
    gather_step(1, 0)
    gather_step(0, 3)
    reduce_step(2, 0)
    back(2)
    feed(2)
    reduce_step(2, 1)
    gather_step(1, 1)
    entry(2)
    relay(1)
    entry_end(0)
    finish(2)
    ready("ma")
    turn_weights()
    reduce_step(2, 2)
    gather_step(1, 2)
    vectors_three()
    entry_end(1)
    entry_end(2)
    reduce_end(2)
    update(2)
    gather_step(2, 0)
    gather_step(1, 3)
    relay(2)
    gather_step(2, 1)
    for s in range(seqs):
        relay_end(s)
        grad_copy(s).wait()
    gather_step(2, 2)
    gather_end(0)
    gather_step(2, 3)
    gather_end(1)
    gather_end(2)
    for j in range(0, width, lanes):
        turned[j:j + lanes, :] = ca[:, :, j:j + lanes].reshape(width, lanes).T
    fetch("out", turned.at[pl.ds(0, 3 * heads)], cq_h)
    fetch("out", turned.at[pl.ds(3 * heads, heads)], co_h)
    net.drain()
    ready("out")


def k2_call(lens, step, warmup, horizon, gains, biases, bias_in, mom_g, mom_b, mom_h, k1, x, weights, moments):
    gattn, gin, gback, dproj, ctx, pick, dres, wal, wpl, wil, wbl, pil, pbl, vec = k1
    count, width = x.shape
    seqs = lens.shape[0]
    wqkv, wout, win, wback = weights
    heads, hidden = wout.shape[0], win.shape[1]
    length = count // seqs
    half, quarter = length // 2, length // 4
    shard = moments[1].shape[1]
    slots = width // shard
    n_u = slots // 2
    total = dres.shape[0]
    any_ = pl.BlockSpec(memory_space=pl.ANY)
    vm = pl.BlockSpec(memory_space=pltpu.VMEM)
    sm = pl.BlockSpec(memory_space=pltpu.SMEM)
    sds = lambda *shape: jax.ShapeDtypeStruct(shape, F32)
    cut = lambda g: g.reshape(slots, shard, width)
    V = pltpu.VMEM
    D = pltpu.SemaphoreType.DMA
    out_shape = (
        sds(count, width), sds(count, width), sds(3 * heads, width), sds(heads, width),
        sds(slots, shard, hidden), sds(slots, shard, hidden),
        sds(*moments[0].shape), sds(*moments[1].shape), sds(*moments[2].shape), sds(*moments[3].shape),
        sds(*gains.shape), sds(*biases.shape), sds(4, hidden), sds(*mom_g.shape), sds(*mom_b.shape), sds(*mom_h.shape),
    )
    scratch = [
        V((count, width), LOW), V((slots, shard, width), F32), V((n_u, shard, hidden), F32), V((n_u, shard, hidden), F32),
        V((count + total, width), LOW), V((count, heads), LOW), V((seqs, SPAN_ROWS, length), LOW), V((total, width), F32),
        V((width, width), LOW), V((width, width), LOW), V((width, hidden), LOW), V((width, hidden), LOW), V((width, hidden), LOW), V((width, hidden), LOW),
        V((shard, hidden), F32), V((shard, hidden), F32), V((shard, width), F32),
        V(moments[0].shape, F32), V(moments[1].shape, F32), V(moments[2].shape, F32), V(moments[3].shape, F32), V((width, width), F32), V((width, 128), F32),
        V((length, heads), LOW), V((length, heads), LOW), V((length, heads), LOW), V((length, heads), LOW), V((length, 3 * heads), LOW),
        V((seqs, half, width), F32), V((seqs, half, width), F32), V((seqs, half, width), F32), V((seqs, half, width), F32),
        V((seqs, quarter, width), F32), V((seqs, quarter, width), F32), V((seqs, half, width), F32),
        V((3, 2, n_u - 1, shard, width), F32), V((n_u, shard, width), F32), V((slots, shard, width), F32), V((3, shard, width), F32),
        V((16, width), F32), V((16, width), F32), V((n_u, 16, width), F32), V((4, 16, width), F32),
        D((48,)), D((3, 2, n_u - 1)), D((3, 2, n_u - 1)), D((3, 2, n_u - 1)), D((3, 2, n_u - 1)), D((3, 2 * n_u - 1)), D((3, 2 * n_u - 1)),
        D((n_u,)), D((n_u,)), D((n_u + 3,)), D((n_u + 3,)), D((7 * seqs,)), D((7 * seqs,)), D((1,)),
    ]
    return pl.pallas_call(
        k2_kernel, out_shape=out_shape,
        in_specs=[sm] * 4 + [vm] * 7 + [any_] * 22,
        out_specs=(any_,) * 10 + (vm,) * 6,
        scratch_shapes=scratch,
        compiler_params=pltpu.CompilerParams(collective_id=2, has_side_effects=True, vmem_limit_bytes=62 * 2**20),
    )(
        lens, step, warmup, horizon, gains, biases, bias_in, mom_g, mom_b, mom_h, vec,
        x, cut(gattn), cut(gin), cut(gback), dproj, ctx, pick, dres, wal, wpl, wil, wbl, pil, pbl,
        wqkv, wout, win, wback, *moments,
    )


def fast(tokens_in, cotangent, span_mask, lengths, step, warmup, total, w_qkv, w_out, w_in, w_back, gains, biases, bias_in,
         mom_qkv, mom_out, mom_in, mom_back, mom_gains, mom_biases, mom_bias_in):
    width = tokens_in.shape[1]
    heads, hidden = w_out.shape[1], w_in.shape[1]
    wqkv_t = jnp.transpose(w_qkv, (1, 2, 0)).reshape(3 * heads, width)
    wout_t = w_out.T
    bias_tiles = bias_in.reshape(-1, 128)
    k1 = k1_call(
        tokens_in, cotangent, span_mask.reshape(-1, 128), lengths, wqkv_t, wout_t, w_in, w_back, gains, biases, bias_tiles
    )
    (
        out, grad, cq, co, ci, cb, nmq, nmo, nmi, nmb, ch_g, ch_b, ch_h, nm_g, nm_b, nm_h
    ) = k2_call(
        lengths, step, warmup, total, gains, biases, bias_tiles, mom_gains, mom_biases, mom_bias_in.reshape(2, 4, hidden),
        k1, tokens_in, (wqkv_t, wout_t, w_in, w_back), (jnp.transpose(mom_qkv, (0, 2, 1, 3)), mom_out, mom_in, mom_back)
    )
    return (
        out.astype(jnp.bfloat16), grad, jnp.transpose(cq.reshape(3, heads, width), (2, 0, 1)), co.T,
        ci.reshape(width, hidden), cb.reshape(width, hidden), ch_g, ch_b, ch_h.reshape(-1),
        jnp.transpose(nmq, (0, 2, 1, 3)), nmo, nmi, nmb, nm_g, nm_b, nm_h.reshape(2, -1),
    )


def layer_norm(values, gain, shift):
    center = values - jnp.mean(values, axis=-1, keepdims=True)
    spread = jnp.mean(center * center, axis=-1, keepdims=True)
    return center * lax.rsqrt(spread + NORM_EPS) * gain + shift


def exact_gelu(values):
    return jax.nn.gelu(values, approximate=False)


def outer_sum(left, right):
    return jnp.einsum("ta,tb->ab", left, right, preferred_element_type=jnp.float32)


def adam_step(weight, grad, moments, ratio, corr_one, corr_two, decay):
    first = BETA_ONE * moments[0] + (1.0 - BETA_ONE) * grad
    second = BETA_TWO * moments[1] + (1.0 - BETA_TWO) * grad * grad
    update = first / corr_one / (jnp.sqrt(second / corr_two) + ADAM_EPS) + decay * weight
    return (-ratio * update, jnp.stack([first, second]))


def on_device(
    tokens_in,
    cotangent,
    span_mask,
    lengths,
    step,
    warmup,
    total,
    w_qkv,
    w_out,
    w_in,
    w_back,
    gains,
    biases,
    bias_in,
    mom_qkv,
    mom_out,
    mom_in,
    mom_back,
    mom_gains,
    mom_biases,
    mom_bias_in,
):
    row_count, model_width = tokens_in.shape
    if mom_out.shape[1] % 8 == 0:
        return fast(
            tokens_in, cotangent, span_mask, lengths, step, warmup, total, w_qkv, w_out, w_in, w_back, gains, biases,
            bias_in, mom_qkv, mom_out, mom_in, mom_back, mom_gains, mom_biases, mom_bias_in
        )
    seq_count = lengths.shape[0]
    seq_length = row_count // seq_count
    head_cols = w_qkv.shape[2]
    hidden_cols = w_in.shape[1]
    head_size = HD
    local_heads = head_cols // head_size
    query_scale = 1.0 / math.sqrt(head_size)
    tensor_slot = lax.axis_index("tensor")
    bias_query = lax.dynamic_slice_in_dim(biases[0], tensor_slot * head_cols, head_cols)
    bias_value = lax.dynamic_slice_in_dim(biases[1], tensor_slot * head_cols, head_cols)
    bias_hidden = lax.dynamic_slice_in_dim(bias_in, tensor_slot * hidden_cols, hidden_cols)
    qkv_low = w_qkv.astype(jnp.bfloat16).reshape(model_width, 3 * head_cols)
    out_low = w_out.astype(jnp.bfloat16)
    in_low = w_in.astype(jnp.bfloat16)
    down_low = w_back.astype(jnp.bfloat16)
    projected = jnp.dot(tokens_in, qkv_low, preferred_element_type=jnp.float32).reshape(
        row_count, 3, head_cols
    )
    attn_shape = (seq_count, seq_length, local_heads, head_size)
    queries = (
        ((projected[:, 0] + bias_query) * query_scale).astype(jnp.bfloat16).reshape(attn_shape)
    )
    keys = projected[:, 1].astype(jnp.bfloat16).reshape(attn_shape)
    values = (projected[:, 2] + bias_value).astype(jnp.bfloat16).reshape(attn_shape)
    positions = jnp.arange(seq_length, dtype=jnp.int32)
    inside = positions[None, :] < lengths[:, None]
    key_bias = jnp.where(inside, 0.0, -1000000000.0).astype(jnp.float32)

    def score_block():
        raw = jnp.einsum("sqhd,skhd->shqk", queries, keys, preferred_element_type=jnp.float32)
        return raw + key_bias[:, None, None, :]

    scores = score_block()
    peak = jnp.max(scores, axis=-1, keepdims=True)
    log_total = peak + jnp.log(jnp.sum(jnp.exp(scores - peak), axis=-1, keepdims=True))
    probs_low = jnp.exp(scores - log_total).astype(jnp.bfloat16)
    context_low = (
        jnp.einsum("shqk,skhd->sqhd", probs_low, values, preferred_element_type=jnp.float32)
        .reshape(row_count, head_cols)
        .astype(jnp.bfloat16)
    )
    attn_part = jnp.einsum("tc,dc->td", context_low, out_low, preferred_element_type=jnp.float32)
    attn_sum = lax.psum(attn_part, "tensor")
    residual_one = tokens_in.astype(jnp.float32) + attn_sum + biases[2]
    normed = layer_norm(residual_one, gains[0], biases[3])
    normed_low = normed.astype(jnp.bfloat16)
    pre_act = jnp.dot(normed_low, in_low, preferred_element_type=jnp.float32) + bias_hidden
    act_low = exact_gelu(pre_act).astype(jnp.bfloat16)
    down_part = jnp.einsum("tf,df->td", act_low, down_low, preferred_element_type=jnp.float32)
    down_sum = lax.psum(down_part, "tensor")
    residual_two = normed + down_sum + biases[4]
    live = (inside.astype(jnp.int32) * span_mask.reshape(seq_count, seq_length)) > 0
    upto = (positions[:, None] <= positions[None, :]).astype(jnp.float32)
    rank = jnp.dot(live.astype(jnp.float32), upto).astype(jnp.int32) - 1
    slots = jnp.arange(SPAN_ROWS, dtype=jnp.int32)
    pick = (live[:, None, :] & (rank[:, None, :] == slots[None, :, None])).astype(jnp.float32)
    pick_low = pick.astype(jnp.bfloat16)

    def rows_of(values):
        width = values.shape[-1]
        return jnp.einsum(
            "srt,std->srd",
            pick,
            values.reshape(seq_count, seq_length, width),
            precision=lax.Precision.HIGHEST,
        ).reshape(seq_count * SPAN_ROWS, width)

    def low_rows_of(values):
        width = values.shape[-1]
        return jnp.einsum(
            "srt,std->srd",
            pick_low,
            values.reshape(seq_count, seq_length, width),
            preferred_element_type=jnp.bfloat16,
        ).reshape(seq_count * SPAN_ROWS, width)

    result = layer_norm(residual_two, gains[1], biases[5])
    normed_out = result.astype(jnp.bfloat16)
    residual_one_rows = rows_of(residual_one)
    residual_two_rows = rows_of(residual_two)
    grad_result = low_rows_of(cotangent).astype(jnp.float32)
    _, norm_two_back = jax.vjp(layer_norm, residual_two_rows, gains[1], biases[5])
    d_res_two, d_gain_two, d_shift_two = norm_two_back(grad_result)
    d_res_two_low = d_res_two.astype(jnp.bfloat16)
    normed_low_rows = low_rows_of(normed_low)
    pre_rows = jnp.dot(normed_low_rows, in_low, preferred_element_type=jnp.float32) + bias_hidden
    act_rows, gelu_back = jax.vjp(exact_gelu, pre_rows)
    grad_back = outer_sum(d_res_two_low, act_rows.astype(jnp.bfloat16))
    d_act = jnp.dot(d_res_two_low, down_low, preferred_element_type=jnp.float32)
    d_pre = gelu_back(d_act)[0]
    d_pre_low = d_pre.astype(jnp.bfloat16)
    grad_in = outer_sum(normed_low_rows, d_pre_low)
    d_normed_part = jnp.einsum("tf,df->td", d_pre_low, in_low, preferred_element_type=jnp.float32)
    d_normed = lax.psum(d_normed_part, "tensor") + d_res_two
    _, norm_one_back = jax.vjp(layer_norm, residual_one_rows, gains[0], biases[3])
    d_res_one, d_gain_one, d_shift_one = norm_one_back(d_normed)
    d_res_one_low = d_res_one.astype(jnp.bfloat16)
    grad_out_proj = outer_sum(d_res_one_low, low_rows_of(context_low))
    row_shape = (seq_count, SPAN_ROWS, local_heads, head_size)
    d_context = (
        jnp.dot(d_res_one_low, out_low, preferred_element_type=jnp.float32)
        .astype(jnp.bfloat16)
        .reshape(row_shape)
    )
    query_rows = low_rows_of(queries.reshape(row_count, head_cols)).reshape(row_shape)
    raw = jnp.einsum("sqhd,skhd->shqk", query_rows, keys, preferred_element_type=jnp.float32)
    probs = jax.nn.softmax(raw + key_bias[:, None, None, :], axis=-1)
    probs_again = probs.astype(jnp.bfloat16)
    d_probs = jnp.einsum("sqhd,skhd->shqk", d_context, values, preferred_element_type=jnp.float32)
    d_values = jnp.einsum(
        "shqk,sqhd->skhd", probs_again, d_context, preferred_element_type=jnp.float32
    ).reshape(row_count, head_cols)
    d_scores = (probs * (d_probs - jnp.sum(probs * d_probs, axis=-1, keepdims=True))).astype(
        jnp.bfloat16
    )
    d_queries = (
        jnp.einsum("shqk,skhd->sqhd", d_scores, keys, preferred_element_type=jnp.float32).reshape(
            seq_count * SPAN_ROWS, head_cols
        )
        * query_scale
    )
    d_keys = jnp.einsum(
        "shqk,sqhd->skhd", d_scores, query_rows, preferred_element_type=jnp.float32
    ).reshape(row_count, head_cols)

    def spread(row_values):
        width = row_values.shape[-1]
        return jnp.einsum(
            "srt,srd->std",
            pick,
            row_values.reshape(seq_count, SPAN_ROWS, width),
            precision=lax.Precision.HIGHEST,
        ).reshape(row_count, width)

    d_proj_low = (
        jnp.stack([spread(d_queries), d_keys, d_values], axis=1)
        .astype(jnp.bfloat16)
        .reshape(row_count, 3 * head_cols)
    )
    grad_qkv = outer_sum(tokens_in, d_proj_low).reshape(model_width, 3, head_cols)
    d_entry_part = jnp.einsum("tc,dc->td", d_proj_low, qkv_low, preferred_element_type=jnp.float32)
    input_grad = lax.psum(d_entry_part, "tensor") + spread(d_res_one)
    first_rank = (tensor_slot == 0).astype(jnp.float32)
    width_zero = jnp.zeros((model_width,), jnp.float32)

    def place_heads(partial_sum):
        return lax.dynamic_update_slice_in_dim(width_zero, partial_sum, tensor_slot * head_cols, 0)

    grad_gains = jnp.stack([d_gain_one, d_gain_two]) * first_rank
    grad_biases = jnp.stack(
        [
            place_heads(jnp.sum(d_queries, axis=0)),
            place_heads(jnp.sum(d_values, axis=0)),
            jnp.sum(d_res_one, axis=0) * first_rank,
            d_shift_one * first_rank,
            jnp.sum(d_res_two, axis=0) * first_rank,
            d_shift_two * first_rank,
        ]
    )
    grad_bias_in = lax.dynamic_update_slice_in_dim(
        jnp.zeros(bias_in.shape, jnp.float32), jnp.sum(d_pre, axis=0), tensor_slot * hidden_cols, 0
    )
    grad_gains, grad_biases, grad_bias_in = lax.psum(
        (grad_gains, grad_biases, grad_bias_in), ("dp", "tensor")
    )
    data_slot = lax.axis_index("dp")
    shard_rows = model_width // lax.axis_size("dp")
    owned = tuple(
        lax.psum_scatter(part, "dp", scatter_dimension=0, tiled=True)
        for part in (grad_qkv, grad_out_proj, grad_in, grad_back)
    )
    clock = step[0].astype(jnp.float32)
    warm = warmup[0].astype(jnp.float32)
    horizon = total[0].astype(jnp.float32)
    ratio = jnp.minimum(clock / warm, (horizon - clock) / (horizon - warm))
    corr_one = 1.0 - jnp.power(BETA_ONE, clock)
    corr_two = 1.0 - jnp.power(BETA_TWO, clock)
    change_rows = []
    fresh_moments = []
    for weight, grad_rows, moment in zip(
        (w_qkv, w_out, w_in, w_back), owned, (mom_qkv, mom_out, mom_in, mom_back)
    ):
        weight_rows = lax.dynamic_slice_in_dim(weight, data_slot * shard_rows, shard_rows, 0)
        row_change, new_moment = adam_step(
            weight_rows, grad_rows, moment, ratio, corr_one, corr_two, WEIGHT_DECAY
        )
        change_rows.append(row_change)
        fresh_moments.append(new_moment)
    change_qkv, change_out_proj, change_in_proj, change_back_proj = (
        lax.all_gather(change_rows[0], "dp", axis=0, tiled=True),
        lax.all_gather(change_rows[1], "dp", axis=0, tiled=True),
        lax.all_gather(change_rows[2], "dp", axis=0, tiled=True),
        lax.all_gather(change_rows[3], "dp", axis=0, tiled=True),
    )
    change_gains, new_mom_gains = adam_step(
        gains, grad_gains, mom_gains, ratio, corr_one, corr_two, 0.0
    )
    change_biases, new_mom_biases = adam_step(
        biases, grad_biases, mom_biases, ratio, corr_one, corr_two, 0.0
    )
    change_bias_in, new_mom_bias_in = adam_step(
        bias_in, grad_bias_in, mom_bias_in, ratio, corr_one, corr_two, 0.0
    )
    return (
        normed_out,
        input_grad,
        change_qkv,
        change_out_proj,
        change_in_proj,
        change_back_proj,
        change_gains,
        change_biases,
        change_bias_in,
        fresh_moments[0],
        fresh_moments[1],
        fresh_moments[2],
        fresh_moments[3],
        new_mom_gains,
        new_mom_biases,
        new_mom_bias_in,
    )


def solution(mesh):
    in_specs = (
        P("dp", None),
        P("dp", None),
        P("dp"),
        P("dp"),
        P(),
        P(),
        P(),
        P(None, None, "tensor"),
        P(None, "tensor"),
        P(None, "tensor"),
        P(None, "tensor"),
        P(),
        P(),
        P(),
        P(None, "dp", None, "tensor"),
        P(None, "dp", "tensor"),
        P(None, "dp", "tensor"),
        P(None, "dp", "tensor"),
        P(),
        P(),
        P(),
    )
    out_specs = (
        P("dp", None),
        P("dp", None),
        P(None, None, "tensor"),
        P(None, "tensor"),
        P(None, "tensor"),
        P(None, "tensor"),
        P(),
        P(),
        P(),
        P(None, "dp", None, "tensor"),
        P(None, "dp", "tensor"),
        P(None, "dp", "tensor"),
        P(None, "dp", "tensor"),
        P(),
        P(),
        P(),
    )
    return jax.shard_map(
        on_device, mesh=mesh, in_specs=in_specs, out_specs=out_specs, check_vma=False
    )
```

```python
import math

import jax
import jax.numpy as jnp
from jax import lax
from jax.experimental import pallas as pl
from jax.experimental.pallas import tpu as pltpu
from jax.sharding import PartitionSpec as P

HD = 64
SPAN_ROWS = 80
NORM_EPS = 1e-12
MESH = pl.DeviceIdType.MESH
F32 = jnp.float32
LOW = jnp.bfloat16


def dot(left, right, left_dim, right_dim):
    return lax.dot_general(
        left, right, (((left_dim,), (right_dim,)), ((), ())), preferred_element_type=F32
    )


def normalize(rows):
    center = rows - jnp.mean(rows, axis=-1, keepdims=True)
    scale = lax.rsqrt(jnp.mean(center * center, axis=-1, keepdims=True) + NORM_EPS)
    return center * scale, scale


def norm_back(grad, gain, unit, scale):
    weighted = grad * gain
    return scale * (
        weighted
        - jnp.mean(weighted, axis=-1, keepdims=True)
        - unit * jnp.mean(weighted * unit, axis=-1, keepdims=True)
    )


def row_sum(rows):
    return jnp.sum(rows, axis=0, keepdims=True)


class Peers:
    def __init__(self):
        self.d = lax.axis_index("dp")
        self.t = lax.axis_index("tensor")
        self.b = lax.rem(self.d, 2)
        self.c = lax.rem(self.t, 2)
        self.p = lax.div(self.t, 2)
        self.u = lax.div(self.d, 2)
        self.core = (self.d, self.t + 1 - 2 * self.c)
        self.y = (self.d, lax.rem(self.t + 2, 4))
        self.x = (self.d + 1 - 2 * self.b, self.t)


def send(src, dst, sems, k, peer):
    copy = pltpu.make_async_remote_copy(
        src_ref=src, dst_ref=dst, send_sem=sems.at[0, k], recv_sem=sems.at[1, k],
        device_id=peer, device_id_type=MESH,
    )
    copy.start()
    return copy


def local(src, dst, sem):
    copy = pltpu.make_async_copy(src, dst, sem)
    copy.start()
    return copy


def greet(peers):
    barrier = pltpu.get_barrier_semaphore()
    for peer in peers:
        pl.semaphore_signal(barrier, inc=1, device_id=peer, device_id_type=MESH)
    pl.semaphore_wait(barrier, len(peers))


def gelu_parts(pre):
    cdf = 0.5 * (1.0 + lax.erf(pre * (1.0 / math.sqrt(2.0))))
    pdf = jnp.exp(-0.5 * pre * pre) * (1.0 / math.sqrt(2.0 * math.pi))
    return pre * cdf, cdf + pre * pdf


def k1_kernel(
    lens, mask, gains, biases, bias_in, x_h, cot_h, wqkv_h, wout_h, win_h, wback_h,
    gi_h, gb_h, full_h, res_h, dres_h, pick_h, pm_h, qm_h, k_h, v_h, cm_h, ctx_h, wal_h, wo_h, wq_h, wil_h, wbl_h, pil_h, pbl_h, vec,
    x, cot, wqkv, wout, win, wback, wp_qkv, wp_out, pwin, pwback, q_o, k_o, v_o, ctx_o, pick_o, wal, wil, wbl, pil, pbl, gin, gback,
    pm, xm, cotm, qm, ctxm, cml, ctxp, ap, apc, normed, nlow, act, gp, part, rc1, h1, ry1,
    part2, rc2, h2, ry2, full2, full, dres2, d2w, d2x, nxw, nxx, dplow,
    lsem, rsem,
):
    seqs, rows = 3, SPAN_ROWS
    count = x_h.shape[0]
    length = count // seqs
    total = seqs * rows
    half = total // 2
    heads = ctx_o.shape[1]
    n_heads = heads // HD
    width = x_h.shape[1]
    me = Peers()

    def seq(s):
        return pl.ds(s * length, length)

    loads = [
        local(wqkv_h, wqkv, lsem.at[0]),
        local(wout_h, wout, lsem.at[1]),
    ] + [local(x_h.at[seq(s)], x.at[seq(s)], lsem.at[2 + s]) for s in range(seqs)] + [
        local(win_h, win, lsem.at[2 + seqs]),
        local(wback_h, wback, lsem.at[3 + seqs]),
        local(cot_h, cot, lsem.at[4 + seqs]),
    ]
    stores = []

    def keep(src, dst):
        stores.append(local(src, dst, lsem.at[8 + len(stores)]))

    greet((me.core, me.y, me.x))

    loads[1].wait()
    out_half = pl.ds(pl.multiple_of(me.b * (heads // 2), 8), heads // 2)
    wo_y = send(wout.at[out_half], wp_out.at[out_half], rsem, 0, me.y)
    loads[0].wait()
    wal[0:3 * heads, :] = wqkv[...].astype(LOW)
    wal[3 * heads:, :] = wout[...].astype(LOW)
    keep(wal, wal_h)

    def pick_bias(row, k=heads):
        out = jnp.zeros((1, k), F32)
        for slot in range(4):
            piece = biases[row:row + 1, slot * k:(slot + 1) * k]
            out = jnp.where(me.t == slot, piece, out)
        return out

    bias_q, bias_v = pick_bias(0), pick_bias(1)
    hidden = win.shape[1]
    lanes = 128
    bias_h = jnp.concatenate(
        [bias_in[pl.ds(me.t * (hidden // lanes) + j, 1), :] for j in range(hidden // lanes)], axis=1
    )
    upto = (
        lax.broadcasted_iota(jnp.int32, (length, length), 0)
        <= lax.broadcasted_iota(jnp.int32, (length, length), 1)
    ).astype(F32).astype(LOW)
    position = lax.broadcasted_iota(jnp.int32, (1, length), 1)
    slot_of = lax.broadcasted_iota(jnp.int32, (rows, length), 0).astype(F32)
    scale = 1.0 / math.sqrt(HD)
    def project(s):
        loads[2 + s].wait()
        at = seq(s)
        xs = x[at, :]
        q = ((dot(xs, wal[0:heads, :], 1, 1) + bias_q) * scale).astype(LOW)
        k = dot(xs, wal[heads:2 * heads, :], 1, 1).astype(LOW)
        v = (dot(xs, wal[2 * heads:3 * heads, :], 1, 1) + bias_v).astype(LOW)
        q_o[at, :] = q
        k_o[at, :] = k
        v_o[at, :] = v
        parts = length // lanes
        marks = jnp.concatenate([mask[pl.ds(s * parts + j, 1), :] for j in range(parts)], axis=1)
        inside = position < lens[s]
        live = jnp.where(inside, marks, 0).astype(F32)
        rank = dot(jnp.broadcast_to(live, (8, length)).astype(LOW), upto, 1, 0)[0:1] - 1.0
        pick = jnp.where((rank == slot_of) & (live > 0.0), 1.0, 0.0).astype(LOW)
        pick_o[s] = pick
        here = pl.ds(s * rows, rows)
        xm[here, :] = dot(pick, xs, 1, 0)
        qrow = dot(pick, q, 1, 0).astype(LOW)
        qm[here, :] = qrow
        key_bias = jnp.where(inside, 0.0, -1000000000.0)
        pieces = []
        for h in range(n_heads):
            col = slice(h * HD, (h + 1) * HD)
            scores = dot(qrow[:, col], k[:, col], 1, 1) + key_bias
            e = jnp.exp(scores - jnp.max(scores, axis=-1, keepdims=True))
            prob = e / jnp.sum(e, axis=-1, keepdims=True)
            pm[s * n_heads + h] = prob
            pieces.append(dot(prob.astype(LOW), v[:, col], 1, 0))
        low = jnp.concatenate(pieces, axis=1).astype(LOW)
        cml[here, :] = low
        ctxm[here, :] = low.astype(F32)
        return send(ctxm.at[here], ctxp.at[here], rsem, 24 + s, me.y)

    ctx_y = [project(s) for s in range(seqs)]
    wo_y.wait()
    wo_x = send(wp_out.at[out_half], wp_out.at[out_half], rsem, 2, me.x)
    third = heads // 2

    def qkv_part(k):
        return pl.ds(pl.multiple_of(me.b * (3 * third) + k * third, 8), third)

    def fetch(k):
        return send(wqkv.at[qkv_part(k)], wp_qkv.at[qkv_part(k)], rsem, 16 + k, me.y)

    def swap(k):
        return send(wp_qkv.at[qkv_part(k)], wp_qkv.at[qkv_part(k)], rsem, 19 + k, me.x)

    def attend_all(s):
        at = slice(s * length, (s + 1) * length)
        key_bias = jnp.where(position < lens[s], 0.0, -1000000000.0)
        pieces = []
        for h in range(n_heads):
            col = slice(h * HD, (h + 1) * HD)
            scores = dot(q_o[at, col], k_o[at, col], 1, 1) + key_bias
            e = jnp.exp(scores - jnp.max(scores, axis=-1, keepdims=True))
            prob = (e / jnp.sum(e, axis=-1, keepdims=True)).astype(LOW)
            pieces.append(dot(prob, v_o[at, col], 1, 0))
        ctx_o[at, :] = jnp.concatenate(pieces, axis=1).astype(LOW)

    for ref, out in ((pm, pm_h), (qm, qm_h), (k_o, k_h), (v_o, v_h), (cml, cm_h), (pick_o, pick_h)):
        keep(ref, out)
    for load in loads[2 + seqs:4 + seqs]:
        load.wait()
    wil[...] = win[...].astype(LOW)
    wbl[...] = wback[...].astype(LOW)
    keep(wil, wil_h)
    keep(wbl, wbl_h)
    loads[4 + seqs].wait()
    for s in range(seqs):
        cotm[s * rows:(s + 1) * rows, :] = dot(pick_o[s], cot[s * length:(s + 1) * length, :], 1, 0)
    wo_x.wait()
    for copy in ctx_y:
        copy.wait()
    woq = wp_out[...].astype(LOW)

    def mix(first, second):
        ap[...] = dot(*first, 1, 0) + dot(*second, 1, 0)

    own_part = lambda: (cml[...], wal[3 * heads:, :])
    twin_part = lambda: (ctxp[...].astype(LOW), woq)
    pl.when(me.p == 0)(lambda: mix(own_part(), twin_part()))
    pl.when(me.p == 1)(lambda: mix(twin_part(), own_part()))
    ap_c = send(ap, apc, rsem, 3, me.core)
    wq_y = fetch(0)
    keep(wp_out, wo_h)
    ap_c.wait()
    xm[...] = xm[...] + (ap[...] + apc[...]) + biases[2:3, :]
    keep(xm, res_h)
    unit, inv = normalize(xm[...])
    normed[...] = unit * gains[0:1, :] + biases[3:4, :]
    nlow[...] = normed[...].astype(LOW)
    nxw[...] = nlow[...].astype(F32)
    mine = pl.ds(pl.multiple_of(me.c * half, 8), half)
    other = pl.ds(pl.multiple_of((1 - me.c) * half, 8), half)
    nx_x = send(nxw.at[mine], nxx.at[mine], rsem, 5, me.x)
    for j in range(0, hidden, 256):
        col = slice(j, j + 256)
        a, g = gelu_parts(dot(nlow[...], wil[:, col], 1, 0) + bias_h[:, col])
        act[:, col] = a.astype(LOW)
        gp[:, col] = g
    part[...] = dot(act[...], wbl[...], 1, 1)

    def all_reduce(src, rc, hs, ry, dst, base, fill):
        first = send(src.at[other], rc, rsem, base, me.core)
        first.wait()
        hs[...] = src[mine, :] + rc[...]
        second = send(hs, ry, rsem, base + 1, me.y)
        fill()
        second.wait()
        dst[mine, :] = hs[...] + ry[...]
        third = send(dst.at[mine], dst.at[mine], rsem, base + 2, me.core)
        third.wait()

    relay = []

    def fill_one():
        wide.append(send(win, pwin, rsem, 22, me.core))
        attend_all(0)
        attend_all(1)
        nx_x.wait()
        relay.append(send(nxx.at[mine], nxx.at[mine], rsem, 6, me.core))
        wq_y.wait()
        relay.append(swap(0))

    wide = []
    all_reduce(part, rc1, h1, ry1, full, 7, fill_one)
    relay[0].wait()
    unit, inv = normalize(normed[...] + full[...] + biases[4:5, :])
    grad = cotm[...]
    d_two = norm_back(grad, gains[1:2, :], unit, inv)
    dres2[...] = d_two
    vec[...] = jnp.zeros(vec.shape, F32)
    vec[1:2, :] = row_sum(grad * unit)
    vec[5:6, :] = row_sum(d_two)
    vec[6:7, :] = row_sum(grad)
    d2w[...] = d_two.astype(LOW).astype(F32)
    d2_x = send(d2w.at[mine], d2x.at[mine], rsem, 10, me.x)
    keep(dres2, dres_h)
    d2low = d2w[...].astype(LOW)
    for j in range(0, hidden, 256):
        col = slice(j, j + 256)
        d_pre = dot(d2low, wbl[:, col], 1, 0) * gp[:, col]
        vec[8:9, col] = row_sum(d_pre)
        dplow[:, col] = d_pre.astype(LOW)
    part2[...] = dot(dplow[...], wil[...], 1, 1)

    slots = gin.shape[0]
    shard = gin.shape[1]

    def cut(rows):
        return rows.reshape(slots, shard, rows.shape[1])

    def fill_two():
        wide.append(send(wback, pwback, rsem, 23, me.core))
        attend_all(2)
        keep(ctx_o, ctx_h)
        for j in range(0, hidden, 256):
            col = slice(j, j + 256)
            gin[:, :, col] = cut(dot(nlow[...], dplow[:, col], 0, 0))
            gback[:, :, col] = cut(dot(d2low, act[:, col], 0, 0))
        wide[0].wait()
        pil[...] = pwin[...].astype(LOW)
        keep(pil, pil_h)
        relay[1].wait()
        keep(wp_qkv, wq_h)
        d2_x.wait()
        relay.append(send(d2x.at[mine], d2x.at[mine], rsem, 11, me.core))

    all_reduce(part2, rc2, h2, ry2, full2, 12, fill_two)
    keep(full2, full_h)
    relay[2].wait()
    nlx = nxx[...].astype(LOW)
    dlx = d2x[...].astype(LOW)
    for j in range(0, hidden, 256):
        col = slice(j, j + 256)
        a, g = gelu_parts(dot(nlx, wil[:, col], 1, 0) + bias_h[:, col])
        d_pre = (dot(dlx, wbl[:, col], 1, 0) * g).astype(LOW)
        gin[:, :, col] += cut(dot(nlx, d_pre, 0, 0))
        gback[:, :, col] += cut(dot(dlx, a.astype(LOW), 0, 0))
    for u in range(slots // 2):
        keep(gin.at[2 * u + me.b], gi_h.at[u])
        keep(gback.at[2 * u + me.b], gb_h.at[u])
    wide[1].wait()
    pbl[...] = pwback[...].astype(LOW)
    keep(pbl, pbl_h)
    for copy in stores:
        copy.wait()


def k1_call(x, cot, mask, lens, wqkv, wout, win, wback, gains, biases, bias_in, slots):
    count, width = x.shape
    seqs = lens.shape[0]
    heads = wout.shape[0]
    hidden = win.shape[1]
    length = count // seqs
    total = seqs * SPAN_ROWS
    half = total // 2
    units = seqs * (heads // HD)
    any_ = pl.BlockSpec(memory_space=pl.ANY)
    vm = pl.BlockSpec(memory_space=pltpu.VMEM)
    sm = pl.BlockSpec(memory_space=pltpu.SMEM)
    sds = jax.ShapeDtypeStruct
    V = pltpu.VMEM
    wide = lambda r, t=F32: V((r, width), t)
    block = (slots // 2, width // slots, hidden)
    square = sds((width, hidden), LOW)
    out_shape = (
        sds(block, F32), sds(block, F32), sds((total, width), F32), sds((total, width), F32), sds((total, width), F32),
        sds((seqs, SPAN_ROWS, length), LOW), sds((units, SPAN_ROWS, length), F32), sds((total, heads), LOW),
        sds((count, heads), LOW), sds((count, heads), LOW), sds((total, heads), LOW), sds((count, heads), LOW),
        sds((4 * heads, width), LOW), sds((heads, width), F32), sds((3 * heads, width), F32), square, square, square, square,
        sds((16, width), F32),
    )
    scratch = [
        wide(count, LOW), wide(count, LOW), wide(3 * heads), wide(heads), V((width, hidden), F32),
        V((width, hidden), F32), wide(3 * heads), wide(heads), V((width, hidden), F32), V((width, hidden), F32),
        V((count, heads), LOW), V((count, heads), LOW), V((count, heads), LOW), V((count, heads), LOW),
        V((seqs, SPAN_ROWS, length), LOW), wide(4 * heads, LOW), V((width, hidden), LOW), V((width, hidden), LOW),
        V((width, hidden), LOW), V((width, hidden), LOW), V((slots, width // slots, hidden), F32), V((slots, width // slots, hidden), F32),
        V((units, SPAN_ROWS, length), F32), wide(total), wide(total), V((total, heads), LOW),
        V((total, heads), F32), V((total, heads), LOW), V((total, heads), F32), wide(total), wide(total),
        wide(total), wide(total, LOW), V((total, hidden), LOW), V((total, hidden), F32), wide(total), wide(half), wide(half), wide(half),
        wide(total), wide(half), wide(half), wide(half), wide(total), wide(total), wide(total), wide(total), wide(total), wide(total), wide(total),
        V((total, hidden), LOW),
        pltpu.SemaphoreType.DMA((8 + 20 + slots,)), pltpu.SemaphoreType.DMA((2, 24 + seqs)),
    ]
    return pl.pallas_call(
        k1_kernel, out_shape=out_shape,
        in_specs=[sm, vm, vm, vm, vm] + [any_] * 6,
        out_specs=(any_,) * (len(out_shape) - 1) + (vm,),
        scratch_shapes=scratch,
        compiler_params=pltpu.CompilerParams(
            collective_id=1, has_side_effects=True, vmem_limit_bytes=60 * 2**20
        ),
    )(lens, mask, gains, biases, bias_in, x, cot, wqkv, wout, win, wback)


BETA_ONE = 0.9
BETA_TWO = 0.999
ADAM_EPS = 1e-06
WEIGHT_DECAY = 0.01


def adam(weight, grad, first, second, ratio, corr_one, corr_two, decay):
    first = BETA_ONE * first + (1.0 - BETA_ONE) * grad
    second = BETA_TWO * second + (1.0 - BETA_TWO) * grad * grad
    update = first / corr_one / (jnp.sqrt(second / corr_two) + ADAM_EPS) + decay * weight
    return -ratio * update, first, second


class Net:
    def __init__(self):
        self.sent = []

    def start(self, make, when=None):
        self.sent.append((make, when))
        self.run(lambda: make().start(), when)

    @staticmethod
    def run(do, when):
        if when is None:
            do()
        else:
            pl.when(when)(do)

    def drain(self):
        for make, when in self.sent:
            self.run(lambda make=make: make().wait_send(), when)


def k2_kernel(
    lens, step, warmup, horizon, gains, biases, bias_in, vec,
    x_h, gi_h, gb_h, full_h, res_h, dtwo_h, pick_h, pm_h, qm_h, k_h, v_h, cm_h, ctx_h, wal_h, wo_h, wq_h, wil_h, wbl_h, pil_h, pbl_h,
    wqkv_h, wout_h, win_h, wback_h, mq_h, mo_h, mi_h, mb_h,
    out_h, grad_h, cq_h, co_h, ci_h, cb_h, nmq_h, nmo_h, nmi_h, nmb_h, vt,
    x, ga, gi, gb, dproj, ctx, pick, dres, full, dtwo, pm, qm, ko, vo, cm, dctx, wp, wo, wal, wpl, wil, wbl, pil, pbl,
    wrow_i, wrow_b, wrow_a, mq, mo, mi, mb, turned, flip,
    qp, kp, vp, ctxp, dpp, sbuf, rbuf, nrm, dsc, rdn, fin, rig,
    ring, xr, ca, own, v0, v1, vx, vz,
    lsem, rs_s, rs_r, ag_s, ag_r, ax_s, ax_r, xs_s, xs_r, vs_s, vs_r, sd_s, sd_r, wsem,
):
    me = Peers()
    n_u = ring.shape[2] + 1
    seqs = sbuf.shape[0]
    count, width = x_h.shape
    length = count // seqs
    rows = SPAN_ROWS
    total = seqs * rows
    heads = ctx.shape[1]
    n_heads = heads // HD
    shard = gi.shape[1]
    hidden = wil.shape[1]
    half = length // 2
    quarter = length // 4
    net = Net()
    z, b = me.u, me.b
    right = (me.d + 2, me.t)
    left = (me.d - 2, me.t)
    diag = (me.d, 3 - me.t)

    def remote(src, dst, ss, rr, peer):
        return pltpu.make_async_remote_copy(
            src_ref=src, dst_ref=dst, send_sem=ss, recv_sem=rr, device_id=peer, device_id_type=MESH
        )

    pend = {}
    order = iter(range(64))

    def fetch(name, src, dst):
        copy = pltpu.make_async_copy(src, dst, lsem.at[next(order)])
        copy.start()
        pend.setdefault(name, []).append(copy)

    def ready(*names):
        for name in names:
            for copy in pend.pop(name, []):
                copy.wait()

    fetch("one", full_h, full)
    fetch("one", res_h, dres)
    fetch("one", dtwo_h, dtwo)
    fetch("gi", gi_h, gi)
    fetch("wal", wal_h, wal)
    fetch("att", pick_h, pick)
    fetch("att", pm_h, pm)
    fetch("att", qm_h, qm)
    fetch("att", k_h, ko)
    fetch("att", v_h, vo)
    fetch("att", cm_h, cm)
    fetch("x", x_h, x.at[pl.ds(0, count)])
    fetch("gb", gb_h, gb)
    fetch("wo", wo_h, wo)
    third = heads // 2
    for b_other in range(2):
        part = pl.ds(b_other * 3 * third, third)
        fetch("wq", wq_h.at[part], wp.at[part])
    fetch("ctx", ctx_h, ctx)
    fetch("low", wil_h, wil)
    fetch("low", wbl_h, wbl)
    fetch("low", pil_h, pil)
    fetch("low", pbl_h, pbl)
    mine = pl.ds(pl.multiple_of(me.d * shard, 8), shard)
    fetch("mi", win_h.at[mine], wrow_i)
    fetch("mi", mi_h, mi)
    fetch("mb", wback_h.at[mine], wrow_b)
    fetch("mb", mb_h, mb)
    fetch("ma", wqkv_h, turned.at[pl.ds(0, 3 * heads)])
    fetch("ma", wout_h, turned.at[pl.ds(3 * heads, heads)])
    fetch("ma", mq_h, mq)
    fetch("ma", mo_h, mo)

    others = [(2 * lax.rem(z + k, n_u) + b, me.t) for k in range(1, n_u)]
    greet([me.core, me.y, diag, me.x] + others)

    def peer_weights(k):
        part = pl.ds(k * 3 * third + third, 2 * third)
        return remote(wqkv_h.at[part], wp.at[part], wsem.at[0, k], wsem.at[1, k], me.y)

    g_of = {0: gi, 1: gb}

    def g_at(ch, u):
        return ga.at[2 * u + b] if ch == 2 else g_of[ch].at[u]

    def ring_copy(ch, way, s, src):
        peer = right if way == 0 else left
        return remote(src, ring.at[ch % 2, way, s], rs_s.at[ch, way, s], rs_r.at[ch, way, s], peer)

    def reduce_step(ch, s):
        for way, place in ((0, z), (1, n_u - 1 - z)):
            active = place <= s
            d = (n_u - 1 - s + z) if way == 0 else (s - (n_u - 1 - z))
            if s > 0:
                def gather_in(way=way, d=d):
                    ring_copy(ch, way, s - 1, ring.at[ch % 2, way, s - 1]).wait_recv()
                    g_at(ch, d)[...] += ring[ch % 2, way, s - 1]
                pl.when(active & (place > 0))(gather_in)
            net.start(lambda way=way, d=d: ring_copy(ch, way, s, g_at(ch, d)), active)

    def reduce_end(ch):
        last = n_u - 2
        for way, place in ((0, z), (1, n_u - 1 - z)):
            def gather_in(way=way):
                ring_copy(ch, way, last, ring.at[ch % 2, way, last]).wait_recv()
                g_at(ch, z)[...] += ring[ch % 2, way, last]
            pl.when(place > 0)(gather_in)

    ratio, corr_one, corr_two = rates(step, warmup, horizon)

    def target(ch, d):
        return ca.at[d] if ch == 2 else (ci_h, cb_h)[ch].at[d]

    def update(ch):
        if ch < 2:
            w, m = ((wrow_i, mi), (wrow_b, mb))[ch]
            change, first, second = adam(
                w[...], g_at(ch, z)[...], m[0], m[1], ratio, corr_one, corr_two, WEIGHT_DECAY
            )
            own[ch] = change
            m[0], m[1] = first, second
            fetch("out", m, (nmi_h, nmb_h)[ch])
            fetch("out", own.at[ch], target(ch, me.d))
        else:
            for k in range(4):
                col = slice(k * heads, (k + 1) * heads)
                old = (mq[0, k], mq[1, k]) if k < 3 else (mo[0], mo[1])
                change, first, second = adam(
                    wrow_a[:, col], ga[me.d][:, col], *old, ratio, corr_one, corr_two, WEIGHT_DECAY
                )
                own[2, :, col] = change
                if k < 3:
                    mq[0, k], mq[1, k] = first, second
                else:
                    mo[0], mo[1] = first, second
            ca[me.d] = own[2]
            fetch("out", mq, nmq_h)
            fetch("out", mo, nmo_h)

    def ag_copy(ch, way, s, src, u):
        peer = right if way == 0 else left
        return remote(src, target(ch, 2 * u + b), ag_s.at[ch, way, s], ag_r.at[ch, way, s], peer)

    def ax_copy(ch, k, src, u, parity):
        return remote(src, target(ch, 2 * u + parity), ax_s.at[ch, k], ax_r.at[ch, k], me.x)

    def gather_step(ch, s):
        for way in (0, 1):
            u = z - s if way == 0 else z + s
            edge = z < n_u - 1 if way == 0 else z > 0
            if s == 0:
                net.start(lambda way=way: ag_copy(ch, way, 0, own.at[ch], z), edge)
                continue
            here = u >= 0 if way == 0 else u <= n_u - 1
            pl.when(here)(lambda way=way, u=u: ag_copy(ch, way, s - 1, target(ch, 2 * u + b), u).wait_recv())
            if s <= n_u - 2:
                net.start(lambda way=way, u=u: ag_copy(ch, way, s, target(ch, 2 * u + b), u), here & edge)
            k = s if way == 0 else n_u - 1 + s
            net.start(lambda k=k, u=u: ax_copy(ch, k, target(ch, 2 * u + b), u, b), here)
        if s == 0:
            net.start(lambda: ax_copy(ch, 0, own.at[ch], z, b))

    def gather_end(ch):
        ax_copy(ch, 0, own.at[ch], z, 1 - b).wait_recv()
        for s in range(1, n_u):
            for k, u, here in ((s, z - s, z >= s), (n_u - 1 + s, z + s, z + s <= n_u - 1)):
                pl.when(here)(lambda k=k, u=u: ax_copy(ch, k, target(ch, 2 * u + 1 - b), u, 1 - b).wait_recv())

    def xswap(u):
        return remote(ga.at[2 * u + 1 - b], xr.at[u], xs_s.at[u], xs_r.at[u], me.x)

    def xswap_end():
        for u in range(n_u):
            xswap(u).wait_recv()
            ga[2 * u + b] += xr[u]

    def vec_x():
        return remote(v0, vx, vs_s.at[0], vs_r.at[0], me.x)

    def vec_z(k):
        peer = (2 * lax.rem(z + k, n_u) + b, me.t)
        return remote(v1, vz.at[z], vs_s.at[k], vs_r.at[k], peer)

    def vec_t(k, peer):
        return remote(v1, vt.at[me.t], vs_s.at[n_u + k], vs_r.at[n_u + k], peer)

    trio = (me.core, me.y, diag)

    def vectors_one():
        vec_x().wait_recv()
        v1[...] = v0[...] + vx[...]
        vz[z] = v1[...]
        for k in range(1, n_u):
            vec_z(k).start()

    def vectors_two():
        for k in range(1, n_u):
            vec_z(k).wait()
        total = vz[0]
        for u in range(1, n_u):
            total = total + vz[u]
        v1[...] = total
        vt[me.t] = total
        for k, peer in enumerate(trio):
            vec_t(k, peer).start()

    def vectors_three():
        for k, peer in enumerate(trio):
            vec_t(k, peer).wait()

    lanes = 128

    def hidden_bias(slot):
        parts = hidden // lanes
        return jnp.concatenate([bias_in[pl.ds(slot * parts + j, 1), :] for j in range(parts)], axis=1)

    twin = lax.rem(me.t + 2, 4)

    def first_norm_back():
        d_normed = full[...] + dtwo[...]
        unit, inv = normalize(dres[...])
        d_one = norm_back(d_normed, gains[0:1, :], unit, inv)
        dres[...] = d_one
        v0[...] = vec[...]
        v0[0:1, :] = row_sum(d_normed * unit)
        v0[3:4, :] = row_sum(d_one)
        v0[4:5, :] = row_sum(d_normed)
        low = d_one.astype(LOW)
        x[count:count + total, :] = low
        dctx[...] = dot(low, wal[3 * heads:, :], 1, 1).astype(LOW)

    def attend_back(q, k, v, dc, probs, pick_s):
        dqs, dks, dvs = [], [], []
        for h in range(n_heads):
            col = slice(h * HD, (h + 1) * HD)
            prob = probs(h)
            d_prob = dot(dc[:, col], v[:, col], 1, 1)
            dvs.append(dot(prob.astype(LOW), dc[:, col], 0, 0))
            ds = (prob * (d_prob - jnp.sum(prob * d_prob, axis=-1, keepdims=True))).astype(LOW)
            dqs.append(dot(ds, k[:, col], 1, 0) * scale)
            dks.append(dot(ds, q[:, col], 0, 0))
        dq = jnp.concatenate(dqs, axis=1)
        dv = jnp.concatenate(dvs, axis=1)
        spread = dot(pick_s, dq.astype(LOW), 0, 0).astype(LOW)
        return jnp.concatenate([spread, jnp.concatenate(dks, axis=1).astype(LOW), dv.astype(LOW)], axis=1), dq, dv

    def own_back():
        dq_sum = jnp.zeros((1, heads), F32)
        dv_sum = dq_sum
        for s in range(seqs):
            here = slice(s * rows, (s + 1) * rows)
            low, dq, dv = attend_back(
                qm[here, :], ko.at[at(s)], vo.at[at(s)], dctx[here, :], lambda h, s=s: pm[s * n_heads + h], pick[s]
            )
            dproj[at(s), 0:3 * heads] = low
            dproj[at(s), 3 * heads:] = jnp.zeros((length, heads), LOW)
            dq_sum = dq_sum + row_sum(dq)
            dv_sum = dv_sum + row_sum(dv)
        dproj[count:count + total, 0:3 * heads] = jnp.zeros((total, 3 * heads), LOW)
        dproj[count:count + total, 3 * heads:] = cm[...]
        v0[2:3, :] = jnp.concatenate([dq_sum, dv_sum, jnp.zeros((1, width - 2 * heads), F32)], axis=1)

    def weight_grads():
        for j in range(0, width, 256):
            col = slice(j, j + 256)
            ga[:, :, col] = dot(x[...], dproj[:, col], 0, 0).reshape(2 * n_u, shard, 256)

    def twin_weights():
        for k in range(2):
            peer_weights(k).wait()
        wpl[0:3 * heads, :] = wp[...].astype(LOW)
        wpl[3 * heads:, :] = wo[...].astype(LOW)
        dctx[...] = dot(x[count:count + total, :], wpl[3 * heads:, :], 1, 1).astype(LOW)

    def pick_bias(row):
        out = jnp.zeros((1, heads), F32)
        for slot in range(4):
            out = jnp.where(twin == slot, biases[row:row + 1, slot * heads:(slot + 1) * heads], out)
        return out

    scale = 1.0 / math.sqrt(HD)
    position = lax.broadcasted_iota(jnp.int32, (1, length), 1)
    my_half = pl.ds(pl.multiple_of(me.c * half, 8), half)
    its_half = pl.ds(pl.multiple_of((1 - me.c) * half, 8), half)
    my_quarter = pl.ds(pl.multiple_of(me.p * quarter, 8), quarter)
    its_quarter = pl.ds(pl.multiple_of((1 - me.p) * quarter, 8), quarter)

    def at(s, start=0, size=None):
        return pl.ds(pl.multiple_of(s * length + start, 8), size or length)

    def key_bias(s):
        return jnp.where(position < lens[s], 0.0, -1000000000.0)

    def project(s):
        xs = x[at(s), :]
        qp[...] = ((dot(xs, wpl[0:heads, :], 1, 1) + pick_bias(0)) * scale).astype(LOW)
        kp[...] = dot(xs, wpl[heads:2 * heads, :], 1, 1).astype(LOW)
        vp[...] = (dot(xs, wpl[2 * heads:3 * heads, :], 1, 1) + pick_bias(1)).astype(LOW)

    def attend_all(s):
        pieces = []
        for h in range(n_heads):
            col = slice(h * HD, (h + 1) * HD)
            e = dot(qp[:, col], kp[:, col], 1, 1) + key_bias(s)
            e = jnp.exp(e - jnp.max(e, axis=-1, keepdims=True))
            prob = (e / jnp.sum(e, axis=-1, keepdims=True)).astype(LOW)
            pieces.append(dot(prob, vp[:, col], 1, 0))
        ctxp[...] = jnp.concatenate(pieces, axis=1).astype(LOW)

    def mix_copy(s):
        return remote(sbuf.at[s], rbuf.at[s], sd_s.at[s], sd_r.at[s], me.core)

    def mix(s):
        for where, into in ((its_half, sbuf), (my_half, nrm)):
            base = at(s, where.start, half)
            into[s] = dot(ctx[base, :], wal[3 * heads:, :], 1, 0) + dot(ctxp[where, :], wpl[3 * heads:, :], 1, 0)
        mix_copy(s).start()

    def down_copy(s):
        return remote(dsc.at[s, its_quarter], rdn.at[s], sd_s.at[seqs + s], sd_r.at[seqs + s], me.y)

    def feed(s):
        mix_copy(s).wait()
        base = at(s, me.c * half, half)
        unit, _ = normalize(x[base, :].astype(F32) + (nrm[s] + rbuf[s]) + biases[2:3, :])
        normed = unit * gains[0:1, :] + biases[3:4, :]
        nrm[s] = normed
        low = normed.astype(LOW)
        total = jnp.zeros((half, width), F32)
        for w_in, w_back, slot in ((wil, wbl, me.t), (pil, pbl, me.t + 1 - 2 * me.c)):
            bias = hidden_bias(slot)
            for j in range(0, hidden, 256):
                col = slice(j, j + 256)
                pre = dot(low, w_in[:, col], 1, 0) + bias[:, col]
                act = pre * (0.5 * (1.0 + lax.erf(pre * (1.0 / math.sqrt(2.0)))))
                total = total + dot(act.astype(LOW), w_back[:, col], 1, 1)
        dsc[s] = total
        down_copy(s).start()

    def out_rows(s, p):
        return at(s, me.c * half + p * quarter, quarter)

    def out_copy(s, k, p, peer):
        src = fin.at[s] if k < 2 else out_h.at[out_rows(s, p)]
        return remote(src, out_h.at[out_rows(s, me.p if k < 2 else p)], sd_s.at[(2 + k) * seqs + s], sd_r.at[(2 + k) * seqs + s], peer)

    def finish(s):
        down_copy(s).wait()
        res = nrm[s, my_quarter] + (dsc[s, my_quarter] + rdn[s]) + biases[4:5, :]
        unit, _ = normalize(res)
        fin[s] = (unit * gains[1:2, :] + biases[5:6, :]).astype(LOW).astype(F32)
        fetch("out", fin.at[s], out_h.at[out_rows(s, me.p)])
        out_copy(s, 0, me.p, me.y).start()
        out_copy(s, 1, me.p, me.core).start()

    def relay(s):
        out_copy(s, 0, me.p, me.y).wait()
        out_copy(s, 2, 1 - me.p, me.core).start()

    def relay_end(s):
        out_copy(s, 1, me.p, me.core).wait()
        out_copy(s, 2, 1 - me.p, me.core).wait()

    def back(s):
        here = slice(s * rows, (s + 1) * rows)
        q = dot(pick[s], qp[...], 1, 0).astype(LOW)
        dc = dctx[here, :]

        def probs(h):
            col = slice(h * HD, (h + 1) * HD)
            scores = dot(q[:, col], kp[:, col], 1, 1) + key_bias(s)
            e = jnp.exp(scores - jnp.max(scores, axis=-1, keepdims=True))
            return e / jnp.sum(e, axis=-1, keepdims=True)

        dpp[...] = attend_back(q, kp, vp, dc, probs, pick[s])[0]

    def entry_copy(s):
        return remote(sbuf.at[s], rig.at[s], sd_s.at[5 * seqs + s], sd_r.at[5 * seqs + s], me.core)

    def entry(s):
        for where, into in ((its_half, sbuf), (my_half, rbuf)):
            base = at(s, where.start, half)
            product = lambda a, w: dot(a, w[0:3 * heads, :], 1, 0)

            def add(low, high, s=s, into=into):
                into[s] = product(*low) + product(*high)

            own_part = lambda base=base: (dproj[base, 0:3 * heads], wal)
            twin_part = lambda where=where: (dpp[where, :], wpl)
            pl.when(me.p == 0)(lambda add=add, a=own_part, b=twin_part: add(a(), b()))
            pl.when(me.p == 1)(lambda add=add, a=own_part, b=twin_part: add(b(), a()))
        entry_copy(s).start()

    def grad_rows(s):
        return at(s, me.c * half, half)

    def grad_copy(s):
        return remote(rbuf.at[s], grad_h.at[grad_rows(s)], sd_s.at[6 * seqs + s], sd_r.at[6 * seqs + s], me.core)

    def entry_end(s):
        entry_copy(s).wait()
        d_one = dres[pl.ds(s * rows, rows), :]
        high = d_one.astype(LOW)
        rest = (d_one - high.astype(F32)).astype(LOW)
        some = pick[s, :, pl.ds(pl.multiple_of(me.c * half, lanes), half)]
        rbuf[s] = (rbuf[s] + rig[s]) + (dot(some, high, 0, 0) + dot(some, rest, 0, 0))
        fetch("out", rbuf.at[s], grad_h.at[grad_rows(s)])
        grad_copy(s).start()

    def turn_weights():
        for j in range(0, width, lanes):
            flip[...] = turned[j:j + lanes, :].T
            wrow_a[:, j:j + lanes] = flip[mine, :]

    for k in range(2):
        peer_weights(k).start()
    ready("gi")
    reduce_step(0, 0)
    ready("one", "wal")
    first_norm_back()
    ready("att")
    own_back()
    ready("x")
    weight_grads()
    for u in range(n_u):
        net.start(lambda u=u: xswap(u))
    net.start(vec_x)
    reduce_step(0, 1)
    ready("mi", "gb", "wo", "wq", "ctx", "low")
    reduce_step(0, 2)
    vectors_one()
    reduce_end(0)
    update(0)
    gather_step(0, 0)
    reduce_step(1, 0)
    twin_weights()
    project(0)
    attend_all(0)
    mix(0)
    back(0)
    reduce_step(1, 1)
    gather_step(0, 1)
    feed(0)
    entry(0)
    vectors_two()
    project(1)
    reduce_step(1, 2)
    gather_step(0, 2)
    attend_all(1)
    mix(1)
    back(1)
    finish(0)
    feed(1)
    xswap_end()
    ready("mb")
    reduce_end(1)
    update(1)
    gather_step(1, 0)
    gather_step(0, 3)
    reduce_step(2, 0)
    entry(1)
    project(2)
    attend_all(2)
    mix(2)
    back(2)
    relay(0)
    reduce_step(2, 1)
    gather_step(1, 1)
    finish(1)
    feed(2)
    entry(2)
    entry_end(0)
    ready("ma")
    turn_weights()
    reduce_step(2, 2)
    gather_step(1, 2)
    entry_end(1)
    entry_end(2)
    vectors_three()
    relay(1)
    reduce_end(2)
    update(2)
    gather_step(2, 0)
    gather_step(1, 3)
    finish(2)
    gather_step(2, 1)
    relay(2)
    for s in range(seqs):
        relay_end(s)
        grad_copy(s).wait()
    gather_step(2, 2)
    gather_end(0)
    gather_step(2, 3)
    gather_end(1)
    gather_end(2)
    for j in range(0, width, lanes):
        turned[j:j + lanes, :] = ca[:, :, j:j + lanes].reshape(width, lanes).T
    fetch("out", turned.at[pl.ds(0, 3 * heads)], cq_h)
    fetch("out", turned.at[pl.ds(3 * heads, heads)], co_h)
    net.drain()
    ready("out")


def k2_call(lens, step, warmup, horizon, gains, biases, bias_in, k1, x, weights, moments):
    wqkv, wout, win, wback = weights
    count, width = x.shape
    seqs = lens.shape[0]
    heads, hidden = wout.shape[0], win.shape[1]
    length = count // seqs
    half, quarter = length // 2, length // 4
    shard = moments[1].shape[1]
    slots = width // shard
    n_u = slots // 2
    total = seqs * SPAN_ROWS
    units = seqs * (heads // HD)
    any_ = pl.BlockSpec(memory_space=pl.ANY)
    vm = pl.BlockSpec(memory_space=pltpu.VMEM)
    sm = pl.BlockSpec(memory_space=pltpu.SMEM)
    sds = lambda *shape: jax.ShapeDtypeStruct(shape, F32)
    V = lambda *shape: pltpu.VMEM(shape, F32)
    B = lambda *shape: pltpu.VMEM(shape, LOW)
    D = pltpu.SemaphoreType.DMA
    out_shape = (
        sds(count, width), sds(count, width), sds(3 * heads, width), sds(heads, width),
        sds(slots, shard, hidden), sds(slots, shard, hidden),
        sds(*moments[0].shape), sds(*moments[1].shape), sds(*moments[2].shape), sds(*moments[3].shape), sds(4, 16, width),
    )
    scratch = [
        B(count + total, width), V(slots, shard, width), V(n_u, shard, hidden), V(n_u, shard, hidden),
        B(count + total, width), B(count, heads), B(seqs, SPAN_ROWS, length), V(total, width),
        V(total, width), V(total, width), V(units, SPAN_ROWS, length), B(total, heads), B(count, heads), B(count, heads), B(total, heads), B(total, heads),
        V(3 * heads, width), V(heads, width),
        B(width, width), B(width, width), B(width, hidden), B(width, hidden), B(width, hidden), B(width, hidden),
        V(shard, hidden), V(shard, hidden), V(shard, width),
        V(*moments[0].shape), V(*moments[1].shape), V(*moments[2].shape), V(*moments[3].shape), V(width, width), V(width, 128),
        B(length, heads), B(length, heads), B(length, heads), B(length, heads), B(length, 3 * heads),
        V(seqs, half, width), V(seqs, half, width), V(seqs, half, width), V(seqs, half, width),
        V(seqs, quarter, width), V(seqs, quarter, width), V(seqs, half, width),
        V(2, 2, n_u - 1, shard, width), V(n_u, shard, width), V(slots, shard, width), V(3, shard, width),
        V(16, width), V(16, width), V(16, width), V(n_u, 16, width),
        D((64,)), D((3, 2, n_u - 1)), D((3, 2, n_u - 1)), D((3, 2, n_u - 1)), D((3, 2, n_u - 1)), D((3, 2 * n_u - 1)), D((3, 2 * n_u - 1)),
        D((n_u,)), D((n_u,)), D((n_u + 3,)), D((n_u + 3,)), D((7 * seqs,)), D((7 * seqs,)), D((2, 2)),
    ]
    return pl.pallas_call(
        k2_kernel, out_shape=out_shape,
        in_specs=[sm] * 4 + [vm] * 4 + [any_] * 28,
        out_specs=(any_,) * 10 + (vm,),
        scratch_shapes=scratch,
        compiler_params=pltpu.CompilerParams(collective_id=2, has_side_effects=True, vmem_limit_bytes=63 * 2**20),
    )(
        lens, step, warmup, horizon, gains, biases, bias_in, k1[-1], x, *k1[:-1], wqkv, wout, win, wback, *moments,
    )


def rates(step, warmup, horizon):
    clock = jnp.full((1, 128), step[0].astype(F32))
    warm = jnp.full((1, 128), warmup[0].astype(F32))
    far = jnp.full((1, 128), horizon[0].astype(F32))
    ratio = jnp.minimum(clock / warm, (far - clock) / (far - warm))[:, 0:1]
    return ratio, (1.0 - jnp.exp(clock * math.log(0.9)))[:, 0:1], (1.0 - jnp.exp(clock * math.log(0.999)))[:, 0:1]


def k3_kernel(
    step, warmup, horizon, gains, biases, bias_in, mom_g, mom_b, mom_h, vt, out_h, *refs
):
    n = 9
    srcs, (normed_o, *dsts), (ch_g, ch_b, ch_h, nm_g, nm_b, nm_h) = refs[:n], refs[n:2 * n + 1], refs[2 * n + 1:2 * n + 7]
    wide, low, held, rsem, wsem = refs[2 * n + 7], refs[2 * n + 8], refs[2 * n + 9:3 * n + 9], refs[-2], refs[-1]
    chunks, size = wide.shape[:2]
    reads, copies = [], []

    def read(src, dst):
        copy = pltpu.make_async_copy(src, dst, rsem.at[len(reads)])
        copy.start()
        reads.append(copy)

    def write(src, dst):
        copy = pltpu.make_async_copy(src, dst, wsem.at[len(copies)])
        copy.start()
        copies.append(copy)

    rows = [pl.ds(j * size, size) for j in range(chunks)]
    for j in range(chunks):
        read(out_h.at[rows[j]], wide.at[j])
    for src, buf in zip(srcs, held):
        read(src, buf)
    for j in range(chunks):
        reads[j].wait()
        low[j] = wide[j].astype(LOW)
        write(low.at[j], normed_o.at[rows[j]])
    for k, (buf, dst) in enumerate(zip(held, dsts)):
        reads[chunks + k].wait()
        write(buf, dst)
    put = (*rates(step, warmup, horizon), 0.0)
    heads = gains.shape[1] // 4
    hidden = vt.shape[2]
    lanes = 128
    common = vt[0]
    ch_g[...], nm_g[0], nm_g[1] = adam(gains[...], common[0:2], mom_g[0], mom_g[1], *put)
    query = jnp.concatenate([vt[k][2:3, 0:heads] for k in range(4)], axis=1)
    value = jnp.concatenate([vt[k][2:3, heads:2 * heads] for k in range(4)], axis=1)
    for row in range(6):
        grad = query if row == 0 else value if row == 1 else common[row + 1:row + 2]
        change, first, second = adam(biases[row:row + 1, :], grad, mom_b[row, 0:1], mom_b[row, 1:2], *put)
        ch_b[row:row + 1, :] = change
        nm_b[row, 0:1] = first
        nm_b[row, 1:2] = second
    parts = hidden // lanes
    for k in range(4):
        col = slice(k * hidden, (k + 1) * hidden)
        bias = jnp.concatenate([bias_in[k * parts + j:k * parts + j + 1, :] for j in range(parts)], axis=1)
        change, first, second = adam(bias, vt[k][8:9, :], mom_h[0:1, col], mom_h[1:2, col], *put)
        nm_h[0:1, col] = first
        nm_h[1:2, col] = second
        for j in range(parts):
            ch_h[k * parts + j:k * parts + j + 1, :] = change[:, j * lanes:(j + 1) * lanes]
    for copy in copies:
        copy.wait()


def k3_call(step, warmup, horizon, gains, biases, bias_in, mom_g, mom_b, mom_h, vt, big):
    any_ = pl.BlockSpec(memory_space=pl.ANY)
    vm = pl.BlockSpec(memory_space=pltpu.VMEM)
    sm = pl.BlockSpec(memory_space=pltpu.SMEM)
    of = lambda a: jax.ShapeDtypeStruct(a.shape, a.dtype)
    count, width = big[0].shape
    chunks = 6
    small = (gains, biases, bias_in, mom_g, mom_b, mom_h)
    return pl.pallas_call(
        k3_kernel,
        out_shape=(jax.ShapeDtypeStruct((count, width), LOW),) + tuple(map(of, big[1:])) + tuple(map(of, small)),
        in_specs=[sm] * 3 + [vm] * 7 + [any_] * len(big),
        out_specs=(any_,) * len(big) + (vm,) * 6,
        scratch_shapes=[
            pltpu.VMEM((chunks, count // chunks, width), F32), pltpu.VMEM((chunks, count // chunks, width), LOW),
            *(pltpu.VMEM(a.shape, F32) for a in big[1:]),
            pltpu.SemaphoreType.DMA((chunks + len(big),)), pltpu.SemaphoreType.DMA((chunks + len(big),)),
        ],
        compiler_params=pltpu.CompilerParams(vmem_limit_bytes=62 * 2**20),
    )(step, warmup, horizon, gains, biases, bias_in, mom_g, mom_b, mom_h, vt, *big)


def fast(tokens_in, cotangent, span_mask, lengths, step, warmup, total, w_qkv, w_out, w_in, w_back, gains, biases, bias_in,
         mom_qkv, mom_out, mom_in, mom_back, mom_gains, mom_biases, mom_bias_in):
    width = tokens_in.shape[1]
    heads, hidden = w_out.shape[1], w_in.shape[1]
    wqkv_t = jnp.transpose(w_qkv, (1, 2, 0)).reshape(3 * heads, width)
    wout_t = w_out.T
    bias_tiles = bias_in.reshape(-1, 128)
    k1 = k1_call(
        tokens_in, cotangent, span_mask.reshape(-1, 128), lengths, wqkv_t, wout_t, w_in, w_back, gains, biases, bias_tiles,
        width // mom_out.shape[1]
    )
    *big, vt = k2_call(
        lengths, step, warmup, total, gains, biases, bias_tiles, k1, tokens_in, (wqkv_t, wout_t, w_in, w_back),
        (jnp.transpose(mom_qkv, (0, 2, 1, 3)), mom_out, mom_in, mom_back)
    )
    (
        out, grad, cq, co, ci, cb, nmq, nmo, nmi, nmb, ch_g, ch_b, ch_h, nm_g, nm_b, nm_h
    ) = k3_call(
        step, warmup, total, gains, biases, bias_tiles, mom_gains, jnp.transpose(mom_biases, (1, 0, 2)), mom_bias_in, vt, big
    )
    return (
        out, grad, jnp.transpose(cq.reshape(3, heads, width), (2, 0, 1)), co.T,
        ci.reshape(width, hidden), cb.reshape(width, hidden), ch_g, ch_b, ch_h.reshape(-1),
        jnp.transpose(nmq, (0, 2, 1, 3)), nmo, nmi, nmb, nm_g, jnp.transpose(nm_b, (1, 0, 2)), nm_h,
    )


def layer_norm(values, gain, shift):
    center = values - jnp.mean(values, axis=-1, keepdims=True)
    spread = jnp.mean(center * center, axis=-1, keepdims=True)
    return center * lax.rsqrt(spread + NORM_EPS) * gain + shift


def exact_gelu(values):
    return jax.nn.gelu(values, approximate=False)


def outer_sum(left, right):
    return jnp.einsum("ta,tb->ab", left, right, preferred_element_type=jnp.float32)


def adam_step(weight, grad, moments, ratio, corr_one, corr_two, decay):
    first = BETA_ONE * moments[0] + (1.0 - BETA_ONE) * grad
    second = BETA_TWO * moments[1] + (1.0 - BETA_TWO) * grad * grad
    update = first / corr_one / (jnp.sqrt(second / corr_two) + ADAM_EPS) + decay * weight
    return (-ratio * update, jnp.stack([first, second]))


def on_device(
    tokens_in,
    cotangent,
    span_mask,
    lengths,
    step,
    warmup,
    total,
    w_qkv,
    w_out,
    w_in,
    w_back,
    gains,
    biases,
    bias_in,
    mom_qkv,
    mom_out,
    mom_in,
    mom_back,
    mom_gains,
    mom_biases,
    mom_bias_in,
):
    row_count, model_width = tokens_in.shape
    if mom_out.shape[1] % 8 == 0:
        return fast(
            tokens_in, cotangent, span_mask, lengths, step, warmup, total, w_qkv, w_out, w_in, w_back, gains, biases,
            bias_in, mom_qkv, mom_out, mom_in, mom_back, mom_gains, mom_biases, mom_bias_in
        )
    seq_count = lengths.shape[0]
    seq_length = row_count // seq_count
    head_cols = w_qkv.shape[2]
    hidden_cols = w_in.shape[1]
    head_size = HD
    local_heads = head_cols // head_size
    query_scale = 1.0 / math.sqrt(head_size)
    tensor_slot = lax.axis_index("tensor")
    bias_query = lax.dynamic_slice_in_dim(biases[0], tensor_slot * head_cols, head_cols)
    bias_value = lax.dynamic_slice_in_dim(biases[1], tensor_slot * head_cols, head_cols)
    bias_hidden = lax.dynamic_slice_in_dim(bias_in, tensor_slot * hidden_cols, hidden_cols)
    qkv_low = w_qkv.astype(jnp.bfloat16).reshape(model_width, 3 * head_cols)
    out_low = w_out.astype(jnp.bfloat16)
    in_low = w_in.astype(jnp.bfloat16)
    down_low = w_back.astype(jnp.bfloat16)
    projected = jnp.dot(tokens_in, qkv_low, preferred_element_type=jnp.float32).reshape(
        row_count, 3, head_cols
    )
    attn_shape = (seq_count, seq_length, local_heads, head_size)
    queries = (
        ((projected[:, 0] + bias_query) * query_scale).astype(jnp.bfloat16).reshape(attn_shape)
    )
    keys = projected[:, 1].astype(jnp.bfloat16).reshape(attn_shape)
    values = (projected[:, 2] + bias_value).astype(jnp.bfloat16).reshape(attn_shape)
    positions = jnp.arange(seq_length, dtype=jnp.int32)
    inside = positions[None, :] < lengths[:, None]
    key_bias = jnp.where(inside, 0.0, -1000000000.0).astype(jnp.float32)

    def score_block():
        raw = jnp.einsum("sqhd,skhd->shqk", queries, keys, preferred_element_type=jnp.float32)
        return raw + key_bias[:, None, None, :]

    scores = score_block()
    peak = jnp.max(scores, axis=-1, keepdims=True)
    log_total = peak + jnp.log(jnp.sum(jnp.exp(scores - peak), axis=-1, keepdims=True))
    probs_low = jnp.exp(scores - log_total).astype(jnp.bfloat16)
    context_low = (
        jnp.einsum("shqk,skhd->sqhd", probs_low, values, preferred_element_type=jnp.float32)
        .reshape(row_count, head_cols)
        .astype(jnp.bfloat16)
    )
    attn_part = jnp.einsum("tc,dc->td", context_low, out_low, preferred_element_type=jnp.float32)
    attn_sum = lax.psum(attn_part, "tensor")
    residual_one = tokens_in.astype(jnp.float32) + attn_sum + biases[2]
    normed = layer_norm(residual_one, gains[0], biases[3])
    normed_low = normed.astype(jnp.bfloat16)
    pre_act = jnp.dot(normed_low, in_low, preferred_element_type=jnp.float32) + bias_hidden
    act_low = exact_gelu(pre_act).astype(jnp.bfloat16)
    down_part = jnp.einsum("tf,df->td", act_low, down_low, preferred_element_type=jnp.float32)
    down_sum = lax.psum(down_part, "tensor")
    residual_two = normed + down_sum + biases[4]
    live = (inside.astype(jnp.int32) * span_mask.reshape(seq_count, seq_length)) > 0
    upto = (positions[:, None] <= positions[None, :]).astype(jnp.float32)
    rank = jnp.dot(live.astype(jnp.float32), upto).astype(jnp.int32) - 1
    slots = jnp.arange(SPAN_ROWS, dtype=jnp.int32)
    pick = (live[:, None, :] & (rank[:, None, :] == slots[None, :, None])).astype(jnp.float32)
    pick_low = pick.astype(jnp.bfloat16)

    def rows_of(values):
        width = values.shape[-1]
        return jnp.einsum(
            "srt,std->srd",
            pick,
            values.reshape(seq_count, seq_length, width),
            precision=lax.Precision.HIGHEST,
        ).reshape(seq_count * SPAN_ROWS, width)

    def low_rows_of(values):
        width = values.shape[-1]
        return jnp.einsum(
            "srt,std->srd",
            pick_low,
            values.reshape(seq_count, seq_length, width),
            preferred_element_type=jnp.bfloat16,
        ).reshape(seq_count * SPAN_ROWS, width)

    result = layer_norm(residual_two, gains[1], biases[5])
    normed_out = result.astype(jnp.bfloat16)
    residual_one_rows = rows_of(residual_one)
    residual_two_rows = rows_of(residual_two)
    grad_result = low_rows_of(cotangent).astype(jnp.float32)
    _, norm_two_back = jax.vjp(layer_norm, residual_two_rows, gains[1], biases[5])
    d_res_two, d_gain_two, d_shift_two = norm_two_back(grad_result)
    d_res_two_low = d_res_two.astype(jnp.bfloat16)
    normed_low_rows = low_rows_of(normed_low)
    pre_rows = jnp.dot(normed_low_rows, in_low, preferred_element_type=jnp.float32) + bias_hidden
    act_rows, gelu_back = jax.vjp(exact_gelu, pre_rows)
    grad_back = outer_sum(d_res_two_low, act_rows.astype(jnp.bfloat16))
    d_act = jnp.dot(d_res_two_low, down_low, preferred_element_type=jnp.float32)
    d_pre = gelu_back(d_act)[0]
    d_pre_low = d_pre.astype(jnp.bfloat16)
    grad_in = outer_sum(normed_low_rows, d_pre_low)
    d_normed_part = jnp.einsum("tf,df->td", d_pre_low, in_low, preferred_element_type=jnp.float32)
    d_normed = lax.psum(d_normed_part, "tensor") + d_res_two
    _, norm_one_back = jax.vjp(layer_norm, residual_one_rows, gains[0], biases[3])
    d_res_one, d_gain_one, d_shift_one = norm_one_back(d_normed)
    d_res_one_low = d_res_one.astype(jnp.bfloat16)
    grad_out_proj = outer_sum(d_res_one_low, low_rows_of(context_low))
    row_shape = (seq_count, SPAN_ROWS, local_heads, head_size)
    d_context = (
        jnp.dot(d_res_one_low, out_low, preferred_element_type=jnp.float32)
        .astype(jnp.bfloat16)
        .reshape(row_shape)
    )
    query_rows = low_rows_of(queries.reshape(row_count, head_cols)).reshape(row_shape)
    raw = jnp.einsum("sqhd,skhd->shqk", query_rows, keys, preferred_element_type=jnp.float32)
    probs = jax.nn.softmax(raw + key_bias[:, None, None, :], axis=-1)
    probs_again = probs.astype(jnp.bfloat16)
    d_probs = jnp.einsum("sqhd,skhd->shqk", d_context, values, preferred_element_type=jnp.float32)
    d_values = jnp.einsum(
        "shqk,sqhd->skhd", probs_again, d_context, preferred_element_type=jnp.float32
    ).reshape(row_count, head_cols)
    d_scores = (probs * (d_probs - jnp.sum(probs * d_probs, axis=-1, keepdims=True))).astype(
        jnp.bfloat16
    )
    d_queries = (
        jnp.einsum("shqk,skhd->sqhd", d_scores, keys, preferred_element_type=jnp.float32).reshape(
            seq_count * SPAN_ROWS, head_cols
        )
        * query_scale
    )
    d_keys = jnp.einsum(
        "shqk,sqhd->skhd", d_scores, query_rows, preferred_element_type=jnp.float32
    ).reshape(row_count, head_cols)

    def spread(row_values):
        width = row_values.shape[-1]
        return jnp.einsum(
            "srt,srd->std",
            pick,
            row_values.reshape(seq_count, SPAN_ROWS, width),
            precision=lax.Precision.HIGHEST,
        ).reshape(row_count, width)

    d_proj_low = (
        jnp.stack([spread(d_queries), d_keys, d_values], axis=1)
        .astype(jnp.bfloat16)
        .reshape(row_count, 3 * head_cols)
    )
    grad_qkv = outer_sum(tokens_in, d_proj_low).reshape(model_width, 3, head_cols)
    d_entry_part = jnp.einsum("tc,dc->td", d_proj_low, qkv_low, preferred_element_type=jnp.float32)
    input_grad = lax.psum(d_entry_part, "tensor") + spread(d_res_one)
    first_rank = (tensor_slot == 0).astype(jnp.float32)
    width_zero = jnp.zeros((model_width,), jnp.float32)

    def place_heads(partial_sum):
        return lax.dynamic_update_slice_in_dim(width_zero, partial_sum, tensor_slot * head_cols, 0)

    grad_gains = jnp.stack([d_gain_one, d_gain_two]) * first_rank
    grad_biases = jnp.stack(
        [
            place_heads(jnp.sum(d_queries, axis=0)),
            place_heads(jnp.sum(d_values, axis=0)),
            jnp.sum(d_res_one, axis=0) * first_rank,
            d_shift_one * first_rank,
            jnp.sum(d_res_two, axis=0) * first_rank,
            d_shift_two * first_rank,
        ]
    )
    grad_bias_in = lax.dynamic_update_slice_in_dim(
        jnp.zeros(bias_in.shape, jnp.float32), jnp.sum(d_pre, axis=0), tensor_slot * hidden_cols, 0
    )
    grad_gains, grad_biases, grad_bias_in = lax.psum(
        (grad_gains, grad_biases, grad_bias_in), ("dp", "tensor")
    )
    data_slot = lax.axis_index("dp")
    shard_rows = model_width // lax.axis_size("dp")
    owned = tuple(
        lax.psum_scatter(part, "dp", scatter_dimension=0, tiled=True)
        for part in (grad_qkv, grad_out_proj, grad_in, grad_back)
    )
    clock = step[0].astype(jnp.float32)
    warm = warmup[0].astype(jnp.float32)
    horizon = total[0].astype(jnp.float32)
    ratio = jnp.minimum(clock / warm, (horizon - clock) / (horizon - warm))
    corr_one = 1.0 - jnp.power(BETA_ONE, clock)
    corr_two = 1.0 - jnp.power(BETA_TWO, clock)
    change_rows = []
    fresh_moments = []
    for weight, grad_rows, moment in zip(
        (w_qkv, w_out, w_in, w_back), owned, (mom_qkv, mom_out, mom_in, mom_back)
    ):
        weight_rows = lax.dynamic_slice_in_dim(weight, data_slot * shard_rows, shard_rows, 0)
        row_change, new_moment = adam_step(
            weight_rows, grad_rows, moment, ratio, corr_one, corr_two, WEIGHT_DECAY
        )
        change_rows.append(row_change)
        fresh_moments.append(new_moment)
    change_qkv, change_out_proj, change_in_proj, change_back_proj = (
        lax.all_gather(change_rows[0], "dp", axis=0, tiled=True),
        lax.all_gather(change_rows[1], "dp", axis=0, tiled=True),
        lax.all_gather(change_rows[2], "dp", axis=0, tiled=True),
        lax.all_gather(change_rows[3], "dp", axis=0, tiled=True),
    )
    change_gains, new_mom_gains = adam_step(
        gains, grad_gains, mom_gains, ratio, corr_one, corr_two, 0.0
    )
    change_biases, new_mom_biases = adam_step(
        biases, grad_biases, mom_biases, ratio, corr_one, corr_two, 0.0
    )
    change_bias_in, new_mom_bias_in = adam_step(
        bias_in, grad_bias_in, mom_bias_in, ratio, corr_one, corr_two, 0.0
    )
    return (
        normed_out,
        input_grad,
        change_qkv,
        change_out_proj,
        change_in_proj,
        change_back_proj,
        change_gains,
        change_biases,
        change_bias_in,
        fresh_moments[0],
        fresh_moments[1],
        fresh_moments[2],
        fresh_moments[3],
        new_mom_gains,
        new_mom_biases,
        new_mom_bias_in,
    )


def solution(mesh):
    in_specs = (
        P("dp", None),
        P("dp", None),
        P("dp"),
        P("dp"),
        P(),
        P(),
        P(),
        P(None, None, "tensor"),
        P(None, "tensor"),
        P(None, "tensor"),
        P(None, "tensor"),
        P(),
        P(),
        P(),
        P(None, "dp", None, "tensor"),
        P(None, "dp", "tensor"),
        P(None, "dp", "tensor"),
        P(None, "dp", "tensor"),
        P(),
        P(),
        P(),
    )
    out_specs = (
        P("dp", None),
        P("dp", None),
        P(None, None, "tensor"),
        P(None, "tensor"),
        P(None, "tensor"),
        P(None, "tensor"),
        P(),
        P(),
        P(),
        P(None, "dp", None, "tensor"),
        P(None, "dp", "tensor"),
        P(None, "dp", "tensor"),
        P(None, "dp", "tensor"),
        P(),
        P(),
        P(),
    )
    return jax.shard_map(
        on_device, mesh=mesh, in_specs=in_specs, out_specs=out_specs, check_vma=False
    )
```

```python
import math

import jax
import jax.numpy as jnp
from jax import lax
from jax.experimental import pallas as pl
from jax.experimental.pallas import tpu as pltpu
from jax.sharding import PartitionSpec as P

HD = 64
SPAN_ROWS = 80
NORM_EPS = 1e-12
MESH = pl.DeviceIdType.MESH
F32 = jnp.float32
LOW = jnp.bfloat16


def dot(left, right, left_dim, right_dim):
    return lax.dot_general(
        left, right, (((left_dim,), (right_dim,)), ((), ())), preferred_element_type=F32
    )


def normalize(rows):
    center = rows - jnp.mean(rows, axis=-1, keepdims=True)
    scale = lax.rsqrt(jnp.mean(center * center, axis=-1, keepdims=True) + NORM_EPS)
    return center * scale, scale


def norm_back(grad, gain, unit, scale):
    weighted = grad * gain
    return scale * (
        weighted
        - jnp.mean(weighted, axis=-1, keepdims=True)
        - unit * jnp.mean(weighted * unit, axis=-1, keepdims=True)
    )


def row_sum(rows):
    return jnp.sum(rows, axis=0, keepdims=True)


class Peers:
    def __init__(self):
        self.d = lax.axis_index("dp")
        self.t = lax.axis_index("tensor")
        self.b = lax.rem(self.d, 2)
        self.c = lax.rem(self.t, 2)
        self.p = lax.div(self.t, 2)
        self.u = lax.div(self.d, 2)
        self.core = (self.d, self.t + 1 - 2 * self.c)
        self.y = (self.d, lax.rem(self.t + 2, 4))
        self.x = (self.d + 1 - 2 * self.b, self.t)


def send(src, dst, sems, k, peer):
    copy = pltpu.make_async_remote_copy(
        src_ref=src, dst_ref=dst, send_sem=sems.at[0, k], recv_sem=sems.at[1, k],
        device_id=peer, device_id_type=MESH,
    )
    copy.start()
    return copy


def local(src, dst, sem):
    copy = pltpu.make_async_copy(src, dst, sem)
    copy.start()
    return copy


def greet(peers):
    barrier = pltpu.get_barrier_semaphore()
    for peer in peers:
        pl.semaphore_signal(barrier, inc=1, device_id=peer, device_id_type=MESH)
    pl.semaphore_wait(barrier, len(peers))


def gelu_parts(pre):
    cdf = 0.5 * (1.0 + lax.erf(pre * (1.0 / math.sqrt(2.0))))
    pdf = jnp.exp(-0.5 * pre * pre) * (1.0 / math.sqrt(2.0 * math.pi))
    return pre * cdf, cdf + pre * pdf


def k1_kernel(
    lens, mask, gains, biases, bias_in, x_h, cot_h, wqkv_h, wout_h, win_h, wback_h,
    gi_h, gb_h, full_h, res_h, dres_h, pick_h, pm_h, qm_h, k_h, v_h, cm_h, ctx_h, wal_h, wpl_h, wil_h, wbl_h, pil_h, pbl_h, vec,
    x, cot, wqkv, wout, win, wback, wp_qkv, wp_out, pwin, pwback, q_o, k_o, v_o, ctx_o, pick_o, wal, wpl, wil, wbl, pil, pbl, gin, gback,
    pm, xm, cotm, qm, ctxm, cml, ctxp, ap, apc, normed, nlow, act, gp, part, rc1, h1, ry1,
    part2, rc2, h2, ry2, full2, full, dres2, d2w, d2x, nxw, nxx, dplow,
    lsem, rsem,
):
    seqs, rows = 3, SPAN_ROWS
    count = x_h.shape[0]
    length = count // seqs
    total = seqs * rows
    half = total // 2
    heads = ctx_o.shape[1]
    n_heads = heads // HD
    width = x_h.shape[1]
    me = Peers()

    def seq(s):
        return pl.ds(s * length, length)

    loads = [
        local(wqkv_h, wqkv, lsem.at[0]),
        local(wout_h, wout, lsem.at[1]),
    ] + [local(x_h.at[seq(s)], x.at[seq(s)], lsem.at[2 + s]) for s in range(seqs)] + [
        local(win_h, win, lsem.at[2 + seqs]),
        local(wback_h, wback, lsem.at[3 + seqs]),
        local(cot_h, cot, lsem.at[4 + seqs]),
    ]
    stores = []

    def keep(src, dst):
        stores.append(local(src, dst, lsem.at[8 + len(stores)]))

    slots = gin.shape[0]
    shard = gin.shape[1]
    n_u = slots // 2
    z = me.u
    greet([me.core, me.y, me.x] + [(2 * lax.rem(z + k, n_u) + me.b, me.t) for k in range(1, n_u)])

    loads[1].wait()
    out_half = pl.ds(pl.multiple_of(me.b * (heads // 2), 8), heads // 2)
    wo_y = send(wout.at[out_half], wp_out.at[out_half], rsem, 0, me.y)
    loads[0].wait()
    wal[0:3 * heads, :] = wqkv[...].astype(LOW)
    wal[3 * heads:, :] = wout[...].astype(LOW)
    keep(wal, wal_h)

    def pick_bias(row, k=heads):
        out = jnp.zeros((1, k), F32)
        for slot in range(4):
            piece = biases[row:row + 1, slot * k:(slot + 1) * k]
            out = jnp.where(me.t == slot, piece, out)
        return out

    bias_q, bias_v = pick_bias(0), pick_bias(1)
    hidden = win.shape[1]
    lanes = 128
    bias_h = jnp.concatenate(
        [bias_in[pl.ds(me.t * (hidden // lanes) + j, 1), :] for j in range(hidden // lanes)], axis=1
    )
    upto = (
        lax.broadcasted_iota(jnp.int32, (length, length), 0)
        <= lax.broadcasted_iota(jnp.int32, (length, length), 1)
    ).astype(F32).astype(LOW)
    position = lax.broadcasted_iota(jnp.int32, (1, length), 1)
    slot_of = lax.broadcasted_iota(jnp.int32, (rows, length), 0).astype(F32)
    scale = 1.0 / math.sqrt(HD)
    def project(s):
        loads[2 + s].wait()
        at = seq(s)
        xs = x[at, :]
        q = ((dot(xs, wal[0:heads, :], 1, 1) + bias_q) * scale).astype(LOW)
        k = dot(xs, wal[heads:2 * heads, :], 1, 1).astype(LOW)
        v = (dot(xs, wal[2 * heads:3 * heads, :], 1, 1) + bias_v).astype(LOW)
        q_o[at, :] = q
        k_o[at, :] = k
        v_o[at, :] = v
        parts = length // lanes
        marks = jnp.concatenate([mask[pl.ds(s * parts + j, 1), :] for j in range(parts)], axis=1)
        inside = position < lens[s]
        live = jnp.where(inside, marks, 0).astype(F32)
        rank = dot(jnp.broadcast_to(live, (8, length)).astype(LOW), upto, 1, 0)[0:1] - 1.0
        pick = jnp.where((rank == slot_of) & (live > 0.0), 1.0, 0.0).astype(LOW)
        pick_o[s] = pick
        here = pl.ds(s * rows, rows)
        xm[here, :] = dot(pick, xs, 1, 0)
        qrow = dot(pick, q, 1, 0).astype(LOW)
        qm[here, :] = qrow
        key_bias = jnp.where(inside, 0.0, -1000000000.0)
        pieces = []
        for h in range(n_heads):
            col = slice(h * HD, (h + 1) * HD)
            scores = dot(qrow[:, col], k[:, col], 1, 1) + key_bias
            e = jnp.exp(scores - jnp.max(scores, axis=-1, keepdims=True))
            prob = e / jnp.sum(e, axis=-1, keepdims=True)
            pm[s * n_heads + h] = prob
            pieces.append(dot(prob.astype(LOW), v[:, col], 1, 0))
        low = jnp.concatenate(pieces, axis=1).astype(LOW)
        cml[here, :] = low
        ctxm[here, :] = low.astype(F32)
        return send(ctxm.at[here], ctxp.at[here], rsem, 24 + s, me.y)

    ctx_y = [project(s) for s in range(seqs)]
    wo_y.wait()
    wo_x = send(wp_out.at[out_half], wp_out.at[out_half], rsem, 2, me.x)
    third = heads // 2

    def qkv_part(k):
        return pl.ds(pl.multiple_of(me.b * (3 * third) + k * third, 8), third)

    def fetch(k):
        return send(wqkv.at[qkv_part(k)], wp_qkv.at[qkv_part(k)], rsem, 16 + k, me.y)

    def swap(k):
        return send(wp_qkv.at[qkv_part(k)], wp_qkv.at[qkv_part(k)], rsem, 19 + k, me.x)

    share = 2 * third // n_u

    def share_of(b, u):
        return pl.ds(pl.multiple_of(b * (3 * third) + third + u * share, 8), share)

    def chain_copy(way, s, b, u):
        place = wp_qkv.at[share_of(b, u)]
        k = 29 + (way * (n_u - 1) + s) * 2 + b
        peer = (me.d + 2, me.t) if way == 0 else (me.d - 2, me.t)
        return pltpu.make_async_remote_copy(
            src_ref=place, dst_ref=place, send_sem=rsem.at[0, k], recv_sem=rsem.at[1, k],
            device_id=peer, device_id_type=MESH,
        )

    def chain_cases(s):
        return [
            (way, b, z - s if way == 0 else z + s, (z >= s) if way == 0 else (z + s <= n_u - 1), (z < n_u - 1) if way == 0 else (z > 0))
            for way in range(2) for b in range(2)
        ]

    def chain_step(s):
        for way, b, u, here, edge in chain_cases(s):
            if s > 0:
                pl.when(here)(lambda way=way, b=b, u=u: chain_copy(way, s - 1, b, u).wait_recv())
            if s < n_u - 1:
                pl.when(here & edge)(lambda way=way, b=b, u=u: chain_copy(way, s, b, u).start())

    def chain_sent():
        for s in range(n_u - 1):
            for way, b, u, here, edge in chain_cases(s):
                pl.when(here & edge)(lambda way=way, b=b, u=u, s=s: chain_copy(way, s, b, u).wait_send())

    def attend_all(s):
        at = slice(s * length, (s + 1) * length)
        key_bias = jnp.where(position < lens[s], 0.0, -1000000000.0)
        pieces = []
        for h in range(n_heads):
            col = slice(h * HD, (h + 1) * HD)
            scores = dot(q_o[at, col], k_o[at, col], 1, 1) + key_bias
            e = jnp.exp(scores - jnp.max(scores, axis=-1, keepdims=True))
            prob = (e / jnp.sum(e, axis=-1, keepdims=True)).astype(LOW)
            pieces.append(dot(prob, v_o[at, col], 1, 0))
        ctx_o[at, :] = jnp.concatenate(pieces, axis=1).astype(LOW)

    mine_share = share_of(me.b, z)
    wz_y = send(wqkv.at[mine_share], wp_qkv.at[mine_share], rsem, 27, me.y)
    for ref, out in ((pm, pm_h), (qm, qm_h), (k_o, k_h), (v_o, v_h), (cml, cm_h), (pick_o, pick_h)):
        keep(ref, out)
    for load in loads[2 + seqs:4 + seqs]:
        load.wait()
    wil[...] = win[...].astype(LOW)
    wbl[...] = wback[...].astype(LOW)
    keep(wil, wil_h)
    keep(wbl, wbl_h)
    loads[4 + seqs].wait()
    for s in range(seqs):
        cotm[s * rows:(s + 1) * rows, :] = dot(pick_o[s], cot[s * length:(s + 1) * length, :], 1, 0)
    wo_x.wait()
    for copy in ctx_y:
        copy.wait()
    woq = wp_out[...].astype(LOW)

    def mix(first, second):
        ap[...] = dot(*first, 1, 0) + dot(*second, 1, 0)

    own_part = lambda: (cml[...], wal[3 * heads:, :])
    twin_part = lambda: (ctxp[...].astype(LOW), woq)
    pl.when(me.p == 0)(lambda: mix(own_part(), twin_part()))
    pl.when(me.p == 1)(lambda: mix(twin_part(), own_part()))
    ap_c = send(ap, apc, rsem, 3, me.core)
    wz_y.wait()
    wz_x = send(wp_qkv.at[mine_share], wp_qkv.at[mine_share], rsem, 28, me.x)
    wq_y = fetch(0)
    ap_c.wait()
    xm[...] = xm[...] + (ap[...] + apc[...]) + biases[2:3, :]
    keep(xm, res_h)
    unit, inv = normalize(xm[...])
    normed[...] = unit * gains[0:1, :] + biases[3:4, :]
    nlow[...] = normed[...].astype(LOW)
    nxw[...] = nlow[...].astype(F32)
    mine = pl.ds(pl.multiple_of(me.c * half, 8), half)
    other = pl.ds(pl.multiple_of((1 - me.c) * half, 8), half)
    nx_x = send(nxw.at[mine], nxx.at[mine], rsem, 5, me.x)
    for j in range(0, hidden, 256):
        col = slice(j, j + 256)
        a, g = gelu_parts(dot(nlow[...], wil[:, col], 1, 0) + bias_h[:, col])
        act[:, col] = a.astype(LOW)
        gp[:, col] = g
    part[...] = dot(act[...], wbl[...], 1, 1)

    def all_reduce(src, rc, hs, ry, dst, base, fill):
        first = send(src.at[other], rc, rsem, base, me.core)
        first.wait()
        hs[...] = src[mine, :] + rc[...]
        second = send(hs, ry, rsem, base + 1, me.y)
        fill()
        second.wait()
        dst[mine, :] = hs[...] + ry[...]
        third = send(dst.at[mine], dst.at[mine], rsem, base + 2, me.core)
        third.wait()

    relay = []

    def fill_one():
        wide.append(send(win, pwin, rsem, 22, me.core))
        wz_x.wait()
        chain_step(0)
        attend_all(0)
        attend_all(1)
        nx_x.wait()
        relay.append(send(nxx.at[mine], nxx.at[mine], rsem, 6, me.core))
        wq_y.wait()
        relay.append(swap(0))
        chain_step(1)

    wide = []
    all_reduce(part, rc1, h1, ry1, full, 7, fill_one)
    relay[0].wait()
    unit, inv = normalize(normed[...] + full[...] + biases[4:5, :])
    grad = cotm[...]
    d_two = norm_back(grad, gains[1:2, :], unit, inv)
    dres2[...] = d_two
    vec[...] = jnp.zeros(vec.shape, F32)
    vec[1:2, :] = row_sum(grad * unit)
    vec[5:6, :] = row_sum(d_two)
    vec[6:7, :] = row_sum(grad)
    d2w[...] = d_two.astype(LOW).astype(F32)
    d2_x = send(d2w.at[mine], d2x.at[mine], rsem, 10, me.x)
    keep(dres2, dres_h)
    d2low = d2w[...].astype(LOW)
    for j in range(0, hidden, 256):
        col = slice(j, j + 256)
        d_pre = dot(d2low, wbl[:, col], 1, 0) * gp[:, col]
        vec[8:9, col] = row_sum(d_pre)
        dplow[:, col] = d_pre.astype(LOW)
    part2[...] = dot(dplow[...], wil[...], 1, 1)

    def cut(rows):
        return rows.reshape(slots, shard, rows.shape[1])

    def fill_two():
        wide.append(send(wback, pwback, rsem, 23, me.core))
        attend_all(2)
        chain_step(2)
        keep(ctx_o, ctx_h)
        for j in range(0, hidden, 256):
            col = slice(j, j + 256)
            gin[:, :, col] = cut(dot(nlow[...], dplow[:, col], 0, 0))
            gback[:, :, col] = cut(dot(d2low, act[:, col], 0, 0))
        wide[0].wait()
        pil[...] = pwin[...].astype(LOW)
        keep(pil, pil_h)
        relay[1].wait()
        d2_x.wait()
        relay.append(send(d2x.at[mine], d2x.at[mine], rsem, 11, me.core))

    all_reduce(part2, rc2, h2, ry2, full2, 12, fill_two)
    keep(full2, full_h)
    relay[2].wait()
    nlx = nxx[...].astype(LOW)
    dlx = d2x[...].astype(LOW)
    for j in range(0, hidden, 256):
        col = slice(j, j + 256)
        a, g = gelu_parts(dot(nlx, wil[:, col], 1, 0) + bias_h[:, col])
        d_pre = (dot(dlx, wbl[:, col], 1, 0) * g).astype(LOW)
        gin[:, :, col] += cut(dot(nlx, d_pre, 0, 0))
        gback[:, :, col] += cut(dot(dlx, a.astype(LOW), 0, 0))
    for u in range(slots // 2):
        keep(gin.at[2 * u + me.b], gi_h.at[u])
        keep(gback.at[2 * u + me.b], gb_h.at[u])
    for step in range(3, n_u):
        chain_step(step)
    wpl[0:3 * heads, :] = wp_qkv[...].astype(LOW)
    wpl[3 * heads:, :] = woq
    keep(wpl, wpl_h)
    wide[1].wait()
    pbl[...] = pwback[...].astype(LOW)
    keep(pbl, pbl_h)
    chain_sent()
    for copy in stores:
        copy.wait()


def k1_call(x, cot, mask, lens, wqkv, wout, win, wback, gains, biases, bias_in, slots):
    count, width = x.shape
    seqs = lens.shape[0]
    heads = wout.shape[0]
    hidden = win.shape[1]
    length = count // seqs
    total = seqs * SPAN_ROWS
    half = total // 2
    units = seqs * (heads // HD)
    any_ = pl.BlockSpec(memory_space=pl.ANY)
    vm = pl.BlockSpec(memory_space=pltpu.VMEM)
    sm = pl.BlockSpec(memory_space=pltpu.SMEM)
    sds = jax.ShapeDtypeStruct
    V = pltpu.VMEM
    wide = lambda r, t=F32: V((r, width), t)
    block = (slots // 2, width // slots, hidden)
    square = sds((width, hidden), LOW)
    out_shape = (
        sds(block, F32), sds(block, F32), sds((total, width), F32), sds((total, width), F32), sds((total, width), F32),
        sds((seqs, SPAN_ROWS, length), LOW), sds((units, SPAN_ROWS, length), F32), sds((total, heads), LOW),
        sds((count, heads), LOW), sds((count, heads), LOW), sds((total, heads), LOW), sds((count, heads), LOW),
        sds((4 * heads, width), LOW), sds((4 * heads, width), LOW), square, square, square, square,
        sds((16, width), F32),
    )
    scratch = [
        wide(count, LOW), wide(count, LOW), wide(3 * heads), wide(heads), V((width, hidden), F32),
        V((width, hidden), F32), wide(3 * heads), wide(heads), V((width, hidden), F32), V((width, hidden), F32),
        V((count, heads), LOW), V((count, heads), LOW), V((count, heads), LOW), V((count, heads), LOW),
        V((seqs, SPAN_ROWS, length), LOW), wide(4 * heads, LOW), wide(4 * heads, LOW), V((width, hidden), LOW), V((width, hidden), LOW),
        V((width, hidden), LOW), V((width, hidden), LOW), V((slots, width // slots, hidden), F32), V((slots, width // slots, hidden), F32),
        V((units, SPAN_ROWS, length), F32), wide(total), wide(total), V((total, heads), LOW),
        V((total, heads), F32), V((total, heads), LOW), V((total, heads), F32), wide(total), wide(total),
        wide(total), wide(total, LOW), V((total, hidden), LOW), V((total, hidden), F32), wide(total), wide(half), wide(half), wide(half),
        wide(total), wide(half), wide(half), wide(half), wide(total), wide(total), wide(total), wide(total), wide(total), wide(total), wide(total),
        V((total, hidden), LOW),
        pltpu.SemaphoreType.DMA((8 + 20 + slots,)), pltpu.SemaphoreType.DMA((2, 29 + 2 * slots)),
    ]
    return pl.pallas_call(
        k1_kernel, out_shape=out_shape,
        in_specs=[sm, vm, vm, vm, vm] + [any_] * 6,
        out_specs=(any_,) * (len(out_shape) - 1) + (vm,),
        scratch_shapes=scratch,
        compiler_params=pltpu.CompilerParams(
            collective_id=1, has_side_effects=True, vmem_limit_bytes=60 * 2**20
        ),
    )(lens, mask, gains, biases, bias_in, x, cot, wqkv, wout, win, wback)


BETA_ONE = 0.9
BETA_TWO = 0.999
ADAM_EPS = 1e-06
WEIGHT_DECAY = 0.01


def adam(weight, grad, first, second, ratio, corr_one, corr_two, decay):
    first = BETA_ONE * first + (1.0 - BETA_ONE) * grad
    second = BETA_TWO * second + (1.0 - BETA_TWO) * grad * grad
    update = first / corr_one / (jnp.sqrt(second / corr_two) + ADAM_EPS) + decay * weight
    return -ratio * update, first, second


FLIGHT = 0.55
PLAN_READY = (1.2, 1.2, 3.2)
SWAP_FIRST = ((0, 0),)
WEIGHT = {("RS", 0, 0): 8.0, ("RS", 1, 0): 7.0, ("RS", 2, 0): -7.0, ("RS", 2, 1): -10.0, ("AG", 0, 0): -10.0}
BLOCK_US = 3.38


def plan(n, weight):
    tasks = {}
    for ch in range(3):
        for p in range(2):
            ready = PLAN_READY[ch]
            swap = ch == 2
            both = (ch, p) in SWAP_FIRST
            for z in range(n):
                if swap:
                    for u in range(n):
                        tasks["XS", ch, p, 0, u, z] = ("X", z), [], ready
                for d in range(n):
                    if d == z:
                        continue
                    step = 1 if d > z else -1
                    kind = "RSR" if d > z else "RSL"
                    need = [(kind, ch, p, 0, d, z - step)] if 0 <= z - step < n else []
                    if swap:
                        need.append(("XS", ch, p, 0, d, z))
                    tasks[kind, ch, p, 0, d, z] = (kind[2], z), need, ready
                end = [("RSR", ch, p, 0, z, z - 1)] if z > 0 else []
                if z < n - 1:
                    end.append(("RSL", ch, p, 0, z, z + 1))
                if swap:
                    end.append(("XS", ch, p, 0, z, z))
                for par in (0, 1) if both else (0,):
                    for u in range(n):
                        if u == z:
                            need = [("AGX", ch, p, 0, z, z)] if par else end
                        else:
                            need = [("AGR", ch, p, par, u, z - 1) if u < z else ("AGL", ch, p, par, u, z + 1)]
                        if u <= z < n - 1:
                            tasks["AGR", ch, p, par, u, z] = ("R", z), need, 0.0
                        if 0 < z <= u:
                            tasks["AGL", ch, p, par, u, z] = ("L", z), need, 0.0
                        if par == 0 and (u == z or not both):
                            tasks["AGX", ch, p, 0, u, z] = ("X", z), need, 0.0
    after = {key: [] for key in tasks}
    for key, (_, need, _) in tasks.items():
        for one in need:
            after[one].append(key)
    rank = {}

    def longest(key):
        if key not in rank:
            rank[key] = 1.0 + FLIGHT + max([longest(k) for k in after[key]], default=0.0)
        return rank[key]

    missing = {key: len(task[1]) for key, task in tasks.items()}
    open_at = {key: task[2] for key, task in tasks.items() if not task[1]}
    free, done, order = {}, {}, []
    while open_at:
        by_link = {}
        for key in open_at:
            by_link.setdefault(tasks[key][0], []).append(key)
        best = None
        for link, keys in by_link.items():
            start = max(free.get(link, 0.0), min(open_at[k] for k in keys))
            able = [k for k in keys if open_at[k] <= start + 1e-9]
            key = max(able, key=lambda k: (longest(k) + weight.get((k[0][:2] if k[0] != "AGX" else "AX", k[1], k[2]), 0.0), -open_at[k]))
            if best is None or start < best[0] - 1e-9:
                best = start, key
        start, key = best
        free[tasks[key][0]] = start + 1.0
        done[key] = start + 1.0 + FLIGHT
        order.append((start, key))
        del open_at[key]
        for k in after[key]:
            missing[k] -= 1
            if missing[k] == 0:
                open_at[k] = max(max(done[q] for q in tasks[k][1]) + 0.15, tasks[k][2])
    return order, tasks, max(done.values())


def k2_kernel(
    lens, step, warmup, horizon, gains, biases, bias_in, vec,
    x_h, gi_h, gb_h, full_h, res_h, dtwo_h, pick_h, pm_h, qm_h, k_h, v_h, cm_h, ctx_h, wal_h, wpl_h, wil_h, wbl_h, pil_h, pbl_h,
    wqkv_h, wout_h, win_h, wback_h, mq_h, mo_h, mi_h, mb_h,
    out_h, grad_h, cq_h, co_h, ci_h, cb_h, nmq_h, nmo_h, nmi_h, nmb_h, vt,
    x, ga, gi, gb, dproj, ctx, pick, dres, full, dtwo, pm, qm, ko, vo, cm, dctx, wal, wpl, wil, wbl, pil, pbl,
    wrow_i, wrow_b, wrow_a, mq, mo, mi, mb, turned, flip,
    qp, kp, vp, ctxp, dpp, sbuf, rbuf, nrm, dsc, rdn, fin, rig,
    ring, xr, ca, own, v0, v1, vx, vz,
    lsem, rs_s, rs_r, ag_s, ag_r, ax_s, ax_r, xs_s, xs_r, vs_s, vs_r, sd_s, sd_r, usem,
):
    me = Peers()
    n_u = gi.shape[0]
    seqs = sbuf.shape[0]
    count, width = x_h.shape
    length = count // seqs
    rows = SPAN_ROWS
    total = seqs * rows
    heads = ctx.shape[1]
    n_heads = heads // HD
    shard = gi.shape[1]
    hidden = wil.shape[1]
    half = length // 2
    quarter = length // 4
    z, b = me.u, me.b
    right = (me.d + 2, me.t)
    left = (me.d - 2, me.t)
    diag = (me.d, 3 - me.t)

    def remote(src, dst, ss, rr, peer):
        return pltpu.make_async_remote_copy(
            src_ref=src, dst_ref=dst, send_sem=ss, recv_sem=rr, device_id=peer, device_id_type=MESH
        )

    pend = {}
    order = iter(range(64))

    def fetch(name, src, dst):
        copy = pltpu.make_async_copy(src, dst, lsem.at[next(order)])
        copy.start()
        pend.setdefault(name, []).append(copy)

    def ready(*names):
        for name in names:
            for copy in pend.pop(name, []):
                copy.wait()

    fetch("one", full_h, full)
    fetch("one", res_h, dres)
    fetch("one", dtwo_h, dtwo)
    fetch("gi", gi_h, gi)
    fetch("gb", gb_h, gb)
    fetch("wal", wal_h, wal)
    fetch("att", pick_h, pick)
    fetch("att", pm_h, pm)
    fetch("att", qm_h, qm)
    fetch("att", k_h, ko)
    fetch("att", v_h, vo)
    fetch("att", cm_h, cm)
    fetch("x", x_h, x.at[pl.ds(0, count)])
    fetch("wpl", wpl_h, wpl)
    fetch("ctx", ctx_h, ctx)
    fetch("low", wil_h, wil)
    fetch("low", wbl_h, wbl)
    fetch("low", pil_h, pil)
    fetch("low", pbl_h, pbl)
    mine = pl.ds(pl.multiple_of(me.d * shard, 8), shard)
    fetch("mi", win_h.at[mine], wrow_i)
    fetch("mi", mi_h, mi)
    fetch("mb", wback_h.at[mine], wrow_b)
    fetch("mb", mb_h, mb)
    fetch("ma", wqkv_h, turned.at[pl.ds(0, 3 * heads)])
    fetch("ma", wout_h, turned.at[pl.ds(3 * heads, heads)])
    fetch("ma", mq_h, mq)
    fetch("ma", mo_h, mo)

    others = [(2 * lax.rem(z + k, n_u) + b, me.t) for k in range(1, n_u)]
    greet([me.core, me.y, diag, me.x] + others)

    order_all, tasks, _ = plan(n_u, WEIGHT)
    part_rows = shard // 2

    def rows_of(p):
        return pl.ds(p * part_rows, part_rows)

    def g_at(ch, u):
        return ga.at[2 * u + b] if ch == 2 else (gi, gb)[ch].at[u]

    def target(ch, d):
        return ca.at[d] if ch == 2 else (ci_h, cb_h)[ch].at[d]

    def xr_at(u, p):
        return xr.at[u, rows_of(p)]

    def ring_at(key):
        kind, ch, p, _, d, node = key
        place = d - (node + 1) if kind == "RSR" else (node - 1) - d
        return ring.at[ch, 0 if kind == "RSR" else 1, place, rows_of(p)]

    def transfer(key, incoming):
        kind, ch, p, par, u, node = key
        way = 0 if kind[2:] == "R" else 1
        if kind == "XS":
            k = p * n_u + u
            return remote(ga.at[2 * u + 1 - b, rows_of(p)], xr_at(u, p), xs_s.at[k], xs_r.at[k], me.x)
        if kind[:2] == "RS":
            k = ((ch * 2 + p) * 2 + way) * n_u + u
            peer = right if way == 0 else left
            return remote(g_at(ch, u).at[rows_of(p)], ring_at(key), rs_s.at[k], rs_r.at[k], peer)
        parity = b if (par == 0) != (incoming and kind == "AGX") else 1 - b
        there = target(ch, 2 * u + parity).at[rows_of(p)]
        here = own.at[ch, rows_of(p)] if u == node and par == 0 else there
        if kind == "AGX":
            k = (ch * 2 + p) * n_u + u
            return remote(here, there, ax_s.at[k], ax_r.at[k], me.x)
        k = (((ch * 2 + p) * 2 + way) * 2 + par) * n_u + u
        return remote(here, there, ag_s.at[k], ag_r.at[k], right if way == 0 else left)

    ratio, corr_one, corr_two = rates(step, warmup, horizon)

    def own_copy(ch, p):
        return pltpu.make_async_copy(own.at[ch, rows_of(p)], target(ch, me.d).at[rows_of(p)], usem.at[ch * 2 + p])

    def update(ch, p):
        at_p = rows_of(p)
        if ch < 2:
            w, m = ((wrow_i, mi), (wrow_b, mb))[ch]
            change, first, second = adam(
                w[at_p, :], g_at(ch, z)[at_p, :], m[0, at_p, :], m[1, at_p, :], ratio, corr_one, corr_two, WEIGHT_DECAY
            )
            own[ch, at_p, :] = change
            m[0, at_p, :] = first
            m[1, at_p, :] = second
        else:
            for k in range(4):
                col = slice(k * heads, (k + 1) * heads)
                first = mo[0, at_p, :] if k == 3 else mq[0, k, at_p, :]
                second = mo[1, at_p, :] if k == 3 else mq[1, k, at_p, :]
                change, first, second = adam(
                    wrow_a[at_p, col], ga[me.d, at_p, col], first, second, ratio, corr_one, corr_two, WEIGHT_DECAY
                )
                own[2, at_p, col] = change
                if k < 3:
                    mq[0, k, at_p, :] = first
                    mq[1, k, at_p, :] = second
                else:
                    mo[0, at_p, :] = first
                    mo[1, at_p, :] = second
        own_copy(ch, p).start()

    queue = [[] for _ in range(n_u)]
    inbound = [[] for _ in range(n_u)]
    for start, key in order_all:
        kind, node = key[0], key[5]
        queue[node].append((start * BLOCK_US, key))
        goes = node if kind in ("XS", "AGX") else node + 1 if kind[2] == "R" else node - 1
        inbound[goes].append(key)
    for node in range(n_u):
        queue[node].sort(key=lambda one: one[0])
    got = [set() for _ in range(n_u)]
    made = [set() for _ in range(n_u)]
    sent = [[] for _ in range(n_u)]

    def arrive(node, key):
        if key in got[node]:
            return
        got[node].add(key)
        transfer(key, True).wait_recv()
        kind, ch, p, _, u, _ = key
        if kind == "XS":
            ga[2 * u + b, rows_of(p)] += xr_at(u, p)[...]
        elif kind[:2] == "RS":
            g_at(ch, u)[rows_of(p), :] += ring_at(key)[...]

    def act(node, key):
        for need in tasks[key][1]:
            arrive(node, need)
        kind, ch, p, par, u, _ = key
        if kind[:2] == "AG" and u == node and par == 0 and (ch, p) not in made[node]:
            made[node].add((ch, p))
            update(ch, p)
        sent[node].append(key)
        transfer(key, False).start()

    def chain_until(until):
        for node in range(n_u):
            due = [key for start, key in queue[node] if start < until]
            queue[node] = [one for one in queue[node] if one[0] >= until]
            if due:
                pl.when(z == node)(lambda node=node, due=due: [act(node, key) for key in due] and None)

    def chain_end():
        for node in range(n_u):
            def settle(node=node):
                for key in inbound[node]:
                    arrive(node, key)
                for key in sent[node]:
                    transfer(key, False).wait_send()
            pl.when(z == node)(settle)
        for ch in range(3):
            for p in range(2):
                own_copy(ch, p).wait()

    def vec_x():
        return remote(v0, vx, vs_s.at[0], vs_r.at[0], me.x)

    def vec_z(k):
        peer = (2 * lax.rem(z + k, n_u) + b, me.t)
        return remote(v1, vz.at[z], vs_s.at[k], vs_r.at[k], peer)

    def vec_t(k, peer):
        return remote(v1, vt.at[me.t], vs_s.at[n_u + k], vs_r.at[n_u + k], peer)

    trio = (me.core, me.y, diag)

    def vectors_one():
        vec_x().wait()
        v1[...] = v0[...] + vx[...]
        vz[z] = v1[...]
        for k in range(1, n_u):
            vec_z(k).start()

    def vectors_two():
        for k in range(1, n_u):
            vec_z(k).wait()
        total = vz[0]
        for u in range(1, n_u):
            total = total + vz[u]
        v1[...] = total
        vt[me.t] = total
        for k, peer in enumerate(trio):
            vec_t(k, peer).start()

    def vectors_three():
        for k, peer in enumerate(trio):
            vec_t(k, peer).wait()

    lanes = 128

    def hidden_bias(slot):
        parts = hidden // lanes
        return jnp.concatenate([bias_in[pl.ds(slot * parts + j, 1), :] for j in range(parts)], axis=1)

    twin = lax.rem(me.t + 2, 4)

    def first_norm_back():
        d_normed = full[...] + dtwo[...]
        unit, inv = normalize(dres[...])
        d_one = norm_back(d_normed, gains[0:1, :], unit, inv)
        dres[...] = d_one
        v0[...] = vec[...]
        v0[0:1, :] = row_sum(d_normed * unit)
        v0[3:4, :] = row_sum(d_one)
        v0[4:5, :] = row_sum(d_normed)
        low = d_one.astype(LOW)
        x[count:count + total, :] = low
        dctx[...] = dot(low, wal[3 * heads:, :], 1, 1).astype(LOW)

    def attend_back(q, k, v, dc, probs, pick_s):
        dqs, dks, dvs = [], [], []
        for h in range(n_heads):
            col = slice(h * HD, (h + 1) * HD)
            prob = probs(h)
            d_prob = dot(dc[:, col], v[:, col], 1, 1)
            dvs.append(dot(prob.astype(LOW), dc[:, col], 0, 0))
            ds = (prob * (d_prob - jnp.sum(prob * d_prob, axis=-1, keepdims=True))).astype(LOW)
            dqs.append(dot(ds, k[:, col], 1, 0) * scale)
            dks.append(dot(ds, q[:, col], 0, 0))
        dq = jnp.concatenate(dqs, axis=1)
        dv = jnp.concatenate(dvs, axis=1)
        spread = dot(pick_s, dq.astype(LOW), 0, 0).astype(LOW)
        return jnp.concatenate([spread, jnp.concatenate(dks, axis=1).astype(LOW), dv.astype(LOW)], axis=1), dq, dv

    def own_back(s):
        here = slice(s * rows, (s + 1) * rows)
        low, dq, dv = attend_back(
            qm[here, :], ko.at[at(s)], vo.at[at(s)], dctx[here, :], lambda h: pm[s * n_heads + h], pick[s]
        )
        dproj[at(s), 0:3 * heads] = low
        dproj[at(s), 3 * heads:] = jnp.zeros((length, heads), LOW)
        sums = jnp.concatenate([row_sum(dq), row_sum(dv)], axis=1)
        v0[2:3, 0:2 * heads] = sums if s == 0 else v0[2:3, 0:2 * heads] + sums

    def weight_grads(j):
        if j == 0:
            dproj[count:count + total, 0:3 * heads] = jnp.zeros((total, 3 * heads), LOW)
            dproj[count:count + total, 3 * heads:] = cm[...]
        col = slice(j * 256, (j + 1) * 256)
        ga[:, :, col] = dot(x[...], dproj[:, col], 0, 0).reshape(2 * n_u, shard, 256)

    def twin_rows():
        dctx[...] = dot(x[count:count + total, :], wpl[3 * heads:, :], 1, 1).astype(LOW)

    def pick_bias(row):
        out = jnp.zeros((1, heads), F32)
        for slot in range(4):
            out = jnp.where(twin == slot, biases[row:row + 1, slot * heads:(slot + 1) * heads], out)
        return out

    scale = 1.0 / math.sqrt(HD)
    position = lax.broadcasted_iota(jnp.int32, (1, length), 1)
    my_half = pl.ds(pl.multiple_of(me.c * half, 8), half)
    its_half = pl.ds(pl.multiple_of((1 - me.c) * half, 8), half)
    my_quarter = pl.ds(pl.multiple_of(me.p * quarter, 8), quarter)
    its_quarter = pl.ds(pl.multiple_of((1 - me.p) * quarter, 8), quarter)

    def at(s, start=0, size=None):
        return pl.ds(pl.multiple_of(s * length + start, 8), size or length)

    def key_bias(s):
        return jnp.where(position < lens[s], 0.0, -1000000000.0)

    def project(s):
        xs = x[at(s), :]
        qp[...] = ((dot(xs, wpl[0:heads, :], 1, 1) + pick_bias(0)) * scale).astype(LOW)
        kp[...] = dot(xs, wpl[heads:2 * heads, :], 1, 1).astype(LOW)
        vp[...] = (dot(xs, wpl[2 * heads:3 * heads, :], 1, 1) + pick_bias(1)).astype(LOW)

    def attend_one(s, h):
        col = slice(h * HD, (h + 1) * HD)
        e = dot(qp[:, col], kp[:, col], 1, 1) + key_bias(s)
        e = jnp.exp(e - jnp.max(e, axis=-1, keepdims=True))
        prob = (e / jnp.sum(e, axis=-1, keepdims=True)).astype(LOW)
        ctxp[:, col] = dot(prob, vp[:, col], 1, 0).astype(LOW)

    def mix_copy(s):
        return remote(sbuf.at[s], rbuf.at[s], sd_s.at[s], sd_r.at[s], me.core)

    def mix(s):
        for where, into in ((its_half, sbuf), (my_half, nrm)):
            base = at(s, where.start, half)
            into[s] = dot(ctx[base, :], wal[3 * heads:, :], 1, 0) + dot(ctxp[where, :], wpl[3 * heads:, :], 1, 0)
        mix_copy(s).start()

    def down_copy(s):
        return remote(dsc.at[s, its_quarter], rdn.at[s], sd_s.at[seqs + s], sd_r.at[seqs + s], me.y)

    def feed_start(s):
        mix_copy(s).wait()
        base = at(s, me.c * half, half)
        unit, _ = normalize(x[base, :].astype(F32) + (nrm[s] + rbuf[s]) + biases[2:3, :])
        nrm[s] = unit * gains[0:1, :] + biases[3:4, :]

    def feed(s, part):
        w_in, w_back, slot = ((wil, wbl, me.t), (pil, pbl, me.t + 1 - 2 * me.c))[part]
        low = nrm[s].astype(LOW)
        bias = hidden_bias(slot)
        total = dsc[s] if part else jnp.zeros((half, width), F32)
        for j in range(0, hidden, 256):
            col = slice(j, j + 256)
            pre = dot(low, w_in[:, col], 1, 0) + bias[:, col]
            act_low = pre * (0.5 * (1.0 + lax.erf(pre * (1.0 / math.sqrt(2.0)))))
            total = total + dot(act_low.astype(LOW), w_back[:, col], 1, 1)
        dsc[s] = total
        if part:
            down_copy(s).start()

    def out_rows(s, p):
        return at(s, me.c * half + p * quarter, quarter)

    def out_copy(s, k, p, peer):
        src = fin.at[s] if k < 2 else out_h.at[out_rows(s, p)]
        return remote(src, out_h.at[out_rows(s, me.p if k < 2 else p)], sd_s.at[(2 + k) * seqs + s], sd_r.at[(2 + k) * seqs + s], peer)

    def finish(s):
        down_copy(s).wait()
        res = nrm[s, my_quarter] + (dsc[s, my_quarter] + rdn[s]) + biases[4:5, :]
        unit, _ = normalize(res)
        fin[s] = (unit * gains[1:2, :] + biases[5:6, :]).astype(LOW).astype(F32)
        fetch("out", fin.at[s], out_h.at[out_rows(s, me.p)])
        out_copy(s, 0, me.p, me.y).start()
        out_copy(s, 1, me.p, me.core).start()

    def relay(s):
        out_copy(s, 0, me.p, me.y).wait()
        out_copy(s, 2, 1 - me.p, me.core).start()

    def relay_end(s):
        out_copy(s, 1, me.p, me.core).wait()
        out_copy(s, 2, 1 - me.p, me.core).wait()

    def back(s):
        here = slice(s * rows, (s + 1) * rows)
        q = dot(pick[s], qp[...], 1, 0).astype(LOW)
        dc = dctx[here, :]

        def probs(h):
            col = slice(h * HD, (h + 1) * HD)
            scores = dot(q[:, col], kp[:, col], 1, 1) + key_bias(s)
            e = jnp.exp(scores - jnp.max(scores, axis=-1, keepdims=True))
            return e / jnp.sum(e, axis=-1, keepdims=True)

        dpp[...] = attend_back(q, kp, vp, dc, probs, pick[s])[0]

    def entry_copy(s):
        return remote(sbuf.at[s], rig.at[s], sd_s.at[5 * seqs + s], sd_r.at[5 * seqs + s], me.core)

    def entry(s):
        for where, into in ((its_half, sbuf), (my_half, rbuf)):
            base = at(s, where.start, half)
            product = lambda a, w: dot(a, w[0:3 * heads, :], 1, 0)

            def add(low, high, s=s, into=into):
                into[s] = product(*low) + product(*high)

            own_part = lambda base=base: (dproj[base, 0:3 * heads], wal)
            twin_part = lambda where=where: (dpp[where, :], wpl)
            pl.when(me.p == 0)(lambda add=add, a=own_part, b=twin_part: add(a(), b()))
            pl.when(me.p == 1)(lambda add=add, a=own_part, b=twin_part: add(b(), a()))
        entry_copy(s).start()

    def grad_rows(s):
        return at(s, me.c * half, half)

    def grad_copy(s):
        return remote(rbuf.at[s], grad_h.at[grad_rows(s)], sd_s.at[6 * seqs + s], sd_r.at[6 * seqs + s], me.core)

    def entry_end(s):
        entry_copy(s).wait()
        d_one = dres[pl.ds(s * rows, rows), :]
        high = d_one.astype(LOW)
        rest = (d_one - high.astype(F32)).astype(LOW)
        some = pick[s, :, pl.ds(pl.multiple_of(me.c * half, lanes), half)]
        rbuf[s] = (rbuf[s] + rig[s]) + (dot(some, high, 0, 0) + dot(some, rest, 0, 0))
        fetch("out", rbuf.at[s], grad_h.at[grad_rows(s)])
        grad_copy(s).start()

    def turn_weights():
        for j in range(0, width, lanes):
            flip[...] = turned[j:j + lanes, :].T
            wrow_a[:, j:j + lanes] = flip[mine, :]

    def begin():
        ready("gi", "gb")

    def own_start():
        ready("one", "wal")
        first_norm_back()
        ready("att")

    def moments_in():
        ready("mi", "mb", "ma")
        turn_weights()

    def twin_start():
        ready("wpl", "ctx", "low")
        twin_rows()

    work = [(0.0, begin), (4.4, own_start)]
    work += [(5.4 + s, lambda s=s: own_back(s)) for s in range(seqs)]
    work += [(8.4, lambda: ready("x"))] + [(8.5 + 0.7 * j, lambda j=j: weight_grads(j)) for j in range(width // 256)]
    work += [(10.7, lambda: vec_x().start()), (14.0, moments_in), (20.0, vectors_one), (28.0, vectors_two)]
    first_twin = 14.0
    for s in range(seqs):
        t = first_twin + 14.0 * s
        work += [(t, lambda s=s: (twin_start() if s == 0 else None, project(s)) and None)]
        work += [(t + 1.5 + h, lambda s=s, h=h: attend_one(s, h)) for h in range(n_heads)]
        work += [(t + 5.0, lambda s=s: mix(s)), (t + 5.5, lambda s=s: back(s)), (t + 7.5, lambda s=s: feed_start(s))]
        work += [(t + 8.0, lambda s=s: feed(s, 0)), (t + 9.5, lambda s=s: feed(s, 1)), (t + 11.0, lambda s=s: entry(s))]
        work += [(t + 20.5, lambda s=s: finish(s)), (t + 34.0, lambda s=s: relay(s)), (t + 17.0, lambda s=s: entry_end(s))]
    work += [(40.0, vectors_three)]
    for when, do in sorted(work, key=lambda one: one[0]):
        chain_until(when)
        do()
    for when in range(80, 120, 2):
        chain_until(float(when))
    chain_until(1e9)
    for s in range(seqs):
        relay_end(s)
        grad_copy(s).wait()
    chain_end()
    for j in range(0, width, lanes):
        turned[j:j + lanes, :] = ca[:, :, j:j + lanes].reshape(width, lanes).T
    fetch("out", turned.at[pl.ds(0, 3 * heads)], cq_h)
    fetch("out", turned.at[pl.ds(3 * heads, heads)], co_h)
    for ref, out in ((mi, nmi_h), (mb, nmb_h), (mq, nmq_h), (mo, nmo_h)):
        fetch("out", ref, out)
    ready("out")


def k2_call(lens, step, warmup, horizon, gains, biases, bias_in, k1, x, weights, moments):
    wqkv, wout, win, wback = weights
    count, width = x.shape
    seqs = lens.shape[0]
    heads, hidden = wout.shape[0], win.shape[1]
    length = count // seqs
    half, quarter = length // 2, length // 4
    shard = moments[1].shape[1]
    slots = width // shard
    n_u = slots // 2
    total = seqs * SPAN_ROWS
    units = seqs * (heads // HD)
    any_ = pl.BlockSpec(memory_space=pl.ANY)
    vm = pl.BlockSpec(memory_space=pltpu.VMEM)
    sm = pl.BlockSpec(memory_space=pltpu.SMEM)
    sds = lambda *shape: jax.ShapeDtypeStruct(shape, F32)
    V = lambda *shape: pltpu.VMEM(shape, F32)
    B = lambda *shape: pltpu.VMEM(shape, LOW)
    D = pltpu.SemaphoreType.DMA
    out_shape = (
        sds(count, width), sds(count, width), sds(3 * heads, width), sds(heads, width),
        sds(slots, shard, hidden), sds(slots, shard, hidden),
        sds(*moments[0].shape), sds(*moments[1].shape), sds(*moments[2].shape), sds(*moments[3].shape), sds(4, 16, width),
    )
    scratch = [
        B(count + total, width), V(slots, shard, width), V(n_u, shard, hidden), V(n_u, shard, hidden),
        B(count + total, width), B(count, heads), B(seqs, SPAN_ROWS, length), V(total, width),
        V(total, width), V(total, width), V(units, SPAN_ROWS, length), B(total, heads), B(count, heads), B(count, heads), B(total, heads), B(total, heads),
        B(width, width), B(width, width), B(width, hidden), B(width, hidden), B(width, hidden), B(width, hidden),
        V(shard, hidden), V(shard, hidden), V(shard, width),
        V(*moments[0].shape), V(*moments[1].shape), V(*moments[2].shape), V(*moments[3].shape), V(width, width), V(width, 128),
        B(length, heads), B(length, heads), B(length, heads), B(length, heads), B(length, 3 * heads),
        V(seqs, half, width), V(seqs, half, width), V(seqs, half, width), V(seqs, half, width),
        V(seqs, quarter, width), V(seqs, quarter, width), V(seqs, half, width),
        V(3, 2, n_u - 1, shard, width), V(n_u, shard, width), V(slots, shard, width), V(3, shard, width),
        V(16, width), V(16, width), V(16, width), V(n_u, 16, width),
        D((64,)), D((12 * n_u,)), D((12 * n_u,)), D((24 * n_u,)), D((24 * n_u,)), D((6 * n_u,)), D((6 * n_u,)),
        D((2 * n_u,)), D((2 * n_u,)), D((n_u + 3,)), D((n_u + 3,)), D((7 * seqs,)), D((7 * seqs,)), D((6,)),
    ]
    return pl.pallas_call(
        k2_kernel, out_shape=out_shape,
        in_specs=[sm] * 4 + [vm] * 4 + [any_] * 27,
        out_specs=(any_,) * 10 + (vm,),
        scratch_shapes=scratch,
        compiler_params=pltpu.CompilerParams(collective_id=2, has_side_effects=True, vmem_limit_bytes=63 * 2**20),
    )(
        lens, step, warmup, horizon, gains, biases, bias_in, k1[-1], x, *k1[:-1], wqkv, wout, win, wback, *moments,
    )


def rates(step, warmup, horizon):
    clock = jnp.full((1, 128), step[0].astype(F32))
    warm = jnp.full((1, 128), warmup[0].astype(F32))
    far = jnp.full((1, 128), horizon[0].astype(F32))
    ratio = jnp.minimum(clock / warm, (far - clock) / (far - warm))[:, 0:1]
    return ratio, (1.0 - jnp.exp(clock * math.log(0.9)))[:, 0:1], (1.0 - jnp.exp(clock * math.log(0.999)))[:, 0:1]


def k3_kernel(
    step, warmup, horizon, gains, biases, bias_in, mom_g, mom_b, mom_h, vt, out_h, *refs
):
    n = 9
    srcs, (normed_o, *dsts), (ch_g, ch_b, ch_h, nm_g, nm_b, nm_h) = refs[:n], refs[n:2 * n + 1], refs[2 * n + 1:2 * n + 7]
    wide, low, held, rsem, wsem = refs[2 * n + 7], refs[2 * n + 8], refs[2 * n + 9:3 * n + 9], refs[-2], refs[-1]
    chunks, size = wide.shape[:2]
    reads, copies = [], []

    def read(src, dst):
        copy = pltpu.make_async_copy(src, dst, rsem.at[len(reads)])
        copy.start()
        reads.append(copy)

    def write(src, dst):
        copy = pltpu.make_async_copy(src, dst, wsem.at[len(copies)])
        copy.start()
        copies.append(copy)

    rows = [pl.ds(j * size, size) for j in range(chunks)]
    for j in range(chunks):
        read(out_h.at[rows[j]], wide.at[j])
    for src, buf in zip(srcs, held):
        read(src, buf)
    for j in range(chunks):
        reads[j].wait()
        low[j] = wide[j].astype(LOW)
        write(low.at[j], normed_o.at[rows[j]])
    for k, (buf, dst) in enumerate(zip(held, dsts)):
        reads[chunks + k].wait()
        write(buf, dst)
    put = (*rates(step, warmup, horizon), 0.0)
    heads = gains.shape[1] // 4
    hidden = vt.shape[2]
    lanes = 128
    common = vt[0]
    ch_g[...], nm_g[0], nm_g[1] = adam(gains[...], common[0:2], mom_g[0], mom_g[1], *put)
    query = jnp.concatenate([vt[k][2:3, 0:heads] for k in range(4)], axis=1)
    value = jnp.concatenate([vt[k][2:3, heads:2 * heads] for k in range(4)], axis=1)
    for row in range(6):
        grad = query if row == 0 else value if row == 1 else common[row + 1:row + 2]
        change, first, second = adam(biases[row:row + 1, :], grad, mom_b[row, 0:1], mom_b[row, 1:2], *put)
        ch_b[row:row + 1, :] = change
        nm_b[row, 0:1] = first
        nm_b[row, 1:2] = second
    parts = hidden // lanes
    for k in range(4):
        col = slice(k * hidden, (k + 1) * hidden)
        bias = jnp.concatenate([bias_in[k * parts + j:k * parts + j + 1, :] for j in range(parts)], axis=1)
        change, first, second = adam(bias, vt[k][8:9, :], mom_h[0:1, col], mom_h[1:2, col], *put)
        nm_h[0:1, col] = first
        nm_h[1:2, col] = second
        for j in range(parts):
            ch_h[k * parts + j:k * parts + j + 1, :] = change[:, j * lanes:(j + 1) * lanes]
    for copy in copies:
        copy.wait()


def k3_call(step, warmup, horizon, gains, biases, bias_in, mom_g, mom_b, mom_h, vt, big):
    any_ = pl.BlockSpec(memory_space=pl.ANY)
    vm = pl.BlockSpec(memory_space=pltpu.VMEM)
    sm = pl.BlockSpec(memory_space=pltpu.SMEM)
    of = lambda a: jax.ShapeDtypeStruct(a.shape, a.dtype)
    count, width = big[0].shape
    chunks = 6
    small = (gains, biases, bias_in, mom_g, mom_b, mom_h)
    return pl.pallas_call(
        k3_kernel,
        out_shape=(jax.ShapeDtypeStruct((count, width), LOW),) + tuple(map(of, big[1:])) + tuple(map(of, small)),
        in_specs=[sm] * 3 + [vm] * 7 + [any_] * len(big),
        out_specs=(any_,) * len(big) + (vm,) * 6,
        scratch_shapes=[
            pltpu.VMEM((chunks, count // chunks, width), F32), pltpu.VMEM((chunks, count // chunks, width), LOW),
            *(pltpu.VMEM(a.shape, F32) for a in big[1:]),
            pltpu.SemaphoreType.DMA((chunks + len(big),)), pltpu.SemaphoreType.DMA((chunks + len(big),)),
        ],
        compiler_params=pltpu.CompilerParams(vmem_limit_bytes=62 * 2**20),
    )(step, warmup, horizon, gains, biases, bias_in, mom_g, mom_b, mom_h, vt, *big)


def fast(tokens_in, cotangent, span_mask, lengths, step, warmup, total, w_qkv, w_out, w_in, w_back, gains, biases, bias_in,
         mom_qkv, mom_out, mom_in, mom_back, mom_gains, mom_biases, mom_bias_in):
    width = tokens_in.shape[1]
    heads, hidden = w_out.shape[1], w_in.shape[1]
    wqkv_t = jnp.transpose(w_qkv, (1, 2, 0)).reshape(3 * heads, width)
    wout_t = w_out.T
    bias_tiles = bias_in.reshape(-1, 128)
    k1 = k1_call(
        tokens_in, cotangent, span_mask.reshape(-1, 128), lengths, wqkv_t, wout_t, w_in, w_back, gains, biases, bias_tiles,
        width // mom_out.shape[1]
    )
    *big, vt = k2_call(
        lengths, step, warmup, total, gains, biases, bias_tiles, k1, tokens_in, (wqkv_t, wout_t, w_in, w_back),
        (jnp.transpose(mom_qkv, (0, 2, 1, 3)), mom_out, mom_in, mom_back)
    )
    (
        out, grad, cq, co, ci, cb, nmq, nmo, nmi, nmb, ch_g, ch_b, ch_h, nm_g, nm_b, nm_h
    ) = k3_call(
        step, warmup, total, gains, biases, bias_tiles, mom_gains, jnp.transpose(mom_biases, (1, 0, 2)), mom_bias_in, vt, big
    )
    return (
        out, grad, jnp.transpose(cq.reshape(3, heads, width), (2, 0, 1)), co.T,
        ci.reshape(width, hidden), cb.reshape(width, hidden), ch_g, ch_b, ch_h.reshape(-1),
        jnp.transpose(nmq, (0, 2, 1, 3)), nmo, nmi, nmb, nm_g, jnp.transpose(nm_b, (1, 0, 2)), nm_h,
    )


def layer_norm(values, gain, shift):
    center = values - jnp.mean(values, axis=-1, keepdims=True)
    spread = jnp.mean(center * center, axis=-1, keepdims=True)
    return center * lax.rsqrt(spread + NORM_EPS) * gain + shift


def exact_gelu(values):
    return jax.nn.gelu(values, approximate=False)


def outer_sum(left, right):
    return jnp.einsum("ta,tb->ab", left, right, preferred_element_type=jnp.float32)


def adam_step(weight, grad, moments, ratio, corr_one, corr_two, decay):
    first = BETA_ONE * moments[0] + (1.0 - BETA_ONE) * grad
    second = BETA_TWO * moments[1] + (1.0 - BETA_TWO) * grad * grad
    update = first / corr_one / (jnp.sqrt(second / corr_two) + ADAM_EPS) + decay * weight
    return (-ratio * update, jnp.stack([first, second]))


def on_device(
    tokens_in,
    cotangent,
    span_mask,
    lengths,
    step,
    warmup,
    total,
    w_qkv,
    w_out,
    w_in,
    w_back,
    gains,
    biases,
    bias_in,
    mom_qkv,
    mom_out,
    mom_in,
    mom_back,
    mom_gains,
    mom_biases,
    mom_bias_in,
):
    row_count, model_width = tokens_in.shape
    if mom_out.shape[1] % 8 == 0:
        return fast(
            tokens_in, cotangent, span_mask, lengths, step, warmup, total, w_qkv, w_out, w_in, w_back, gains, biases,
            bias_in, mom_qkv, mom_out, mom_in, mom_back, mom_gains, mom_biases, mom_bias_in
        )
    seq_count = lengths.shape[0]
    seq_length = row_count // seq_count
    head_cols = w_qkv.shape[2]
    hidden_cols = w_in.shape[1]
    head_size = HD
    local_heads = head_cols // head_size
    query_scale = 1.0 / math.sqrt(head_size)
    tensor_slot = lax.axis_index("tensor")
    bias_query = lax.dynamic_slice_in_dim(biases[0], tensor_slot * head_cols, head_cols)
    bias_value = lax.dynamic_slice_in_dim(biases[1], tensor_slot * head_cols, head_cols)
    bias_hidden = lax.dynamic_slice_in_dim(bias_in, tensor_slot * hidden_cols, hidden_cols)
    qkv_low = w_qkv.astype(jnp.bfloat16).reshape(model_width, 3 * head_cols)
    out_low = w_out.astype(jnp.bfloat16)
    in_low = w_in.astype(jnp.bfloat16)
    down_low = w_back.astype(jnp.bfloat16)
    projected = jnp.dot(tokens_in, qkv_low, preferred_element_type=jnp.float32).reshape(
        row_count, 3, head_cols
    )
    attn_shape = (seq_count, seq_length, local_heads, head_size)
    queries = (
        ((projected[:, 0] + bias_query) * query_scale).astype(jnp.bfloat16).reshape(attn_shape)
    )
    keys = projected[:, 1].astype(jnp.bfloat16).reshape(attn_shape)
    values = (projected[:, 2] + bias_value).astype(jnp.bfloat16).reshape(attn_shape)
    positions = jnp.arange(seq_length, dtype=jnp.int32)
    inside = positions[None, :] < lengths[:, None]
    key_bias = jnp.where(inside, 0.0, -1000000000.0).astype(jnp.float32)

    def score_block():
        raw = jnp.einsum("sqhd,skhd->shqk", queries, keys, preferred_element_type=jnp.float32)
        return raw + key_bias[:, None, None, :]

    scores = score_block()
    peak = jnp.max(scores, axis=-1, keepdims=True)
    log_total = peak + jnp.log(jnp.sum(jnp.exp(scores - peak), axis=-1, keepdims=True))
    probs_low = jnp.exp(scores - log_total).astype(jnp.bfloat16)
    context_low = (
        jnp.einsum("shqk,skhd->sqhd", probs_low, values, preferred_element_type=jnp.float32)
        .reshape(row_count, head_cols)
        .astype(jnp.bfloat16)
    )
    attn_part = jnp.einsum("tc,dc->td", context_low, out_low, preferred_element_type=jnp.float32)
    attn_sum = lax.psum(attn_part, "tensor")
    residual_one = tokens_in.astype(jnp.float32) + attn_sum + biases[2]
    normed = layer_norm(residual_one, gains[0], biases[3])
    normed_low = normed.astype(jnp.bfloat16)
    pre_act = jnp.dot(normed_low, in_low, preferred_element_type=jnp.float32) + bias_hidden
    act_low = exact_gelu(pre_act).astype(jnp.bfloat16)
    down_part = jnp.einsum("tf,df->td", act_low, down_low, preferred_element_type=jnp.float32)
    down_sum = lax.psum(down_part, "tensor")
    residual_two = normed + down_sum + biases[4]
    live = (inside.astype(jnp.int32) * span_mask.reshape(seq_count, seq_length)) > 0
    upto = (positions[:, None] <= positions[None, :]).astype(jnp.float32)
    rank = jnp.dot(live.astype(jnp.float32), upto).astype(jnp.int32) - 1
    slots = jnp.arange(SPAN_ROWS, dtype=jnp.int32)
    pick = (live[:, None, :] & (rank[:, None, :] == slots[None, :, None])).astype(jnp.float32)
    pick_low = pick.astype(jnp.bfloat16)

    def rows_of(values):
        width = values.shape[-1]
        return jnp.einsum(
            "srt,std->srd",
            pick,
            values.reshape(seq_count, seq_length, width),
            precision=lax.Precision.HIGHEST,
        ).reshape(seq_count * SPAN_ROWS, width)

    def low_rows_of(values):
        width = values.shape[-1]
        return jnp.einsum(
            "srt,std->srd",
            pick_low,
            values.reshape(seq_count, seq_length, width),
            preferred_element_type=jnp.bfloat16,
        ).reshape(seq_count * SPAN_ROWS, width)

    result = layer_norm(residual_two, gains[1], biases[5])
    normed_out = result.astype(jnp.bfloat16)
    residual_one_rows = rows_of(residual_one)
    residual_two_rows = rows_of(residual_two)
    grad_result = low_rows_of(cotangent).astype(jnp.float32)
    _, norm_two_back = jax.vjp(layer_norm, residual_two_rows, gains[1], biases[5])
    d_res_two, d_gain_two, d_shift_two = norm_two_back(grad_result)
    d_res_two_low = d_res_two.astype(jnp.bfloat16)
    normed_low_rows = low_rows_of(normed_low)
    pre_rows = jnp.dot(normed_low_rows, in_low, preferred_element_type=jnp.float32) + bias_hidden
    act_rows, gelu_back = jax.vjp(exact_gelu, pre_rows)
    grad_back = outer_sum(d_res_two_low, act_rows.astype(jnp.bfloat16))
    d_act = jnp.dot(d_res_two_low, down_low, preferred_element_type=jnp.float32)
    d_pre = gelu_back(d_act)[0]
    d_pre_low = d_pre.astype(jnp.bfloat16)
    grad_in = outer_sum(normed_low_rows, d_pre_low)
    d_normed_part = jnp.einsum("tf,df->td", d_pre_low, in_low, preferred_element_type=jnp.float32)
    d_normed = lax.psum(d_normed_part, "tensor") + d_res_two
    _, norm_one_back = jax.vjp(layer_norm, residual_one_rows, gains[0], biases[3])
    d_res_one, d_gain_one, d_shift_one = norm_one_back(d_normed)
    d_res_one_low = d_res_one.astype(jnp.bfloat16)
    grad_out_proj = outer_sum(d_res_one_low, low_rows_of(context_low))
    row_shape = (seq_count, SPAN_ROWS, local_heads, head_size)
    d_context = (
        jnp.dot(d_res_one_low, out_low, preferred_element_type=jnp.float32)
        .astype(jnp.bfloat16)
        .reshape(row_shape)
    )
    query_rows = low_rows_of(queries.reshape(row_count, head_cols)).reshape(row_shape)
    raw = jnp.einsum("sqhd,skhd->shqk", query_rows, keys, preferred_element_type=jnp.float32)
    probs = jax.nn.softmax(raw + key_bias[:, None, None, :], axis=-1)
    probs_again = probs.astype(jnp.bfloat16)
    d_probs = jnp.einsum("sqhd,skhd->shqk", d_context, values, preferred_element_type=jnp.float32)
    d_values = jnp.einsum(
        "shqk,sqhd->skhd", probs_again, d_context, preferred_element_type=jnp.float32
    ).reshape(row_count, head_cols)
    d_scores = (probs * (d_probs - jnp.sum(probs * d_probs, axis=-1, keepdims=True))).astype(
        jnp.bfloat16
    )
    d_queries = (
        jnp.einsum("shqk,skhd->sqhd", d_scores, keys, preferred_element_type=jnp.float32).reshape(
            seq_count * SPAN_ROWS, head_cols
        )
        * query_scale
    )
    d_keys = jnp.einsum(
        "shqk,sqhd->skhd", d_scores, query_rows, preferred_element_type=jnp.float32
    ).reshape(row_count, head_cols)

    def spread(row_values):
        width = row_values.shape[-1]
        return jnp.einsum(
            "srt,srd->std",
            pick,
            row_values.reshape(seq_count, SPAN_ROWS, width),
            precision=lax.Precision.HIGHEST,
        ).reshape(row_count, width)

    d_proj_low = (
        jnp.stack([spread(d_queries), d_keys, d_values], axis=1)
        .astype(jnp.bfloat16)
        .reshape(row_count, 3 * head_cols)
    )
    grad_qkv = outer_sum(tokens_in, d_proj_low).reshape(model_width, 3, head_cols)
    d_entry_part = jnp.einsum("tc,dc->td", d_proj_low, qkv_low, preferred_element_type=jnp.float32)
    input_grad = lax.psum(d_entry_part, "tensor") + spread(d_res_one)
    first_rank = (tensor_slot == 0).astype(jnp.float32)
    width_zero = jnp.zeros((model_width,), jnp.float32)

    def place_heads(partial_sum):
        return lax.dynamic_update_slice_in_dim(width_zero, partial_sum, tensor_slot * head_cols, 0)

    grad_gains = jnp.stack([d_gain_one, d_gain_two]) * first_rank
    grad_biases = jnp.stack(
        [
            place_heads(jnp.sum(d_queries, axis=0)),
            place_heads(jnp.sum(d_values, axis=0)),
            jnp.sum(d_res_one, axis=0) * first_rank,
            d_shift_one * first_rank,
            jnp.sum(d_res_two, axis=0) * first_rank,
            d_shift_two * first_rank,
        ]
    )
    grad_bias_in = lax.dynamic_update_slice_in_dim(
        jnp.zeros(bias_in.shape, jnp.float32), jnp.sum(d_pre, axis=0), tensor_slot * hidden_cols, 0
    )
    grad_gains, grad_biases, grad_bias_in = lax.psum(
        (grad_gains, grad_biases, grad_bias_in), ("dp", "tensor")
    )
    data_slot = lax.axis_index("dp")
    shard_rows = model_width // lax.axis_size("dp")
    owned = tuple(
        lax.psum_scatter(part, "dp", scatter_dimension=0, tiled=True)
        for part in (grad_qkv, grad_out_proj, grad_in, grad_back)
    )
    clock = step[0].astype(jnp.float32)
    warm = warmup[0].astype(jnp.float32)
    horizon = total[0].astype(jnp.float32)
    ratio = jnp.minimum(clock / warm, (horizon - clock) / (horizon - warm))
    corr_one = 1.0 - jnp.power(BETA_ONE, clock)
    corr_two = 1.0 - jnp.power(BETA_TWO, clock)
    change_rows = []
    fresh_moments = []
    for weight, grad_rows, moment in zip(
        (w_qkv, w_out, w_in, w_back), owned, (mom_qkv, mom_out, mom_in, mom_back)
    ):
        weight_rows = lax.dynamic_slice_in_dim(weight, data_slot * shard_rows, shard_rows, 0)
        row_change, new_moment = adam_step(
            weight_rows, grad_rows, moment, ratio, corr_one, corr_two, WEIGHT_DECAY
        )
        change_rows.append(row_change)
        fresh_moments.append(new_moment)
    change_qkv, change_out_proj, change_in_proj, change_back_proj = (
        lax.all_gather(change_rows[0], "dp", axis=0, tiled=True),
        lax.all_gather(change_rows[1], "dp", axis=0, tiled=True),
        lax.all_gather(change_rows[2], "dp", axis=0, tiled=True),
        lax.all_gather(change_rows[3], "dp", axis=0, tiled=True),
    )
    change_gains, new_mom_gains = adam_step(
        gains, grad_gains, mom_gains, ratio, corr_one, corr_two, 0.0
    )
    change_biases, new_mom_biases = adam_step(
        biases, grad_biases, mom_biases, ratio, corr_one, corr_two, 0.0
    )
    change_bias_in, new_mom_bias_in = adam_step(
        bias_in, grad_bias_in, mom_bias_in, ratio, corr_one, corr_two, 0.0
    )
    return (
        normed_out,
        input_grad,
        change_qkv,
        change_out_proj,
        change_in_proj,
        change_back_proj,
        change_gains,
        change_biases,
        change_bias_in,
        fresh_moments[0],
        fresh_moments[1],
        fresh_moments[2],
        fresh_moments[3],
        new_mom_gains,
        new_mom_biases,
        new_mom_bias_in,
    )


def solution(mesh):
    in_specs = (
        P("dp", None),
        P("dp", None),
        P("dp"),
        P("dp"),
        P(),
        P(),
        P(),
        P(None, None, "tensor"),
        P(None, "tensor"),
        P(None, "tensor"),
        P(None, "tensor"),
        P(),
        P(),
        P(),
        P(None, "dp", None, "tensor"),
        P(None, "dp", "tensor"),
        P(None, "dp", "tensor"),
        P(None, "dp", "tensor"),
        P(),
        P(),
        P(),
    )
    out_specs = (
        P("dp", None),
        P("dp", None),
        P(None, None, "tensor"),
        P(None, "tensor"),
        P(None, "tensor"),
        P(None, "tensor"),
        P(),
        P(),
        P(),
        P(None, "dp", None, "tensor"),
        P(None, "dp", "tensor"),
        P(None, "dp", "tensor"),
        P(None, "dp", "tensor"),
        P(),
        P(),
        P(),
    )
    return jax.shard_map(
        on_device, mesh=mesh, in_specs=in_specs, out_specs=out_specs, check_vma=False
    )
```

```python
import math

import jax
import jax.numpy as jnp
from jax import lax
from jax.experimental import pallas as pl
from jax.experimental.pallas import tpu as pltpu
from jax.sharding import PartitionSpec as P

HD = 64
SPAN_ROWS = 80
NORM_EPS = 1e-12
MESH = pl.DeviceIdType.MESH
F32 = jnp.float32
LOW = jnp.bfloat16


def dot(left, right, left_dim, right_dim):
    return lax.dot_general(
        left, right, (((left_dim,), (right_dim,)), ((), ())), preferred_element_type=F32
    )


def normalize(rows):
    center = rows - jnp.mean(rows, axis=-1, keepdims=True)
    scale = lax.rsqrt(jnp.mean(center * center, axis=-1, keepdims=True) + NORM_EPS)
    return center * scale, scale


def norm_back(grad, gain, unit, scale):
    weighted = grad * gain
    return scale * (
        weighted
        - jnp.mean(weighted, axis=-1, keepdims=True)
        - unit * jnp.mean(weighted * unit, axis=-1, keepdims=True)
    )


def row_sum(rows):
    return jnp.sum(rows, axis=0, keepdims=True)


class Peers:
    def __init__(self):
        self.d = lax.axis_index("dp")
        self.t = lax.axis_index("tensor")
        self.b = lax.rem(self.d, 2)
        self.c = lax.rem(self.t, 2)
        self.p = lax.div(self.t, 2)
        self.u = lax.div(self.d, 2)
        self.core = (self.d, self.t + 1 - 2 * self.c)
        self.y = (self.d, lax.rem(self.t + 2, 4))
        self.x = (self.d + 1 - 2 * self.b, self.t)


def send(src, dst, sems, k, peer):
    copy = pltpu.make_async_remote_copy(
        src_ref=src, dst_ref=dst, send_sem=sems.at[0, k], recv_sem=sems.at[1, k],
        device_id=peer, device_id_type=MESH,
    )
    copy.start()
    return copy


def local(src, dst, sem):
    copy = pltpu.make_async_copy(src, dst, sem)
    copy.start()
    return copy


def greet(peers):
    barrier = pltpu.get_barrier_semaphore()
    for peer in peers:
        pl.semaphore_signal(barrier, inc=1, device_id=peer, device_id_type=MESH)
    pl.semaphore_wait(barrier, len(peers))


def gelu_parts(pre):
    cdf = 0.5 * (1.0 + lax.erf(pre * (1.0 / math.sqrt(2.0))))
    pdf = jnp.exp(-0.5 * pre * pre) * (1.0 / math.sqrt(2.0 * math.pi))
    return pre * cdf, cdf + pre * pdf


def k1_kernel(
    lens, mask, gains, biases, bias_in, x_h, cot_h, wqkv_h, wout_h, win_h, wback_h,
    gi_h, gb_h, full_h, res_h, dres_h, pick_h, pm_h, qm_h, k_h, v_h, cm_h, ctx_h, wal_h, wpl_h, wil_h, wbl_h, pil_h, pbl_h, vec,
    x, cot, wqkv, wout, win, wback, wp_qkv, wp_out, pwin, pwback, q_o, k_o, v_o, ctx_o, pick_o, wal, wpl, wil, wbl, pil, pbl, gin, gback,
    pm, xm, cotm, qm, ctxm, cml, ctxp, ap, apc, normed, nlow, act, gp, part, rc1, h1, ry1,
    part2, rc2, h2, ry2, full2, full, dres2, d2w, d2x, nxw, nxx, dplow,
    lsem, rsem,
):
    seqs, rows = 3, SPAN_ROWS
    count = x_h.shape[0]
    length = count // seqs
    total = seqs * rows
    half = total // 2
    heads = ctx_o.shape[1]
    n_heads = heads // HD
    width = x_h.shape[1]
    me = Peers()

    def seq(s):
        return pl.ds(s * length, length)

    loads = [
        local(wqkv_h, wqkv, lsem.at[0]),
        local(wout_h, wout, lsem.at[1]),
    ] + [local(x_h.at[seq(s)], x.at[seq(s)], lsem.at[2 + s]) for s in range(seqs)] + [
        local(win_h, win, lsem.at[2 + seqs]),
        local(wback_h, wback, lsem.at[3 + seqs]),
        local(cot_h, cot, lsem.at[4 + seqs]),
    ]
    stores = []

    def keep(src, dst):
        stores.append(local(src, dst, lsem.at[8 + len(stores)]))

    slots = gin.shape[0]
    shard = gin.shape[1]
    n_u = slots // 2
    z = me.u
    greet([me.core, me.y, me.x] + [(2 * lax.rem(z + k, n_u) + me.b, me.t) for k in range(1, n_u)])

    loads[1].wait()
    out_half = pl.ds(pl.multiple_of(me.b * (heads // 2), 8), heads // 2)
    wo_y = send(wout.at[out_half], wp_out.at[out_half], rsem, 0, me.y)
    loads[0].wait()
    wal[0:3 * heads, :] = wqkv[...].astype(LOW)
    wal[3 * heads:, :] = wout[...].astype(LOW)
    keep(wal, wal_h)

    def pick_bias(row, k=heads):
        out = jnp.zeros((1, k), F32)
        for slot in range(4):
            piece = biases[row:row + 1, slot * k:(slot + 1) * k]
            out = jnp.where(me.t == slot, piece, out)
        return out

    bias_q, bias_v = pick_bias(0), pick_bias(1)
    hidden = win.shape[1]
    lanes = 128
    bias_h = jnp.concatenate(
        [bias_in[pl.ds(me.t * (hidden // lanes) + j, 1), :] for j in range(hidden // lanes)], axis=1
    )
    upto = (
        lax.broadcasted_iota(jnp.int32, (length, length), 0)
        <= lax.broadcasted_iota(jnp.int32, (length, length), 1)
    ).astype(F32).astype(LOW)
    position = lax.broadcasted_iota(jnp.int32, (1, length), 1)
    slot_of = lax.broadcasted_iota(jnp.int32, (rows, length), 0).astype(F32)
    scale = 1.0 / math.sqrt(HD)
    def project(s):
        loads[2 + s].wait()
        at = seq(s)
        xs = x[at, :]
        q = ((dot(xs, wal[0:heads, :], 1, 1) + bias_q) * scale).astype(LOW)
        k = dot(xs, wal[heads:2 * heads, :], 1, 1).astype(LOW)
        v = (dot(xs, wal[2 * heads:3 * heads, :], 1, 1) + bias_v).astype(LOW)
        q_o[at, :] = q
        k_o[at, :] = k
        v_o[at, :] = v
        parts = length // lanes
        marks = jnp.concatenate([mask[pl.ds(s * parts + j, 1), :] for j in range(parts)], axis=1)
        inside = position < lens[s]
        live = jnp.where(inside, marks, 0).astype(F32)
        rank = dot(jnp.broadcast_to(live, (8, length)).astype(LOW), upto, 1, 0)[0:1] - 1.0
        pick = jnp.where((rank == slot_of) & (live > 0.0), 1.0, 0.0).astype(LOW)
        pick_o[s] = pick
        here = pl.ds(s * rows, rows)
        xm[here, :] = dot(pick, xs, 1, 0)
        qrow = dot(pick, q, 1, 0).astype(LOW)
        qm[here, :] = qrow
        key_bias = jnp.where(inside, 0.0, -1000000000.0)
        pieces = []
        for h in range(n_heads):
            col = slice(h * HD, (h + 1) * HD)
            scores = dot(qrow[:, col], k[:, col], 1, 1) + key_bias
            e = jnp.exp(scores - jnp.max(scores, axis=-1, keepdims=True))
            prob = e / jnp.sum(e, axis=-1, keepdims=True)
            pm[s * n_heads + h] = prob
            pieces.append(dot(prob.astype(LOW), v[:, col], 1, 0))
        low = jnp.concatenate(pieces, axis=1).astype(LOW)
        cml[here, :] = low
        ctxm[here, :] = low.astype(F32)
        return send(ctxm.at[here], ctxp.at[here], rsem, 24 + s, me.y)

    ctx_y = [project(s) for s in range(seqs)]
    wo_y.wait()
    wo_x = send(wp_out.at[out_half], wp_out.at[out_half], rsem, 2, me.x)
    third = heads // 2

    def qkv_part(k):
        return pl.ds(pl.multiple_of(me.b * (3 * third) + k * third, 8), third)

    def fetch(k):
        return send(wqkv.at[qkv_part(k)], wp_qkv.at[qkv_part(k)], rsem, 16 + k, me.y)

    def swap(k):
        return send(wp_qkv.at[qkv_part(k)], wp_qkv.at[qkv_part(k)], rsem, 19 + k, me.x)

    share = 2 * third // n_u

    def share_of(b, u):
        return pl.ds(pl.multiple_of(b * (3 * third) + third + u * share, 8), share)

    def chain_copy(way, s, b, u):
        place = wp_qkv.at[share_of(b, u)]
        k = 29 + (way * (n_u - 1) + s) * 2 + b
        peer = (me.d + 2, me.t) if way == 0 else (me.d - 2, me.t)
        return pltpu.make_async_remote_copy(
            src_ref=place, dst_ref=place, send_sem=rsem.at[0, k], recv_sem=rsem.at[1, k],
            device_id=peer, device_id_type=MESH,
        )

    def chain_cases(s):
        return [
            (way, b, z - s if way == 0 else z + s, (z >= s) if way == 0 else (z + s <= n_u - 1), (z < n_u - 1) if way == 0 else (z > 0))
            for way in range(2) for b in range(2)
        ]

    def chain_step(s):
        for way, b, u, here, edge in chain_cases(s):
            if s > 0:
                pl.when(here)(lambda way=way, b=b, u=u: chain_copy(way, s - 1, b, u).wait_recv())
            if s < n_u - 1:
                pl.when(here & edge)(lambda way=way, b=b, u=u: chain_copy(way, s, b, u).start())

    def chain_sent():
        for s in range(n_u - 1):
            for way, b, u, here, edge in chain_cases(s):
                pl.when(here & edge)(lambda way=way, b=b, u=u, s=s: chain_copy(way, s, b, u).wait_send())

    def attend_all(s):
        at = slice(s * length, (s + 1) * length)
        key_bias = jnp.where(position < lens[s], 0.0, -1000000000.0)
        pieces = []
        for h in range(n_heads):
            col = slice(h * HD, (h + 1) * HD)
            scores = dot(q_o[at, col], k_o[at, col], 1, 1) + key_bias
            e = jnp.exp(scores - jnp.max(scores, axis=-1, keepdims=True))
            prob = (e / jnp.sum(e, axis=-1, keepdims=True)).astype(LOW)
            pieces.append(dot(prob, v_o[at, col], 1, 0))
        ctx_o[at, :] = jnp.concatenate(pieces, axis=1).astype(LOW)

    mine_share = share_of(me.b, z)
    wz_y = send(wqkv.at[mine_share], wp_qkv.at[mine_share], rsem, 27, me.y)
    for ref, out in ((pm, pm_h), (qm, qm_h), (k_o, k_h), (v_o, v_h), (cml, cm_h), (pick_o, pick_h)):
        keep(ref, out)
    for load in loads[2 + seqs:4 + seqs]:
        load.wait()
    wil[...] = win[...].astype(LOW)
    wbl[...] = wback[...].astype(LOW)
    keep(wil, wil_h)
    keep(wbl, wbl_h)
    loads[4 + seqs].wait()
    for s in range(seqs):
        cotm[s * rows:(s + 1) * rows, :] = dot(pick_o[s], cot[s * length:(s + 1) * length, :], 1, 0)
    wo_x.wait()
    for copy in ctx_y:
        copy.wait()
    woq = wp_out[...].astype(LOW)

    def mix(first, second):
        ap[...] = dot(*first, 1, 0) + dot(*second, 1, 0)

    own_part = lambda: (cml[...], wal[3 * heads:, :])
    twin_part = lambda: (ctxp[...].astype(LOW), woq)
    pl.when(me.p == 0)(lambda: mix(own_part(), twin_part()))
    pl.when(me.p == 1)(lambda: mix(twin_part(), own_part()))
    ap_c = send(ap, apc, rsem, 3, me.core)
    wz_y.wait()
    wz_x = send(wp_qkv.at[mine_share], wp_qkv.at[mine_share], rsem, 28, me.x)
    wq_y = fetch(0)
    ap_c.wait()
    xm[...] = xm[...] + (ap[...] + apc[...]) + biases[2:3, :]
    keep(xm, res_h)
    unit, inv = normalize(xm[...])
    normed[...] = unit * gains[0:1, :] + biases[3:4, :]
    nlow[...] = normed[...].astype(LOW)
    nxw[...] = nlow[...].astype(F32)
    mine = pl.ds(pl.multiple_of(me.c * half, 8), half)
    other = pl.ds(pl.multiple_of((1 - me.c) * half, 8), half)
    nx_x = send(nxw.at[mine], nxx.at[mine], rsem, 5, me.x)
    for j in range(0, hidden, 256):
        col = slice(j, j + 256)
        a, g = gelu_parts(dot(nlow[...], wil[:, col], 1, 0) + bias_h[:, col])
        act[:, col] = a.astype(LOW)
        gp[:, col] = g
    part[...] = dot(act[...], wbl[...], 1, 1)

    cuts = ((0, 64), (64, half - 64))

    def all_reduce(src, rc, hs, ry, dst, base, fill):
        pieces = []
        for k, (start, size) in enumerate(cuts):
            mine_k = pl.ds(pl.multiple_of(me.c * half + start, 8), size)
            other_k = pl.ds(pl.multiple_of((1 - me.c) * half + start, 8), size)
            pieces.append((k, pl.ds(start, size), mine_k, other_k))
        first = [send(src.at[other_k], rc.at[row], rsem, base + k, me.core) for k, row, _, other_k in pieces]
        second, third = [], []
        for k, row, mine_k, _ in pieces:
            first[k].wait()
            hs[row, :] = src[mine_k, :] + rc[row, :]
            second.append(send(hs.at[row], ry.at[row], rsem, base + 2 + k, me.y))
        fill()
        for k, row, mine_k, _ in pieces:
            second[k].wait()
            dst[mine_k, :] = hs[row, :] + ry[row, :]
            third.append(send(dst.at[mine_k], dst.at[mine_k], rsem, base + 4 + k, me.core))
        for copy in third:
            copy.wait()

    relay = []

    def fill_one():
        wide.append(send(win, pwin, rsem, 22, me.core))
        wz_x.wait()
        chain_step(0)
        attend_all(0)
        attend_all(1)
        nx_x.wait()
        relay.append(send(nxx.at[mine], nxx.at[mine], rsem, 6, me.core))
        wq_y.wait()
        relay.append(swap(0))
        chain_step(1)

    wide = []
    all_reduce(part, rc1, h1, ry1, full, 29 + 2 * slots, fill_one)
    relay[0].wait()
    unit, inv = normalize(normed[...] + full[...] + biases[4:5, :])
    grad = cotm[...]
    d_two = norm_back(grad, gains[1:2, :], unit, inv)
    dres2[...] = d_two
    vec[...] = jnp.zeros(vec.shape, F32)
    vec[1:2, :] = row_sum(grad * unit)
    vec[5:6, :] = row_sum(d_two)
    vec[6:7, :] = row_sum(grad)
    d2w[...] = d_two.astype(LOW).astype(F32)
    d2_x = send(d2w.at[mine], d2x.at[mine], rsem, 10, me.x)
    keep(dres2, dres_h)
    d2low = d2w[...].astype(LOW)
    for j in range(0, hidden, 256):
        col = slice(j, j + 256)
        d_pre = dot(d2low, wbl[:, col], 1, 0) * gp[:, col]
        vec[8:9, col] = row_sum(d_pre)
        dplow[:, col] = d_pre.astype(LOW)
    part2[...] = dot(dplow[...], wil[...], 1, 1)

    def cut(rows):
        return rows.reshape(slots, shard, rows.shape[1])

    def fill_two():
        wide.append(send(wback, pwback, rsem, 23, me.core))
        attend_all(2)
        chain_step(2)
        keep(ctx_o, ctx_h)
        for j in range(0, hidden, 256):
            col = slice(j, j + 256)
            gin[:, :, col] = cut(dot(nlow[...], dplow[:, col], 0, 0))
            gback[:, :, col] = cut(dot(d2low, act[:, col], 0, 0))
        wide[0].wait()
        pil[...] = pwin[...].astype(LOW)
        keep(pil, pil_h)
        relay[1].wait()
        d2_x.wait()
        relay.append(send(d2x.at[mine], d2x.at[mine], rsem, 11, me.core))

    all_reduce(part2, rc2, h2, ry2, full2, 35 + 2 * slots, fill_two)
    keep(full2, full_h)
    relay[2].wait()
    nlx = nxx[...].astype(LOW)
    dlx = d2x[...].astype(LOW)
    for j in range(0, hidden, 256):
        col = slice(j, j + 256)
        a, g = gelu_parts(dot(nlx, wil[:, col], 1, 0) + bias_h[:, col])
        d_pre = (dot(dlx, wbl[:, col], 1, 0) * g).astype(LOW)
        gin[:, :, col] += cut(dot(nlx, d_pre, 0, 0))
        gback[:, :, col] += cut(dot(dlx, a.astype(LOW), 0, 0))
    for u in range(slots // 2):
        keep(gin.at[2 * u + me.b], gi_h.at[u])
        keep(gback.at[2 * u + me.b], gb_h.at[u])
    for step in range(3, n_u):
        chain_step(step)
    wpl[0:3 * heads, :] = wp_qkv[...].astype(LOW)
    wpl[3 * heads:, :] = woq
    keep(wpl, wpl_h)
    wide[1].wait()
    pbl[...] = pwback[...].astype(LOW)
    keep(pbl, pbl_h)
    chain_sent()
    for copy in stores:
        copy.wait()


def k1_call(x, cot, mask, lens, wqkv, wout, win, wback, gains, biases, bias_in, slots):
    count, width = x.shape
    seqs = lens.shape[0]
    heads = wout.shape[0]
    hidden = win.shape[1]
    length = count // seqs
    total = seqs * SPAN_ROWS
    half = total // 2
    units = seqs * (heads // HD)
    any_ = pl.BlockSpec(memory_space=pl.ANY)
    vm = pl.BlockSpec(memory_space=pltpu.VMEM)
    sm = pl.BlockSpec(memory_space=pltpu.SMEM)
    sds = jax.ShapeDtypeStruct
    V = pltpu.VMEM
    wide = lambda r, t=F32: V((r, width), t)
    block = (slots // 2, width // slots, hidden)
    square = sds((width, hidden), LOW)
    out_shape = (
        sds(block, F32), sds(block, F32), sds((total, width), F32), sds((total, width), F32), sds((total, width), F32),
        sds((seqs, SPAN_ROWS, length), LOW), sds((units, SPAN_ROWS, length), F32), sds((total, heads), LOW),
        sds((count, heads), LOW), sds((count, heads), LOW), sds((total, heads), LOW), sds((count, heads), LOW),
        sds((4 * heads, width), LOW), sds((4 * heads, width), LOW), square, square, square, square,
        sds((16, width), F32),
    )
    scratch = [
        wide(count, LOW), wide(count, LOW), wide(3 * heads), wide(heads), V((width, hidden), F32),
        V((width, hidden), F32), wide(3 * heads), wide(heads), V((width, hidden), F32), V((width, hidden), F32),
        V((count, heads), LOW), V((count, heads), LOW), V((count, heads), LOW), V((count, heads), LOW),
        V((seqs, SPAN_ROWS, length), LOW), wide(4 * heads, LOW), wide(4 * heads, LOW), V((width, hidden), LOW), V((width, hidden), LOW),
        V((width, hidden), LOW), V((width, hidden), LOW), V((slots, width // slots, hidden), F32), V((slots, width // slots, hidden), F32),
        V((units, SPAN_ROWS, length), F32), wide(total), wide(total), V((total, heads), LOW),
        V((total, heads), F32), V((total, heads), LOW), V((total, heads), F32), wide(total), wide(total),
        wide(total), wide(total, LOW), V((total, hidden), LOW), V((total, hidden), F32), wide(total), wide(half), wide(half), wide(half),
        wide(total), wide(half), wide(half), wide(half), wide(total), wide(total), wide(total), wide(total), wide(total), wide(total), wide(total),
        V((total, hidden), LOW),
        pltpu.SemaphoreType.DMA((8 + 20 + slots,)), pltpu.SemaphoreType.DMA((2, 41 + 2 * slots)),
    ]
    return pl.pallas_call(
        k1_kernel, out_shape=out_shape,
        in_specs=[sm, vm, vm, vm, vm] + [any_] * 6,
        out_specs=(any_,) * (len(out_shape) - 1) + (vm,),
        scratch_shapes=scratch,
        compiler_params=pltpu.CompilerParams(
            collective_id=1, has_side_effects=True, vmem_limit_bytes=60 * 2**20
        ),
    )(lens, mask, gains, biases, bias_in, x, cot, wqkv, wout, win, wback)


BETA_ONE = 0.9
BETA_TWO = 0.999
ADAM_EPS = 1e-06
WEIGHT_DECAY = 0.01


def adam(weight, grad, first, second, ratio, corr_one, corr_two, decay):
    first = BETA_ONE * first + (1.0 - BETA_ONE) * grad
    second = BETA_TWO * second + (1.0 - BETA_TWO) * grad * grad
    update = first / corr_one / (jnp.sqrt(second / corr_two) + ADAM_EPS) + decay * weight
    return -ratio * update, first, second


FLIGHT = 0.55
PLAN_READY = (1.2, 1.2, 3.2)
SWAP_FIRST = ((0, 0),)
WEIGHT = {("RS", 0, 0): 8.0, ("RS", 1, 0): 7.0, ("RS", 2, 0): -7.0, ("RS", 2, 1): -10.0, ("AG", 0, 0): -10.0}
BLOCK_US = 3.38


def plan(n, weight):
    tasks = {}
    for ch in range(3):
        for p in range(2):
            ready = PLAN_READY[ch]
            swap = ch == 2
            both = (ch, p) in SWAP_FIRST
            for z in range(n):
                if swap:
                    for u in range(n):
                        tasks["XS", ch, p, 0, u, z] = ("X", z), [], ready
                for d in range(n):
                    if d == z:
                        continue
                    step = 1 if d > z else -1
                    kind = "RSR" if d > z else "RSL"
                    need = [(kind, ch, p, 0, d, z - step)] if 0 <= z - step < n else []
                    if swap:
                        need.append(("XS", ch, p, 0, d, z))
                    tasks[kind, ch, p, 0, d, z] = (kind[2], z), need, ready
                end = [("RSR", ch, p, 0, z, z - 1)] if z > 0 else []
                if z < n - 1:
                    end.append(("RSL", ch, p, 0, z, z + 1))
                if swap:
                    end.append(("XS", ch, p, 0, z, z))
                for par in (0, 1) if both else (0,):
                    for u in range(n):
                        if u == z:
                            need = [("AGX", ch, p, 0, z, z)] if par else end
                        else:
                            need = [("AGR", ch, p, par, u, z - 1) if u < z else ("AGL", ch, p, par, u, z + 1)]
                        if u <= z < n - 1:
                            tasks["AGR", ch, p, par, u, z] = ("R", z), need, 0.0
                        if 0 < z <= u:
                            tasks["AGL", ch, p, par, u, z] = ("L", z), need, 0.0
                        if par == 0 and (u == z or not both):
                            tasks["AGX", ch, p, 0, u, z] = ("X", z), need, 0.0
    after = {key: [] for key in tasks}
    for key, (_, need, _) in tasks.items():
        for one in need:
            after[one].append(key)
    rank = {}

    def longest(key):
        if key not in rank:
            rank[key] = 1.0 + FLIGHT + max([longest(k) for k in after[key]], default=0.0)
        return rank[key]

    missing = {key: len(task[1]) for key, task in tasks.items()}
    open_at = {key: task[2] for key, task in tasks.items() if not task[1]}
    free, done, order = {}, {}, []
    while open_at:
        by_link = {}
        for key in open_at:
            by_link.setdefault(tasks[key][0], []).append(key)
        best = None
        for link, keys in by_link.items():
            start = max(free.get(link, 0.0), min(open_at[k] for k in keys))
            able = [k for k in keys if open_at[k] <= start + 1e-9]
            key = max(able, key=lambda k: (longest(k) + weight.get((k[0][:2] if k[0] != "AGX" else "AX", k[1], k[2]), 0.0), -open_at[k]))
            if best is None or start < best[0] - 1e-9:
                best = start, key
        start, key = best
        free[tasks[key][0]] = start + 1.0
        done[key] = start + 1.0 + FLIGHT
        order.append((start, key))
        del open_at[key]
        for k in after[key]:
            missing[k] -= 1
            if missing[k] == 0:
                open_at[k] = max(max(done[q] for q in tasks[k][1]) + 0.15, tasks[k][2])
    return order, tasks, max(done.values())


def k2_kernel(
    lens, step, warmup, horizon, gains, biases, bias_in, vec,
    x_h, gi_h, gb_h, full_h, res_h, dtwo_h, pick_h, pm_h, qm_h, k_h, v_h, cm_h, ctx_h, wal_h, wpl_h, wil_h, wbl_h, pil_h, pbl_h,
    wqkv_h, wout_h, win_h, wback_h, mq_h, mo_h, mi_h, mb_h,
    out_h, grad_h, ci_h, cb_h, ca_h, nmq_h, nmo_h, nmi_h, nmb_h, vt,
    x, ga, gi, gb, dproj, ctx, pick, dres, full, dtwo, pm, qm, ko, vo, cm, dctx, wal, wpl, wil, wbl, pil, pbl,
    wrow_i, wrow_b, wrow_a, mq, mo, mi, mb, turned, flip,
    qp, kp, vp, ctxp, dpp, sbuf, rbuf, nrm, dsc, rdn, fin, rig,
    ring, xr, own, v0, v1, vx, vz,
    lsem, rs_s, rs_r, ag_s, ag_r, ax_s, ax_r, xs_s, xs_r, vs_s, vs_r, sd_s, sd_r, usem,
):
    me = Peers()
    n_u = gi.shape[0]
    seqs = sbuf.shape[0]
    count, width = x_h.shape
    length = count // seqs
    rows = SPAN_ROWS
    total = seqs * rows
    heads = ctx.shape[1]
    n_heads = heads // HD
    shard = gi.shape[1]
    hidden = wil.shape[1]
    half = length // 2
    quarter = length // 4
    z, b = me.u, me.b
    right = (me.d + 2, me.t)
    left = (me.d - 2, me.t)
    diag = (me.d, 3 - me.t)

    def remote(src, dst, ss, rr, peer):
        return pltpu.make_async_remote_copy(
            src_ref=src, dst_ref=dst, send_sem=ss, recv_sem=rr, device_id=peer, device_id_type=MESH
        )

    pend = {}
    order = iter(range(64))

    def fetch(name, src, dst):
        copy = pltpu.make_async_copy(src, dst, lsem.at[next(order)])
        copy.start()
        pend.setdefault(name, []).append(copy)

    def ready(*names):
        for name in names:
            for copy in pend.pop(name, []):
                copy.wait()

    fetch("one", full_h, full)
    fetch("one", res_h, dres)
    fetch("one", dtwo_h, dtwo)
    fetch("gi", gi_h, gi)
    fetch("gb", gb_h, gb)
    fetch("wal", wal_h, wal)
    fetch("att", pick_h, pick)
    fetch("att", pm_h, pm)
    fetch("att", qm_h, qm)
    fetch("att", k_h, ko)
    fetch("att", v_h, vo)
    fetch("att", cm_h, cm)
    fetch("x", x_h, x.at[pl.ds(0, count)])
    fetch("wpl", wpl_h, wpl)
    fetch("ctx", ctx_h, ctx)
    fetch("low", wil_h, wil)
    fetch("low", wbl_h, wbl)
    fetch("low", pil_h, pil)
    fetch("low", pbl_h, pbl)
    mine = pl.ds(pl.multiple_of(me.d * shard, 8), shard)
    fetch("mi", win_h.at[mine], wrow_i)
    fetch("mi", mi_h, mi)
    fetch("mb", wback_h.at[mine], wrow_b)
    fetch("mb", mb_h, mb)
    fetch("ma", wqkv_h, turned.at[pl.ds(0, 3 * heads)])
    fetch("ma", wout_h, turned.at[pl.ds(3 * heads, heads)])
    fetch("ma", mq_h, mq)
    fetch("ma", mo_h, mo)

    others = [(2 * lax.rem(z + k, n_u) + b, me.t) for k in range(1, n_u)]
    greet([me.core, me.y, diag, me.x] + others)

    order_all, tasks, _ = plan(n_u, WEIGHT)
    part_rows = shard // 2

    def rows_of(p):
        return pl.ds(p * part_rows, part_rows)

    def g_at(ch, u):
        return ga.at[2 * u + b] if ch == 2 else (gi, gb)[ch].at[u]

    def target(ch, d):
        return (ci_h, cb_h, ca_h)[ch].at[d]

    def xr_at(u, p):
        return xr.at[u, rows_of(p)]

    def ring_at(key):
        kind, ch, p, _, d, node = key
        place = d - (node + 1) if kind == "RSR" else (node - 1) - d
        return ring.at[ch, 0 if kind == "RSR" else 1, place, rows_of(p)]

    def transfer(key, incoming):
        kind, ch, p, par, u, node = key
        way = 0 if kind[2:] == "R" else 1
        if kind == "XS":
            k = p * n_u + u
            return remote(ga.at[2 * u + 1 - b, rows_of(p)], xr_at(u, p), xs_s.at[k], xs_r.at[k], me.x)
        if kind[:2] == "RS":
            k = ((ch * 2 + p) * 2 + way) * n_u + u
            peer = right if way == 0 else left
            return remote(g_at(ch, u).at[rows_of(p)], ring_at(key), rs_s.at[k], rs_r.at[k], peer)
        parity = b if (par == 0) != (incoming and kind == "AGX") else 1 - b
        there = target(ch, 2 * u + parity).at[rows_of(p)]
        here = own.at[ch, rows_of(p)] if u == node and par == 0 else there
        if kind == "AGX":
            k = (ch * 2 + p) * n_u + u
            return remote(here, there, ax_s.at[k], ax_r.at[k], me.x)
        k = (((ch * 2 + p) * 2 + way) * 2 + par) * n_u + u
        return remote(here, there, ag_s.at[k], ag_r.at[k], right if way == 0 else left)

    ratio, corr_one, corr_two = rates(step, warmup, horizon)

    def own_copy(ch, p):
        return pltpu.make_async_copy(own.at[ch, rows_of(p)], target(ch, me.d).at[rows_of(p)], usem.at[ch * 2 + p])

    def update(ch, p):
        at_p = rows_of(p)
        if ch < 2:
            w, m = ((wrow_i, mi), (wrow_b, mb))[ch]
            change, first, second = adam(
                w[at_p, :], g_at(ch, z)[at_p, :], m[0, at_p, :], m[1, at_p, :], ratio, corr_one, corr_two, WEIGHT_DECAY
            )
            own[ch, at_p, :] = change
            m[0, at_p, :] = first
            m[1, at_p, :] = second
        else:
            for k in range(4):
                col = slice(k * heads, (k + 1) * heads)
                first = mo[0, at_p, :] if k == 3 else mq[0, k, at_p, :]
                second = mo[1, at_p, :] if k == 3 else mq[1, k, at_p, :]
                change, first, second = adam(
                    wrow_a[at_p, col], ga[me.d, at_p, col], first, second, ratio, corr_one, corr_two, WEIGHT_DECAY
                )
                own[2, at_p, col] = change
                if k < 3:
                    mq[0, k, at_p, :] = first
                    mq[1, k, at_p, :] = second
                else:
                    mo[0, at_p, :] = first
                    mo[1, at_p, :] = second
        own_copy(ch, p).start()

    queue = [[] for _ in range(n_u)]
    inbound = [[] for _ in range(n_u)]
    for start, key in order_all:
        kind, node = key[0], key[5]
        queue[node].append((start * BLOCK_US, key))
        goes = node if kind in ("XS", "AGX") else node + 1 if kind[2] == "R" else node - 1
        inbound[goes].append(key)
    for node in range(n_u):
        queue[node].sort(key=lambda one: one[0])
    got = [set() for _ in range(n_u)]
    made = [set() for _ in range(n_u)]
    sent = [[] for _ in range(n_u)]

    def arrive(node, key):
        if key in got[node]:
            return
        got[node].add(key)
        transfer(key, True).wait_recv()
        kind, ch, p, _, u, _ = key
        if kind == "XS":
            ga[2 * u + b, rows_of(p)] += xr_at(u, p)[...]
        elif kind[:2] == "RS":
            g_at(ch, u)[rows_of(p), :] += ring_at(key)[...]

    def act(node, key):
        for need in tasks[key][1]:
            arrive(node, need)
        kind, ch, p, par, u, _ = key
        if kind[:2] == "AG" and u == node and par == 0 and (ch, p) not in made[node]:
            made[node].add((ch, p))
            update(ch, p)
        sent[node].append(key)
        transfer(key, False).start()

    def chain_until(until):
        for node in range(n_u):
            due = [key for start, key in queue[node] if start < until]
            queue[node] = [one for one in queue[node] if one[0] >= until]
            if due:
                pl.when(z == node)(lambda node=node, due=due: [act(node, key) for key in due] and None)

    def chain_end():
        for node in range(n_u):
            def settle(node=node):
                for key in inbound[node]:
                    arrive(node, key)
                for key in sent[node]:
                    transfer(key, False).wait_send()
            pl.when(z == node)(settle)
        for ch in range(3):
            for p in range(2):
                own_copy(ch, p).wait()

    def vec_x():
        return remote(v0, vx, vs_s.at[0], vs_r.at[0], me.x)

    def vec_z(k):
        peer = (2 * lax.rem(z + k, n_u) + b, me.t)
        return remote(v1, vz.at[z], vs_s.at[k], vs_r.at[k], peer)

    def vec_t(k, peer):
        return remote(v1, vt.at[me.t], vs_s.at[n_u + k], vs_r.at[n_u + k], peer)

    trio = (me.core, me.y, diag)

    def vectors_one():
        vec_x().wait()
        v1[...] = v0[...] + vx[...]
        vz[z] = v1[...]
        for k in range(1, n_u):
            vec_z(k).start()

    def vectors_two():
        for k in range(1, n_u):
            vec_z(k).wait()
        total = vz[0]
        for u in range(1, n_u):
            total = total + vz[u]
        v1[...] = total
        vt[me.t] = total
        for k, peer in enumerate(trio):
            vec_t(k, peer).start()

    def vectors_three():
        for k, peer in enumerate(trio):
            vec_t(k, peer).wait()

    lanes = 128

    def hidden_bias(slot):
        parts = hidden // lanes
        return jnp.concatenate([bias_in[pl.ds(slot * parts + j, 1), :] for j in range(parts)], axis=1)

    twin = lax.rem(me.t + 2, 4)

    def first_norm_back():
        d_normed = full[...] + dtwo[...]
        unit, inv = normalize(dres[...])
        d_one = norm_back(d_normed, gains[0:1, :], unit, inv)
        dres[...] = d_one
        v0[...] = vec[...]
        v0[0:1, :] = row_sum(d_normed * unit)
        v0[3:4, :] = row_sum(d_one)
        v0[4:5, :] = row_sum(d_normed)
        low = d_one.astype(LOW)
        x[count:count + total, :] = low
        dctx[...] = dot(low, wal[3 * heads:, :], 1, 1).astype(LOW)

    def attend_back(q, k, v, dc, probs, pick_s):
        dqs, dks, dvs = [], [], []
        for h in range(n_heads):
            col = slice(h * HD, (h + 1) * HD)
            prob = probs(h)
            d_prob = dot(dc[:, col], v[:, col], 1, 1)
            dvs.append(dot(prob.astype(LOW), dc[:, col], 0, 0))
            ds = (prob * (d_prob - jnp.sum(prob * d_prob, axis=-1, keepdims=True))).astype(LOW)
            dqs.append(dot(ds, k[:, col], 1, 0) * scale)
            dks.append(dot(ds, q[:, col], 0, 0))
        dq = jnp.concatenate(dqs, axis=1)
        dv = jnp.concatenate(dvs, axis=1)
        spread = dot(pick_s, dq.astype(LOW), 0, 0).astype(LOW)
        return jnp.concatenate([spread, jnp.concatenate(dks, axis=1).astype(LOW), dv.astype(LOW)], axis=1), dq, dv

    def own_back(s):
        here = slice(s * rows, (s + 1) * rows)
        low, dq, dv = attend_back(
            qm[here, :], ko.at[at(s)], vo.at[at(s)], dctx[here, :], lambda h: pm[s * n_heads + h], pick[s]
        )
        dproj[at(s), 0:3 * heads] = low
        dproj[at(s), 3 * heads:] = jnp.zeros((length, heads), LOW)
        sums = jnp.concatenate([row_sum(dq), row_sum(dv)], axis=1)
        v0[2:3, 0:2 * heads] = sums if s == 0 else v0[2:3, 0:2 * heads] + sums

    def weight_grads(j):
        if j == 0:
            dproj[count:count + total, 0:3 * heads] = jnp.zeros((total, 3 * heads), LOW)
            dproj[count:count + total, 3 * heads:] = cm[...]
        col = slice(j * 256, (j + 1) * 256)
        ga[:, :, col] = dot(x[...], dproj[:, col], 0, 0).reshape(2 * n_u, shard, 256)

    def twin_rows():
        dctx[...] = dot(x[count:count + total, :], wpl[3 * heads:, :], 1, 1).astype(LOW)

    def pick_bias(row):
        out = jnp.zeros((1, heads), F32)
        for slot in range(4):
            out = jnp.where(twin == slot, biases[row:row + 1, slot * heads:(slot + 1) * heads], out)
        return out

    scale = 1.0 / math.sqrt(HD)
    position = lax.broadcasted_iota(jnp.int32, (1, length), 1)
    my_half = pl.ds(pl.multiple_of(me.c * half, 8), half)
    its_half = pl.ds(pl.multiple_of((1 - me.c) * half, 8), half)
    my_quarter = pl.ds(pl.multiple_of(me.p * quarter, 8), quarter)
    its_quarter = pl.ds(pl.multiple_of((1 - me.p) * quarter, 8), quarter)

    def at(s, start=0, size=None):
        return pl.ds(pl.multiple_of(s * length + start, 8), size or length)

    def key_bias(s):
        return jnp.where(position < lens[s], 0.0, -1000000000.0)

    def project(s):
        xs = x[at(s), :]
        qp[...] = ((dot(xs, wpl[0:heads, :], 1, 1) + pick_bias(0)) * scale).astype(LOW)
        kp[...] = dot(xs, wpl[heads:2 * heads, :], 1, 1).astype(LOW)
        vp[...] = (dot(xs, wpl[2 * heads:3 * heads, :], 1, 1) + pick_bias(1)).astype(LOW)

    def attend_one(s, h):
        col = slice(h * HD, (h + 1) * HD)
        e = dot(qp[:, col], kp[:, col], 1, 1) + key_bias(s)
        e = jnp.exp(e - jnp.max(e, axis=-1, keepdims=True))
        prob = (e / jnp.sum(e, axis=-1, keepdims=True)).astype(LOW)
        ctxp[:, col] = dot(prob, vp[:, col], 1, 0).astype(LOW)

    def mix_copy(s):
        return remote(sbuf.at[s], rbuf.at[s], sd_s.at[s], sd_r.at[s], me.core)

    def mix(s):
        for where, into in ((its_half, sbuf), (my_half, nrm)):
            base = at(s, where.start, half)
            into[s] = dot(ctx[base, :], wal[3 * heads:, :], 1, 0) + dot(ctxp[where, :], wpl[3 * heads:, :], 1, 0)
        mix_copy(s).start()

    def down_copy(s):
        return remote(dsc.at[s, its_quarter], rdn.at[s], sd_s.at[seqs + s], sd_r.at[seqs + s], me.y)

    def feed_start(s):
        mix_copy(s).wait()
        base = at(s, me.c * half, half)
        unit, _ = normalize(x[base, :].astype(F32) + (nrm[s] + rbuf[s]) + biases[2:3, :])
        nrm[s] = unit * gains[0:1, :] + biases[3:4, :]

    def feed(s, part):
        w_in, w_back, slot = ((wil, wbl, me.t), (pil, pbl, me.t + 1 - 2 * me.c))[part]
        low = nrm[s].astype(LOW)
        bias = hidden_bias(slot)
        total = dsc[s] if part else jnp.zeros((half, width), F32)
        for j in range(0, hidden, 256):
            col = slice(j, j + 256)
            pre = dot(low, w_in[:, col], 1, 0) + bias[:, col]
            act_low = pre * (0.5 * (1.0 + lax.erf(pre * (1.0 / math.sqrt(2.0)))))
            total = total + dot(act_low.astype(LOW), w_back[:, col], 1, 1)
        dsc[s] = total
        if part:
            down_copy(s).start()

    def out_rows(s, p):
        return at(s, me.c * half + p * quarter, quarter)

    def out_copy(s, k, p, peer):
        src = fin.at[s] if k < 2 else out_h.at[out_rows(s, p)]
        return remote(src, out_h.at[out_rows(s, me.p if k < 2 else p)], sd_s.at[(2 + k) * seqs + s], sd_r.at[(2 + k) * seqs + s], peer)

    def finish(s):
        down_copy(s).wait()
        res = nrm[s, my_quarter] + (dsc[s, my_quarter] + rdn[s]) + biases[4:5, :]
        unit, _ = normalize(res)
        fin[s] = (unit * gains[1:2, :] + biases[5:6, :]).astype(LOW).astype(F32)
        fetch("out", fin.at[s], out_h.at[out_rows(s, me.p)])
        out_copy(s, 0, me.p, me.y).start()
        out_copy(s, 1, me.p, me.core).start()

    def relay(s):
        out_copy(s, 0, me.p, me.y).wait()
        out_copy(s, 2, 1 - me.p, me.core).start()

    def relay_end(s):
        out_copy(s, 1, me.p, me.core).wait()
        out_copy(s, 2, 1 - me.p, me.core).wait()

    def back(s):
        here = slice(s * rows, (s + 1) * rows)
        q = dot(pick[s], qp[...], 1, 0).astype(LOW)
        dc = dctx[here, :]

        def probs(h):
            col = slice(h * HD, (h + 1) * HD)
            scores = dot(q[:, col], kp[:, col], 1, 1) + key_bias(s)
            e = jnp.exp(scores - jnp.max(scores, axis=-1, keepdims=True))
            return e / jnp.sum(e, axis=-1, keepdims=True)

        dpp[...] = attend_back(q, kp, vp, dc, probs, pick[s])[0]

    def entry_copy(s):
        return remote(sbuf.at[s], rig.at[s], sd_s.at[5 * seqs + s], sd_r.at[5 * seqs + s], me.core)

    def entry(s):
        for where, into in ((its_half, sbuf), (my_half, rbuf)):
            base = at(s, where.start, half)
            product = lambda a, w: dot(a, w[0:3 * heads, :], 1, 0)

            def add(low, high, s=s, into=into):
                into[s] = product(*low) + product(*high)

            own_part = lambda base=base: (dproj[base, 0:3 * heads], wal)
            twin_part = lambda where=where: (dpp[where, :], wpl)
            pl.when(me.p == 0)(lambda add=add, a=own_part, b=twin_part: add(a(), b()))
            pl.when(me.p == 1)(lambda add=add, a=own_part, b=twin_part: add(b(), a()))
        entry_copy(s).start()

    def grad_rows(s):
        return at(s, me.c * half, half)

    def grad_copy(s):
        return remote(rbuf.at[s], grad_h.at[grad_rows(s)], sd_s.at[6 * seqs + s], sd_r.at[6 * seqs + s], me.core)

    def entry_end(s):
        entry_copy(s).wait()
        d_one = dres[pl.ds(s * rows, rows), :]
        high = d_one.astype(LOW)
        rest = (d_one - high.astype(F32)).astype(LOW)
        some = pick[s, :, pl.ds(pl.multiple_of(me.c * half, lanes), half)]
        rbuf[s] = (rbuf[s] + rig[s]) + (dot(some, high, 0, 0) + dot(some, rest, 0, 0))
        fetch("out", rbuf.at[s], grad_h.at[grad_rows(s)])
        grad_copy(s).start()

    def turn_weights():
        for j in range(0, width, lanes):
            flip[...] = turned[j:j + lanes, :].T
            wrow_a[:, j:j + lanes] = flip[mine, :]

    def begin():
        ready("gi", "gb")

    def own_start():
        ready("one", "wal")
        first_norm_back()
        ready("att")

    def moments_in():
        ready("mi", "mb", "ma")
        turn_weights()

    def twin_start():
        ready("wpl", "ctx", "low")
        twin_rows()

    work = [(0.0, begin), (4.4, own_start)]
    work += [(5.4 + s, lambda s=s: own_back(s)) for s in range(seqs)]
    work += [(8.4, lambda: ready("x"))] + [(8.5 + 0.7 * j, lambda j=j: weight_grads(j)) for j in range(width // 256)]
    work += [(10.7, lambda: vec_x().start()), (14.0, moments_in), (20.0, vectors_one), (28.0, vectors_two)]
    first_twin = 14.0
    for s in range(seqs):
        t = first_twin + 14.0 * s
        work += [(t, lambda s=s: (twin_start() if s == 0 else None, project(s)) and None)]
        work += [(t + 1.5 + h, lambda s=s, h=h: attend_one(s, h)) for h in range(n_heads)]
        work += [(t + 5.0, lambda s=s: mix(s)), (t + 5.5, lambda s=s: back(s)), (t + 7.5, lambda s=s: feed_start(s))]
        work += [(t + 8.0, lambda s=s: feed(s, 0)), (t + 9.5, lambda s=s: feed(s, 1)), (t + 11.0, lambda s=s: entry(s))]
        work += [(t + 24.0, lambda s=s: finish(s)), (t + 44.0, lambda s=s: relay(s)), (t + 18.0, lambda s=s: entry_end(s))]
    work += [(40.0, vectors_three)]
    for when, do in sorted(work, key=lambda one: one[0]):
        chain_until(when)
        do()
    for when in range(80, 120, 2):
        chain_until(float(when))
    chain_until(1e9)
    for s in range(seqs):
        relay_end(s)
        grad_copy(s).wait()
    for ref, out in ((mi, nmi_h), (mb, nmb_h), (mq, nmq_h), (mo, nmo_h)):
        fetch("out", ref, out)
    chain_end()
    ready("out")


def k2_call(lens, step, warmup, horizon, gains, biases, bias_in, k1, x, weights, moments):
    wqkv, wout, win, wback = weights
    count, width = x.shape
    seqs = lens.shape[0]
    heads, hidden = wout.shape[0], win.shape[1]
    length = count // seqs
    half, quarter = length // 2, length // 4
    shard = moments[1].shape[1]
    slots = width // shard
    n_u = slots // 2
    total = seqs * SPAN_ROWS
    units = seqs * (heads // HD)
    any_ = pl.BlockSpec(memory_space=pl.ANY)
    vm = pl.BlockSpec(memory_space=pltpu.VMEM)
    sm = pl.BlockSpec(memory_space=pltpu.SMEM)
    sds = lambda *shape: jax.ShapeDtypeStruct(shape, F32)
    V = lambda *shape: pltpu.VMEM(shape, F32)
    B = lambda *shape: pltpu.VMEM(shape, LOW)
    D = pltpu.SemaphoreType.DMA
    out_shape = (
        sds(count, width), sds(count, width), sds(slots, shard, hidden), sds(slots, shard, hidden), sds(slots, shard, width),
        sds(*moments[0].shape), sds(*moments[1].shape), sds(*moments[2].shape), sds(*moments[3].shape), sds(4, 16, width),
    )
    scratch = [
        B(count + total, width), V(slots, shard, width), V(n_u, shard, hidden), V(n_u, shard, hidden),
        B(count + total, width), B(count, heads), B(seqs, SPAN_ROWS, length), V(total, width),
        V(total, width), V(total, width), V(units, SPAN_ROWS, length), B(total, heads), B(count, heads), B(count, heads), B(total, heads), B(total, heads),
        B(width, width), B(width, width), B(width, hidden), B(width, hidden), B(width, hidden), B(width, hidden),
        V(shard, hidden), V(shard, hidden), V(shard, width),
        V(*moments[0].shape), V(*moments[1].shape), V(*moments[2].shape), V(*moments[3].shape), V(width, width), V(width, 128),
        B(length, heads), B(length, heads), B(length, heads), B(length, heads), B(length, 3 * heads),
        V(seqs, half, width), V(seqs, half, width), V(seqs, half, width), V(seqs, half, width),
        V(seqs, quarter, width), V(seqs, quarter, width), V(seqs, half, width),
        V(3, 2, n_u - 1, shard, width), V(n_u, shard, width), V(3, shard, width),
        V(16, width), V(16, width), V(16, width), V(n_u, 16, width),
        D((64,)), D((12 * n_u,)), D((12 * n_u,)), D((24 * n_u,)), D((24 * n_u,)), D((6 * n_u,)), D((6 * n_u,)),
        D((2 * n_u,)), D((2 * n_u,)), D((n_u + 3,)), D((n_u + 3,)), D((7 * seqs,)), D((7 * seqs,)), D((6,)),
    ]
    return pl.pallas_call(
        k2_kernel, out_shape=out_shape,
        in_specs=[sm] * 4 + [vm] * 4 + [any_] * 27,
        out_specs=(any_,) * 9 + (vm,),
        scratch_shapes=scratch,
        compiler_params=pltpu.CompilerParams(collective_id=2, has_side_effects=True, vmem_limit_bytes=63 * 2**20),
    )(
        lens, step, warmup, horizon, gains, biases, bias_in, k1[-1], x, *k1[:-1], wqkv, wout, win, wback, *moments,
    )


def rates(step, warmup, horizon):
    clock = jnp.full((1, 128), step[0].astype(F32))
    warm = jnp.full((1, 128), warmup[0].astype(F32))
    far = jnp.full((1, 128), horizon[0].astype(F32))
    ratio = jnp.minimum(clock / warm, (far - clock) / (far - warm))[:, 0:1]
    return ratio, (1.0 - jnp.exp(clock * math.log(0.9)))[:, 0:1], (1.0 - jnp.exp(clock * math.log(0.999)))[:, 0:1]


def k3_kernel(step, warmup, horizon, *refs):
    n_big, n_small = 9, 7
    (out_h, grad_h, ci_h, cb_h, ca_h, *moms_h), refs = refs[:n_big], refs[n_big:]
    small_h, refs = refs[:n_small], refs[n_small:]
    (normed_o, grad_o, ci_o, cb_o, cq_o, co_o, *moms_o), refs = refs[:n_big + 1], refs[n_big + 1:]
    small_o, refs = refs[:6], refs[6:]
    (wide, low, turned, grad, ci, cb, ca, *moms), refs = refs[:n_big + 2], refs[n_big + 2:]
    (gains, biases, bias_in, mom_g, mom_b, mom_h, vt), refs = refs[:n_small], refs[n_small:]
    (ch_g, ch_b, ch_h, nm_g, nm_b, nm_h), (rsem, wsem) = refs[:6], refs[6:]
    chunks, size = wide.shape[:2]
    reads, copies = [], []

    def read(src, dst):
        copy = pltpu.make_async_copy(src, dst, rsem.at[len(reads)])
        copy.start()
        reads.append(copy)
        return copy

    def write(src, dst):
        copy = pltpu.make_async_copy(src, dst, wsem.at[len(copies)])
        copy.start()
        copies.append(copy)

    rows = [pl.ds(j * size, size) for j in range(chunks)]
    got = [read(out_h.at[row], wide.at[j]) for j, row in enumerate(rows)]
    got_ca = read(ca_h, ca)
    plain = [(read(src, buf), buf, dst) for src, buf, dst in zip((grad_h, ci_h, cb_h), (grad, ci, cb), (grad_o, ci_o, cb_o))]
    got_small = [read(src, dst) for src, dst in zip(small_h, (gains, biases, bias_in, mom_g, mom_b, mom_h, vt))]
    plain += [(read(src, buf), buf, dst) for src, buf, dst in zip(moms_h, moms, moms_o)]
    for j, row in enumerate(rows):
        got[j].wait()
        low[j] = wide[j].astype(LOW)
        write(low.at[j], normed_o.at[row])
    got_ca.wait()
    width = turned.shape[1]
    lanes = 128
    for j in range(0, width, lanes):
        turned[j:j + lanes, :] = ca[:, :, j:j + lanes].reshape(width, lanes).T
    split = cq_o.shape[0]
    write(turned.at[pl.ds(0, split)], cq_o)
    write(turned.at[pl.ds(split, width - split)], co_o)
    for copy, buf, dst in plain[:3]:
        copy.wait()
        write(buf, dst)
    for copy in got_small:
        copy.wait()
    put = (*rates(step, warmup, horizon), 0.0)
    heads = gains.shape[1] // 4
    hidden = vt.shape[2]
    common = vt[0]
    ch_g[...], nm_g[0], nm_g[1] = adam(gains[...], common[0:2], mom_g[0], mom_g[1], *put)
    query = jnp.concatenate([vt[k][2:3, 0:heads] for k in range(4)], axis=1)
    value = jnp.concatenate([vt[k][2:3, heads:2 * heads] for k in range(4)], axis=1)
    for row in range(6):
        grad_row = query if row == 0 else value if row == 1 else common[row + 1:row + 2]
        change, first, second = adam(biases[row:row + 1, :], grad_row, mom_b[row, 0:1], mom_b[row, 1:2], *put)
        ch_b[row:row + 1, :] = change
        nm_b[row, 0:1] = first
        nm_b[row, 1:2] = second
    parts = hidden // lanes
    for k in range(4):
        col = slice(k * hidden, (k + 1) * hidden)
        bias = jnp.concatenate([bias_in[k * parts + j:k * parts + j + 1, :] for j in range(parts)], axis=1)
        change, first, second = adam(bias, vt[k][8:9, :], mom_h[0:1, col], mom_h[1:2, col], *put)
        nm_h[0:1, col] = first
        nm_h[1:2, col] = second
        for j in range(parts):
            ch_h[k * parts + j:k * parts + j + 1, :] = change[:, j * lanes:(j + 1) * lanes]
    for src, dst in zip((ch_g, ch_b, ch_h, nm_g, nm_b, nm_h), small_o):
        write(src, dst)
    for copy, buf, dst in plain[3:]:
        copy.wait()
        write(buf, dst)
    for copy in copies:
        copy.wait()


def k3_call(step, warmup, horizon, gains, biases, bias_in, mom_g, mom_b, mom_h, vt, big, heads):
    any_ = pl.BlockSpec(memory_space=pl.ANY)
    sm = pl.BlockSpec(memory_space=pltpu.SMEM)
    of = lambda a: jax.ShapeDtypeStruct(a.shape, a.dtype)
    held = lambda a: pltpu.VMEM(a.shape, F32)
    count, width = big[0].shape
    chunks = 6
    small = (gains, biases, bias_in, mom_g, mom_b, mom_h)
    sds = lambda *shape: jax.ShapeDtypeStruct(shape, F32)
    out_shape = (
        jax.ShapeDtypeStruct((count, width), LOW), *map(of, big[1:4]), sds(3 * heads, width), sds(heads, width),
        *map(of, big[5:]), *map(of, small),
    )
    return pl.pallas_call(
        k3_kernel,
        out_shape=out_shape,
        in_specs=[sm] * 3 + [any_] * (len(big) + 7),
        out_specs=(any_,) * len(out_shape),
        scratch_shapes=[
            pltpu.VMEM((chunks, count // chunks, width), F32), pltpu.VMEM((chunks, count // chunks, width), LOW),
            pltpu.VMEM((width, width), F32), *map(held, big[1:]), *map(held, small), held(vt), *map(held, small),
            pltpu.SemaphoreType.DMA((32,)), pltpu.SemaphoreType.DMA((32,)),
        ],
        compiler_params=pltpu.CompilerParams(vmem_limit_bytes=62 * 2**20),
    )(step, warmup, horizon, *big, *small, vt)


def fast(tokens_in, cotangent, span_mask, lengths, step, warmup, total, w_qkv, w_out, w_in, w_back, gains, biases, bias_in,
         mom_qkv, mom_out, mom_in, mom_back, mom_gains, mom_biases, mom_bias_in):
    width = tokens_in.shape[1]
    heads, hidden = w_out.shape[1], w_in.shape[1]
    wqkv_t = jnp.transpose(w_qkv, (1, 2, 0)).reshape(3 * heads, width)
    wout_t = w_out.T
    bias_tiles = bias_in.reshape(-1, 128)
    k1 = k1_call(
        tokens_in, cotangent, span_mask.reshape(-1, 128), lengths, wqkv_t, wout_t, w_in, w_back, gains, biases, bias_tiles,
        width // mom_out.shape[1]
    )
    *big, vt = k2_call(
        lengths, step, warmup, total, gains, biases, bias_tiles, k1, tokens_in, (wqkv_t, wout_t, w_in, w_back),
        (jnp.transpose(mom_qkv, (0, 2, 1, 3)), mom_out, mom_in, mom_back)
    )
    (
        out, grad, ci, cb, cq, co, nmq, nmo, nmi, nmb, ch_g, ch_b, ch_h, nm_g, nm_b, nm_h
    ) = k3_call(
        step, warmup, total, gains, biases, bias_tiles, mom_gains, jnp.transpose(mom_biases, (1, 0, 2)), mom_bias_in, vt, big, heads
    )
    return (
        out, grad, jnp.transpose(cq.reshape(3, heads, width), (2, 0, 1)), co.T,
        ci.reshape(width, hidden), cb.reshape(width, hidden), ch_g, ch_b, ch_h.reshape(-1),
        jnp.transpose(nmq, (0, 2, 1, 3)), nmo, nmi, nmb, nm_g, jnp.transpose(nm_b, (1, 0, 2)), nm_h,
    )


def layer_norm(values, gain, shift):
    center = values - jnp.mean(values, axis=-1, keepdims=True)
    spread = jnp.mean(center * center, axis=-1, keepdims=True)
    return center * lax.rsqrt(spread + NORM_EPS) * gain + shift


def exact_gelu(values):
    return jax.nn.gelu(values, approximate=False)


def outer_sum(left, right):
    return jnp.einsum("ta,tb->ab", left, right, preferred_element_type=jnp.float32)


def adam_step(weight, grad, moments, ratio, corr_one, corr_two, decay):
    first = BETA_ONE * moments[0] + (1.0 - BETA_ONE) * grad
    second = BETA_TWO * moments[1] + (1.0 - BETA_TWO) * grad * grad
    update = first / corr_one / (jnp.sqrt(second / corr_two) + ADAM_EPS) + decay * weight
    return (-ratio * update, jnp.stack([first, second]))


def on_device(
    tokens_in,
    cotangent,
    span_mask,
    lengths,
    step,
    warmup,
    total,
    w_qkv,
    w_out,
    w_in,
    w_back,
    gains,
    biases,
    bias_in,
    mom_qkv,
    mom_out,
    mom_in,
    mom_back,
    mom_gains,
    mom_biases,
    mom_bias_in,
):
    row_count, model_width = tokens_in.shape
    if mom_out.shape[1] % 8 == 0:
        return fast(
            tokens_in, cotangent, span_mask, lengths, step, warmup, total, w_qkv, w_out, w_in, w_back, gains, biases,
            bias_in, mom_qkv, mom_out, mom_in, mom_back, mom_gains, mom_biases, mom_bias_in
        )
    seq_count = lengths.shape[0]
    seq_length = row_count // seq_count
    head_cols = w_qkv.shape[2]
    hidden_cols = w_in.shape[1]
    head_size = HD
    local_heads = head_cols // head_size
    query_scale = 1.0 / math.sqrt(head_size)
    tensor_slot = lax.axis_index("tensor")
    bias_query = lax.dynamic_slice_in_dim(biases[0], tensor_slot * head_cols, head_cols)
    bias_value = lax.dynamic_slice_in_dim(biases[1], tensor_slot * head_cols, head_cols)
    bias_hidden = lax.dynamic_slice_in_dim(bias_in, tensor_slot * hidden_cols, hidden_cols)
    qkv_low = w_qkv.astype(jnp.bfloat16).reshape(model_width, 3 * head_cols)
    out_low = w_out.astype(jnp.bfloat16)
    in_low = w_in.astype(jnp.bfloat16)
    down_low = w_back.astype(jnp.bfloat16)
    projected = jnp.dot(tokens_in, qkv_low, preferred_element_type=jnp.float32).reshape(
        row_count, 3, head_cols
    )
    attn_shape = (seq_count, seq_length, local_heads, head_size)
    queries = (
        ((projected[:, 0] + bias_query) * query_scale).astype(jnp.bfloat16).reshape(attn_shape)
    )
    keys = projected[:, 1].astype(jnp.bfloat16).reshape(attn_shape)
    values = (projected[:, 2] + bias_value).astype(jnp.bfloat16).reshape(attn_shape)
    positions = jnp.arange(seq_length, dtype=jnp.int32)
    inside = positions[None, :] < lengths[:, None]
    key_bias = jnp.where(inside, 0.0, -1000000000.0).astype(jnp.float32)

    def score_block():
        raw = jnp.einsum("sqhd,skhd->shqk", queries, keys, preferred_element_type=jnp.float32)
        return raw + key_bias[:, None, None, :]

    scores = score_block()
    peak = jnp.max(scores, axis=-1, keepdims=True)
    log_total = peak + jnp.log(jnp.sum(jnp.exp(scores - peak), axis=-1, keepdims=True))
    probs_low = jnp.exp(scores - log_total).astype(jnp.bfloat16)
    context_low = (
        jnp.einsum("shqk,skhd->sqhd", probs_low, values, preferred_element_type=jnp.float32)
        .reshape(row_count, head_cols)
        .astype(jnp.bfloat16)
    )
    attn_part = jnp.einsum("tc,dc->td", context_low, out_low, preferred_element_type=jnp.float32)
    attn_sum = lax.psum(attn_part, "tensor")
    residual_one = tokens_in.astype(jnp.float32) + attn_sum + biases[2]
    normed = layer_norm(residual_one, gains[0], biases[3])
    normed_low = normed.astype(jnp.bfloat16)
    pre_act = jnp.dot(normed_low, in_low, preferred_element_type=jnp.float32) + bias_hidden
    act_low = exact_gelu(pre_act).astype(jnp.bfloat16)
    down_part = jnp.einsum("tf,df->td", act_low, down_low, preferred_element_type=jnp.float32)
    down_sum = lax.psum(down_part, "tensor")
    residual_two = normed + down_sum + biases[4]
    live = (inside.astype(jnp.int32) * span_mask.reshape(seq_count, seq_length)) > 0
    upto = (positions[:, None] <= positions[None, :]).astype(jnp.float32)
    rank = jnp.dot(live.astype(jnp.float32), upto).astype(jnp.int32) - 1
    slots = jnp.arange(SPAN_ROWS, dtype=jnp.int32)
    pick = (live[:, None, :] & (rank[:, None, :] == slots[None, :, None])).astype(jnp.float32)
    pick_low = pick.astype(jnp.bfloat16)

    def rows_of(values):
        width = values.shape[-1]
        return jnp.einsum(
            "srt,std->srd",
            pick,
            values.reshape(seq_count, seq_length, width),
            precision=lax.Precision.HIGHEST,
        ).reshape(seq_count * SPAN_ROWS, width)

    def low_rows_of(values):
        width = values.shape[-1]
        return jnp.einsum(
            "srt,std->srd",
            pick_low,
            values.reshape(seq_count, seq_length, width),
            preferred_element_type=jnp.bfloat16,
        ).reshape(seq_count * SPAN_ROWS, width)

    result = layer_norm(residual_two, gains[1], biases[5])
    normed_out = result.astype(jnp.bfloat16)
    residual_one_rows = rows_of(residual_one)
    residual_two_rows = rows_of(residual_two)
    grad_result = low_rows_of(cotangent).astype(jnp.float32)
    _, norm_two_back = jax.vjp(layer_norm, residual_two_rows, gains[1], biases[5])
    d_res_two, d_gain_two, d_shift_two = norm_two_back(grad_result)
    d_res_two_low = d_res_two.astype(jnp.bfloat16)
    normed_low_rows = low_rows_of(normed_low)
    pre_rows = jnp.dot(normed_low_rows, in_low, preferred_element_type=jnp.float32) + bias_hidden
    act_rows, gelu_back = jax.vjp(exact_gelu, pre_rows)
    grad_back = outer_sum(d_res_two_low, act_rows.astype(jnp.bfloat16))
    d_act = jnp.dot(d_res_two_low, down_low, preferred_element_type=jnp.float32)
    d_pre = gelu_back(d_act)[0]
    d_pre_low = d_pre.astype(jnp.bfloat16)
    grad_in = outer_sum(normed_low_rows, d_pre_low)
    d_normed_part = jnp.einsum("tf,df->td", d_pre_low, in_low, preferred_element_type=jnp.float32)
    d_normed = lax.psum(d_normed_part, "tensor") + d_res_two
    _, norm_one_back = jax.vjp(layer_norm, residual_one_rows, gains[0], biases[3])
    d_res_one, d_gain_one, d_shift_one = norm_one_back(d_normed)
    d_res_one_low = d_res_one.astype(jnp.bfloat16)
    grad_out_proj = outer_sum(d_res_one_low, low_rows_of(context_low))
    row_shape = (seq_count, SPAN_ROWS, local_heads, head_size)
    d_context = (
        jnp.dot(d_res_one_low, out_low, preferred_element_type=jnp.float32)
        .astype(jnp.bfloat16)
        .reshape(row_shape)
    )
    query_rows = low_rows_of(queries.reshape(row_count, head_cols)).reshape(row_shape)
    raw = jnp.einsum("sqhd,skhd->shqk", query_rows, keys, preferred_element_type=jnp.float32)
    probs = jax.nn.softmax(raw + key_bias[:, None, None, :], axis=-1)
    probs_again = probs.astype(jnp.bfloat16)
    d_probs = jnp.einsum("sqhd,skhd->shqk", d_context, values, preferred_element_type=jnp.float32)
    d_values = jnp.einsum(
        "shqk,sqhd->skhd", probs_again, d_context, preferred_element_type=jnp.float32
    ).reshape(row_count, head_cols)
    d_scores = (probs * (d_probs - jnp.sum(probs * d_probs, axis=-1, keepdims=True))).astype(
        jnp.bfloat16
    )
    d_queries = (
        jnp.einsum("shqk,skhd->sqhd", d_scores, keys, preferred_element_type=jnp.float32).reshape(
            seq_count * SPAN_ROWS, head_cols
        )
        * query_scale
    )
    d_keys = jnp.einsum(
        "shqk,sqhd->skhd", d_scores, query_rows, preferred_element_type=jnp.float32
    ).reshape(row_count, head_cols)

    def spread(row_values):
        width = row_values.shape[-1]
        return jnp.einsum(
            "srt,srd->std",
            pick,
            row_values.reshape(seq_count, SPAN_ROWS, width),
            precision=lax.Precision.HIGHEST,
        ).reshape(row_count, width)

    d_proj_low = (
        jnp.stack([spread(d_queries), d_keys, d_values], axis=1)
        .astype(jnp.bfloat16)
        .reshape(row_count, 3 * head_cols)
    )
    grad_qkv = outer_sum(tokens_in, d_proj_low).reshape(model_width, 3, head_cols)
    d_entry_part = jnp.einsum("tc,dc->td", d_proj_low, qkv_low, preferred_element_type=jnp.float32)
    input_grad = lax.psum(d_entry_part, "tensor") + spread(d_res_one)
    first_rank = (tensor_slot == 0).astype(jnp.float32)
    width_zero = jnp.zeros((model_width,), jnp.float32)

    def place_heads(partial_sum):
        return lax.dynamic_update_slice_in_dim(width_zero, partial_sum, tensor_slot * head_cols, 0)

    grad_gains = jnp.stack([d_gain_one, d_gain_two]) * first_rank
    grad_biases = jnp.stack(
        [
            place_heads(jnp.sum(d_queries, axis=0)),
            place_heads(jnp.sum(d_values, axis=0)),
            jnp.sum(d_res_one, axis=0) * first_rank,
            d_shift_one * first_rank,
            jnp.sum(d_res_two, axis=0) * first_rank,
            d_shift_two * first_rank,
        ]
    )
    grad_bias_in = lax.dynamic_update_slice_in_dim(
        jnp.zeros(bias_in.shape, jnp.float32), jnp.sum(d_pre, axis=0), tensor_slot * hidden_cols, 0
    )
    grad_gains, grad_biases, grad_bias_in = lax.psum(
        (grad_gains, grad_biases, grad_bias_in), ("dp", "tensor")
    )
    data_slot = lax.axis_index("dp")
    shard_rows = model_width // lax.axis_size("dp")
    owned = tuple(
        lax.psum_scatter(part, "dp", scatter_dimension=0, tiled=True)
        for part in (grad_qkv, grad_out_proj, grad_in, grad_back)
    )
    clock = step[0].astype(jnp.float32)
    warm = warmup[0].astype(jnp.float32)
    horizon = total[0].astype(jnp.float32)
    ratio = jnp.minimum(clock / warm, (horizon - clock) / (horizon - warm))
    corr_one = 1.0 - jnp.power(BETA_ONE, clock)
    corr_two = 1.0 - jnp.power(BETA_TWO, clock)
    change_rows = []
    fresh_moments = []
    for weight, grad_rows, moment in zip(
        (w_qkv, w_out, w_in, w_back), owned, (mom_qkv, mom_out, mom_in, mom_back)
    ):
        weight_rows = lax.dynamic_slice_in_dim(weight, data_slot * shard_rows, shard_rows, 0)
        row_change, new_moment = adam_step(
            weight_rows, grad_rows, moment, ratio, corr_one, corr_two, WEIGHT_DECAY
        )
        change_rows.append(row_change)
        fresh_moments.append(new_moment)
    change_qkv, change_out_proj, change_in_proj, change_back_proj = (
        lax.all_gather(change_rows[0], "dp", axis=0, tiled=True),
        lax.all_gather(change_rows[1], "dp", axis=0, tiled=True),
        lax.all_gather(change_rows[2], "dp", axis=0, tiled=True),
        lax.all_gather(change_rows[3], "dp", axis=0, tiled=True),
    )
    change_gains, new_mom_gains = adam_step(
        gains, grad_gains, mom_gains, ratio, corr_one, corr_two, 0.0
    )
    change_biases, new_mom_biases = adam_step(
        biases, grad_biases, mom_biases, ratio, corr_one, corr_two, 0.0
    )
    change_bias_in, new_mom_bias_in = adam_step(
        bias_in, grad_bias_in, mom_bias_in, ratio, corr_one, corr_two, 0.0
    )
    return (
        normed_out,
        input_grad,
        change_qkv,
        change_out_proj,
        change_in_proj,
        change_back_proj,
        change_gains,
        change_biases,
        change_bias_in,
        fresh_moments[0],
        fresh_moments[1],
        fresh_moments[2],
        fresh_moments[3],
        new_mom_gains,
        new_mom_biases,
        new_mom_bias_in,
    )


def solution(mesh):
    in_specs = (
        P("dp", None),
        P("dp", None),
        P("dp"),
        P("dp"),
        P(),
        P(),
        P(),
        P(None, None, "tensor"),
        P(None, "tensor"),
        P(None, "tensor"),
        P(None, "tensor"),
        P(),
        P(),
        P(),
        P(None, "dp", None, "tensor"),
        P(None, "dp", "tensor"),
        P(None, "dp", "tensor"),
        P(None, "dp", "tensor"),
        P(),
        P(),
        P(),
    )
    out_specs = (
        P("dp", None),
        P("dp", None),
        P(None, None, "tensor"),
        P(None, "tensor"),
        P(None, "tensor"),
        P(None, "tensor"),
        P(),
        P(),
        P(),
        P(None, "dp", None, "tensor"),
        P(None, "dp", "tensor"),
        P(None, "dp", "tensor"),
        P(None, "dp", "tensor"),
        P(),
        P(),
        P(),
    )
    return jax.shard_map(
        on_device, mesh=mesh, in_specs=in_specs, out_specs=out_specs, check_vma=False
    )
```

```python
import math

import jax
import jax.numpy as jnp
from jax import lax
from jax.experimental import pallas as pl
from jax.experimental.pallas import tpu as pltpu
from jax.sharding import PartitionSpec as P

HD = 64
SPAN_ROWS = 80
NORM_EPS = 1e-12
MESH = pl.DeviceIdType.MESH
F32 = jnp.float32
LOW = jnp.bfloat16


def dot(left, right, left_dim, right_dim):
    return lax.dot_general(
        left, right, (((left_dim,), (right_dim,)), ((), ())), preferred_element_type=F32
    )


def normalize(rows):
    center = rows - jnp.mean(rows, axis=-1, keepdims=True)
    scale = lax.rsqrt(jnp.mean(center * center, axis=-1, keepdims=True) + NORM_EPS)
    return center * scale, scale


def norm_back(grad, gain, unit, scale):
    weighted = grad * gain
    return scale * (
        weighted
        - jnp.mean(weighted, axis=-1, keepdims=True)
        - unit * jnp.mean(weighted * unit, axis=-1, keepdims=True)
    )


def row_sum(rows):
    return jnp.sum(rows, axis=0, keepdims=True)


class Peers:
    def __init__(self):
        self.d = lax.axis_index("dp")
        self.t = lax.axis_index("tensor")
        self.b = lax.rem(self.d, 2)
        self.c = lax.rem(self.t, 2)
        self.p = lax.div(self.t, 2)
        self.u = lax.div(self.d, 2)
        self.core = (self.d, self.t + 1 - 2 * self.c)
        self.y = (self.d, lax.rem(self.t + 2, 4))
        self.x = (self.d + 1 - 2 * self.b, self.t)


def send(src, dst, sems, k, peer):
    copy = pltpu.make_async_remote_copy(
        src_ref=src, dst_ref=dst, send_sem=sems.at[0, k], recv_sem=sems.at[1, k],
        device_id=peer, device_id_type=MESH,
    )
    copy.start()
    return copy


def local(src, dst, sem):
    copy = pltpu.make_async_copy(src, dst, sem)
    copy.start()
    return copy


def greet(peers):
    barrier = pltpu.get_barrier_semaphore()
    for peer in peers:
        pl.semaphore_signal(barrier, inc=1, device_id=peer, device_id_type=MESH)
    pl.semaphore_wait(barrier, len(peers))


def gelu_parts(pre):
    cdf = 0.5 * (1.0 + lax.erf(pre * (1.0 / math.sqrt(2.0))))
    pdf = jnp.exp(-0.5 * pre * pre) * (1.0 / math.sqrt(2.0 * math.pi))
    return pre * cdf, cdf + pre * pdf


def k1_kernel(
    lens, mask_h, gains_h, biases_h, bias_in_h, x_h, cot_h, wqkv_h, wout_h, win_h, wback_h,
    gi_h, gb_h, full_h, res_h, dres_h, pick_h, pm_h, qm_h, k_h, v_h, cm_h, ctx_h, wal_h, wpl_h, wil_h, wbl_h, pil_h, pbl_h, vec_h,
    mask, gains, biases, bias_in, vec, x, cot, wqkv, wout, win, wback, wp_qkv, wp_out, pwin, pwback, q_o, k_o, v_o, ctx_o, pick_o, wal, wpl, wil, wbl, pil, pbl, gin, gback,
    pm, xm, cotm, qm, ctxm, cml, ctxp, ap, apc, normed, nlow, act, gp, part, rc1, h1, ry1,
    part2, rc2, h2, ry2, full2, full, dres2, d2w, d2x, nxw, nxx, dplow,
    lsem, rsem, ssem,
):
    seqs, rows = 3, SPAN_ROWS
    count = x_h.shape[0]
    length = count // seqs
    total = seqs * rows
    half = total // 2
    heads = ctx_o.shape[1]
    n_heads = heads // HD
    width = x_h.shape[1]
    me = Peers()

    def seq(s):
        return pl.ds(s * length, length)

    small = [
        local(src, dst, ssem.at[k])
        for k, (src, dst) in enumerate(((mask_h, mask), (gains_h, gains), (biases_h, biases), (bias_in_h, bias_in)))
    ]
    loads = [
        local(wqkv_h, wqkv, lsem.at[0]),
        local(wout_h, wout, lsem.at[1]),
    ] + [local(x_h.at[seq(s)], x.at[seq(s)], lsem.at[2 + s]) for s in range(seqs)] + [
        local(win_h, win, lsem.at[2 + seqs]),
        local(wback_h, wback, lsem.at[3 + seqs]),
        local(cot_h, cot, lsem.at[4 + seqs]),
    ]
    stores = []

    def keep(src, dst):
        stores.append(local(src, dst, lsem.at[8 + len(stores)]))

    slots = gin.shape[0]
    wo_base = 41 + 2 * slots
    shard = gin.shape[1]
    n_u = slots // 2
    z = me.u
    greet([me.core, me.y, me.x] + [(2 * lax.rem(z + k, n_u) + me.b, me.t) for k in range(1, n_u)])

    out_rows = heads // 2 // seqs

    def out_part(k):
        return pl.ds(pl.multiple_of(me.b * (heads // 2) + k * out_rows, 8), out_rows)

    wo_y = [send(wout_h.at[out_part(k)], wp_out.at[out_part(k)], rsem, wo_base + k, me.y) for k in range(seqs)]
    for load in small:
        load.wait()
    loads[0].wait()
    wal[0:3 * heads, :] = wqkv[...].astype(LOW)
    loads[1].wait()
    wal[3 * heads:, :] = wout[...].astype(LOW)
    keep(wal, wal_h)

    def pick_bias(row, k=heads):
        out = jnp.zeros((1, k), F32)
        for slot in range(4):
            piece = biases[row:row + 1, slot * k:(slot + 1) * k]
            out = jnp.where(me.t == slot, piece, out)
        return out

    bias_q, bias_v = pick_bias(0), pick_bias(1)
    hidden = win.shape[1]
    lanes = 128
    bias_h = jnp.concatenate(
        [bias_in[pl.ds(me.t * (hidden // lanes) + j, 1), :] for j in range(hidden // lanes)], axis=1
    )
    upto = (
        lax.broadcasted_iota(jnp.int32, (length, length), 0)
        <= lax.broadcasted_iota(jnp.int32, (length, length), 1)
    ).astype(F32).astype(LOW)
    position = lax.broadcasted_iota(jnp.int32, (1, length), 1)
    slot_of = lax.broadcasted_iota(jnp.int32, (rows, length), 0).astype(F32)
    scale = 1.0 / math.sqrt(HD)
    def project(s):
        loads[2 + s].wait()
        at = seq(s)
        xs = x[at, :]
        q = ((dot(xs, wal[0:heads, :], 1, 1) + bias_q) * scale).astype(LOW)
        k = dot(xs, wal[heads:2 * heads, :], 1, 1).astype(LOW)
        v = (dot(xs, wal[2 * heads:3 * heads, :], 1, 1) + bias_v).astype(LOW)
        q_o[at, :] = q
        k_o[at, :] = k
        v_o[at, :] = v
        parts = length // lanes
        marks = jnp.concatenate([mask[pl.ds(s * parts + j, 1), :] for j in range(parts)], axis=1)
        inside = position < lens[s]
        live = jnp.where(inside, marks, 0).astype(F32)
        rank = dot(jnp.broadcast_to(live, (8, length)).astype(LOW), upto, 1, 0)[0:1] - 1.0
        pick = jnp.where((rank == slot_of) & (live > 0.0), 1.0, 0.0).astype(LOW)
        pick_o[s] = pick
        here = pl.ds(s * rows, rows)
        xm[here, :] = dot(pick, xs, 1, 0)
        qrow = dot(pick, q, 1, 0).astype(LOW)
        qm[here, :] = qrow
        key_bias = jnp.where(inside, 0.0, -1000000000.0)
        pieces = []
        for h in range(n_heads):
            col = slice(h * HD, (h + 1) * HD)
            scores = dot(qrow[:, col], k[:, col], 1, 1) + key_bias
            e = jnp.exp(scores - jnp.max(scores, axis=-1, keepdims=True))
            prob = e / jnp.sum(e, axis=-1, keepdims=True)
            pm[s * n_heads + h] = prob
            pieces.append(dot(prob.astype(LOW), v[:, col], 1, 0))
        low = jnp.concatenate(pieces, axis=1).astype(LOW)
        cml[here, :] = low
        ctxm[here, :] = low.astype(F32)
        return send(ctxm.at[here], ctxp.at[here], rsem, 24 + s, me.y)

    ctx_y, wo_x = [], []
    for s in range(seqs):
        ctx_y.append(project(s))
        wo_y[s].wait()
        wo_x.append(send(wp_out.at[out_part(s)], wp_out.at[out_part(s)], rsem, wo_base + seqs + s, me.x))
    third = heads // 2

    share = 2 * third // n_u

    def share_of(b, u):
        return pl.ds(pl.multiple_of(b * (3 * third) + third + u * share, 8), share)

    def chain_copy(way, s, b, u):
        place = wp_qkv.at[share_of(b, u)]
        k = 29 + (way * (n_u - 1) + s) * 2 + b
        peer = (me.d + 2, me.t) if way == 0 else (me.d - 2, me.t)
        return pltpu.make_async_remote_copy(
            src_ref=place, dst_ref=place, send_sem=rsem.at[0, k], recv_sem=rsem.at[1, k],
            device_id=peer, device_id_type=MESH,
        )

    def chain_cases(s):
        return [
            (way, b, z - s if way == 0 else z + s, (z >= s) if way == 0 else (z + s <= n_u - 1), (z < n_u - 1) if way == 0 else (z > 0))
            for way in range(2) for b in range(2)
        ]

    def chain_step(s):
        for way, b, u, here, edge in chain_cases(s):
            if s > 0:
                pl.when(here)(lambda way=way, b=b, u=u: chain_copy(way, s - 1, b, u).wait_recv())
            if s < n_u - 1:
                pl.when(here & edge)(lambda way=way, b=b, u=u: chain_copy(way, s, b, u).start())

    def chain_sent():
        for s in range(n_u - 1):
            for way, b, u, here, edge in chain_cases(s):
                pl.when(here & edge)(lambda way=way, b=b, u=u, s=s: chain_copy(way, s, b, u).wait_send())

    def attend_all(s):
        at = slice(s * length, (s + 1) * length)
        key_bias = jnp.where(position < lens[s], 0.0, -1000000000.0)
        pieces = []
        for h in range(n_heads):
            col = slice(h * HD, (h + 1) * HD)
            scores = dot(q_o[at, col], k_o[at, col], 1, 1) + key_bias
            e = jnp.exp(scores - jnp.max(scores, axis=-1, keepdims=True))
            prob = (e / jnp.sum(e, axis=-1, keepdims=True)).astype(LOW)
            pieces.append(dot(prob, v_o[at, col], 1, 0))
        ctx_o[at, :] = jnp.concatenate(pieces, axis=1).astype(LOW)

    mine_share = share_of(me.b, z)
    wz_y = send(wqkv.at[mine_share], wp_qkv.at[mine_share], rsem, 27, me.y)
    for ref, out in ((pm, pm_h), (qm, qm_h), (k_o, k_h), (v_o, v_h), (cml, cm_h), (pick_o, pick_h)):
        keep(ref, out)
    for load in loads[2 + seqs:4 + seqs]:
        load.wait()
    wil[...] = win[...].astype(LOW)
    wbl[...] = wback[...].astype(LOW)
    keep(wil, wil_h)
    keep(wbl, wbl_h)
    loads[4 + seqs].wait()
    for s in range(seqs):
        cotm[s * rows:(s + 1) * rows, :] = dot(pick_o[s], cot[s * length:(s + 1) * length, :], 1, 0)
    for copy in wo_x:
        copy.wait()
    for copy in ctx_y:
        copy.wait()
    woq = wp_out[...].astype(LOW)

    def mix(first, second):
        ap[...] = dot(*first, 1, 0) + dot(*second, 1, 0)

    own_part = lambda: (cml[...], wal[3 * heads:, :])
    twin_part = lambda: (ctxp[...].astype(LOW), woq)
    pl.when(me.p == 0)(lambda: mix(own_part(), twin_part()))
    pl.when(me.p == 1)(lambda: mix(twin_part(), own_part()))
    ap_c = send(ap, apc, rsem, 3, me.core)
    wz_y.wait()
    wz_x = send(wp_qkv.at[mine_share], wp_qkv.at[mine_share], rsem, 28, me.x)
    ap_c.wait()
    xm[...] = xm[...] + (ap[...] + apc[...]) + biases[2:3, :]
    keep(xm, res_h)
    unit, inv = normalize(xm[...])
    normed[...] = unit * gains[0:1, :] + biases[3:4, :]
    nlow[...] = normed[...].astype(LOW)
    nxw[...] = nlow[...].astype(F32)
    mine = pl.ds(pl.multiple_of(me.c * half, 8), half)
    other = pl.ds(pl.multiple_of((1 - me.c) * half, 8), half)
    nx_x = send(nxw.at[mine], nxx.at[mine], rsem, 5, me.x)
    for j in range(0, hidden, 256):
        col = slice(j, j + 256)
        a, g = gelu_parts(dot(nlow[...], wil[:, col], 1, 0) + bias_h[:, col])
        act[:, col] = a.astype(LOW)
        gp[:, col] = g
    part[...] = dot(act[...], wbl[...], 1, 1)

    cuts = ((0, 64), (64, half - 64))

    def all_reduce(src, rc, hs, ry, dst, base, fill, late=None):
        pieces = []
        for k, (start, size) in enumerate(cuts):
            mine_k = pl.ds(pl.multiple_of(me.c * half + start, 8), size)
            other_k = pl.ds(pl.multiple_of((1 - me.c) * half + start, 8), size)
            pieces.append((k, pl.ds(start, size), mine_k, other_k))
        first = [send(src.at[other_k], rc.at[row], rsem, base + k, me.core) for k, row, _, other_k in pieces]
        second, third = [], []
        for k, row, mine_k, _ in pieces:
            first[k].wait()
            hs[row, :] = src[mine_k, :] + rc[row, :]
            second.append(send(hs.at[row], ry.at[row], rsem, base + 2 + k, me.y))
        fill()
        for k, row, mine_k, _ in pieces:
            second[k].wait()
            dst[mine_k, :] = hs[row, :] + ry[row, :]
            third.append(send(dst.at[mine_k], dst.at[mine_k], rsem, base + 4 + k, me.core))
        if late:
            late()
        for copy in third:
            copy.wait()

    relay = []

    def fill_one():
        wide.append(send(win, pwin, rsem, 22, me.core))
        wz_x.wait()
        chain_step(0)
        attend_all(0)
        attend_all(1)
        nx_x.wait()
        relay.append(send(nxx.at[mine], nxx.at[mine], rsem, 6, me.core))
        chain_step(1)

    wide = []
    all_reduce(part, rc1, h1, ry1, full, 29 + 2 * slots, fill_one)
    relay[0].wait()
    unit, inv = normalize(normed[...] + full[...] + biases[4:5, :])
    grad = cotm[...]
    d_two = norm_back(grad, gains[1:2, :], unit, inv)
    dres2[...] = d_two
    vec[...] = jnp.zeros(vec.shape, F32)
    vec[1:2, :] = row_sum(grad * unit)
    vec[5:6, :] = row_sum(d_two)
    vec[6:7, :] = row_sum(grad)
    d2w[...] = d_two.astype(LOW).astype(F32)
    rows_k = [pl.ds(pl.multiple_of(me.c * half + start, 8), size) for start, size in cuts]
    d2_base = wo_base + 2 * seqs
    d2_x = [send(d2w.at[row], d2x.at[row], rsem, d2_base + k, me.x) for k, row in enumerate(rows_k)]
    keep(dres2, dres_h)
    d2low = d2w[...].astype(LOW)
    for j in range(0, hidden, 256):
        col = slice(j, j + 256)
        d_pre = dot(d2low, wbl[:, col], 1, 0) * gp[:, col]
        vec[8:9, col] = row_sum(d_pre)
        dplow[:, col] = d_pre.astype(LOW)
    part2[...] = dot(dplow[...], wil[...], 1, 1)

    def cut(rows):
        return rows.reshape(slots, shard, rows.shape[1])

    def fill_two():
        wide.append(send(wback, pwback, rsem, 23, me.core))
        attend_all(2)
        chain_step(2)
        keep(ctx_o, ctx_h)
        for j in range(0, hidden, 256):
            col = slice(j, j + 256)
            gin[:, :, col] = cut(dot(nlow[...], dplow[:, col], 0, 0))
            gback[:, :, col] = cut(dot(d2low, act[:, col], 0, 0))
        wide[0].wait()
        pil[...] = pwin[...].astype(LOW)
        keep(pil, pil_h)
        for k, row in enumerate(rows_k):
            d2_x[k].wait()
            relay.append(send(d2x.at[row], d2x.at[row], rsem, d2_base + 2 + k, me.core))

    def other_x():
        for copy in relay[1:]:
            copy.wait()
        nlx = nxx[...].astype(LOW)
        dlx = d2x[...].astype(LOW)
        for j in range(0, hidden, 256):
            col = slice(j, j + 256)
            a, g = gelu_parts(dot(nlx, wil[:, col], 1, 0) + bias_h[:, col])
            d_pre = (dot(dlx, wbl[:, col], 1, 0) * g).astype(LOW)
            gin[:, :, col] += cut(dot(nlx, d_pre, 0, 0))
            gback[:, :, col] += cut(dot(dlx, a.astype(LOW), 0, 0))
        for u in range(slots // 2):
            keep(gin.at[2 * u + me.b], gi_h.at[u])
            keep(gback.at[2 * u + me.b], gb_h.at[u])

    all_reduce(part2, rc2, h2, ry2, full2, 35 + 2 * slots, fill_two, other_x)
    keep(full2, full_h)
    keep(vec, vec_h)
    for step in range(3, n_u):
        chain_step(step)
    for b in range(2):
        start = b * 3 * third
        wpl[start:start + third, :] = jnp.zeros((third, width), LOW)
        rest = slice(start + third, start + 3 * third)
        wpl[rest, :] = wp_qkv[rest, :].astype(LOW)
    wpl[3 * heads:, :] = woq
    keep(wpl, wpl_h)
    wide[1].wait()
    pbl[...] = pwback[...].astype(LOW)
    keep(pbl, pbl_h)
    chain_sent()
    for copy in stores:
        copy.wait()


def k1_call(x, cot, mask, lens, wqkv, wout, win, wback, gains, biases, bias_in, slots):
    count, width = x.shape
    seqs = lens.shape[0]
    heads = wout.shape[0]
    hidden = win.shape[1]
    length = count // seqs
    total = seqs * SPAN_ROWS
    half = total // 2
    units = seqs * (heads // HD)
    any_ = pl.BlockSpec(memory_space=pl.ANY)
    sm = pl.BlockSpec(memory_space=pltpu.SMEM)
    sds = jax.ShapeDtypeStruct
    V = pltpu.VMEM
    wide = lambda r, t=F32: V((r, width), t)
    block = (slots // 2, width // slots, hidden)
    square = sds((width, hidden), LOW)
    out_shape = (
        sds(block, F32), sds(block, F32), sds((total, width), F32), sds((total, width), F32), sds((total, width), F32),
        sds((seqs, SPAN_ROWS, length), LOW), sds((units, SPAN_ROWS, length), F32), sds((total, heads), LOW),
        sds((count, heads), LOW), sds((count, heads), LOW), sds((total, heads), LOW), sds((count, heads), LOW),
        sds((4 * heads, width), LOW), sds((4 * heads, width), LOW), square, square, square, square,
        sds((16, width), F32),
    )
    scratch = [
        V(mask.shape, jnp.int32), V(gains.shape, F32), V(biases.shape, F32), V(bias_in.shape, F32), wide(16),
        wide(count, LOW), wide(count, LOW), wide(3 * heads), wide(heads), V((width, hidden), F32),
        V((width, hidden), F32), wide(3 * heads), wide(heads), V((width, hidden), F32), V((width, hidden), F32),
        V((count, heads), LOW), V((count, heads), LOW), V((count, heads), LOW), V((count, heads), LOW),
        V((seqs, SPAN_ROWS, length), LOW), wide(4 * heads, LOW), wide(4 * heads, LOW), V((width, hidden), LOW), V((width, hidden), LOW),
        V((width, hidden), LOW), V((width, hidden), LOW), V((slots, width // slots, hidden), F32), V((slots, width // slots, hidden), F32),
        V((units, SPAN_ROWS, length), F32), wide(total), wide(total), V((total, heads), LOW),
        V((total, heads), F32), V((total, heads), LOW), V((total, heads), F32), wide(total), wide(total),
        wide(total), wide(total, LOW), V((total, hidden), LOW), V((total, hidden), F32), wide(total), wide(half), wide(half), wide(half),
        wide(total), wide(half), wide(half), wide(half), wide(total), wide(total), wide(total), wide(total), wide(total), wide(total), wide(total),
        V((total, hidden), LOW),
        pltpu.SemaphoreType.DMA((8 + 20 + slots,)), pltpu.SemaphoreType.DMA((2, 45 + 2 * slots + 2 * seqs)), pltpu.SemaphoreType.DMA((4,)),
    ]
    return pl.pallas_call(
        k1_kernel, out_shape=out_shape,
        in_specs=[sm] + [any_] * 10,
        out_specs=(any_,) * len(out_shape),
        scratch_shapes=scratch,
        compiler_params=pltpu.CompilerParams(
            collective_id=1, has_side_effects=True, vmem_limit_bytes=60 * 2**20
        ),
    )(lens, mask, gains, biases, bias_in, x, cot, wqkv, wout, win, wback)


BETA_ONE = 0.9
BETA_TWO = 0.999
ADAM_EPS = 1e-06
WEIGHT_DECAY = 0.01


def adam(weight, grad, first, second, ratio, corr_one, corr_two, decay):
    first = BETA_ONE * first + (1.0 - BETA_ONE) * grad
    second = BETA_TWO * second + (1.0 - BETA_TWO) * grad * grad
    update = first / corr_one / (jnp.sqrt(second / corr_two) + ADAM_EPS) + decay * weight
    return -ratio * update, first, second


FLIGHT = 0.55
PLAN_READY = (1.2, 1.2, 3.2)
SWAP_FIRST = ((0, 0),)
WEIGHT = {("RS", 0, 0): 8.0, ("RS", 1, 0): 7.0, ("RS", 2, 0): -7.0, ("RS", 2, 1): -10.0, ("AG", 0, 0): -10.0}
BLOCK_US = 3.2


def plan(n, weight):
    tasks = {}
    for ch in range(3):
        for p in range(2):
            ready = PLAN_READY[ch]
            swap = ch == 2
            both = (ch, p) in SWAP_FIRST
            for z in range(n):
                if swap:
                    for u in range(n):
                        tasks["XS", ch, p, 0, u, z] = ("X", z), [], ready
                for d in range(n):
                    if d == z:
                        continue
                    step = 1 if d > z else -1
                    kind = "RSR" if d > z else "RSL"
                    need = [(kind, ch, p, 0, d, z - step)] if 0 <= z - step < n else []
                    if swap:
                        need.append(("XS", ch, p, 0, d, z))
                    tasks[kind, ch, p, 0, d, z] = (kind[2], z), need, ready
                end = [("RSR", ch, p, 0, z, z - 1)] if z > 0 else []
                if z < n - 1:
                    end.append(("RSL", ch, p, 0, z, z + 1))
                if swap:
                    end.append(("XS", ch, p, 0, z, z))
                for par in (0, 1) if both else (0,):
                    for u in range(n):
                        if u == z:
                            need = [("AGX", ch, p, 0, z, z)] if par else end
                        else:
                            need = [("AGR", ch, p, par, u, z - 1) if u < z else ("AGL", ch, p, par, u, z + 1)]
                        if u <= z < n - 1:
                            tasks["AGR", ch, p, par, u, z] = ("R", z), need, 0.0
                        if 0 < z <= u:
                            tasks["AGL", ch, p, par, u, z] = ("L", z), need, 0.0
                        if par == 0 and (u == z or not both):
                            tasks["AGX", ch, p, 0, u, z] = ("X", z), need, 0.0
    after = {key: [] for key in tasks}
    for key, (_, need, _) in tasks.items():
        for one in need:
            after[one].append(key)
    rank = {}

    def longest(key):
        if key not in rank:
            rank[key] = 1.0 + FLIGHT + max([longest(k) for k in after[key]], default=0.0)
        return rank[key]

    missing = {key: len(task[1]) for key, task in tasks.items()}
    open_at = {key: task[2] for key, task in tasks.items() if not task[1]}
    free, done, order = {}, {}, []
    while open_at:
        by_link = {}
        for key in open_at:
            by_link.setdefault(tasks[key][0], []).append(key)
        best = None
        for link, keys in by_link.items():
            start = max(free.get(link, 0.0), min(open_at[k] for k in keys))
            able = [k for k in keys if open_at[k] <= start + 1e-9]
            key = max(able, key=lambda k: (longest(k) + weight.get((k[0][:2] if k[0] != "AGX" else "AX", k[1], k[2]), 0.0), -open_at[k]))
            if best is None or start < best[0] - 1e-9:
                best = start, key
        start, key = best
        free[tasks[key][0]] = start + 1.0
        done[key] = start + 1.0 + FLIGHT
        order.append((start, key))
        del open_at[key]
        for k in after[key]:
            missing[k] -= 1
            if missing[k] == 0:
                open_at[k] = max(max(done[q] for q in tasks[k][1]) + 0.15, tasks[k][2])
    return order, tasks, max(done.values())


def k2_kernel(
    lens, step, warmup, horizon, gains_h, biases_h, bias_in_h, vec_h,
    x_h, gi_h, gb_h, full_h, res_h, dtwo_h, pick_h, pm_h, qm_h, k_h, v_h, cm_h, ctx_h, wal_h, wpl_h, wil_h, wbl_h, pil_h, pbl_h,
    wqkv_h, wout_h, win_h, wback_h, mq_h, mo_h, mi_h, mb_h,
    out_h, grad_h, ci_h, cb_h, ca_h, nmq_h, nmo_h, nmi_h, nmb_h, vt_h,
    gains, biases, bias_in, vec, vt, wp, x, ga, gi, gb, dproj, ctx, pick, dres, full, dtwo, pm, qm, ko, vo, cm, dctx, wal, wpl, wil, wbl, pil, pbl,
    wrow_i, wrow_b, wrow_a, mq, mo, mi, mb, turned, flip,
    qp, kp, vp, ctxp, dpp, sbuf, rbuf, nrm, dsc, rdn, fin, rig,
    ring, xr, own, v0, v1, vx, vz,
    lsem, rs_s, rs_r, ag_s, ag_r, ax_s, ax_r, xs_s, xs_r, vs_s, vs_r, sd_s, sd_r, usem, wsem,
):
    me = Peers()
    n_u = gi.shape[0]
    seqs = sbuf.shape[0]
    count, width = x_h.shape
    length = count // seqs
    rows = SPAN_ROWS
    total = seqs * rows
    heads = ctx.shape[1]
    n_heads = heads // HD
    shard = gi.shape[1]
    hidden = wil.shape[1]
    half = length // 2
    quarter = length // 4
    z, b = me.u, me.b
    right = (me.d + 2, me.t)
    left = (me.d - 2, me.t)
    diag = (me.d, 3 - me.t)

    def remote(src, dst, ss, rr, peer):
        return pltpu.make_async_remote_copy(
            src_ref=src, dst_ref=dst, send_sem=ss, recv_sem=rr, device_id=peer, device_id_type=MESH
        )

    pend = {}
    order = iter(range(64))

    def fetch(name, src, dst):
        copy = pltpu.make_async_copy(src, dst, lsem.at[next(order)])
        copy.start()
        pend.setdefault(name, []).append(copy)

    def ready(*names):
        for name in names:
            for copy in pend.pop(name, []):
                copy.wait()

    for src, dst in ((gains_h, gains), (biases_h, biases), (bias_in_h, bias_in), (vec_h, vec)):
        fetch("small", src, dst)
    fetch("one", full_h, full)
    fetch("one", res_h, dres)
    fetch("one", dtwo_h, dtwo)
    fetch("gi", gi_h, gi)
    fetch("gb", gb_h, gb)
    fetch("wal", wal_h, wal)
    fetch("att", pick_h, pick)
    fetch("att", pm_h, pm)
    fetch("att", qm_h, qm)
    fetch("att", k_h, ko)
    fetch("att", v_h, vo)
    fetch("att", cm_h, cm)
    fetch("x", x_h, x.at[pl.ds(0, count)])
    fetch("wpl", wpl_h, wpl)
    fetch("ctx", ctx_h, ctx)
    fetch("low", wil_h, wil)
    fetch("low", wbl_h, wbl)
    fetch("low", pil_h, pil)
    fetch("low", pbl_h, pbl)
    mine = pl.ds(pl.multiple_of(me.d * shard, 8), shard)
    fetch("mi", win_h.at[mine], wrow_i)
    fetch("mi", mi_h, mi)
    fetch("mb", wback_h.at[mine], wrow_b)
    fetch("mb", mb_h, mb)
    fetch("ma", wqkv_h, turned.at[pl.ds(0, 3 * heads)])
    fetch("ma", wout_h, turned.at[pl.ds(3 * heads, heads)])
    fetch("ma", mq_h, mq)
    fetch("ma", mo_h, mo)

    others = [(2 * lax.rem(z + k, n_u) + b, me.t) for k in range(1, n_u)]
    greet([me.core, me.y, diag, me.x] + others)

    third = heads // 2

    def first_third(k):
        return remote(wqkv_h.at[pl.ds(k * 3 * third, third)], wp.at[k], wsem.at[0, k], wsem.at[1, k], me.y)

    order_all, tasks, _ = plan(n_u, WEIGHT)
    part_rows = shard // 2

    def rows_of(p):
        return pl.ds(p * part_rows, part_rows)

    def g_at(ch, u):
        return ga.at[2 * u + b] if ch == 2 else (gi, gb)[ch].at[u]

    def target(ch, d):
        return (ci_h, cb_h, ca_h)[ch].at[d]

    def xr_at(u, p):
        return xr.at[u, rows_of(p)]

    def ring_at(key):
        kind, ch, p, _, d, node = key
        place = d - (node + 1) if kind == "RSR" else (node - 1) - d
        return ring.at[ch, 0 if kind == "RSR" else 1, place, rows_of(p)]

    def transfer(key, incoming):
        kind, ch, p, par, u, node = key
        way = 0 if kind[2:] == "R" else 1
        if kind == "XS":
            k = p * n_u + u
            return remote(ga.at[2 * u + 1 - b, rows_of(p)], xr_at(u, p), xs_s.at[k], xs_r.at[k], me.x)
        if kind[:2] == "RS":
            k = ((ch * 2 + p) * 2 + way) * n_u + u
            peer = right if way == 0 else left
            return remote(g_at(ch, u).at[rows_of(p)], ring_at(key), rs_s.at[k], rs_r.at[k], peer)
        parity = b if (par == 0) != (incoming and kind == "AGX") else 1 - b
        there = target(ch, 2 * u + parity).at[rows_of(p)]
        here = own.at[ch, rows_of(p)] if u == node and par == 0 else there
        if kind == "AGX":
            k = (ch * 2 + p) * n_u + u
            return remote(here, there, ax_s.at[k], ax_r.at[k], me.x)
        k = (((ch * 2 + p) * 2 + way) * 2 + par) * n_u + u
        return remote(here, there, ag_s.at[k], ag_r.at[k], right if way == 0 else left)

    ratio, corr_one, corr_two = rates(step, warmup, horizon)

    def own_copy(ch, p):
        return pltpu.make_async_copy(own.at[ch, rows_of(p)], target(ch, me.d).at[rows_of(p)], usem.at[ch * 2 + p])

    def update(ch, p):
        at_p = rows_of(p)
        if ch < 2:
            w, m = ((wrow_i, mi), (wrow_b, mb))[ch]
            change, first, second = adam(
                w[at_p, :], g_at(ch, z)[at_p, :], m[0, at_p, :], m[1, at_p, :], ratio, corr_one, corr_two, WEIGHT_DECAY
            )
            own[ch, at_p, :] = change
            m[0, at_p, :] = first
            m[1, at_p, :] = second
        else:
            for k in range(4):
                col = slice(k * heads, (k + 1) * heads)
                first = mo[0, at_p, :] if k == 3 else mq[0, k, at_p, :]
                second = mo[1, at_p, :] if k == 3 else mq[1, k, at_p, :]
                change, first, second = adam(
                    wrow_a[at_p, col], ga[me.d, at_p, col], first, second, ratio, corr_one, corr_two, WEIGHT_DECAY
                )
                own[2, at_p, col] = change
                if k < 3:
                    mq[0, k, at_p, :] = first
                    mq[1, k, at_p, :] = second
                else:
                    mo[0, at_p, :] = first
                    mo[1, at_p, :] = second
        own_copy(ch, p).start()

    queue = [[] for _ in range(n_u)]
    inbound = [[] for _ in range(n_u)]
    for start, key in order_all:
        kind, node = key[0], key[5]
        queue[node].append((start * BLOCK_US, key))
        goes = node if kind in ("XS", "AGX") else node + 1 if kind[2] == "R" else node - 1
        inbound[goes].append(key)
    for node in range(n_u):
        queue[node].sort(key=lambda one: one[0])
    got = [set() for _ in range(n_u)]
    made = [set() for _ in range(n_u)]
    sent = [[] for _ in range(n_u)]

    def arrive(node, key):
        if key in got[node]:
            return
        got[node].add(key)
        transfer(key, True).wait_recv()
        kind, ch, p, _, u, _ = key
        if kind == "XS":
            ga[2 * u + b, rows_of(p)] += xr_at(u, p)[...]
        elif kind[:2] == "RS":
            g_at(ch, u)[rows_of(p), :] += ring_at(key)[...]

    def act(node, key):
        for need in tasks[key][1]:
            arrive(node, need)
        kind, ch, p, par, u, _ = key
        if kind[:2] == "AG" and u == node and par == 0 and (ch, p) not in made[node]:
            made[node].add((ch, p))
            update(ch, p)
        sent[node].append(key)
        transfer(key, False).start()

    def chain_until(until):
        for node in range(n_u):
            due = [key for start, key in queue[node] if start < until]
            queue[node] = [one for one in queue[node] if one[0] >= until]
            if due:
                pl.when(z == node)(lambda node=node, due=due: [act(node, key) for key in due] and None)

    def chain_end():
        for node in range(n_u):
            def settle(node=node):
                for key in inbound[node]:
                    arrive(node, key)
                for key in sent[node]:
                    transfer(key, False).wait_send()
            pl.when(z == node)(settle)
        for ch in range(3):
            for p in range(2):
                own_copy(ch, p).wait()

    def vec_x():
        return remote(v0, vx, vs_s.at[0], vs_r.at[0], me.x)

    def vec_z(k):
        peer = (2 * lax.rem(z + k, n_u) + b, me.t)
        return remote(v1, vz.at[z], vs_s.at[k], vs_r.at[k], peer)

    def vec_t(k, peer):
        return remote(v1, vt.at[me.t], vs_s.at[n_u + k], vs_r.at[n_u + k], peer)

    trio = (me.core, me.y, diag)

    def vectors_one():
        vec_x().wait()
        v1[...] = v0[...] + vx[...]
        vz[z] = v1[...]
        for k in range(1, n_u):
            vec_z(k).start()

    def vectors_two():
        for k in range(1, n_u):
            vec_z(k).wait()
        total = vz[0]
        for u in range(1, n_u):
            total = total + vz[u]
        v1[...] = total
        vt[me.t] = total
        for k, peer in enumerate(trio):
            vec_t(k, peer).start()

    def vectors_three():
        for k, peer in enumerate(trio):
            vec_t(k, peer).wait()
        fetch("out", vt, vt_h)

    lanes = 128

    def hidden_bias(slot):
        parts = hidden // lanes
        return jnp.concatenate([bias_in[pl.ds(slot * parts + j, 1), :] for j in range(parts)], axis=1)

    twin = lax.rem(me.t + 2, 4)

    def first_norm_back():
        d_normed = full[...] + dtwo[...]
        unit, inv = normalize(dres[...])
        d_one = norm_back(d_normed, gains[0:1, :], unit, inv)
        dres[...] = d_one
        v0[...] = vec[...]
        v0[0:1, :] = row_sum(d_normed * unit)
        v0[3:4, :] = row_sum(d_one)
        v0[4:5, :] = row_sum(d_normed)
        low = d_one.astype(LOW)
        x[count:count + total, :] = low
        dctx[...] = dot(low, wal[3 * heads:, :], 1, 1).astype(LOW)

    def attend_back(q, k, v, dc, probs, pick_s):
        dqs, dks, dvs = [], [], []
        for h in range(n_heads):
            col = slice(h * HD, (h + 1) * HD)
            prob = probs(h)
            d_prob = dot(dc[:, col], v[:, col], 1, 1)
            dvs.append(dot(prob.astype(LOW), dc[:, col], 0, 0))
            ds = (prob * (d_prob - jnp.sum(prob * d_prob, axis=-1, keepdims=True))).astype(LOW)
            dqs.append(dot(ds, k[:, col], 1, 0) * scale)
            dks.append(dot(ds, q[:, col], 0, 0))
        dq = jnp.concatenate(dqs, axis=1)
        dv = jnp.concatenate(dvs, axis=1)
        spread = dot(pick_s, dq.astype(LOW), 0, 0).astype(LOW)
        return jnp.concatenate([spread, jnp.concatenate(dks, axis=1).astype(LOW), dv.astype(LOW)], axis=1), dq, dv

    def own_back(s):
        here = slice(s * rows, (s + 1) * rows)
        low, dq, dv = attend_back(
            qm[here, :], ko.at[at(s)], vo.at[at(s)], dctx[here, :], lambda h: pm[s * n_heads + h], pick[s]
        )
        dproj[at(s), 0:3 * heads] = low
        dproj[at(s), 3 * heads:] = jnp.zeros((length, heads), LOW)
        sums = jnp.concatenate([row_sum(dq), row_sum(dv)], axis=1)
        v0[2:3, 0:2 * heads] = sums if s == 0 else v0[2:3, 0:2 * heads] + sums

    def weight_grads(j):
        if j == 0:
            dproj[count:count + total, 0:3 * heads] = jnp.zeros((total, 3 * heads), LOW)
            dproj[count:count + total, 3 * heads:] = cm[...]
        col = slice(j * 256, (j + 1) * 256)
        ga[:, :, col] = dot(x[...], dproj[:, col], 0, 0).reshape(2 * n_u, shard, 256)

    def twin_rows():
        dctx[...] = dot(x[count:count + total, :], wpl[3 * heads:, :], 1, 1).astype(LOW)

    def pick_bias(row):
        out = jnp.zeros((1, heads), F32)
        for slot in range(4):
            out = jnp.where(twin == slot, biases[row:row + 1, slot * heads:(slot + 1) * heads], out)
        return out

    scale = 1.0 / math.sqrt(HD)
    position = lax.broadcasted_iota(jnp.int32, (1, length), 1)
    my_half = pl.ds(pl.multiple_of(me.c * half, 8), half)
    its_half = pl.ds(pl.multiple_of((1 - me.c) * half, 8), half)
    my_quarter = pl.ds(pl.multiple_of(me.p * quarter, 8), quarter)
    its_quarter = pl.ds(pl.multiple_of((1 - me.p) * quarter, 8), quarter)

    def at(s, start=0, size=None):
        return pl.ds(pl.multiple_of(s * length + start, 8), size or length)

    def key_bias(s):
        return jnp.where(position < lens[s], 0.0, -1000000000.0)

    def project(s):
        xs = x[at(s), :]
        qp[...] = ((dot(xs, wpl[0:heads, :], 1, 1) + pick_bias(0)) * scale).astype(LOW)
        kp[...] = dot(xs, wpl[heads:2 * heads, :], 1, 1).astype(LOW)
        vp[...] = (dot(xs, wpl[2 * heads:3 * heads, :], 1, 1) + pick_bias(1)).astype(LOW)

    def attend_one(s, h):
        col = slice(h * HD, (h + 1) * HD)
        e = dot(qp[:, col], kp[:, col], 1, 1) + key_bias(s)
        e = jnp.exp(e - jnp.max(e, axis=-1, keepdims=True))
        prob = (e / jnp.sum(e, axis=-1, keepdims=True)).astype(LOW)
        ctxp[:, col] = dot(prob, vp[:, col], 1, 0).astype(LOW)

    def mix_copy(s):
        return remote(sbuf.at[s], rbuf.at[s], sd_s.at[s], sd_r.at[s], me.core)

    def mix(s):
        for where, into in ((its_half, sbuf), (my_half, nrm)):
            base = at(s, where.start, half)
            into[s] = dot(ctx[base, :], wal[3 * heads:, :], 1, 0) + dot(ctxp[where, :], wpl[3 * heads:, :], 1, 0)
        mix_copy(s).start()

    def down_copy(s):
        return remote(dsc.at[s, its_quarter], rdn.at[s], sd_s.at[seqs + s], sd_r.at[seqs + s], me.y)

    def feed_start(s):
        mix_copy(s).wait()
        base = at(s, me.c * half, half)
        unit, _ = normalize(x[base, :].astype(F32) + (nrm[s] + rbuf[s]) + biases[2:3, :])
        nrm[s] = unit * gains[0:1, :] + biases[3:4, :]

    def feed(s, part):
        w_in, w_back, slot = ((wil, wbl, me.t), (pil, pbl, me.t + 1 - 2 * me.c))[part]
        low = nrm[s].astype(LOW)
        bias = hidden_bias(slot)
        total = dsc[s] if part else jnp.zeros((half, width), F32)
        for j in range(0, hidden, 256):
            col = slice(j, j + 256)
            pre = dot(low, w_in[:, col], 1, 0) + bias[:, col]
            act_low = pre * (0.5 * (1.0 + lax.erf(pre * (1.0 / math.sqrt(2.0)))))
            total = total + dot(act_low.astype(LOW), w_back[:, col], 1, 1)
        dsc[s] = total
        if part:
            down_copy(s).start()

    def out_rows(s, p):
        return at(s, me.c * half + p * quarter, quarter)

    def out_copy(s, k, p, peer):
        src = fin.at[s] if k < 2 else out_h.at[out_rows(s, p)]
        return remote(src, out_h.at[out_rows(s, me.p if k < 2 else p)], sd_s.at[(2 + k) * seqs + s], sd_r.at[(2 + k) * seqs + s], peer)

    def finish(s):
        down_copy(s).wait()
        res = nrm[s, my_quarter] + (dsc[s, my_quarter] + rdn[s]) + biases[4:5, :]
        unit, _ = normalize(res)
        fin[s] = (unit * gains[1:2, :] + biases[5:6, :]).astype(LOW).astype(F32)
        fetch("out", fin.at[s], out_h.at[out_rows(s, me.p)])
        out_copy(s, 0, me.p, me.y).start()
        out_copy(s, 1, me.p, me.core).start()

    def relay(s):
        out_copy(s, 0, me.p, me.y).wait()
        out_copy(s, 2, 1 - me.p, me.core).start()

    def relay_end(s):
        out_copy(s, 1, me.p, me.core).wait()
        out_copy(s, 2, 1 - me.p, me.core).wait()

    def back(s):
        here = slice(s * rows, (s + 1) * rows)
        q = dot(pick[s], qp[...], 1, 0).astype(LOW)
        dc = dctx[here, :]

        def probs(h):
            col = slice(h * HD, (h + 1) * HD)
            scores = dot(q[:, col], kp[:, col], 1, 1) + key_bias(s)
            e = jnp.exp(scores - jnp.max(scores, axis=-1, keepdims=True))
            return e / jnp.sum(e, axis=-1, keepdims=True)

        dpp[...] = attend_back(q, kp, vp, dc, probs, pick[s])[0]

    def entry_copy(s):
        return remote(sbuf.at[s], rig.at[s], sd_s.at[5 * seqs + s], sd_r.at[5 * seqs + s], me.core)

    def entry(s):
        for where, into in ((its_half, sbuf), (my_half, rbuf)):
            base = at(s, where.start, half)
            product = lambda a, w: dot(a, w[0:3 * heads, :], 1, 0)

            def add(low, high, s=s, into=into):
                into[s] = product(*low) + product(*high)

            own_part = lambda base=base: (dproj[base, 0:3 * heads], wal)
            twin_part = lambda where=where: (dpp[where, :], wpl)
            pl.when(me.p == 0)(lambda add=add, a=own_part, b=twin_part: add(a(), b()))
            pl.when(me.p == 1)(lambda add=add, a=own_part, b=twin_part: add(b(), a()))
        entry_copy(s).start()

    def grad_rows(s):
        return at(s, me.c * half, half)

    def grad_copy(s):
        return remote(rbuf.at[s], grad_h.at[grad_rows(s)], sd_s.at[6 * seqs + s], sd_r.at[6 * seqs + s], me.core)

    def entry_end(s):
        entry_copy(s).wait()
        d_one = dres[pl.ds(s * rows, rows), :]
        high = d_one.astype(LOW)
        rest = (d_one - high.astype(F32)).astype(LOW)
        some = pick[s, :, pl.ds(pl.multiple_of(me.c * half, lanes), half)]
        rbuf[s] = (rbuf[s] + rig[s]) + (dot(some, high, 0, 0) + dot(some, rest, 0, 0))
        fetch("out", rbuf.at[s], grad_h.at[grad_rows(s)])
        grad_copy(s).start()

    def turn_weights():
        for j in range(0, width, lanes):
            flip[...] = turned[j:j + lanes, :].T
            wrow_a[:, j:j + lanes] = flip[mine, :]

    def begin():
        for k in range(2):
            first_third(k).start()
        ready("gi", "gb")

    def own_start():
        ready("small", "one", "wal")
        first_norm_back()
        ready("att")

    def moments_in():
        ready("mi", "mb", "ma")
        turn_weights()

    def twin_start():
        ready("wpl", "ctx", "low")
        for k in range(2):
            first_third(k).wait()
            wpl[k * 3 * third:k * 3 * third + third, :] = wp[k].astype(LOW)
        twin_rows()

    work = [(0.0, begin), (4.4, own_start)]
    work += [(5.4 + s, lambda s=s: own_back(s)) for s in range(seqs)]
    work += [(8.4, lambda: ready("x"))] + [(8.5 + 0.7 * j, lambda j=j: weight_grads(j)) for j in range(width // 256)]
    work += [(10.7, lambda: vec_x().start()), (14.0, moments_in), (20.0, vectors_one), (28.0, vectors_two)]
    first_twin = 22.0
    for s in range(seqs):
        t = first_twin + 18.0 * s
        work += [(t, lambda s=s: (twin_start() if s == 0 else None, project(s)) and None)]
        work += [(t + 1.5 + h, lambda s=s, h=h: attend_one(s, h)) for h in range(n_heads)]
        work += [(t + 5.0, lambda s=s: mix(s)), (t + 5.5, lambda s=s: back(s)), (t + 7.5, lambda s=s: feed_start(s))]
        work += [(t + 8.0, lambda s=s: feed(s, 0)), (t + 9.5, lambda s=s: feed(s, 1)), (t + 11.0, lambda s=s: entry(s))]
        work += [(t + 24.0, lambda s=s: finish(s)), (t + 44.0, lambda s=s: relay(s)), (t + 18.0, lambda s=s: entry_end(s))]
    work += [(40.0, vectors_three)]
    for when, do in sorted(work, key=lambda one: one[0]):
        chain_until(when)
        do()
    for when in range(80, 120, 2):
        chain_until(float(when))
    chain_until(1e9)
    for s in range(seqs):
        relay_end(s)
        grad_copy(s).wait()
    for ref, out in ((mi, nmi_h), (mb, nmb_h), (mq, nmq_h), (mo, nmo_h)):
        fetch("out", ref, out)
    chain_end()
    ready("out")


def k2_call(lens, step, warmup, horizon, gains, biases, bias_in, k1, x, weights, moments):
    wqkv, wout, win, wback = weights
    count, width = x.shape
    seqs = lens.shape[0]
    heads, hidden = wout.shape[0], win.shape[1]
    length = count // seqs
    half, quarter = length // 2, length // 4
    shard = moments[1].shape[1]
    slots = width // shard
    n_u = slots // 2
    total = seqs * SPAN_ROWS
    units = seqs * (heads // HD)
    any_ = pl.BlockSpec(memory_space=pl.ANY)
    vm = pl.BlockSpec(memory_space=pltpu.VMEM)
    sm = pl.BlockSpec(memory_space=pltpu.SMEM)
    sds = lambda *shape: jax.ShapeDtypeStruct(shape, F32)
    V = lambda *shape: pltpu.VMEM(shape, F32)
    B = lambda *shape: pltpu.VMEM(shape, LOW)
    D = pltpu.SemaphoreType.DMA
    out_shape = (
        sds(count, width), sds(count, width), sds(slots, shard, hidden), sds(slots, shard, hidden), sds(slots, shard, width),
        sds(*moments[0].shape), sds(*moments[1].shape), sds(*moments[2].shape), sds(*moments[3].shape), sds(4, 16, width),
    )
    scratch = [
        V(*gains.shape), V(*biases.shape), V(*bias_in.shape), V(16, width), V(4, 16, width), V(2, heads // 2, width),
        B(count + total, width), V(slots, shard, width), V(n_u, shard, hidden), V(n_u, shard, hidden),
        B(count + total, width), B(count, heads), B(seqs, SPAN_ROWS, length), V(total, width),
        V(total, width), V(total, width), V(units, SPAN_ROWS, length), B(total, heads), B(count, heads), B(count, heads), B(total, heads), B(total, heads),
        B(width, width), B(width, width), B(width, hidden), B(width, hidden), B(width, hidden), B(width, hidden),
        V(shard, hidden), V(shard, hidden), V(shard, width),
        V(*moments[0].shape), V(*moments[1].shape), V(*moments[2].shape), V(*moments[3].shape), V(width, width), V(width, 128),
        B(length, heads), B(length, heads), B(length, heads), B(length, heads), B(length, 3 * heads),
        V(seqs, half, width), V(seqs, half, width), V(seqs, half, width), V(seqs, half, width),
        V(seqs, quarter, width), V(seqs, quarter, width), V(seqs, half, width),
        V(3, 2, n_u - 1, shard, width), V(n_u, shard, width), V(3, shard, width),
        V(16, width), V(16, width), V(16, width), V(n_u, 16, width),
        D((64,)), D((12 * n_u,)), D((12 * n_u,)), D((24 * n_u,)), D((24 * n_u,)), D((6 * n_u,)), D((6 * n_u,)),
        D((2 * n_u,)), D((2 * n_u,)), D((n_u + 3,)), D((n_u + 3,)), D((7 * seqs,)), D((7 * seqs,)), D((6,)), D((2, 2)),
    ]
    return pl.pallas_call(
        k2_kernel, out_shape=out_shape,
        in_specs=[sm] * 4 + [any_] * 31,
        out_specs=(any_,) * 10,
        scratch_shapes=scratch,
        compiler_params=pltpu.CompilerParams(collective_id=2, has_side_effects=True, vmem_limit_bytes=63 * 2**20),
    )(
        lens, step, warmup, horizon, gains, biases, bias_in, k1[-1], x, *k1[:-1], wqkv, wout, win, wback, *moments,
    )


def rates(step, warmup, horizon):
    clock = jnp.full((1, 128), step[0].astype(F32))
    warm = jnp.full((1, 128), warmup[0].astype(F32))
    far = jnp.full((1, 128), horizon[0].astype(F32))
    ratio = jnp.minimum(clock / warm, (far - clock) / (far - warm))[:, 0:1]
    return ratio, (1.0 - jnp.exp(clock * math.log(0.9)))[:, 0:1], (1.0 - jnp.exp(clock * math.log(0.999)))[:, 0:1]


def k3_kernel(step, warmup, horizon, *refs):
    n_big, n_small = 9, 7
    (out_h, grad_h, ci_h, cb_h, ca_h, *moms_h), refs = refs[:n_big], refs[n_big:]
    small_h, refs = refs[:n_small], refs[n_small:]
    (normed_o, grad_o, ci_o, cb_o, cq_o, co_o, *moms_o), refs = refs[:n_big + 1], refs[n_big + 1:]
    small_o, refs = refs[:6], refs[6:]
    (wide, low, turned, grad, ci, cb, ca, *moms), refs = refs[:n_big + 2], refs[n_big + 2:]
    (gains, biases, bias_in, mom_g, mom_b, mom_h, vt), refs = refs[:n_small], refs[n_small:]
    (ch_g, ch_b, ch_h, nm_g, nm_b, nm_h), (rsem, wsem) = refs[:6], refs[6:]
    chunks, size = wide.shape[:2]
    reads, copies = [], []

    def read(src, dst):
        copy = pltpu.make_async_copy(src, dst, rsem.at[len(reads)])
        copy.start()
        reads.append(copy)
        return copy

    def write(src, dst):
        copy = pltpu.make_async_copy(src, dst, wsem.at[len(copies)])
        copy.start()
        copies.append(copy)

    rows = [pl.ds(j * size, size) for j in range(chunks)]
    got = [read(out_h.at[row], wide.at[j]) for j, row in enumerate(rows)]
    got_ca = read(ca_h, ca)
    plain = [(read(src, buf), buf, dst) for src, buf, dst in zip((grad_h, ci_h, cb_h), (grad, ci, cb), (grad_o, ci_o, cb_o))]
    got_small = [read(src, dst) for src, dst in zip(small_h, (gains, biases, bias_in, mom_g, mom_b, mom_h, vt))]
    plain += [(read(src, buf), buf, dst) for src, buf, dst in zip(moms_h, moms, moms_o)]
    for j, row in enumerate(rows):
        got[j].wait()
        low[j] = wide[j].astype(LOW)
        write(low.at[j], normed_o.at[row])
    got_ca.wait()
    width = turned.shape[1]
    lanes = 128
    for j in range(0, width, lanes):
        turned[j:j + lanes, :] = ca[:, :, j:j + lanes].reshape(width, lanes).T
    split = cq_o.shape[0]
    write(turned.at[pl.ds(0, split)], cq_o)
    write(turned.at[pl.ds(split, width - split)], co_o)
    for copy, buf, dst in plain[:3]:
        copy.wait()
        write(buf, dst)
    for copy in got_small:
        copy.wait()
    put = (*rates(step, warmup, horizon), 0.0)
    heads = gains.shape[1] // 4
    hidden = vt.shape[2]
    common = vt[0]
    ch_g[...], nm_g[0], nm_g[1] = adam(gains[...], common[0:2], mom_g[0], mom_g[1], *put)
    query = jnp.concatenate([vt[k][2:3, 0:heads] for k in range(4)], axis=1)
    value = jnp.concatenate([vt[k][2:3, heads:2 * heads] for k in range(4)], axis=1)
    for row in range(6):
        grad_row = query if row == 0 else value if row == 1 else common[row + 1:row + 2]
        change, first, second = adam(biases[row:row + 1, :], grad_row, mom_b[row, 0:1], mom_b[row, 1:2], *put)
        ch_b[row:row + 1, :] = change
        nm_b[row, 0:1] = first
        nm_b[row, 1:2] = second
    parts = hidden // lanes
    for k in range(4):
        col = slice(k * hidden, (k + 1) * hidden)
        bias = jnp.concatenate([bias_in[k * parts + j:k * parts + j + 1, :] for j in range(parts)], axis=1)
        change, first, second = adam(bias, vt[k][8:9, :], mom_h[0:1, col], mom_h[1:2, col], *put)
        nm_h[0:1, col] = first
        nm_h[1:2, col] = second
        for j in range(parts):
            ch_h[k * parts + j:k * parts + j + 1, :] = change[:, j * lanes:(j + 1) * lanes]
    for src, dst in zip((ch_g, ch_b, ch_h, nm_g, nm_b, nm_h), small_o):
        write(src, dst)
    for copy, buf, dst in plain[3:]:
        copy.wait()
        write(buf, dst)
    for copy in copies:
        copy.wait()


def k3_call(step, warmup, horizon, gains, biases, bias_in, mom_g, mom_b, mom_h, vt, big, heads):
    any_ = pl.BlockSpec(memory_space=pl.ANY)
    sm = pl.BlockSpec(memory_space=pltpu.SMEM)
    of = lambda a: jax.ShapeDtypeStruct(a.shape, a.dtype)
    held = lambda a: pltpu.VMEM(a.shape, F32)
    count, width = big[0].shape
    chunks = 6
    small = (gains, biases, bias_in, mom_g, mom_b, mom_h)
    sds = lambda *shape: jax.ShapeDtypeStruct(shape, F32)
    out_shape = (
        jax.ShapeDtypeStruct((count, width), LOW), *map(of, big[1:4]), sds(3 * heads, width), sds(heads, width),
        *map(of, big[5:]), *map(of, small),
    )
    return pl.pallas_call(
        k3_kernel,
        out_shape=out_shape,
        in_specs=[sm] * 3 + [any_] * (len(big) + 7),
        out_specs=(any_,) * len(out_shape),
        scratch_shapes=[
            pltpu.VMEM((chunks, count // chunks, width), F32), pltpu.VMEM((chunks, count // chunks, width), LOW),
            pltpu.VMEM((width, width), F32), *map(held, big[1:]), *map(held, small), held(vt), *map(held, small),
            pltpu.SemaphoreType.DMA((32,)), pltpu.SemaphoreType.DMA((32,)),
        ],
        compiler_params=pltpu.CompilerParams(vmem_limit_bytes=62 * 2**20),
    )(step, warmup, horizon, *big, *small, vt)


def fast(tokens_in, cotangent, span_mask, lengths, step, warmup, total, w_qkv, w_out, w_in, w_back, gains, biases, bias_in,
         mom_qkv, mom_out, mom_in, mom_back, mom_gains, mom_biases, mom_bias_in):
    width = tokens_in.shape[1]
    heads, hidden = w_out.shape[1], w_in.shape[1]
    wqkv_t = jnp.transpose(w_qkv, (1, 2, 0)).reshape(3 * heads, width)
    wout_t = w_out.T
    bias_tiles = bias_in.reshape(-1, 128)
    k1 = k1_call(
        tokens_in, cotangent, span_mask.reshape(-1, 128), lengths, wqkv_t, wout_t, w_in, w_back, gains, biases, bias_tiles,
        width // mom_out.shape[1]
    )
    *big, vt = k2_call(
        lengths, step, warmup, total, gains, biases, bias_tiles, k1, tokens_in, (wqkv_t, wout_t, w_in, w_back),
        (jnp.transpose(mom_qkv, (0, 2, 1, 3)), mom_out, mom_in, mom_back)
    )
    (
        out, grad, ci, cb, cq, co, nmq, nmo, nmi, nmb, ch_g, ch_b, ch_h, nm_g, nm_b, nm_h
    ) = k3_call(
        step, warmup, total, gains, biases, bias_tiles, mom_gains, jnp.transpose(mom_biases, (1, 0, 2)), mom_bias_in, vt, big, heads
    )
    return (
        out, grad, jnp.transpose(cq.reshape(3, heads, width), (2, 0, 1)), co.T,
        ci.reshape(width, hidden), cb.reshape(width, hidden), ch_g, ch_b, ch_h.reshape(-1),
        jnp.transpose(nmq, (0, 2, 1, 3)), nmo, nmi, nmb, nm_g, jnp.transpose(nm_b, (1, 0, 2)), nm_h,
    )


def layer_norm(values, gain, shift):
    center = values - jnp.mean(values, axis=-1, keepdims=True)
    spread = jnp.mean(center * center, axis=-1, keepdims=True)
    return center * lax.rsqrt(spread + NORM_EPS) * gain + shift


def exact_gelu(values):
    return jax.nn.gelu(values, approximate=False)


def outer_sum(left, right):
    return jnp.einsum("ta,tb->ab", left, right, preferred_element_type=jnp.float32)


def adam_step(weight, grad, moments, ratio, corr_one, corr_two, decay):
    first = BETA_ONE * moments[0] + (1.0 - BETA_ONE) * grad
    second = BETA_TWO * moments[1] + (1.0 - BETA_TWO) * grad * grad
    update = first / corr_one / (jnp.sqrt(second / corr_two) + ADAM_EPS) + decay * weight
    return (-ratio * update, jnp.stack([first, second]))


def on_device(
    tokens_in,
    cotangent,
    span_mask,
    lengths,
    step,
    warmup,
    total,
    w_qkv,
    w_out,
    w_in,
    w_back,
    gains,
    biases,
    bias_in,
    mom_qkv,
    mom_out,
    mom_in,
    mom_back,
    mom_gains,
    mom_biases,
    mom_bias_in,
):
    row_count, model_width = tokens_in.shape
    if mom_out.shape[1] % 8 == 0:
        return fast(
            tokens_in, cotangent, span_mask, lengths, step, warmup, total, w_qkv, w_out, w_in, w_back, gains, biases,
            bias_in, mom_qkv, mom_out, mom_in, mom_back, mom_gains, mom_biases, mom_bias_in
        )
    seq_count = lengths.shape[0]
    seq_length = row_count // seq_count
    head_cols = w_qkv.shape[2]
    hidden_cols = w_in.shape[1]
    head_size = HD
    local_heads = head_cols // head_size
    query_scale = 1.0 / math.sqrt(head_size)
    tensor_slot = lax.axis_index("tensor")
    bias_query = lax.dynamic_slice_in_dim(biases[0], tensor_slot * head_cols, head_cols)
    bias_value = lax.dynamic_slice_in_dim(biases[1], tensor_slot * head_cols, head_cols)
    bias_hidden = lax.dynamic_slice_in_dim(bias_in, tensor_slot * hidden_cols, hidden_cols)
    qkv_low = w_qkv.astype(jnp.bfloat16).reshape(model_width, 3 * head_cols)
    out_low = w_out.astype(jnp.bfloat16)
    in_low = w_in.astype(jnp.bfloat16)
    down_low = w_back.astype(jnp.bfloat16)
    projected = jnp.dot(tokens_in, qkv_low, preferred_element_type=jnp.float32).reshape(
        row_count, 3, head_cols
    )
    attn_shape = (seq_count, seq_length, local_heads, head_size)
    queries = (
        ((projected[:, 0] + bias_query) * query_scale).astype(jnp.bfloat16).reshape(attn_shape)
    )
    keys = projected[:, 1].astype(jnp.bfloat16).reshape(attn_shape)
    values = (projected[:, 2] + bias_value).astype(jnp.bfloat16).reshape(attn_shape)
    positions = jnp.arange(seq_length, dtype=jnp.int32)
    inside = positions[None, :] < lengths[:, None]
    key_bias = jnp.where(inside, 0.0, -1000000000.0).astype(jnp.float32)

    def score_block():
        raw = jnp.einsum("sqhd,skhd->shqk", queries, keys, preferred_element_type=jnp.float32)
        return raw + key_bias[:, None, None, :]

    scores = score_block()
    peak = jnp.max(scores, axis=-1, keepdims=True)
    log_total = peak + jnp.log(jnp.sum(jnp.exp(scores - peak), axis=-1, keepdims=True))
    probs_low = jnp.exp(scores - log_total).astype(jnp.bfloat16)
    context_low = (
        jnp.einsum("shqk,skhd->sqhd", probs_low, values, preferred_element_type=jnp.float32)
        .reshape(row_count, head_cols)
        .astype(jnp.bfloat16)
    )
    attn_part = jnp.einsum("tc,dc->td", context_low, out_low, preferred_element_type=jnp.float32)
    attn_sum = lax.psum(attn_part, "tensor")
    residual_one = tokens_in.astype(jnp.float32) + attn_sum + biases[2]
    normed = layer_norm(residual_one, gains[0], biases[3])
    normed_low = normed.astype(jnp.bfloat16)
    pre_act = jnp.dot(normed_low, in_low, preferred_element_type=jnp.float32) + bias_hidden
    act_low = exact_gelu(pre_act).astype(jnp.bfloat16)
    down_part = jnp.einsum("tf,df->td", act_low, down_low, preferred_element_type=jnp.float32)
    down_sum = lax.psum(down_part, "tensor")
    residual_two = normed + down_sum + biases[4]
    live = (inside.astype(jnp.int32) * span_mask.reshape(seq_count, seq_length)) > 0
    upto = (positions[:, None] <= positions[None, :]).astype(jnp.float32)
    rank = jnp.dot(live.astype(jnp.float32), upto).astype(jnp.int32) - 1
    slots = jnp.arange(SPAN_ROWS, dtype=jnp.int32)
    pick = (live[:, None, :] & (rank[:, None, :] == slots[None, :, None])).astype(jnp.float32)
    pick_low = pick.astype(jnp.bfloat16)

    def rows_of(values):
        width = values.shape[-1]
        return jnp.einsum(
            "srt,std->srd",
            pick,
            values.reshape(seq_count, seq_length, width),
            precision=lax.Precision.HIGHEST,
        ).reshape(seq_count * SPAN_ROWS, width)

    def low_rows_of(values):
        width = values.shape[-1]
        return jnp.einsum(
            "srt,std->srd",
            pick_low,
            values.reshape(seq_count, seq_length, width),
            preferred_element_type=jnp.bfloat16,
        ).reshape(seq_count * SPAN_ROWS, width)

    result = layer_norm(residual_two, gains[1], biases[5])
    normed_out = result.astype(jnp.bfloat16)
    residual_one_rows = rows_of(residual_one)
    residual_two_rows = rows_of(residual_two)
    grad_result = low_rows_of(cotangent).astype(jnp.float32)
    _, norm_two_back = jax.vjp(layer_norm, residual_two_rows, gains[1], biases[5])
    d_res_two, d_gain_two, d_shift_two = norm_two_back(grad_result)
    d_res_two_low = d_res_two.astype(jnp.bfloat16)
    normed_low_rows = low_rows_of(normed_low)
    pre_rows = jnp.dot(normed_low_rows, in_low, preferred_element_type=jnp.float32) + bias_hidden
    act_rows, gelu_back = jax.vjp(exact_gelu, pre_rows)
    grad_back = outer_sum(d_res_two_low, act_rows.astype(jnp.bfloat16))
    d_act = jnp.dot(d_res_two_low, down_low, preferred_element_type=jnp.float32)
    d_pre = gelu_back(d_act)[0]
    d_pre_low = d_pre.astype(jnp.bfloat16)
    grad_in = outer_sum(normed_low_rows, d_pre_low)
    d_normed_part = jnp.einsum("tf,df->td", d_pre_low, in_low, preferred_element_type=jnp.float32)
    d_normed = lax.psum(d_normed_part, "tensor") + d_res_two
    _, norm_one_back = jax.vjp(layer_norm, residual_one_rows, gains[0], biases[3])
    d_res_one, d_gain_one, d_shift_one = norm_one_back(d_normed)
    d_res_one_low = d_res_one.astype(jnp.bfloat16)
    grad_out_proj = outer_sum(d_res_one_low, low_rows_of(context_low))
    row_shape = (seq_count, SPAN_ROWS, local_heads, head_size)
    d_context = (
        jnp.dot(d_res_one_low, out_low, preferred_element_type=jnp.float32)
        .astype(jnp.bfloat16)
        .reshape(row_shape)
    )
    query_rows = low_rows_of(queries.reshape(row_count, head_cols)).reshape(row_shape)
    raw = jnp.einsum("sqhd,skhd->shqk", query_rows, keys, preferred_element_type=jnp.float32)
    probs = jax.nn.softmax(raw + key_bias[:, None, None, :], axis=-1)
    probs_again = probs.astype(jnp.bfloat16)
    d_probs = jnp.einsum("sqhd,skhd->shqk", d_context, values, preferred_element_type=jnp.float32)
    d_values = jnp.einsum(
        "shqk,sqhd->skhd", probs_again, d_context, preferred_element_type=jnp.float32
    ).reshape(row_count, head_cols)
    d_scores = (probs * (d_probs - jnp.sum(probs * d_probs, axis=-1, keepdims=True))).astype(
        jnp.bfloat16
    )
    d_queries = (
        jnp.einsum("shqk,skhd->sqhd", d_scores, keys, preferred_element_type=jnp.float32).reshape(
            seq_count * SPAN_ROWS, head_cols
        )
        * query_scale
    )
    d_keys = jnp.einsum(
        "shqk,sqhd->skhd", d_scores, query_rows, preferred_element_type=jnp.float32
    ).reshape(row_count, head_cols)

    def spread(row_values):
        width = row_values.shape[-1]
        return jnp.einsum(
            "srt,srd->std",
            pick,
            row_values.reshape(seq_count, SPAN_ROWS, width),
            precision=lax.Precision.HIGHEST,
        ).reshape(row_count, width)

    d_proj_low = (
        jnp.stack([spread(d_queries), d_keys, d_values], axis=1)
        .astype(jnp.bfloat16)
        .reshape(row_count, 3 * head_cols)
    )
    grad_qkv = outer_sum(tokens_in, d_proj_low).reshape(model_width, 3, head_cols)
    d_entry_part = jnp.einsum("tc,dc->td", d_proj_low, qkv_low, preferred_element_type=jnp.float32)
    input_grad = lax.psum(d_entry_part, "tensor") + spread(d_res_one)
    first_rank = (tensor_slot == 0).astype(jnp.float32)
    width_zero = jnp.zeros((model_width,), jnp.float32)

    def place_heads(partial_sum):
        return lax.dynamic_update_slice_in_dim(width_zero, partial_sum, tensor_slot * head_cols, 0)

    grad_gains = jnp.stack([d_gain_one, d_gain_two]) * first_rank
    grad_biases = jnp.stack(
        [
            place_heads(jnp.sum(d_queries, axis=0)),
            place_heads(jnp.sum(d_values, axis=0)),
            jnp.sum(d_res_one, axis=0) * first_rank,
            d_shift_one * first_rank,
            jnp.sum(d_res_two, axis=0) * first_rank,
            d_shift_two * first_rank,
        ]
    )
    grad_bias_in = lax.dynamic_update_slice_in_dim(
        jnp.zeros(bias_in.shape, jnp.float32), jnp.sum(d_pre, axis=0), tensor_slot * hidden_cols, 0
    )
    grad_gains, grad_biases, grad_bias_in = lax.psum(
        (grad_gains, grad_biases, grad_bias_in), ("dp", "tensor")
    )
    data_slot = lax.axis_index("dp")
    shard_rows = model_width // lax.axis_size("dp")
    owned = tuple(
        lax.psum_scatter(part, "dp", scatter_dimension=0, tiled=True)
        for part in (grad_qkv, grad_out_proj, grad_in, grad_back)
    )
    clock = step[0].astype(jnp.float32)
    warm = warmup[0].astype(jnp.float32)
    horizon = total[0].astype(jnp.float32)
    ratio = jnp.minimum(clock / warm, (horizon - clock) / (horizon - warm))
    corr_one = 1.0 - jnp.power(BETA_ONE, clock)
    corr_two = 1.0 - jnp.power(BETA_TWO, clock)
    change_rows = []
    fresh_moments = []
    for weight, grad_rows, moment in zip(
        (w_qkv, w_out, w_in, w_back), owned, (mom_qkv, mom_out, mom_in, mom_back)
    ):
        weight_rows = lax.dynamic_slice_in_dim(weight, data_slot * shard_rows, shard_rows, 0)
        row_change, new_moment = adam_step(
            weight_rows, grad_rows, moment, ratio, corr_one, corr_two, WEIGHT_DECAY
        )
        change_rows.append(row_change)
        fresh_moments.append(new_moment)
    change_qkv, change_out_proj, change_in_proj, change_back_proj = (
        lax.all_gather(change_rows[0], "dp", axis=0, tiled=True),
        lax.all_gather(change_rows[1], "dp", axis=0, tiled=True),
        lax.all_gather(change_rows[2], "dp", axis=0, tiled=True),
        lax.all_gather(change_rows[3], "dp", axis=0, tiled=True),
    )
    change_gains, new_mom_gains = adam_step(
        gains, grad_gains, mom_gains, ratio, corr_one, corr_two, 0.0
    )
    change_biases, new_mom_biases = adam_step(
        biases, grad_biases, mom_biases, ratio, corr_one, corr_two, 0.0
    )
    change_bias_in, new_mom_bias_in = adam_step(
        bias_in, grad_bias_in, mom_bias_in, ratio, corr_one, corr_two, 0.0
    )
    return (
        normed_out,
        input_grad,
        change_qkv,
        change_out_proj,
        change_in_proj,
        change_back_proj,
        change_gains,
        change_biases,
        change_bias_in,
        fresh_moments[0],
        fresh_moments[1],
        fresh_moments[2],
        fresh_moments[3],
        new_mom_gains,
        new_mom_biases,
        new_mom_bias_in,
    )


def solution(mesh):
    in_specs = (
        P("dp", None),
        P("dp", None),
        P("dp"),
        P("dp"),
        P(),
        P(),
        P(),
        P(None, None, "tensor"),
        P(None, "tensor"),
        P(None, "tensor"),
        P(None, "tensor"),
        P(),
        P(),
        P(),
        P(None, "dp", None, "tensor"),
        P(None, "dp", "tensor"),
        P(None, "dp", "tensor"),
        P(None, "dp", "tensor"),
        P(),
        P(),
        P(),
    )
    out_specs = (
        P("dp", None),
        P("dp", None),
        P(None, None, "tensor"),
        P(None, "tensor"),
        P(None, "tensor"),
        P(None, "tensor"),
        P(),
        P(),
        P(),
        P(None, "dp", None, "tensor"),
        P(None, "dp", "tensor"),
        P(None, "dp", "tensor"),
        P(None, "dp", "tensor"),
        P(),
        P(),
        P(),
    )
    return jax.shard_map(
        on_device, mesh=mesh, in_specs=in_specs, out_specs=out_specs, check_vma=False
    )
```

```python
import math

import jax
import jax.numpy as jnp
from jax import lax
from jax.experimental import pallas as pl
from jax.experimental.pallas import tpu as pltpu
from jax.sharding import PartitionSpec as P

HD = 64
SPAN_ROWS = 80
NORM_EPS = 1e-12
MESH = pl.DeviceIdType.MESH
F32 = jnp.float32
LOW = jnp.bfloat16


def dot(left, right, left_dim, right_dim):
    return lax.dot_general(
        left, right, (((left_dim,), (right_dim,)), ((), ())), preferred_element_type=F32
    )


def normalize(rows):
    center = rows - jnp.mean(rows, axis=-1, keepdims=True)
    scale = lax.rsqrt(jnp.mean(center * center, axis=-1, keepdims=True) + NORM_EPS)
    return center * scale, scale


def norm_back(grad, gain, unit, scale):
    weighted = grad * gain
    return scale * (
        weighted
        - jnp.mean(weighted, axis=-1, keepdims=True)
        - unit * jnp.mean(weighted * unit, axis=-1, keepdims=True)
    )


def row_sum(rows):
    return jnp.sum(rows, axis=0, keepdims=True)


class Peers:
    def __init__(self):
        self.d = lax.axis_index("dp")
        self.t = lax.axis_index("tensor")
        self.b = lax.rem(self.d, 2)
        self.c = lax.rem(self.t, 2)
        self.p = lax.div(self.t, 2)
        self.u = lax.div(self.d, 2)
        self.core = (self.d, self.t + 1 - 2 * self.c)
        self.y = (self.d, lax.rem(self.t + 2, 4))
        self.x = (self.d + 1 - 2 * self.b, self.t)


def send(src, dst, sems, k, peer):
    copy = pltpu.make_async_remote_copy(
        src_ref=src, dst_ref=dst, send_sem=sems.at[0, k], recv_sem=sems.at[1, k],
        device_id=peer, device_id_type=MESH,
    )
    copy.start()
    return copy


def local(src, dst, sem):
    copy = pltpu.make_async_copy(src, dst, sem)
    copy.start()
    return copy


def greet(peers):
    barrier = pltpu.get_barrier_semaphore()
    for peer in peers:
        pl.semaphore_signal(barrier, inc=1, device_id=peer, device_id_type=MESH)
    pl.semaphore_wait(barrier, len(peers))


def gelu_parts(pre):
    cdf = 0.5 * (1.0 + lax.erf(pre * (1.0 / math.sqrt(2.0))))
    pdf = jnp.exp(-0.5 * pre * pre) * (1.0 / math.sqrt(2.0 * math.pi))
    return pre * cdf, cdf + pre * pdf


def k1_kernel(
    lens, mask_h, gains_h, biases_h, bias_in_h, x_h, cot_h, wqkv_h, wout_h, win_h, wback_h,
    gi_h, gb_h, full_h, res_h, dres_h, pick_h, pm_h, qm_h, k_h, v_h, cm_h, ctx_h, wal_h, wpl_h, wil_h, wbl_h, pil_h, pbl_h, vec_h,
    mask, gains, biases, bias_in, vec, x, cot, wqkv, wout, win, wback, wp_qkv, wp_out, pwin, pwback, q_o, k_o, v_o, ctx_o, pick_o, wal, wpl, wil, wbl, pil, pbl, gin, gback,
    pm, xm, cotm, qm, ctxm, cml, ctxp, ap, apc, normed, nlow, act, gp, part, rc1, h1, ry1,
    part2, rc2, h2, ry2, full2, full, dres2, d2w, d2x, nxw, nxx, dplow,
    lsem, rsem, ssem,
):
    seqs, rows = 3, SPAN_ROWS
    count = x_h.shape[0]
    length = count // seqs
    total = seqs * rows
    half = total // 2
    heads = ctx_o.shape[1]
    n_heads = heads // HD
    width = x_h.shape[1]
    me = Peers()

    def seq(s):
        return pl.ds(s * length, length)

    small = [
        local(src, dst, ssem.at[k])
        for k, (src, dst) in enumerate(((mask_h, mask), (gains_h, gains), (biases_h, biases), (bias_in_h, bias_in)))
    ]
    loads = [
        local(wqkv_h, wqkv, lsem.at[0]),
        local(wout_h, wout, lsem.at[1]),
    ] + [local(x_h.at[seq(s)], x.at[seq(s)], lsem.at[2 + s]) for s in range(seqs)]
    stores = []

    def keep(src, dst):
        stores.append(local(src, dst, lsem.at[8 + len(stores)]))

    slots = gin.shape[0]
    wo_base = 47 + 2 * slots
    shard = gin.shape[1]
    n_u = slots // 2
    z = me.u
    greet([me.core, me.y, me.x] + [(2 * lax.rem(z + k, n_u) + me.b, me.t) for k in range(1, n_u)])

    out_rows = heads // 2 // seqs

    def out_part(k):
        return pl.ds(pl.multiple_of(me.b * (heads // 2) + k * out_rows, 8), out_rows)

    wo_y = [send(wout_h.at[out_part(k)], wp_out.at[out_part(k)], rsem, wo_base + k, me.y) for k in range(seqs)]
    for load in small:
        load.wait()
    loads[0].wait()
    wal[0:3 * heads, :] = wqkv[...].astype(LOW)
    loads[1].wait()
    wal[3 * heads:, :] = wout[...].astype(LOW)
    loads += [
        local(win_h, win, lsem.at[2 + seqs]),
        local(wback_h, wback, lsem.at[3 + seqs]),
        local(cot_h, cot, lsem.at[4 + seqs]),
    ]
    keep(wal, wal_h)

    def pick_bias(row, k=heads):
        out = jnp.zeros((1, k), F32)
        for slot in range(4):
            piece = biases[row:row + 1, slot * k:(slot + 1) * k]
            out = jnp.where(me.t == slot, piece, out)
        return out

    bias_q, bias_v = pick_bias(0), pick_bias(1)
    hidden = win.shape[1]
    lanes = 128
    bias_h = jnp.concatenate(
        [bias_in[pl.ds(me.t * (hidden // lanes) + j, 1), :] for j in range(hidden // lanes)], axis=1
    )
    upto = (
        lax.broadcasted_iota(jnp.int32, (length, length), 0)
        <= lax.broadcasted_iota(jnp.int32, (length, length), 1)
    ).astype(F32).astype(LOW)
    position = lax.broadcasted_iota(jnp.int32, (1, length), 1)
    slot_of = lax.broadcasted_iota(jnp.int32, (rows, length), 0).astype(F32)
    scale = 1.0 / math.sqrt(HD)
    def project(s):
        loads[2 + s].wait()
        at = seq(s)
        xs = x[at, :]
        q = ((dot(xs, wal[0:heads, :], 1, 1) + bias_q) * scale).astype(LOW)
        k = dot(xs, wal[heads:2 * heads, :], 1, 1).astype(LOW)
        v = (dot(xs, wal[2 * heads:3 * heads, :], 1, 1) + bias_v).astype(LOW)
        q_o[at, :] = q
        k_o[at, :] = k
        v_o[at, :] = v
        parts = length // lanes
        marks = jnp.concatenate([mask[pl.ds(s * parts + j, 1), :] for j in range(parts)], axis=1)
        inside = position < lens[s]
        live = jnp.where(inside, marks, 0).astype(F32)
        rank = dot(jnp.broadcast_to(live, (8, length)).astype(LOW), upto, 1, 0)[0:1] - 1.0
        pick = jnp.where((rank == slot_of) & (live > 0.0), 1.0, 0.0).astype(LOW)
        pick_o[s] = pick
        here = pl.ds(s * rows, rows)
        xm[here, :] = dot(pick, xs, 1, 0)
        qrow = dot(pick, q, 1, 0).astype(LOW)
        qm[here, :] = qrow
        key_bias = jnp.where(inside, 0.0, -1000000000.0)
        pieces = []
        for h in range(n_heads):
            col = slice(h * HD, (h + 1) * HD)
            scores = dot(qrow[:, col], k[:, col], 1, 1) + key_bias
            e = jnp.exp(scores - jnp.max(scores, axis=-1, keepdims=True))
            prob = e / jnp.sum(e, axis=-1, keepdims=True)
            pm[s * n_heads + h] = prob
            pieces.append(dot(prob.astype(LOW), v[:, col], 1, 0))
        low = jnp.concatenate(pieces, axis=1).astype(LOW)
        cml[here, :] = low
        ctxm[here, :] = low.astype(F32)
        return send(ctxm.at[here], ctxp.at[here], rsem, 24 + s, me.y)

    ctx_y, wo_x = [], []
    for s in range(seqs):
        ctx_y.append(project(s))
        wo_y[s].wait()
        wo_x.append(send(wp_out.at[out_part(s)], wp_out.at[out_part(s)], rsem, wo_base + seqs + s, me.x))
    third = heads // 2

    share = 2 * third // n_u

    def share_of(b, u):
        return pl.ds(pl.multiple_of(b * (3 * third) + third + u * share, 8), share)

    def chain_copy(way, s, b, u):
        place = wp_qkv.at[share_of(b, u)]
        k = 29 + (way * (n_u - 1) + s) * 2 + b
        peer = (me.d + 2, me.t) if way == 0 else (me.d - 2, me.t)
        return pltpu.make_async_remote_copy(
            src_ref=place, dst_ref=place, send_sem=rsem.at[0, k], recv_sem=rsem.at[1, k],
            device_id=peer, device_id_type=MESH,
        )

    def chain_cases(s):
        return [
            (way, b, z - s if way == 0 else z + s, (z >= s) if way == 0 else (z + s <= n_u - 1), (z < n_u - 1) if way == 0 else (z > 0))
            for way in range(2) for b in range(2)
        ]

    def chain_step(s):
        for way, b, u, here, edge in chain_cases(s):
            if s > 0:
                pl.when(here)(lambda way=way, b=b, u=u: chain_copy(way, s - 1, b, u).wait_recv())
            if s < n_u - 1:
                pl.when(here & edge)(lambda way=way, b=b, u=u: chain_copy(way, s, b, u).start())

    def chain_sent():
        for s in range(n_u - 1):
            for way, b, u, here, edge in chain_cases(s):
                pl.when(here & edge)(lambda way=way, b=b, u=u, s=s: chain_copy(way, s, b, u).wait_send())

    def attend_all(s):
        at = slice(s * length, (s + 1) * length)
        key_bias = jnp.where(position < lens[s], 0.0, -1000000000.0)
        pieces = []
        for h in range(n_heads):
            col = slice(h * HD, (h + 1) * HD)
            scores = dot(q_o[at, col], k_o[at, col], 1, 1) + key_bias
            e = jnp.exp(scores - jnp.max(scores, axis=-1, keepdims=True))
            prob = (e / jnp.sum(e, axis=-1, keepdims=True)).astype(LOW)
            pieces.append(dot(prob, v_o[at, col], 1, 0))
        ctx_o[at, :] = jnp.concatenate(pieces, axis=1).astype(LOW)

    mine_share = share_of(me.b, z)
    wz_y = send(wqkv.at[mine_share], wp_qkv.at[mine_share], rsem, 27, me.y)
    for ref, out in ((pm, pm_h), (qm, qm_h), (k_o, k_h), (v_o, v_h), (cml, cm_h), (pick_o, pick_h)):
        keep(ref, out)
    for load in loads[2 + seqs:4 + seqs]:
        load.wait()
    wil[...] = win[...].astype(LOW)
    wbl[...] = wback[...].astype(LOW)
    keep(wil, wil_h)
    keep(wbl, wbl_h)
    loads[4 + seqs].wait()
    for s in range(seqs):
        cotm[s * rows:(s + 1) * rows, :] = dot(pick_o[s], cot[s * length:(s + 1) * length, :], 1, 0)
    for copy in wo_x:
        copy.wait()
    for copy in ctx_y:
        copy.wait()
    woq = wp_out[...].astype(LOW)

    def mix(first, second):
        ap[...] = dot(*first, 1, 0) + dot(*second, 1, 0)

    own_part = lambda: (cml[...], wal[3 * heads:, :])
    twin_part = lambda: (ctxp[...].astype(LOW), woq)
    pl.when(me.p == 0)(lambda: mix(own_part(), twin_part()))
    pl.when(me.p == 1)(lambda: mix(twin_part(), own_part()))
    ap_c = send(ap, apc, rsem, 3, me.core)
    wz_y.wait()
    wz_x = send(wp_qkv.at[mine_share], wp_qkv.at[mine_share], rsem, 28, me.x)
    ap_c.wait()
    xm[...] = xm[...] + (ap[...] + apc[...]) + biases[2:3, :]
    keep(xm, res_h)
    unit, inv = normalize(xm[...])
    normed[...] = unit * gains[0:1, :] + biases[3:4, :]
    nlow[...] = normed[...].astype(LOW)
    nxw[...] = nlow[...].astype(F32)
    mine = pl.ds(pl.multiple_of(me.c * half, 8), half)
    other = pl.ds(pl.multiple_of((1 - me.c) * half, 8), half)
    nx_x = send(nxw.at[mine], nxx.at[mine], rsem, 5, me.x)
    for j in range(0, hidden, 256):
        col = slice(j, j + 256)
        a, g = gelu_parts(dot(nlow[...], wil[:, col], 1, 0) + bias_h[:, col])
        act[:, col] = a.astype(LOW)
        gp[:, col] = g
    part[...] = dot(act[...], wbl[...], 1, 1)

    cuts = tuple((start, half // 3) for start in range(0, half, half // 3))

    def all_reduce(src, rc, hs, ry, dst, base, fill, late=None):
        pieces = []
        for k, (start, size) in enumerate(cuts):
            mine_k = pl.ds(pl.multiple_of(me.c * half + start, 8), size)
            other_k = pl.ds(pl.multiple_of((1 - me.c) * half + start, 8), size)
            pieces.append((k, pl.ds(start, size), mine_k, other_k))
        first = [send(src.at[other_k], rc.at[row], rsem, base + k, me.core) for k, row, _, other_k in pieces]
        second, third = [], []
        for k, row, mine_k, _ in pieces:
            first[k].wait()
            hs[row, :] = src[mine_k, :] + rc[row, :]
            second.append(send(hs.at[row], ry.at[row], rsem, base + len(cuts) + k, me.y))
        fill()
        for k, row, mine_k, _ in pieces:
            second[k].wait()
            dst[mine_k, :] = hs[row, :] + ry[row, :]
            third.append(send(dst.at[mine_k], dst.at[mine_k], rsem, base + 2 * len(cuts) + k, me.core))
        if late:
            late()
        for copy in third:
            copy.wait()

    relay = []

    def fill_one():
        wide.append(send(win, pwin, rsem, 22, me.core))
        wz_x.wait()
        chain_step(0)
        attend_all(0)
        attend_all(1)
        nx_x.wait()
        relay.append(send(nxx.at[mine], nxx.at[mine], rsem, 6, me.core))
        chain_step(1)

    wide = []
    all_reduce(part, rc1, h1, ry1, full, 29 + 2 * slots, fill_one)
    relay[0].wait()
    unit, inv = normalize(normed[...] + full[...] + biases[4:5, :])
    grad = cotm[...]
    d_two = norm_back(grad, gains[1:2, :], unit, inv)
    dres2[...] = d_two
    vec[...] = jnp.zeros(vec.shape, F32)
    vec[1:2, :] = row_sum(grad * unit)
    vec[5:6, :] = row_sum(d_two)
    vec[6:7, :] = row_sum(grad)
    d2w[...] = d_two.astype(LOW).astype(F32)
    rows_k = [pl.ds(pl.multiple_of(me.c * half + start, 8), size) for start, size in cuts]
    d2_base = wo_base + 2 * seqs
    d2_x = [send(d2w.at[row], d2x.at[row], rsem, d2_base + k, me.x) for k, row in enumerate(rows_k)]
    keep(dres2, dres_h)
    d2low = d2w[...].astype(LOW)
    for j in range(0, hidden, 256):
        col = slice(j, j + 256)
        d_pre = dot(d2low, wbl[:, col], 1, 0) * gp[:, col]
        vec[8:9, col] = row_sum(d_pre)
        dplow[:, col] = d_pre.astype(LOW)
    part2[...] = dot(dplow[...], wil[...], 1, 1)

    def cut(rows):
        return rows.reshape(slots, shard, rows.shape[1])

    def fill_two():
        wide.append(send(wback, pwback, rsem, 23, me.core))
        attend_all(2)
        chain_step(2)
        keep(ctx_o, ctx_h)
        for j in range(0, hidden, 256):
            col = slice(j, j + 256)
            gin[:, :, col] = cut(dot(nlow[...], dplow[:, col], 0, 0))
            gback[:, :, col] = cut(dot(d2low, act[:, col], 0, 0))
        wide[0].wait()
        pil[...] = pwin[...].astype(LOW)
        keep(pil, pil_h)
        for k, row in enumerate(rows_k):
            d2_x[k].wait()
            relay.append(send(d2x.at[row], d2x.at[row], rsem, d2_base + len(cuts) + k, me.core))

    def other_x():
        for copy in relay[1:]:
            copy.wait()
        nlx = nxx[...].astype(LOW)
        dlx = d2x[...].astype(LOW)
        for j in range(0, hidden, 256):
            col = slice(j, j + 256)
            a, g = gelu_parts(dot(nlx, wil[:, col], 1, 0) + bias_h[:, col])
            d_pre = (dot(dlx, wbl[:, col], 1, 0) * g).astype(LOW)
            gin[:, :, col] += cut(dot(nlx, d_pre, 0, 0))
            gback[:, :, col] += cut(dot(dlx, a.astype(LOW), 0, 0))
        for u in range(slots // 2):
            keep(gin.at[2 * u + me.b], gi_h.at[u])
            keep(gback.at[2 * u + me.b], gb_h.at[u])

    all_reduce(part2, rc2, h2, ry2, full2, 38 + 2 * slots, fill_two, other_x)
    keep(full2, full_h)
    keep(vec, vec_h)
    for step in range(3, n_u):
        chain_step(step)
    for b in range(2):
        start = b * 3 * third
        wpl[start:start + third, :] = jnp.zeros((third, width), LOW)
        rest = slice(start + third, start + 3 * third)
        wpl[rest, :] = wp_qkv[rest, :].astype(LOW)
    wpl[3 * heads:, :] = woq
    keep(wpl, wpl_h)
    wide[1].wait()
    pbl[...] = pwback[...].astype(LOW)
    keep(pbl, pbl_h)
    chain_sent()
    for copy in stores:
        copy.wait()


def k1_call(x, cot, mask, lens, wqkv, wout, win, wback, gains, biases, bias_in, slots):
    count, width = x.shape
    seqs = lens.shape[0]
    heads = wout.shape[0]
    hidden = win.shape[1]
    length = count // seqs
    total = seqs * SPAN_ROWS
    half = total // 2
    units = seqs * (heads // HD)
    any_ = pl.BlockSpec(memory_space=pl.ANY)
    sm = pl.BlockSpec(memory_space=pltpu.SMEM)
    sds = jax.ShapeDtypeStruct
    V = pltpu.VMEM
    wide = lambda r, t=F32: V((r, width), t)
    block = (slots // 2, width // slots, hidden)
    square = sds((width, hidden), LOW)
    out_shape = (
        sds(block, F32), sds(block, F32), sds((total, width), F32), sds((total, width), F32), sds((total, width), F32),
        sds((seqs, SPAN_ROWS, length), LOW), sds((units, SPAN_ROWS, length), F32), sds((total, heads), LOW),
        sds((count, heads), LOW), sds((count, heads), LOW), sds((total, heads), LOW), sds((count, heads), LOW),
        sds((4 * heads, width), LOW), sds((4 * heads, width), LOW), square, square, square, square,
        sds((16, width), F32),
    )
    scratch = [
        V(mask.shape, jnp.int32), V(gains.shape, F32), V(biases.shape, F32), V(bias_in.shape, F32), wide(16),
        wide(count, LOW), wide(count, LOW), wide(3 * heads), wide(heads), V((width, hidden), F32),
        V((width, hidden), F32), wide(3 * heads), wide(heads), V((width, hidden), F32), V((width, hidden), F32),
        V((count, heads), LOW), V((count, heads), LOW), V((count, heads), LOW), V((count, heads), LOW),
        V((seqs, SPAN_ROWS, length), LOW), wide(4 * heads, LOW), wide(4 * heads, LOW), V((width, hidden), LOW), V((width, hidden), LOW),
        V((width, hidden), LOW), V((width, hidden), LOW), V((slots, width // slots, hidden), F32), V((slots, width // slots, hidden), F32),
        V((units, SPAN_ROWS, length), F32), wide(total), wide(total), V((total, heads), LOW),
        V((total, heads), F32), V((total, heads), LOW), V((total, heads), F32), wide(total), wide(total),
        wide(total), wide(total, LOW), V((total, hidden), LOW), V((total, hidden), F32), wide(total), wide(half), wide(half), wide(half),
        wide(total), wide(half), wide(half), wide(half), wide(total), wide(total), wide(total), wide(total), wide(total), wide(total), wide(total),
        V((total, hidden), LOW),
        pltpu.SemaphoreType.DMA((8 + 20 + slots,)), pltpu.SemaphoreType.DMA((2, 53 + 2 * slots + 2 * seqs)), pltpu.SemaphoreType.DMA((4,)),
    ]
    return pl.pallas_call(
        k1_kernel, out_shape=out_shape,
        in_specs=[sm] + [any_] * 10,
        out_specs=(any_,) * len(out_shape),
        scratch_shapes=scratch,
        compiler_params=pltpu.CompilerParams(
            collective_id=1, has_side_effects=True, vmem_limit_bytes=60 * 2**20
        ),
    )(lens, mask, gains, biases, bias_in, x, cot, wqkv, wout, win, wback)


BETA_ONE = 0.9
BETA_TWO = 0.999
ADAM_EPS = 1e-06
WEIGHT_DECAY = 0.01


def adam(weight, grad, first, second, ratio, corr_one, corr_two, decay):
    first = BETA_ONE * first + (1.0 - BETA_ONE) * grad
    second = BETA_TWO * second + (1.0 - BETA_TWO) * grad * grad
    update = first / corr_one / (jnp.sqrt(second / corr_two) + ADAM_EPS) + decay * weight
    return -ratio * update, first, second


FLIGHT = 0.55
PLAN_READY = (1.2, 1.2, 3.2)
SWAP_FIRST = ((0, 0),)
WEIGHT = {("RS", 0, 0): 8.0, ("RS", 1, 0): 7.0, ("RS", 2, 0): -7.0, ("RS", 2, 1): -10.0, ("AG", 0, 0): -10.0}
BLOCK_US = 3.2


def plan(n, weight):
    tasks = {}
    for ch in range(3):
        for p in range(2):
            ready = PLAN_READY[ch]
            swap = ch == 2
            both = (ch, p) in SWAP_FIRST
            for z in range(n):
                if swap:
                    for u in range(n):
                        tasks["XS", ch, p, 0, u, z] = ("X", z), [], ready
                for d in range(n):
                    if d == z:
                        continue
                    step = 1 if d > z else -1
                    kind = "RSR" if d > z else "RSL"
                    need = [(kind, ch, p, 0, d, z - step)] if 0 <= z - step < n else []
                    if swap:
                        need.append(("XS", ch, p, 0, d, z))
                    tasks[kind, ch, p, 0, d, z] = (kind[2], z), need, ready
                end = [("RSR", ch, p, 0, z, z - 1)] if z > 0 else []
                if z < n - 1:
                    end.append(("RSL", ch, p, 0, z, z + 1))
                if swap:
                    end.append(("XS", ch, p, 0, z, z))
                for par in (0, 1) if both else (0,):
                    for u in range(n):
                        if u == z:
                            need = [("AGX", ch, p, 0, z, z)] if par else end
                        else:
                            need = [("AGR", ch, p, par, u, z - 1) if u < z else ("AGL", ch, p, par, u, z + 1)]
                        if u <= z < n - 1:
                            tasks["AGR", ch, p, par, u, z] = ("R", z), need, 0.0
                        if 0 < z <= u:
                            tasks["AGL", ch, p, par, u, z] = ("L", z), need, 0.0
                        if par == 0 and (u == z or not both):
                            tasks["AGX", ch, p, 0, u, z] = ("X", z), need, 0.0
    after = {key: [] for key in tasks}
    for key, (_, need, _) in tasks.items():
        for one in need:
            after[one].append(key)
    rank = {}

    def longest(key):
        if key not in rank:
            rank[key] = 1.0 + FLIGHT + max([longest(k) for k in after[key]], default=0.0)
        return rank[key]

    missing = {key: len(task[1]) for key, task in tasks.items()}
    open_at = {key: task[2] for key, task in tasks.items() if not task[1]}
    free, done, order = {}, {}, []
    while open_at:
        by_link = {}
        for key in open_at:
            by_link.setdefault(tasks[key][0], []).append(key)
        best = None
        for link, keys in by_link.items():
            start = max(free.get(link, 0.0), min(open_at[k] for k in keys))
            able = [k for k in keys if open_at[k] <= start + 1e-9]
            key = max(able, key=lambda k: (longest(k) + weight.get((k[0][:2] if k[0] != "AGX" else "AX", k[1], k[2]), 0.0), -open_at[k]))
            if best is None or start < best[0] - 1e-9:
                best = start, key
        start, key = best
        free[tasks[key][0]] = start + 1.0
        done[key] = start + 1.0 + FLIGHT
        order.append((start, key))
        del open_at[key]
        for k in after[key]:
            missing[k] -= 1
            if missing[k] == 0:
                open_at[k] = max(max(done[q] for q in tasks[k][1]) + 0.15, tasks[k][2])
    return order, tasks, max(done.values())


def k2_kernel(
    lens, step, warmup, horizon, gains_h, biases_h, bias_in_h, vec_h,
    x_h, gi_h, gb_h, full_h, res_h, dtwo_h, pick_h, pm_h, qm_h, k_h, v_h, cm_h, ctx_h, wal_h, wpl_h, wil_h, wbl_h, pil_h, pbl_h,
    wqkv_h, wout_h, win_h, wback_h, mq_h, mo_h, mi_h, mb_h,
    out_h, grad_h, ci_h, cb_h, ca_h, nmq_h, nmo_h, nmi_h, nmb_h, vt_h,
    gains, biases, bias_in, vec, vt, wp, x, ga, gi, gb, dproj, ctx, pick, dres, full, dtwo, pm, qm, ko, vo, cm, dctx, wal, wpl, wil, wbl, pil, pbl,
    wrow_i, wrow_b, wrow_a, mq, mo, mi, mb, turned, flip,
    qp, kp, vp, ctxp, dpp, sbuf, rbuf, nrm, dsc, rdn, fin, rig,
    ring, xr, own, v0, v1, vx, vz,
    lsem, rs_s, rs_r, ag_s, ag_r, ax_s, ax_r, xs_s, xs_r, vs_s, vs_r, sd_s, sd_r, usem, wsem,
):
    me = Peers()
    n_u = gi.shape[0]
    seqs = sbuf.shape[0]
    count, width = x_h.shape
    length = count // seqs
    rows = SPAN_ROWS
    total = seqs * rows
    heads = ctx.shape[1]
    n_heads = heads // HD
    shard = gi.shape[1]
    hidden = wil.shape[1]
    half = length // 2
    quarter = length // 4
    z, b = me.u, me.b
    right = (me.d + 2, me.t)
    left = (me.d - 2, me.t)
    diag = (me.d, 3 - me.t)

    def remote(src, dst, ss, rr, peer):
        return pltpu.make_async_remote_copy(
            src_ref=src, dst_ref=dst, send_sem=ss, recv_sem=rr, device_id=peer, device_id_type=MESH
        )

    pend = {}
    order = iter(range(64))

    def fetch(name, src, dst):
        copy = pltpu.make_async_copy(src, dst, lsem.at[next(order)])
        copy.start()
        pend.setdefault(name, []).append(copy)

    def ready(*names):
        for name in names:
            for copy in pend.pop(name, []):
                copy.wait()

    for src, dst in ((gains_h, gains), (biases_h, biases), (bias_in_h, bias_in), (vec_h, vec)):
        fetch("small", src, dst)
    fetch("one", full_h, full)
    fetch("one", res_h, dres)
    fetch("one", dtwo_h, dtwo)
    fetch("gi", gi_h, gi)
    fetch("gb", gb_h, gb)
    fetch("wal", wal_h, wal)
    mine = pl.ds(pl.multiple_of(me.d * shard, 8), shard)

    def load_second():
        fetch("att", pick_h, pick)
        fetch("att", pm_h, pm)
        fetch("att", qm_h, qm)
        fetch("att", k_h, ko)
        fetch("att", v_h, vo)
        fetch("att", cm_h, cm)
        fetch("x", x_h, x.at[pl.ds(0, count)])

    def load_third():
        fetch("wpl", wpl_h, wpl)
        fetch("ctx", ctx_h, ctx)
        fetch("low", wil_h, wil)
        fetch("low", wbl_h, wbl)
        fetch("low", pil_h, pil)
        fetch("low", pbl_h, pbl)
        fetch("mi", win_h.at[mine], wrow_i)
        fetch("mi", mi_h, mi)
        fetch("mb", wback_h.at[mine], wrow_b)
        fetch("mb", mb_h, mb)
        fetch("ma", wqkv_h, turned.at[pl.ds(0, 3 * heads)])
        fetch("ma", wout_h, turned.at[pl.ds(3 * heads, heads)])
        fetch("ma", mq_h, mq)
        fetch("ma", mo_h, mo)


    others = [(2 * lax.rem(z + k, n_u) + b, me.t) for k in range(1, n_u)]
    greet([me.core, me.y, diag, me.x] + others)

    third = heads // 2

    def first_third(k):
        return remote(wqkv_h.at[pl.ds(k * 3 * third, third)], wp.at[k], wsem.at[0, k], wsem.at[1, k], me.y)

    order_all, tasks, _ = plan(n_u, WEIGHT)
    part_rows = shard // 2

    def rows_of(p):
        return pl.ds(p * part_rows, part_rows)

    def g_at(ch, u):
        return ga.at[2 * u + b] if ch == 2 else (gi, gb)[ch].at[u]

    def target(ch, d):
        return (ci_h, cb_h, ca_h)[ch].at[d]

    def xr_at(u, p):
        return xr.at[u, rows_of(p)]

    def ring_at(key):
        kind, ch, p, _, d, node = key
        place = d - (node + 1) if kind == "RSR" else (node - 1) - d
        return ring.at[ch, 0 if kind == "RSR" else 1, place, rows_of(p)]

    def transfer(key, incoming):
        kind, ch, p, par, u, node = key
        way = 0 if kind[2:] == "R" else 1
        if kind == "XS":
            k = p * n_u + u
            return remote(ga.at[2 * u + 1 - b, rows_of(p)], xr_at(u, p), xs_s.at[k], xs_r.at[k], me.x)
        if kind[:2] == "RS":
            k = ((ch * 2 + p) * 2 + way) * n_u + u
            peer = right if way == 0 else left
            return remote(g_at(ch, u).at[rows_of(p)], ring_at(key), rs_s.at[k], rs_r.at[k], peer)
        parity = b if (par == 0) != (incoming and kind == "AGX") else 1 - b
        there = target(ch, 2 * u + parity).at[rows_of(p)]
        here = own.at[ch, rows_of(p)] if u == node and par == 0 else there
        if kind == "AGX":
            k = (ch * 2 + p) * n_u + u
            return remote(here, there, ax_s.at[k], ax_r.at[k], me.x)
        k = (((ch * 2 + p) * 2 + way) * 2 + par) * n_u + u
        return remote(here, there, ag_s.at[k], ag_r.at[k], right if way == 0 else left)

    ratio, corr_one, corr_two = rates(step, warmup, horizon)

    def own_copy(ch, p):
        return pltpu.make_async_copy(own.at[ch, rows_of(p)], target(ch, me.d).at[rows_of(p)], usem.at[ch * 2 + p])

    def update(ch, p):
        at_p = rows_of(p)
        if ch < 2:
            w, m = ((wrow_i, mi), (wrow_b, mb))[ch]
            change, first, second = adam(
                w[at_p, :], g_at(ch, z)[at_p, :], m[0, at_p, :], m[1, at_p, :], ratio, corr_one, corr_two, WEIGHT_DECAY
            )
            own[ch, at_p, :] = change
            m[0, at_p, :] = first
            m[1, at_p, :] = second
        else:
            for k in range(4):
                col = slice(k * heads, (k + 1) * heads)
                first = mo[0, at_p, :] if k == 3 else mq[0, k, at_p, :]
                second = mo[1, at_p, :] if k == 3 else mq[1, k, at_p, :]
                change, first, second = adam(
                    wrow_a[at_p, col], ga[me.d, at_p, col], first, second, ratio, corr_one, corr_two, WEIGHT_DECAY
                )
                own[2, at_p, col] = change
                if k < 3:
                    mq[0, k, at_p, :] = first
                    mq[1, k, at_p, :] = second
                else:
                    mo[0, at_p, :] = first
                    mo[1, at_p, :] = second
        own_copy(ch, p).start()

    queue = [[] for _ in range(n_u)]
    inbound = [[] for _ in range(n_u)]
    for start, key in order_all:
        kind, node = key[0], key[5]
        queue[node].append((start * BLOCK_US, key))
        goes = node if kind in ("XS", "AGX") else node + 1 if kind[2] == "R" else node - 1
        inbound[goes].append(key)
    for node in range(n_u):
        queue[node].sort(key=lambda one: one[0])
    got = [set() for _ in range(n_u)]
    made = [set() for _ in range(n_u)]
    sent = [[] for _ in range(n_u)]

    def arrive(node, key):
        if key in got[node]:
            return
        got[node].add(key)
        transfer(key, True).wait_recv()
        kind, ch, p, _, u, _ = key
        if kind == "XS":
            ga[2 * u + b, rows_of(p)] += xr_at(u, p)[...]
        elif kind[:2] == "RS":
            g_at(ch, u)[rows_of(p), :] += ring_at(key)[...]

    def act(node, key):
        for need in tasks[key][1]:
            arrive(node, need)
        kind, ch, p, par, u, _ = key
        if kind[:2] == "AG" and u == node and par == 0 and (ch, p) not in made[node]:
            made[node].add((ch, p))
            update(ch, p)
        sent[node].append(key)
        transfer(key, False).start()

    def chain_until(until):
        for node in range(n_u):
            due = [key for start, key in queue[node] if start < until]
            queue[node] = [one for one in queue[node] if one[0] >= until]
            if due:
                pl.when(z == node)(lambda node=node, due=due: [act(node, key) for key in due] and None)

    def chain_end():
        for node in range(n_u):
            def settle(node=node):
                for key in inbound[node]:
                    arrive(node, key)
                for key in sent[node]:
                    transfer(key, False).wait_send()
            pl.when(z == node)(settle)
        for ch in range(3):
            for p in range(2):
                own_copy(ch, p).wait()

    def vec_x():
        return remote(v0, vx, vs_s.at[0], vs_r.at[0], me.x)

    def vec_z(k):
        peer = (2 * lax.rem(z + k, n_u) + b, me.t)
        return remote(v1, vz.at[z], vs_s.at[k], vs_r.at[k], peer)

    def vec_t(k, peer):
        return remote(v1, vt.at[me.t], vs_s.at[n_u + k], vs_r.at[n_u + k], peer)

    trio = (me.core, me.y, diag)

    def vectors_one():
        vec_x().wait()
        v1[...] = v0[...] + vx[...]
        vz[z] = v1[...]
        for k in range(1, n_u):
            vec_z(k).start()

    def vectors_two():
        for k in range(1, n_u):
            vec_z(k).wait()
        total = vz[0]
        for u in range(1, n_u):
            total = total + vz[u]
        v1[...] = total
        vt[me.t] = total
        for k, peer in enumerate(trio):
            vec_t(k, peer).start()

    def vectors_three():
        for k, peer in enumerate(trio):
            vec_t(k, peer).wait()
        fetch("out", vt, vt_h)

    lanes = 128

    def hidden_bias(slot):
        parts = hidden // lanes
        return jnp.concatenate([bias_in[pl.ds(slot * parts + j, 1), :] for j in range(parts)], axis=1)

    twin = lax.rem(me.t + 2, 4)

    def first_norm_back():
        d_normed = full[...] + dtwo[...]
        unit, inv = normalize(dres[...])
        d_one = norm_back(d_normed, gains[0:1, :], unit, inv)
        dres[...] = d_one
        v0[...] = vec[...]
        v0[0:1, :] = row_sum(d_normed * unit)
        v0[3:4, :] = row_sum(d_one)
        v0[4:5, :] = row_sum(d_normed)
        low = d_one.astype(LOW)
        x[count:count + total, :] = low
        dctx[...] = dot(low, wal[3 * heads:, :], 1, 1).astype(LOW)

    def attend_back(q, k, v, dc, probs, pick_s):
        dqs, dks, dvs = [], [], []
        for h in range(n_heads):
            col = slice(h * HD, (h + 1) * HD)
            prob = probs(h)
            d_prob = dot(dc[:, col], v[:, col], 1, 1)
            dvs.append(dot(prob.astype(LOW), dc[:, col], 0, 0))
            ds = (prob * (d_prob - jnp.sum(prob * d_prob, axis=-1, keepdims=True))).astype(LOW)
            dqs.append(dot(ds, k[:, col], 1, 0) * scale)
            dks.append(dot(ds, q[:, col], 0, 0))
        dq = jnp.concatenate(dqs, axis=1)
        dv = jnp.concatenate(dvs, axis=1)
        spread = dot(pick_s, dq.astype(LOW), 0, 0).astype(LOW)
        return jnp.concatenate([spread, jnp.concatenate(dks, axis=1).astype(LOW), dv.astype(LOW)], axis=1), dq, dv

    def own_back(s):
        here = slice(s * rows, (s + 1) * rows)
        low, dq, dv = attend_back(
            qm[here, :], ko.at[at(s)], vo.at[at(s)], dctx[here, :], lambda h: pm[s * n_heads + h], pick[s]
        )
        dproj[at(s), 0:3 * heads] = low
        dproj[at(s), 3 * heads:] = jnp.zeros((length, heads), LOW)
        sums = jnp.concatenate([row_sum(dq), row_sum(dv)], axis=1)
        v0[2:3, 0:2 * heads] = sums if s == 0 else v0[2:3, 0:2 * heads] + sums

    def weight_grads(j):
        if j == 0:
            dproj[count:count + total, 0:3 * heads] = jnp.zeros((total, 3 * heads), LOW)
            dproj[count:count + total, 3 * heads:] = cm[...]
        col = slice(j * 256, (j + 1) * 256)
        ga[:, :, col] = dot(x[...], dproj[:, col], 0, 0).reshape(2 * n_u, shard, 256)

    def twin_rows():
        dctx[...] = dot(x[count:count + total, :], wpl[3 * heads:, :], 1, 1).astype(LOW)

    def pick_bias(row):
        out = jnp.zeros((1, heads), F32)
        for slot in range(4):
            out = jnp.where(twin == slot, biases[row:row + 1, slot * heads:(slot + 1) * heads], out)
        return out

    scale = 1.0 / math.sqrt(HD)
    position = lax.broadcasted_iota(jnp.int32, (1, length), 1)
    my_half = pl.ds(pl.multiple_of(me.c * half, 8), half)
    its_half = pl.ds(pl.multiple_of((1 - me.c) * half, 8), half)
    my_quarter = pl.ds(pl.multiple_of(me.p * quarter, 8), quarter)
    its_quarter = pl.ds(pl.multiple_of((1 - me.p) * quarter, 8), quarter)

    def at(s, start=0, size=None):
        return pl.ds(pl.multiple_of(s * length + start, 8), size or length)

    def key_bias(s):
        return jnp.where(position < lens[s], 0.0, -1000000000.0)

    def project(s):
        xs = x[at(s), :]
        qp[...] = ((dot(xs, wpl[0:heads, :], 1, 1) + pick_bias(0)) * scale).astype(LOW)
        kp[...] = dot(xs, wpl[heads:2 * heads, :], 1, 1).astype(LOW)
        vp[...] = (dot(xs, wpl[2 * heads:3 * heads, :], 1, 1) + pick_bias(1)).astype(LOW)

    def attend_one(s, h):
        col = slice(h * HD, (h + 1) * HD)
        e = dot(qp[:, col], kp[:, col], 1, 1) + key_bias(s)
        e = jnp.exp(e - jnp.max(e, axis=-1, keepdims=True))
        prob = (e / jnp.sum(e, axis=-1, keepdims=True)).astype(LOW)
        ctxp[:, col] = dot(prob, vp[:, col], 1, 0).astype(LOW)

    def mix_copy(s):
        return remote(sbuf.at[s], rbuf.at[s], sd_s.at[s], sd_r.at[s], me.core)

    def mix(s):
        for where, into in ((its_half, sbuf), (my_half, nrm)):
            base = at(s, where.start, half)
            into[s] = dot(ctx[base, :], wal[3 * heads:, :], 1, 0) + dot(ctxp[where, :], wpl[3 * heads:, :], 1, 0)
        mix_copy(s).start()

    def down_copy(s):
        return remote(dsc.at[s, its_quarter], rdn.at[s], sd_s.at[seqs + s], sd_r.at[seqs + s], me.y)

    def feed_start(s):
        mix_copy(s).wait()
        base = at(s, me.c * half, half)
        unit, _ = normalize(x[base, :].astype(F32) + (nrm[s] + rbuf[s]) + biases[2:3, :])
        nrm[s] = unit * gains[0:1, :] + biases[3:4, :]

    def feed(s, part):
        w_in, w_back, slot = ((wil, wbl, me.t), (pil, pbl, me.t + 1 - 2 * me.c))[part]
        low = nrm[s].astype(LOW)
        bias = hidden_bias(slot)
        total = dsc[s] if part else jnp.zeros((half, width), F32)
        for j in range(0, hidden, 256):
            col = slice(j, j + 256)
            pre = dot(low, w_in[:, col], 1, 0) + bias[:, col]
            act_low = pre * (0.5 * (1.0 + lax.erf(pre * (1.0 / math.sqrt(2.0)))))
            total = total + dot(act_low.astype(LOW), w_back[:, col], 1, 1)
        dsc[s] = total
        if part:
            down_copy(s).start()

    def out_rows(s, p):
        return at(s, me.c * half + p * quarter, quarter)

    def out_copy(s, k, p, peer):
        src = fin.at[s] if k < 2 else out_h.at[out_rows(s, p)]
        return remote(src, out_h.at[out_rows(s, me.p if k < 2 else p)], sd_s.at[(2 + k) * seqs + s], sd_r.at[(2 + k) * seqs + s], peer)

    def finish(s):
        down_copy(s).wait()
        res = nrm[s, my_quarter] + (dsc[s, my_quarter] + rdn[s]) + biases[4:5, :]
        unit, _ = normalize(res)
        fin[s] = (unit * gains[1:2, :] + biases[5:6, :]).astype(LOW).astype(F32)
        fetch("out", fin.at[s], out_h.at[out_rows(s, me.p)])
        out_copy(s, 0, me.p, me.y).start()
        out_copy(s, 1, me.p, me.core).start()

    def relay(s):
        out_copy(s, 0, me.p, me.y).wait()
        out_copy(s, 2, 1 - me.p, me.core).start()

    def relay_end(s):
        out_copy(s, 1, me.p, me.core).wait()
        out_copy(s, 2, 1 - me.p, me.core).wait()

    def back(s):
        here = slice(s * rows, (s + 1) * rows)
        q = dot(pick[s], qp[...], 1, 0).astype(LOW)
        dc = dctx[here, :]

        def probs(h):
            col = slice(h * HD, (h + 1) * HD)
            scores = dot(q[:, col], kp[:, col], 1, 1) + key_bias(s)
            e = jnp.exp(scores - jnp.max(scores, axis=-1, keepdims=True))
            return e / jnp.sum(e, axis=-1, keepdims=True)

        dpp[...] = attend_back(q, kp, vp, dc, probs, pick[s])[0]

    def entry_copy(s):
        return remote(sbuf.at[s], rig.at[s], sd_s.at[5 * seqs + s], sd_r.at[5 * seqs + s], me.core)

    def entry(s):
        for where, into in ((its_half, sbuf), (my_half, rbuf)):
            base = at(s, where.start, half)
            product = lambda a, w: dot(a, w[0:3 * heads, :], 1, 0)

            def add(low, high, s=s, into=into):
                into[s] = product(*low) + product(*high)

            own_part = lambda base=base: (dproj[base, 0:3 * heads], wal)
            twin_part = lambda where=where: (dpp[where, :], wpl)
            pl.when(me.p == 0)(lambda add=add, a=own_part, b=twin_part: add(a(), b()))
            pl.when(me.p == 1)(lambda add=add, a=own_part, b=twin_part: add(b(), a()))
        entry_copy(s).start()

    def grad_rows(s):
        return at(s, me.c * half, half)

    def grad_copy(s):
        return remote(rbuf.at[s], grad_h.at[grad_rows(s)], sd_s.at[6 * seqs + s], sd_r.at[6 * seqs + s], me.core)

    def entry_end(s):
        entry_copy(s).wait()
        d_one = dres[pl.ds(s * rows, rows), :]
        high = d_one.astype(LOW)
        rest = (d_one - high.astype(F32)).astype(LOW)
        some = pick[s, :, pl.ds(pl.multiple_of(me.c * half, lanes), half)]
        rbuf[s] = (rbuf[s] + rig[s]) + (dot(some, high, 0, 0) + dot(some, rest, 0, 0))
        fetch("out", rbuf.at[s], grad_h.at[grad_rows(s)])
        grad_copy(s).start()

    def turn_weights():
        for j in range(0, width, lanes):
            flip[...] = turned[j:j + lanes, :].T
            wrow_a[:, j:j + lanes] = flip[mine, :]

    def begin():
        for k in range(2):
            first_third(k).start()
        ready("gi", "gb")
        load_second()

    def own_start():
        ready("small", "one", "wal")
        first_norm_back()
        ready("att")
        load_third()

    def moments_in():
        ready("mi", "mb", "ma")
        turn_weights()

    def twin_start():
        ready("wpl", "ctx", "low")
        for k in range(2):
            first_third(k).wait()
            wpl[k * 3 * third:k * 3 * third + third, :] = wp[k].astype(LOW)
        twin_rows()

    work = [(0.0, begin), (4.4, own_start)]
    work += [(5.4 + s, lambda s=s: own_back(s)) for s in range(seqs)]
    work += [(8.4, lambda: ready("x"))] + [(8.5 + 0.7 * j, lambda j=j: weight_grads(j)) for j in range(width // 256)]
    work += [(10.7, lambda: vec_x().start()), (14.0, moments_in), (20.0, vectors_one), (28.0, vectors_two)]
    first_twin = 24.0
    for s in range(seqs):
        t = first_twin + 20.0 * s
        work += [(t, lambda s=s: (twin_start() if s == 0 else None, project(s)) and None)]
        work += [(t + 1.5 + h, lambda s=s, h=h: attend_one(s, h)) for h in range(n_heads)]
        work += [(t + 5.0, lambda s=s: mix(s)), (t + 5.5, lambda s=s: back(s)), (t + 7.5, lambda s=s: feed_start(s))]
        work += [(t + 8.0, lambda s=s: feed(s, 0)), (t + 9.5, lambda s=s: feed(s, 1)), (t + 11.0, lambda s=s: entry(s))]
        work += [(t + 24.0, lambda s=s: finish(s)), (t + 40.0, lambda s=s: relay(s)), (t + 20.0, lambda s=s: entry_end(s))]
    work += [(40.0, vectors_three)]
    for when, do in sorted(work, key=lambda one: one[0]):
        chain_until(when)
        do()
    for when in range(80, 120, 2):
        chain_until(float(when))
    chain_until(1e9)
    for s in range(seqs):
        relay_end(s)
        grad_copy(s).wait()
    for ref, out in ((mi, nmi_h), (mb, nmb_h), (mq, nmq_h), (mo, nmo_h)):
        fetch("out", ref, out)
    chain_end()
    ready("out")


def k2_call(lens, step, warmup, horizon, gains, biases, bias_in, k1, x, weights, moments):
    wqkv, wout, win, wback = weights
    count, width = x.shape
    seqs = lens.shape[0]
    heads, hidden = wout.shape[0], win.shape[1]
    length = count // seqs
    half, quarter = length // 2, length // 4
    shard = moments[1].shape[1]
    slots = width // shard
    n_u = slots // 2
    total = seqs * SPAN_ROWS
    units = seqs * (heads // HD)
    any_ = pl.BlockSpec(memory_space=pl.ANY)
    vm = pl.BlockSpec(memory_space=pltpu.VMEM)
    sm = pl.BlockSpec(memory_space=pltpu.SMEM)
    sds = lambda *shape: jax.ShapeDtypeStruct(shape, F32)
    V = lambda *shape: pltpu.VMEM(shape, F32)
    B = lambda *shape: pltpu.VMEM(shape, LOW)
    D = pltpu.SemaphoreType.DMA
    out_shape = (
        sds(count, width), sds(count, width), sds(slots, shard, hidden), sds(slots, shard, hidden), sds(slots, shard, width),
        sds(*moments[0].shape), sds(*moments[1].shape), sds(*moments[2].shape), sds(*moments[3].shape), sds(4, 16, width),
    )
    scratch = [
        V(*gains.shape), V(*biases.shape), V(*bias_in.shape), V(16, width), V(4, 16, width), V(2, heads // 2, width),
        B(count + total, width), V(slots, shard, width), V(n_u, shard, hidden), V(n_u, shard, hidden),
        B(count + total, width), B(count, heads), B(seqs, SPAN_ROWS, length), V(total, width),
        V(total, width), V(total, width), V(units, SPAN_ROWS, length), B(total, heads), B(count, heads), B(count, heads), B(total, heads), B(total, heads),
        B(width, width), B(width, width), B(width, hidden), B(width, hidden), B(width, hidden), B(width, hidden),
        V(shard, hidden), V(shard, hidden), V(shard, width),
        V(*moments[0].shape), V(*moments[1].shape), V(*moments[2].shape), V(*moments[3].shape), V(width, width), V(width, 128),
        B(length, heads), B(length, heads), B(length, heads), B(length, heads), B(length, 3 * heads),
        V(seqs, half, width), V(seqs, half, width), V(seqs, half, width), V(seqs, half, width),
        V(seqs, quarter, width), V(seqs, quarter, width), V(seqs, half, width),
        V(3, 2, n_u - 1, shard, width), V(n_u, shard, width), V(3, shard, width),
        V(16, width), V(16, width), V(16, width), V(n_u, 16, width),
        D((64,)), D((12 * n_u,)), D((12 * n_u,)), D((24 * n_u,)), D((24 * n_u,)), D((6 * n_u,)), D((6 * n_u,)),
        D((2 * n_u,)), D((2 * n_u,)), D((n_u + 3,)), D((n_u + 3,)), D((7 * seqs,)), D((7 * seqs,)), D((6,)), D((2, 2)),
    ]
    return pl.pallas_call(
        k2_kernel, out_shape=out_shape,
        in_specs=[sm] * 4 + [any_] * 31,
        out_specs=(any_,) * 10,
        scratch_shapes=scratch,
        compiler_params=pltpu.CompilerParams(collective_id=2, has_side_effects=True, vmem_limit_bytes=63 * 2**20),
    )(
        lens, step, warmup, horizon, gains, biases, bias_in, k1[-1], x, *k1[:-1], wqkv, wout, win, wback, *moments,
    )


def rates(step, warmup, horizon):
    clock = jnp.full((1, 128), step[0].astype(F32))
    warm = jnp.full((1, 128), warmup[0].astype(F32))
    far = jnp.full((1, 128), horizon[0].astype(F32))
    ratio = jnp.minimum(clock / warm, (far - clock) / (far - warm))[:, 0:1]
    return ratio, (1.0 - jnp.exp(clock * math.log(0.9)))[:, 0:1], (1.0 - jnp.exp(clock * math.log(0.999)))[:, 0:1]


def k3_kernel(step, warmup, horizon, *refs):
    n_big, n_small = 9, 7
    (out_h, grad_h, ci_h, cb_h, ca_h, *moms_h), refs = refs[:n_big], refs[n_big:]
    small_h, refs = refs[:n_small], refs[n_small:]
    (normed_o, grad_o, ci_o, cb_o, cq_o, co_o, *moms_o), refs = refs[:n_big + 1], refs[n_big + 1:]
    small_o, refs = refs[:6], refs[6:]
    (wide, low, turned, grad, ci, cb, ca, *moms), refs = refs[:n_big + 2], refs[n_big + 2:]
    (gains, biases, bias_in, mom_g, mom_b, mom_h, vt), refs = refs[:n_small], refs[n_small:]
    (ch_g, ch_b, ch_h, nm_g, nm_b, nm_h), (rsem, wsem) = refs[:6], refs[6:]
    chunks, size = wide.shape[:2]
    reads, copies = [], []

    def read(src, dst):
        copy = pltpu.make_async_copy(src, dst, rsem.at[len(reads)])
        copy.start()
        reads.append(copy)
        return copy

    def write(src, dst):
        copy = pltpu.make_async_copy(src, dst, wsem.at[len(copies)])
        copy.start()
        copies.append(copy)

    rows = [pl.ds(j * size, size) for j in range(chunks)]

    def pieces(src, buf, dst, n):
        step = src.shape[0] // n
        cuts = [pl.ds(j * step, step) for j in range(n)]
        return [(read(src.at[cut], buf.at[cut]), buf.at[cut], dst.at[cut]) for cut in cuts]

    first = pieces(grad_h, grad, grad_o, 4)
    got_ca = read(ca_h, ca)
    second = pieces(ci_h, ci, ci_o, 2) + pieces(cb_h, cb, cb_o, 2)
    got = [read(out_h.at[row], wide.at[j]) for j, row in enumerate(rows)]
    got_small = [read(src, dst) for src, dst in zip(small_h, (gains, biases, bias_in, mom_g, mom_b, mom_h, vt))]
    last = [(read(src, buf), buf, dst) for src, buf, dst in zip(moms_h, moms, moms_o)]
    for copy, buf, dst in first:
        copy.wait()
        write(buf, dst)
    got_ca.wait()
    width = turned.shape[1]
    lanes = 128
    for j in range(0, width, lanes):
        turned[j:j + lanes, :] = ca[:, :, j:j + lanes].reshape(width, lanes).T
    split = cq_o.shape[0]
    write(turned.at[pl.ds(0, split)], cq_o)
    write(turned.at[pl.ds(split, width - split)], co_o)
    for copy, buf, dst in second:
        copy.wait()
        write(buf, dst)
    for j, row in enumerate(rows):
        got[j].wait()
        low[j] = wide[j].astype(LOW)
        write(low.at[j], normed_o.at[row])
    for copy in got_small:
        copy.wait()
    put = (*rates(step, warmup, horizon), 0.0)
    heads = gains.shape[1] // 4
    hidden = vt.shape[2]
    common = vt[0]
    ch_g[...], nm_g[0], nm_g[1] = adam(gains[...], common[0:2], mom_g[0], mom_g[1], *put)
    query = jnp.concatenate([vt[k][2:3, 0:heads] for k in range(4)], axis=1)
    value = jnp.concatenate([vt[k][2:3, heads:2 * heads] for k in range(4)], axis=1)
    for row in range(6):
        grad_row = query if row == 0 else value if row == 1 else common[row + 1:row + 2]
        change, first, second = adam(biases[row:row + 1, :], grad_row, mom_b[row, 0:1], mom_b[row, 1:2], *put)
        ch_b[row:row + 1, :] = change
        nm_b[row, 0:1] = first
        nm_b[row, 1:2] = second
    parts = hidden // lanes
    for k in range(4):
        col = slice(k * hidden, (k + 1) * hidden)
        bias = jnp.concatenate([bias_in[k * parts + j:k * parts + j + 1, :] for j in range(parts)], axis=1)
        change, first, second = adam(bias, vt[k][8:9, :], mom_h[0:1, col], mom_h[1:2, col], *put)
        nm_h[0:1, col] = first
        nm_h[1:2, col] = second
        for j in range(parts):
            ch_h[k * parts + j:k * parts + j + 1, :] = change[:, j * lanes:(j + 1) * lanes]
    for src, dst in zip((ch_g, ch_b, ch_h, nm_g, nm_b, nm_h), small_o):
        write(src, dst)
    for copy, buf, dst in last:
        copy.wait()
        write(buf, dst)
    for copy in copies:
        copy.wait()


def k3_call(step, warmup, horizon, gains, biases, bias_in, mom_g, mom_b, mom_h, vt, big, heads):
    any_ = pl.BlockSpec(memory_space=pl.ANY)
    sm = pl.BlockSpec(memory_space=pltpu.SMEM)
    of = lambda a: jax.ShapeDtypeStruct(a.shape, a.dtype)
    held = lambda a: pltpu.VMEM(a.shape, F32)
    count, width = big[0].shape
    chunks = 6
    small = (gains, biases, bias_in, mom_g, mom_b, mom_h)
    sds = lambda *shape: jax.ShapeDtypeStruct(shape, F32)
    out_shape = (
        jax.ShapeDtypeStruct((count, width), LOW), *map(of, big[1:4]), sds(3 * heads, width), sds(heads, width),
        *map(of, big[5:]), *map(of, small),
    )
    return pl.pallas_call(
        k3_kernel,
        out_shape=out_shape,
        in_specs=[sm] * 3 + [any_] * (len(big) + 7),
        out_specs=(any_,) * len(out_shape),
        scratch_shapes=[
            pltpu.VMEM((chunks, count // chunks, width), F32), pltpu.VMEM((chunks, count // chunks, width), LOW),
            pltpu.VMEM((width, width), F32), *map(held, big[1:]), *map(held, small), held(vt), *map(held, small),
            pltpu.SemaphoreType.DMA((32,)), pltpu.SemaphoreType.DMA((32,)),
        ],
        compiler_params=pltpu.CompilerParams(vmem_limit_bytes=62 * 2**20),
    )(step, warmup, horizon, *big, *small, vt)


def fast(tokens_in, cotangent, span_mask, lengths, step, warmup, total, w_qkv, w_out, w_in, w_back, gains, biases, bias_in,
         mom_qkv, mom_out, mom_in, mom_back, mom_gains, mom_biases, mom_bias_in):
    width = tokens_in.shape[1]
    heads, hidden = w_out.shape[1], w_in.shape[1]
    wqkv_t = jnp.transpose(w_qkv, (1, 2, 0)).reshape(3 * heads, width)
    wout_t = w_out.T
    bias_tiles = bias_in.reshape(-1, 128)
    k1 = k1_call(
        tokens_in, cotangent, span_mask.reshape(-1, 128), lengths, wqkv_t, wout_t, w_in, w_back, gains, biases, bias_tiles,
        width // mom_out.shape[1]
    )
    *big, vt = k2_call(
        lengths, step, warmup, total, gains, biases, bias_tiles, k1, tokens_in, (wqkv_t, wout_t, w_in, w_back),
        (jnp.transpose(mom_qkv, (0, 2, 1, 3)), mom_out, mom_in, mom_back)
    )
    (
        out, grad, ci, cb, cq, co, nmq, nmo, nmi, nmb, ch_g, ch_b, ch_h, nm_g, nm_b, nm_h
    ) = k3_call(
        step, warmup, total, gains, biases, bias_tiles, mom_gains, jnp.transpose(mom_biases, (1, 0, 2)), mom_bias_in, vt, big, heads
    )
    return (
        out, grad, jnp.transpose(cq.reshape(3, heads, width), (2, 0, 1)), co.T,
        ci.reshape(width, hidden), cb.reshape(width, hidden), ch_g, ch_b, ch_h.reshape(-1),
        jnp.transpose(nmq, (0, 2, 1, 3)), nmo, nmi, nmb, nm_g, jnp.transpose(nm_b, (1, 0, 2)), nm_h,
    )


def layer_norm(values, gain, shift):
    center = values - jnp.mean(values, axis=-1, keepdims=True)
    spread = jnp.mean(center * center, axis=-1, keepdims=True)
    return center * lax.rsqrt(spread + NORM_EPS) * gain + shift


def exact_gelu(values):
    return jax.nn.gelu(values, approximate=False)


def outer_sum(left, right):
    return jnp.einsum("ta,tb->ab", left, right, preferred_element_type=jnp.float32)


def adam_step(weight, grad, moments, ratio, corr_one, corr_two, decay):
    first = BETA_ONE * moments[0] + (1.0 - BETA_ONE) * grad
    second = BETA_TWO * moments[1] + (1.0 - BETA_TWO) * grad * grad
    update = first / corr_one / (jnp.sqrt(second / corr_two) + ADAM_EPS) + decay * weight
    return (-ratio * update, jnp.stack([first, second]))


def on_device(
    tokens_in,
    cotangent,
    span_mask,
    lengths,
    step,
    warmup,
    total,
    w_qkv,
    w_out,
    w_in,
    w_back,
    gains,
    biases,
    bias_in,
    mom_qkv,
    mom_out,
    mom_in,
    mom_back,
    mom_gains,
    mom_biases,
    mom_bias_in,
):
    row_count, model_width = tokens_in.shape
    if mom_out.shape[1] % 8 == 0:
        return fast(
            tokens_in, cotangent, span_mask, lengths, step, warmup, total, w_qkv, w_out, w_in, w_back, gains, biases,
            bias_in, mom_qkv, mom_out, mom_in, mom_back, mom_gains, mom_biases, mom_bias_in
        )
    seq_count = lengths.shape[0]
    seq_length = row_count // seq_count
    head_cols = w_qkv.shape[2]
    hidden_cols = w_in.shape[1]
    head_size = HD
    local_heads = head_cols // head_size
    query_scale = 1.0 / math.sqrt(head_size)
    tensor_slot = lax.axis_index("tensor")
    bias_query = lax.dynamic_slice_in_dim(biases[0], tensor_slot * head_cols, head_cols)
    bias_value = lax.dynamic_slice_in_dim(biases[1], tensor_slot * head_cols, head_cols)
    bias_hidden = lax.dynamic_slice_in_dim(bias_in, tensor_slot * hidden_cols, hidden_cols)
    qkv_low = w_qkv.astype(jnp.bfloat16).reshape(model_width, 3 * head_cols)
    out_low = w_out.astype(jnp.bfloat16)
    in_low = w_in.astype(jnp.bfloat16)
    down_low = w_back.astype(jnp.bfloat16)
    projected = jnp.dot(tokens_in, qkv_low, preferred_element_type=jnp.float32).reshape(
        row_count, 3, head_cols
    )
    attn_shape = (seq_count, seq_length, local_heads, head_size)
    queries = (
        ((projected[:, 0] + bias_query) * query_scale).astype(jnp.bfloat16).reshape(attn_shape)
    )
    keys = projected[:, 1].astype(jnp.bfloat16).reshape(attn_shape)
    values = (projected[:, 2] + bias_value).astype(jnp.bfloat16).reshape(attn_shape)
    positions = jnp.arange(seq_length, dtype=jnp.int32)
    inside = positions[None, :] < lengths[:, None]
    key_bias = jnp.where(inside, 0.0, -1000000000.0).astype(jnp.float32)

    def score_block():
        raw = jnp.einsum("sqhd,skhd->shqk", queries, keys, preferred_element_type=jnp.float32)
        return raw + key_bias[:, None, None, :]

    scores = score_block()
    peak = jnp.max(scores, axis=-1, keepdims=True)
    log_total = peak + jnp.log(jnp.sum(jnp.exp(scores - peak), axis=-1, keepdims=True))
    probs_low = jnp.exp(scores - log_total).astype(jnp.bfloat16)
    context_low = (
        jnp.einsum("shqk,skhd->sqhd", probs_low, values, preferred_element_type=jnp.float32)
        .reshape(row_count, head_cols)
        .astype(jnp.bfloat16)
    )
    attn_part = jnp.einsum("tc,dc->td", context_low, out_low, preferred_element_type=jnp.float32)
    attn_sum = lax.psum(attn_part, "tensor")
    residual_one = tokens_in.astype(jnp.float32) + attn_sum + biases[2]
    normed = layer_norm(residual_one, gains[0], biases[3])
    normed_low = normed.astype(jnp.bfloat16)
    pre_act = jnp.dot(normed_low, in_low, preferred_element_type=jnp.float32) + bias_hidden
    act_low = exact_gelu(pre_act).astype(jnp.bfloat16)
    down_part = jnp.einsum("tf,df->td", act_low, down_low, preferred_element_type=jnp.float32)
    down_sum = lax.psum(down_part, "tensor")
    residual_two = normed + down_sum + biases[4]
    live = (inside.astype(jnp.int32) * span_mask.reshape(seq_count, seq_length)) > 0
    upto = (positions[:, None] <= positions[None, :]).astype(jnp.float32)
    rank = jnp.dot(live.astype(jnp.float32), upto).astype(jnp.int32) - 1
    slots = jnp.arange(SPAN_ROWS, dtype=jnp.int32)
    pick = (live[:, None, :] & (rank[:, None, :] == slots[None, :, None])).astype(jnp.float32)
    pick_low = pick.astype(jnp.bfloat16)

    def rows_of(values):
        width = values.shape[-1]
        return jnp.einsum(
            "srt,std->srd",
            pick,
            values.reshape(seq_count, seq_length, width),
            precision=lax.Precision.HIGHEST,
        ).reshape(seq_count * SPAN_ROWS, width)

    def low_rows_of(values):
        width = values.shape[-1]
        return jnp.einsum(
            "srt,std->srd",
            pick_low,
            values.reshape(seq_count, seq_length, width),
            preferred_element_type=jnp.bfloat16,
        ).reshape(seq_count * SPAN_ROWS, width)

    result = layer_norm(residual_two, gains[1], biases[5])
    normed_out = result.astype(jnp.bfloat16)
    residual_one_rows = rows_of(residual_one)
    residual_two_rows = rows_of(residual_two)
    grad_result = low_rows_of(cotangent).astype(jnp.float32)
    _, norm_two_back = jax.vjp(layer_norm, residual_two_rows, gains[1], biases[5])
    d_res_two, d_gain_two, d_shift_two = norm_two_back(grad_result)
    d_res_two_low = d_res_two.astype(jnp.bfloat16)
    normed_low_rows = low_rows_of(normed_low)
    pre_rows = jnp.dot(normed_low_rows, in_low, preferred_element_type=jnp.float32) + bias_hidden
    act_rows, gelu_back = jax.vjp(exact_gelu, pre_rows)
    grad_back = outer_sum(d_res_two_low, act_rows.astype(jnp.bfloat16))
    d_act = jnp.dot(d_res_two_low, down_low, preferred_element_type=jnp.float32)
    d_pre = gelu_back(d_act)[0]
    d_pre_low = d_pre.astype(jnp.bfloat16)
    grad_in = outer_sum(normed_low_rows, d_pre_low)
    d_normed_part = jnp.einsum("tf,df->td", d_pre_low, in_low, preferred_element_type=jnp.float32)
    d_normed = lax.psum(d_normed_part, "tensor") + d_res_two
    _, norm_one_back = jax.vjp(layer_norm, residual_one_rows, gains[0], biases[3])
    d_res_one, d_gain_one, d_shift_one = norm_one_back(d_normed)
    d_res_one_low = d_res_one.astype(jnp.bfloat16)
    grad_out_proj = outer_sum(d_res_one_low, low_rows_of(context_low))
    row_shape = (seq_count, SPAN_ROWS, local_heads, head_size)
    d_context = (
        jnp.dot(d_res_one_low, out_low, preferred_element_type=jnp.float32)
        .astype(jnp.bfloat16)
        .reshape(row_shape)
    )
    query_rows = low_rows_of(queries.reshape(row_count, head_cols)).reshape(row_shape)
    raw = jnp.einsum("sqhd,skhd->shqk", query_rows, keys, preferred_element_type=jnp.float32)
    probs = jax.nn.softmax(raw + key_bias[:, None, None, :], axis=-1)
    probs_again = probs.astype(jnp.bfloat16)
    d_probs = jnp.einsum("sqhd,skhd->shqk", d_context, values, preferred_element_type=jnp.float32)
    d_values = jnp.einsum(
        "shqk,sqhd->skhd", probs_again, d_context, preferred_element_type=jnp.float32
    ).reshape(row_count, head_cols)
    d_scores = (probs * (d_probs - jnp.sum(probs * d_probs, axis=-1, keepdims=True))).astype(
        jnp.bfloat16
    )
    d_queries = (
        jnp.einsum("shqk,skhd->sqhd", d_scores, keys, preferred_element_type=jnp.float32).reshape(
            seq_count * SPAN_ROWS, head_cols
        )
        * query_scale
    )
    d_keys = jnp.einsum(
        "shqk,sqhd->skhd", d_scores, query_rows, preferred_element_type=jnp.float32
    ).reshape(row_count, head_cols)

    def spread(row_values):
        width = row_values.shape[-1]
        return jnp.einsum(
            "srt,srd->std",
            pick,
            row_values.reshape(seq_count, SPAN_ROWS, width),
            precision=lax.Precision.HIGHEST,
        ).reshape(row_count, width)

    d_proj_low = (
        jnp.stack([spread(d_queries), d_keys, d_values], axis=1)
        .astype(jnp.bfloat16)
        .reshape(row_count, 3 * head_cols)
    )
    grad_qkv = outer_sum(tokens_in, d_proj_low).reshape(model_width, 3, head_cols)
    d_entry_part = jnp.einsum("tc,dc->td", d_proj_low, qkv_low, preferred_element_type=jnp.float32)
    input_grad = lax.psum(d_entry_part, "tensor") + spread(d_res_one)
    first_rank = (tensor_slot == 0).astype(jnp.float32)
    width_zero = jnp.zeros((model_width,), jnp.float32)

    def place_heads(partial_sum):
        return lax.dynamic_update_slice_in_dim(width_zero, partial_sum, tensor_slot * head_cols, 0)

    grad_gains = jnp.stack([d_gain_one, d_gain_two]) * first_rank
    grad_biases = jnp.stack(
        [
            place_heads(jnp.sum(d_queries, axis=0)),
            place_heads(jnp.sum(d_values, axis=0)),
            jnp.sum(d_res_one, axis=0) * first_rank,
            d_shift_one * first_rank,
            jnp.sum(d_res_two, axis=0) * first_rank,
            d_shift_two * first_rank,
        ]
    )
    grad_bias_in = lax.dynamic_update_slice_in_dim(
        jnp.zeros(bias_in.shape, jnp.float32), jnp.sum(d_pre, axis=0), tensor_slot * hidden_cols, 0
    )
    grad_gains, grad_biases, grad_bias_in = lax.psum(
        (grad_gains, grad_biases, grad_bias_in), ("dp", "tensor")
    )
    data_slot = lax.axis_index("dp")
    shard_rows = model_width // lax.axis_size("dp")
    owned = tuple(
        lax.psum_scatter(part, "dp", scatter_dimension=0, tiled=True)
        for part in (grad_qkv, grad_out_proj, grad_in, grad_back)
    )
    clock = step[0].astype(jnp.float32)
    warm = warmup[0].astype(jnp.float32)
    horizon = total[0].astype(jnp.float32)
    ratio = jnp.minimum(clock / warm, (horizon - clock) / (horizon - warm))
    corr_one = 1.0 - jnp.power(BETA_ONE, clock)
    corr_two = 1.0 - jnp.power(BETA_TWO, clock)
    change_rows = []
    fresh_moments = []
    for weight, grad_rows, moment in zip(
        (w_qkv, w_out, w_in, w_back), owned, (mom_qkv, mom_out, mom_in, mom_back)
    ):
        weight_rows = lax.dynamic_slice_in_dim(weight, data_slot * shard_rows, shard_rows, 0)
        row_change, new_moment = adam_step(
            weight_rows, grad_rows, moment, ratio, corr_one, corr_two, WEIGHT_DECAY
        )
        change_rows.append(row_change)
        fresh_moments.append(new_moment)
    change_qkv, change_out_proj, change_in_proj, change_back_proj = (
        lax.all_gather(change_rows[0], "dp", axis=0, tiled=True),
        lax.all_gather(change_rows[1], "dp", axis=0, tiled=True),
        lax.all_gather(change_rows[2], "dp", axis=0, tiled=True),
        lax.all_gather(change_rows[3], "dp", axis=0, tiled=True),
    )
    change_gains, new_mom_gains = adam_step(
        gains, grad_gains, mom_gains, ratio, corr_one, corr_two, 0.0
    )
    change_biases, new_mom_biases = adam_step(
        biases, grad_biases, mom_biases, ratio, corr_one, corr_two, 0.0
    )
    change_bias_in, new_mom_bias_in = adam_step(
        bias_in, grad_bias_in, mom_bias_in, ratio, corr_one, corr_two, 0.0
    )
    return (
        normed_out,
        input_grad,
        change_qkv,
        change_out_proj,
        change_in_proj,
        change_back_proj,
        change_gains,
        change_biases,
        change_bias_in,
        fresh_moments[0],
        fresh_moments[1],
        fresh_moments[2],
        fresh_moments[3],
        new_mom_gains,
        new_mom_biases,
        new_mom_bias_in,
    )


def solution(mesh):
    in_specs = (
        P("dp", None),
        P("dp", None),
        P("dp"),
        P("dp"),
        P(),
        P(),
        P(),
        P(None, None, "tensor"),
        P(None, "tensor"),
        P(None, "tensor"),
        P(None, "tensor"),
        P(),
        P(),
        P(),
        P(None, "dp", None, "tensor"),
        P(None, "dp", "tensor"),
        P(None, "dp", "tensor"),
        P(None, "dp", "tensor"),
        P(),
        P(),
        P(),
    )
    out_specs = (
        P("dp", None),
        P("dp", None),
        P(None, None, "tensor"),
        P(None, "tensor"),
        P(None, "tensor"),
        P(None, "tensor"),
        P(),
        P(),
        P(),
        P(None, "dp", None, "tensor"),
        P(None, "dp", "tensor"),
        P(None, "dp", "tensor"),
        P(None, "dp", "tensor"),
        P(),
        P(),
        P(),
    )
    return jax.shard_map(
        on_device, mesh=mesh, in_specs=in_specs, out_specs=out_specs, check_vma=False
    )
```

```python
import math

import jax
import jax.numpy as jnp
from jax import lax
from jax.experimental import pallas as pl
from jax.experimental.pallas import tpu as pltpu
from jax.sharding import PartitionSpec as P

HD = 64
SPAN_ROWS = 80
NORM_EPS = 1e-12
MESH = pl.DeviceIdType.MESH
F32 = jnp.float32
LOW = jnp.bfloat16


def dot(left, right, left_dim, right_dim):
    return lax.dot_general(
        left, right, (((left_dim,), (right_dim,)), ((), ())), preferred_element_type=F32
    )


def normalize(rows):
    center = rows - jnp.mean(rows, axis=-1, keepdims=True)
    scale = lax.rsqrt(jnp.mean(center * center, axis=-1, keepdims=True) + NORM_EPS)
    return center * scale, scale


def norm_back(grad, gain, unit, scale):
    weighted = grad * gain
    return scale * (
        weighted
        - jnp.mean(weighted, axis=-1, keepdims=True)
        - unit * jnp.mean(weighted * unit, axis=-1, keepdims=True)
    )


def row_sum(rows):
    return jnp.sum(rows, axis=0, keepdims=True)


class Peers:
    def __init__(self):
        self.d = lax.axis_index("dp")
        self.t = lax.axis_index("tensor")
        self.b = lax.rem(self.d, 2)
        self.c = lax.rem(self.t, 2)
        self.p = lax.div(self.t, 2)
        self.u = lax.div(self.d, 2)
        self.core = (self.d, self.t + 1 - 2 * self.c)
        self.y = (self.d, lax.rem(self.t + 2, 4))
        self.x = (self.d + 1 - 2 * self.b, self.t)


def send(src, dst, sems, k, peer):
    copy = pltpu.make_async_remote_copy(
        src_ref=src, dst_ref=dst, send_sem=sems.at[0, k], recv_sem=sems.at[1, k],
        device_id=peer, device_id_type=MESH,
    )
    copy.start()
    return copy


def local(src, dst, sem):
    copy = pltpu.make_async_copy(src, dst, sem)
    copy.start()
    return copy


def greet(peers):
    barrier = pltpu.get_barrier_semaphore()
    for peer in peers:
        pl.semaphore_signal(barrier, inc=1, device_id=peer, device_id_type=MESH)
    pl.semaphore_wait(barrier, len(peers))


def gelu_parts(pre):
    cdf = 0.5 * (1.0 + lax.erf(pre * (1.0 / math.sqrt(2.0))))
    pdf = jnp.exp(-0.5 * pre * pre) * (1.0 / math.sqrt(2.0 * math.pi))
    return pre * cdf, cdf + pre * pdf


def k1_kernel(
    lens, mask_h, gains_h, biases_h, bias_in_h, x_h, cot_h, wqkv_h, wout_h, win_h, wback_h,
    gi_h, gb_h, full_h, res_h, dres_h, pick_h, pm_h, qm_h, k_h, v_h, cm_h, ctx_h, wal_h, wpl_h, wil_h, wbl_h, pil_h, pbl_h, vec_h,
    mask, gains, biases, bias_in, vec, x, cot, wqkv, wout, win, wback, wp_qkv, wp_out, pwin, pwback, q_o, k_o, v_o, ctx_o, pick_o, wal, wpl, wil, wbl, pil, pbl, gin, gback,
    pm, xm, cotm, qm, ctxm, cml, ctxp, ap, apc, normed, nlow, act, gp, part, rc1, h1, ry1,
    part2, rc2, h2, ry2, full2, full, dres2, d2w, d2x, nxw, nxx, dplow,
    lsem, rsem, ssem,
):
    seqs, rows = 3, SPAN_ROWS
    count = x_h.shape[0]
    length = count // seqs
    total = seqs * rows
    half = total // 2
    heads = ctx_o.shape[1]
    n_heads = heads // HD
    width = x_h.shape[1]
    me = Peers()

    def seq(s):
        return pl.ds(s * length, length)

    small = [
        local(src, dst, ssem.at[k])
        for k, (src, dst) in enumerate(((mask_h, mask), (gains_h, gains), (biases_h, biases), (bias_in_h, bias_in)))
    ]
    loads = [
        local(wqkv_h, wqkv, lsem.at[0]),
        local(wout_h, wout, lsem.at[1]),
    ] + [local(x_h.at[seq(s)], x.at[seq(s)], lsem.at[2 + s]) for s in range(seqs)]
    stores = []

    def keep(src, dst):
        stores.append(local(src, dst, lsem.at[8 + len(stores)]))

    slots = gin.shape[0]
    wo_base = 47 + 2 * slots
    shard = gin.shape[1]
    n_u = slots // 2
    z = me.u
    greet([me.core, me.y, me.x] + [(2 * lax.rem(z + k, n_u) + me.b, me.t) for k in range(1, n_u)])

    out_rows = heads // 2 // seqs

    def out_part(k):
        return pl.ds(pl.multiple_of(me.b * (heads // 2) + k * out_rows, 8), out_rows)

    wo_y = [send(wout_h.at[out_part(k)], wp_out.at[out_part(k)], rsem, wo_base + k, me.y) for k in range(seqs)]
    for load in small:
        load.wait()
    loads[0].wait()
    wal[0:3 * heads, :] = wqkv[...].astype(LOW)
    loads[1].wait()
    wal[3 * heads:, :] = wout[...].astype(LOW)
    loads += [
        local(win_h, win, lsem.at[2 + seqs]),
        local(wback_h, wback, lsem.at[3 + seqs]),
        local(cot_h, cot, lsem.at[4 + seqs]),
    ]
    keep(wal, wal_h)

    def pick_bias(row, k=heads):
        out = jnp.zeros((1, k), F32)
        for slot in range(4):
            piece = biases[row:row + 1, slot * k:(slot + 1) * k]
            out = jnp.where(me.t == slot, piece, out)
        return out

    bias_q, bias_v = pick_bias(0), pick_bias(1)
    hidden = win.shape[1]
    lanes = 128
    bias_h = jnp.concatenate(
        [bias_in[pl.ds(me.t * (hidden // lanes) + j, 1), :] for j in range(hidden // lanes)], axis=1
    )
    upto = (
        lax.broadcasted_iota(jnp.int32, (length, length), 0)
        <= lax.broadcasted_iota(jnp.int32, (length, length), 1)
    ).astype(F32).astype(LOW)
    position = lax.broadcasted_iota(jnp.int32, (1, length), 1)
    slot_of = lax.broadcasted_iota(jnp.int32, (rows, length), 0).astype(F32)
    scale = 1.0 / math.sqrt(HD)
    def project(s):
        loads[2 + s].wait()
        at = seq(s)
        xs = x[at, :]
        q = ((dot(xs, wal[0:heads, :], 1, 1) + bias_q) * scale).astype(LOW)
        k = dot(xs, wal[heads:2 * heads, :], 1, 1).astype(LOW)
        v = (dot(xs, wal[2 * heads:3 * heads, :], 1, 1) + bias_v).astype(LOW)
        q_o[at, :] = q
        k_o[at, :] = k
        v_o[at, :] = v
        parts = length // lanes
        marks = jnp.concatenate([mask[pl.ds(s * parts + j, 1), :] for j in range(parts)], axis=1)
        inside = position < lens[s]
        live = jnp.where(inside, marks, 0).astype(F32)
        rank = dot(jnp.broadcast_to(live, (8, length)).astype(LOW), upto, 1, 0)[0:1] - 1.0
        pick = jnp.where((rank == slot_of) & (live > 0.0), 1.0, 0.0).astype(LOW)
        pick_o[s] = pick
        here = pl.ds(s * rows, rows)
        xm[here, :] = dot(pick, xs, 1, 0)
        qrow = dot(pick, q, 1, 0).astype(LOW)
        qm[here, :] = qrow
        key_bias = jnp.where(inside, 0.0, -1000000000.0)
        pieces = []
        for h in range(n_heads):
            col = slice(h * HD, (h + 1) * HD)
            scores = dot(qrow[:, col], k[:, col], 1, 1) + key_bias
            e = jnp.exp(scores - jnp.max(scores, axis=-1, keepdims=True))
            prob = e / jnp.sum(e, axis=-1, keepdims=True)
            pm[s * n_heads + h] = prob
            pieces.append(dot(prob.astype(LOW), v[:, col], 1, 0))
        low = jnp.concatenate(pieces, axis=1).astype(LOW)
        cml[here, :] = low
        ctxm[here, :] = low.astype(F32)
        return send(ctxm.at[here], ctxp.at[here], rsem, 24 + s, me.y)

    ctx_y, wo_x = [], []
    for s in range(seqs):
        ctx_y.append(project(s))
        wo_y[s].wait()
        wo_x.append(send(wp_out.at[out_part(s)], wp_out.at[out_part(s)], rsem, wo_base + seqs + s, me.x))
    third = heads // 2

    share = 2 * third // n_u

    def share_of(b, u):
        return pl.ds(pl.multiple_of(b * (3 * third) + third + u * share, 8), share)

    def chain_copy(way, s, b, u):
        place = wp_qkv.at[share_of(b, u)]
        k = 29 + (way * (n_u - 1) + s) * 2 + b
        peer = (me.d + 2, me.t) if way == 0 else (me.d - 2, me.t)
        return pltpu.make_async_remote_copy(
            src_ref=place, dst_ref=place, send_sem=rsem.at[0, k], recv_sem=rsem.at[1, k],
            device_id=peer, device_id_type=MESH,
        )

    def chain_cases(s):
        return [
            (way, b, z - s if way == 0 else z + s, (z >= s) if way == 0 else (z + s <= n_u - 1), (z < n_u - 1) if way == 0 else (z > 0))
            for way in range(2) for b in range(2)
        ]

    def chain_step(s):
        for way, b, u, here, edge in chain_cases(s):
            if s > 0:
                pl.when(here)(lambda way=way, b=b, u=u: chain_copy(way, s - 1, b, u).wait_recv())
            if s < n_u - 1:
                pl.when(here & edge)(lambda way=way, b=b, u=u: chain_copy(way, s, b, u).start())

    def chain_sent():
        for s in range(n_u - 1):
            for way, b, u, here, edge in chain_cases(s):
                pl.when(here & edge)(lambda way=way, b=b, u=u, s=s: chain_copy(way, s, b, u).wait_send())

    def attend_all(s):
        at = slice(s * length, (s + 1) * length)
        key_bias = jnp.where(position < lens[s], 0.0, -1000000000.0)
        pieces = []
        for h in range(n_heads):
            col = slice(h * HD, (h + 1) * HD)
            scores = dot(q_o[at, col], k_o[at, col], 1, 1) + key_bias
            e = jnp.exp(scores - jnp.max(scores, axis=-1, keepdims=True))
            prob = (e / jnp.sum(e, axis=-1, keepdims=True)).astype(LOW)
            pieces.append(dot(prob, v_o[at, col], 1, 0))
        ctx_o[at, :] = jnp.concatenate(pieces, axis=1).astype(LOW)

    mine_share = share_of(me.b, z)
    wz_y = send(wqkv.at[mine_share], wp_qkv.at[mine_share], rsem, 27, me.y)
    for ref, out in ((pm, pm_h), (qm, qm_h), (k_o, k_h), (v_o, v_h), (cml, cm_h), (pick_o, pick_h)):
        keep(ref, out)
    for load in loads[2 + seqs:4 + seqs]:
        load.wait()
    wil[...] = win[...].astype(LOW)
    wbl[...] = wback[...].astype(LOW)
    keep(wil, wil_h)
    keep(wbl, wbl_h)
    loads[4 + seqs].wait()
    for s in range(seqs):
        cotm[s * rows:(s + 1) * rows, :] = dot(pick_o[s], cot[s * length:(s + 1) * length, :], 1, 0)
    for copy in wo_x:
        copy.wait()
    for copy in ctx_y:
        copy.wait()
    woq = wp_out[...].astype(LOW)

    def mix(first, second):
        ap[...] = dot(*first, 1, 0) + dot(*second, 1, 0)

    own_part = lambda: (cml[...], wal[3 * heads:, :])
    twin_part = lambda: (ctxp[...].astype(LOW), woq)
    pl.when(me.p == 0)(lambda: mix(own_part(), twin_part()))
    pl.when(me.p == 1)(lambda: mix(twin_part(), own_part()))
    ap_c = send(ap, apc, rsem, 3, me.core)
    wz_y.wait()
    wz_x = send(wp_qkv.at[mine_share], wp_qkv.at[mine_share], rsem, 28, me.x)
    ap_c.wait()
    xm[...] = xm[...] + (ap[...] + apc[...]) + biases[2:3, :]
    keep(xm, res_h)
    unit, inv = normalize(xm[...])
    normed[...] = unit * gains[0:1, :] + biases[3:4, :]
    nlow[...] = normed[...].astype(LOW)
    nxw[...] = nlow[...].astype(F32)
    mine = pl.ds(pl.multiple_of(me.c * half, 8), half)
    other = pl.ds(pl.multiple_of((1 - me.c) * half, 8), half)
    nx_x = send(nxw.at[mine], nxx.at[mine], rsem, 5, me.x)
    for j in range(0, hidden, 256):
        col = slice(j, j + 256)
        a, g = gelu_parts(dot(nlow[...], wil[:, col], 1, 0) + bias_h[:, col])
        act[:, col] = a.astype(LOW)
        gp[:, col] = g
    part[...] = dot(act[...], wbl[...], 1, 1)

    cuts = tuple((start, half // 3) for start in range(0, half, half // 3))

    def all_reduce(src, rc, hs, ry, dst, base, fill, late=None):
        pieces = []
        for k, (start, size) in enumerate(cuts):
            mine_k = pl.ds(pl.multiple_of(me.c * half + start, 8), size)
            other_k = pl.ds(pl.multiple_of((1 - me.c) * half + start, 8), size)
            pieces.append((k, pl.ds(start, size), mine_k, other_k))
        first = [send(src.at[other_k], rc.at[row], rsem, base + k, me.core) for k, row, _, other_k in pieces]
        second, third = [], []
        for k, row, mine_k, _ in pieces:
            first[k].wait()
            hs[row, :] = src[mine_k, :] + rc[row, :]
            second.append(send(hs.at[row], ry.at[row], rsem, base + len(cuts) + k, me.y))
        fill()
        for k, row, mine_k, _ in pieces:
            second[k].wait()
            dst[mine_k, :] = hs[row, :] + ry[row, :]
            third.append(send(dst.at[mine_k], dst.at[mine_k], rsem, base + 2 * len(cuts) + k, me.core))
        if late:
            late()
        for copy in third:
            copy.wait()

    relay = []

    def fill_one():
        wide.append(send(win, pwin, rsem, 22, me.core))
        wz_x.wait()
        chain_step(0)
        attend_all(0)
        attend_all(1)
        nx_x.wait()
        relay.append(send(nxx.at[mine], nxx.at[mine], rsem, 6, me.core))
        chain_step(1)

    wide = []
    all_reduce(part, rc1, h1, ry1, full, 29 + 2 * slots, fill_one)
    relay[0].wait()
    unit, inv = normalize(normed[...] + full[...] + biases[4:5, :])
    grad = cotm[...]
    d_two = norm_back(grad, gains[1:2, :], unit, inv)
    dres2[...] = d_two
    vec[...] = jnp.zeros(vec.shape, F32)
    vec[1:2, :] = row_sum(grad * unit)
    vec[5:6, :] = row_sum(d_two)
    vec[6:7, :] = row_sum(grad)
    d2w[...] = d_two.astype(LOW).astype(F32)
    rows_k = [pl.ds(pl.multiple_of(me.c * half + start, 8), size) for start, size in cuts]
    d2_base = wo_base + 2 * seqs
    d2_x = [send(d2w.at[row], d2x.at[row], rsem, d2_base + k, me.x) for k, row in enumerate(rows_k)]
    keep(dres2, dres_h)
    d2low = d2w[...].astype(LOW)
    for j in range(0, hidden, 256):
        col = slice(j, j + 256)
        d_pre = dot(d2low, wbl[:, col], 1, 0) * gp[:, col]
        vec[8:9, col] = row_sum(d_pre)
        dplow[:, col] = d_pre.astype(LOW)
    part2[...] = dot(dplow[...], wil[...], 1, 1)

    def cut(rows):
        return rows.reshape(slots, shard, rows.shape[1])

    def fill_two():
        wide.append(send(wback, pwback, rsem, 23, me.core))
        attend_all(2)
        chain_step(2)
        keep(ctx_o, ctx_h)
        for j in range(0, hidden, 256):
            col = slice(j, j + 256)
            gin[:, :, col] = cut(dot(nlow[...], dplow[:, col], 0, 0))
            gback[:, :, col] = cut(dot(d2low, act[:, col], 0, 0))
        wide[0].wait()
        pil[...] = pwin[...].astype(LOW)
        keep(pil, pil_h)
        for k, row in enumerate(rows_k):
            d2_x[k].wait()
            relay.append(send(d2x.at[row], d2x.at[row], rsem, d2_base + len(cuts) + k, me.core))

    def other_x():
        for copy in relay[1:]:
            copy.wait()
        nlx = nxx[...].astype(LOW)
        dlx = d2x[...].astype(LOW)
        for j in range(0, hidden, 256):
            col = slice(j, j + 256)
            a, g = gelu_parts(dot(nlx, wil[:, col], 1, 0) + bias_h[:, col])
            d_pre = (dot(dlx, wbl[:, col], 1, 0) * g).astype(LOW)
            gin[:, :, col] += cut(dot(nlx, d_pre, 0, 0))
            gback[:, :, col] += cut(dot(dlx, a.astype(LOW), 0, 0))
        for u in range(slots // 2):
            keep(gin.at[2 * u + me.b], gi_h.at[u])
            keep(gback.at[2 * u + me.b], gb_h.at[u])

    all_reduce(part2, rc2, h2, ry2, full2, 38 + 2 * slots, fill_two, other_x)
    keep(full2, full_h)
    keep(vec, vec_h)
    for step in range(3, n_u):
        chain_step(step)
    for b in range(2):
        start = b * 3 * third
        wpl[start:start + third, :] = jnp.zeros((third, width), LOW)
        rest = slice(start + third, start + 3 * third)
        wpl[rest, :] = wp_qkv[rest, :].astype(LOW)
    wpl[3 * heads:, :] = woq
    keep(wpl, wpl_h)
    wide[1].wait()
    pbl[...] = pwback[...].astype(LOW)
    keep(pbl, pbl_h)
    chain_sent()
    for copy in stores:
        copy.wait()


def k1_call(x, cot, mask, lens, wqkv, wout, win, wback, gains, biases, bias_in, slots):
    count, width = x.shape
    seqs = lens.shape[0]
    heads = wout.shape[0]
    hidden = win.shape[1]
    length = count // seqs
    total = seqs * SPAN_ROWS
    half = total // 2
    units = seqs * (heads // HD)
    any_ = pl.BlockSpec(memory_space=pl.ANY)
    sm = pl.BlockSpec(memory_space=pltpu.SMEM)
    sds = jax.ShapeDtypeStruct
    V = pltpu.VMEM
    wide = lambda r, t=F32: V((r, width), t)
    block = (slots // 2, width // slots, hidden)
    square = sds((width, hidden), LOW)
    out_shape = (
        sds(block, F32), sds(block, F32), sds((total, width), F32), sds((total, width), F32), sds((total, width), F32),
        sds((seqs, SPAN_ROWS, length), LOW), sds((units, SPAN_ROWS, length), F32), sds((total, heads), LOW),
        sds((count, heads), LOW), sds((count, heads), LOW), sds((total, heads), LOW), sds((count, heads), LOW),
        sds((4 * heads, width), LOW), sds((4 * heads, width), LOW), square, square, square, square,
        sds((16, width), F32),
    )
    scratch = [
        V(mask.shape, jnp.int32), V(gains.shape, F32), V(biases.shape, F32), V(bias_in.shape, F32), wide(16),
        wide(count, LOW), wide(count, LOW), wide(3 * heads), wide(heads), V((width, hidden), F32),
        V((width, hidden), F32), wide(3 * heads), wide(heads), V((width, hidden), F32), V((width, hidden), F32),
        V((count, heads), LOW), V((count, heads), LOW), V((count, heads), LOW), V((count, heads), LOW),
        V((seqs, SPAN_ROWS, length), LOW), wide(4 * heads, LOW), wide(4 * heads, LOW), V((width, hidden), LOW), V((width, hidden), LOW),
        V((width, hidden), LOW), V((width, hidden), LOW), V((slots, width // slots, hidden), F32), V((slots, width // slots, hidden), F32),
        V((units, SPAN_ROWS, length), F32), wide(total), wide(total), V((total, heads), LOW),
        V((total, heads), F32), V((total, heads), LOW), V((total, heads), F32), wide(total), wide(total),
        wide(total), wide(total, LOW), V((total, hidden), LOW), V((total, hidden), F32), wide(total), wide(half), wide(half), wide(half),
        wide(total), wide(half), wide(half), wide(half), wide(total), wide(total), wide(total), wide(total), wide(total), wide(total), wide(total),
        V((total, hidden), LOW),
        pltpu.SemaphoreType.DMA((8 + 20 + slots,)), pltpu.SemaphoreType.DMA((2, 53 + 2 * slots + 2 * seqs)), pltpu.SemaphoreType.DMA((4,)),
    ]
    return pl.pallas_call(
        k1_kernel, out_shape=out_shape,
        in_specs=[sm] + [any_] * 10,
        out_specs=(any_,) * len(out_shape),
        scratch_shapes=scratch,
        compiler_params=pltpu.CompilerParams(
            collective_id=1, has_side_effects=True, vmem_limit_bytes=60 * 2**20
        ),
    )(lens, mask, gains, biases, bias_in, x, cot, wqkv, wout, win, wback)


BETA_ONE = 0.9
BETA_TWO = 0.999
ADAM_EPS = 1e-06
WEIGHT_DECAY = 0.01


def adam(weight, grad, first, second, ratio, corr_one, corr_two, decay):
    first = BETA_ONE * first + (1.0 - BETA_ONE) * grad
    second = BETA_TWO * second + (1.0 - BETA_TWO) * grad * grad
    update = first / corr_one / (jnp.sqrt(second / corr_two) + ADAM_EPS) + decay * weight
    return -ratio * update, first, second


FLIGHT = 0.8
PLAN_READY = (1.2, 1.2, 3.2)
SWAP_FIRST = ((0, 0),)
WEIGHT = {("RS", 0, 0): 8.0, ("RS", 1, 0): 7.0, ("RS", 2, 0): -7.0, ("RS", 2, 1): -10.0, ("AG", 0, 0): -10.0}
BLOCK_US = 3.2


def plan(n, weight):
    tasks = {}
    for ch in range(3):
        for p in range(2):
            ready = PLAN_READY[ch]
            swap = ch == 2
            both = (ch, p) in SWAP_FIRST
            for z in range(n):
                if swap:
                    for u in range(n):
                        tasks["XS", ch, p, 0, u, z] = ("X", z), [], ready
                for d in range(n):
                    if d == z:
                        continue
                    step = 1 if d > z else -1
                    kind = "RSR" if d > z else "RSL"
                    need = [(kind, ch, p, 0, d, z - step)] if 0 <= z - step < n else []
                    if swap:
                        need.append(("XS", ch, p, 0, d, z))
                    tasks[kind, ch, p, 0, d, z] = (kind[2], z), need, ready
                end = [("RSR", ch, p, 0, z, z - 1)] if z > 0 else []
                if z < n - 1:
                    end.append(("RSL", ch, p, 0, z, z + 1))
                if swap:
                    end.append(("XS", ch, p, 0, z, z))
                for par in (0, 1) if both else (0,):
                    for u in range(n):
                        if u == z:
                            need = [("AGX", ch, p, 0, z, z)] if par else end
                        else:
                            need = [("AGR", ch, p, par, u, z - 1) if u < z else ("AGL", ch, p, par, u, z + 1)]
                        if u <= z < n - 1:
                            tasks["AGR", ch, p, par, u, z] = ("R", z), need, 0.0
                        if 0 < z <= u:
                            tasks["AGL", ch, p, par, u, z] = ("L", z), need, 0.0
                        if par == 0 and (u == z or not both):
                            tasks["AGX", ch, p, 0, u, z] = ("X", z), need, 0.0
    after = {key: [] for key in tasks}
    for key, (_, need, _) in tasks.items():
        for one in need:
            after[one].append(key)
    rank = {}

    def longest(key):
        if key not in rank:
            rank[key] = 1.0 + FLIGHT + max([longest(k) for k in after[key]], default=0.0)
        return rank[key]

    missing = {key: len(task[1]) for key, task in tasks.items()}
    open_at = {key: task[2] for key, task in tasks.items() if not task[1]}
    free, done, order = {}, {}, []
    while open_at:
        by_link = {}
        for key in open_at:
            by_link.setdefault(tasks[key][0], []).append(key)
        best = None
        for link, keys in by_link.items():
            start = max(free.get(link, 0.0), min(open_at[k] for k in keys))
            able = [k for k in keys if open_at[k] <= start + 1e-9]
            key = max(able, key=lambda k: (longest(k) + weight.get((k[0][:2] if k[0] != "AGX" else "AX", k[1], k[2]), 0.0), -open_at[k]))
            if best is None or start < best[0] - 1e-9:
                best = start, key
        start, key = best
        free[tasks[key][0]] = start + 1.0
        done[key] = start + 1.0 + FLIGHT
        order.append((start, key))
        del open_at[key]
        for k in after[key]:
            missing[k] -= 1
            if missing[k] == 0:
                open_at[k] = max(max(done[q] for q in tasks[k][1]) + 0.15, tasks[k][2])
    return order, tasks, max(done.values())


def k2_kernel(
    lens, step, warmup, horizon, gains_h, biases_h, bias_in_h, vec_h,
    x_h, gi_h, gb_h, full_h, res_h, dtwo_h, pick_h, pm_h, qm_h, k_h, v_h, cm_h, ctx_h, wal_h, wpl_h, wil_h, wbl_h, pil_h, pbl_h,
    wqkv_h, wout_h, win_h, wback_h, mq_h, mo_h, mi_h, mb_h,
    out_h, grad_h, ci_h, cb_h, ca_h, nmq_h, nmo_h, nmi_h, nmb_h, vt_h,
    gains, biases, bias_in, vec, vt, wp, x, ga, gi, gb, dproj, ctx, pick, dres, full, dtwo, pm, qm, ko, vo, cm, dctx, wal, wpl, wil, wbl, pil, pbl,
    wrow_i, wrow_b, wrow_a, mq, mo, mi, mb, turned, flip,
    qp, kp, vp, ctxp, dpp, sbuf, rbuf, nrm, dsc, rdn, fin, rig,
    ring, xr, own, v0, v1, vx, vz,
    lsem, rs_s, rs_r, ag_s, ag_r, ax_s, ax_r, xs_s, xs_r, vs_s, vs_r, sd_s, sd_r, usem, wsem,
):
    me = Peers()
    n_u = gi.shape[0]
    seqs = sbuf.shape[0]
    count, width = x_h.shape
    length = count // seqs
    rows = SPAN_ROWS
    total = seqs * rows
    heads = ctx.shape[1]
    n_heads = heads // HD
    shard = gi.shape[1]
    hidden = wil.shape[1]
    half = length // 2
    quarter = length // 4
    z, b = me.u, me.b
    right = (me.d + 2, me.t)
    left = (me.d - 2, me.t)
    diag = (me.d, 3 - me.t)

    def remote(src, dst, ss, rr, peer):
        return pltpu.make_async_remote_copy(
            src_ref=src, dst_ref=dst, send_sem=ss, recv_sem=rr, device_id=peer, device_id_type=MESH
        )

    pend = {}
    order = iter(range(64))

    def fetch(name, src, dst):
        copy = pltpu.make_async_copy(src, dst, lsem.at[next(order)])
        copy.start()
        pend.setdefault(name, []).append(copy)

    def ready(*names):
        for name in names:
            for copy in pend.pop(name, []):
                copy.wait()

    for src, dst in ((gains_h, gains), (biases_h, biases), (bias_in_h, bias_in), (vec_h, vec)):
        fetch("small", src, dst)
    fetch("one", full_h, full)
    fetch("one", res_h, dres)
    fetch("one", dtwo_h, dtwo)
    fetch("gi", gi_h, gi)
    fetch("gb", gb_h, gb)
    fetch("wal", wal_h, wal)
    mine = pl.ds(pl.multiple_of(me.d * shard, 8), shard)

    def load_second():
        fetch("att", pick_h, pick)
        fetch("att", pm_h, pm)
        fetch("att", qm_h, qm)
        fetch("att", k_h, ko)
        fetch("att", v_h, vo)
        fetch("att", cm_h, cm)
        fetch("x", x_h, x.at[pl.ds(0, count)])

    def load_third():
        fetch("wpl", wpl_h, wpl)
        fetch("ctx", ctx_h, ctx)
        fetch("low", wil_h, wil)
        fetch("low", wbl_h, wbl)
        fetch("low", pil_h, pil)
        fetch("low", pbl_h, pbl)
        fetch("mi", win_h.at[mine], wrow_i)
        fetch("mi", mi_h, mi)
        fetch("mb", wback_h.at[mine], wrow_b)
        fetch("mb", mb_h, mb)
        fetch("ma", wqkv_h, turned.at[pl.ds(0, 3 * heads)])
        fetch("ma", wout_h, turned.at[pl.ds(3 * heads, heads)])
        fetch("ma", mq_h, mq)
        fetch("ma", mo_h, mo)


    others = [(2 * lax.rem(z + k, n_u) + b, me.t) for k in range(1, n_u)]
    greet([me.core, me.y, diag, me.x] + others)

    third = heads // 2

    def first_third(k):
        return remote(wqkv_h.at[pl.ds(k * 3 * third, third)], wp.at[k], wsem.at[0, k], wsem.at[1, k], me.y)

    order_all, tasks, _ = plan(n_u, WEIGHT)
    part_rows = shard // 2

    def rows_of(p):
        return pl.ds(p * part_rows, part_rows)

    def g_at(ch, u):
        return ga.at[2 * u + b] if ch == 2 else (gi, gb)[ch].at[u]

    def target(ch, d):
        return (ci_h, cb_h, ca_h)[ch].at[d]

    def xr_at(u, p):
        return xr.at[u, rows_of(p)]

    def ring_at(key):
        kind, ch, p, _, d, node = key
        place = d - (node + 1) if kind == "RSR" else (node - 1) - d
        return ring.at[ch, 0 if kind == "RSR" else 1, place, rows_of(p)]

    def transfer(key, incoming):
        kind, ch, p, par, u, node = key
        way = 0 if kind[2:] == "R" else 1
        if kind == "XS":
            k = p * n_u + u
            return remote(ga.at[2 * u + 1 - b, rows_of(p)], xr_at(u, p), xs_s.at[k], xs_r.at[k], me.x)
        if kind[:2] == "RS":
            k = ((ch * 2 + p) * 2 + way) * n_u + u
            peer = right if way == 0 else left
            return remote(g_at(ch, u).at[rows_of(p)], ring_at(key), rs_s.at[k], rs_r.at[k], peer)
        parity = b if (par == 0) != (incoming and kind == "AGX") else 1 - b
        there = target(ch, 2 * u + parity).at[rows_of(p)]
        here = own.at[ch, rows_of(p)] if u == node and par == 0 else there
        if kind == "AGX":
            k = (ch * 2 + p) * n_u + u
            return remote(here, there, ax_s.at[k], ax_r.at[k], me.x)
        k = (((ch * 2 + p) * 2 + way) * 2 + par) * n_u + u
        return remote(here, there, ag_s.at[k], ag_r.at[k], right if way == 0 else left)

    ratio, corr_one, corr_two = rates(step, warmup, horizon)

    def own_copy(ch, p):
        return pltpu.make_async_copy(own.at[ch, rows_of(p)], target(ch, me.d).at[rows_of(p)], usem.at[ch * 2 + p])

    def update(ch, p):
        at_p = rows_of(p)
        if ch < 2:
            w, m = ((wrow_i, mi), (wrow_b, mb))[ch]
            change, first, second = adam(
                w[at_p, :], g_at(ch, z)[at_p, :], m[0, at_p, :], m[1, at_p, :], ratio, corr_one, corr_two, WEIGHT_DECAY
            )
            own[ch, at_p, :] = change
            m[0, at_p, :] = first
            m[1, at_p, :] = second
        else:
            for k in range(4):
                col = slice(k * heads, (k + 1) * heads)
                first = mo[0, at_p, :] if k == 3 else mq[0, k, at_p, :]
                second = mo[1, at_p, :] if k == 3 else mq[1, k, at_p, :]
                change, first, second = adam(
                    wrow_a[at_p, col], ga[me.d, at_p, col], first, second, ratio, corr_one, corr_two, WEIGHT_DECAY
                )
                own[2, at_p, col] = change
                if k < 3:
                    mq[0, k, at_p, :] = first
                    mq[1, k, at_p, :] = second
                else:
                    mo[0, at_p, :] = first
                    mo[1, at_p, :] = second
        own_copy(ch, p).start()

    queue = [[] for _ in range(n_u)]
    inbound = [[] for _ in range(n_u)]
    for start, key in order_all:
        kind, node = key[0], key[5]
        queue[node].append((start * BLOCK_US, key))
        goes = node if kind in ("XS", "AGX") else node + 1 if kind[2] == "R" else node - 1
        inbound[goes].append(key)
    for node in range(n_u):
        queue[node].sort(key=lambda one: one[0])
    got = [set() for _ in range(n_u)]
    made = [set() for _ in range(n_u)]
    sent = [[] for _ in range(n_u)]

    def arrive(node, key):
        if key in got[node]:
            return
        got[node].add(key)
        transfer(key, True).wait_recv()
        kind, ch, p, _, u, _ = key
        if kind == "XS":
            ga[2 * u + b, rows_of(p)] += xr_at(u, p)[...]
        elif kind[:2] == "RS":
            g_at(ch, u)[rows_of(p), :] += ring_at(key)[...]

    def act(node, key):
        for need in tasks[key][1]:
            arrive(node, need)
        kind, ch, p, par, u, _ = key
        if kind[:2] == "AG" and u == node and par == 0 and (ch, p) not in made[node]:
            made[node].add((ch, p))
            update(ch, p)
        sent[node].append(key)
        transfer(key, False).start()

    def chain_until(until):
        for node in range(n_u):
            due = [key for start, key in queue[node] if start < until]
            queue[node] = [one for one in queue[node] if one[0] >= until]
            if due:
                pl.when(z == node)(lambda node=node, due=due: [act(node, key) for key in due] and None)

    def chain_end():
        for node in range(n_u):
            def settle(node=node):
                for key in inbound[node]:
                    arrive(node, key)
                for key in sent[node]:
                    transfer(key, False).wait_send()
            pl.when(z == node)(settle)
        for ch in range(3):
            for p in range(2):
                own_copy(ch, p).wait()

    def vec_x():
        return remote(v0, vx, vs_s.at[0], vs_r.at[0], me.x)

    def vec_z(k):
        peer = (2 * lax.rem(z + k, n_u) + b, me.t)
        return remote(v1, vz.at[z], vs_s.at[k], vs_r.at[k], peer)

    def vec_t(k, peer):
        return remote(v1, vt.at[me.t], vs_s.at[n_u + k], vs_r.at[n_u + k], peer)

    trio = (me.core, me.y, diag)

    def vectors_one():
        vec_x().wait()
        v1[...] = v0[...] + vx[...]
        vz[z] = v1[...]
        for k in range(1, n_u):
            vec_z(k).start()

    def vectors_two():
        for k in range(1, n_u):
            vec_z(k).wait()
        total = vz[0]
        for u in range(1, n_u):
            total = total + vz[u]
        v1[...] = total
        vt[me.t] = total
        for k, peer in enumerate(trio):
            vec_t(k, peer).start()

    def vectors_three():
        for k, peer in enumerate(trio):
            vec_t(k, peer).wait()
        fetch("out", vt, vt_h)

    lanes = 128

    def hidden_bias(slot):
        parts = hidden // lanes
        return jnp.concatenate([bias_in[pl.ds(slot * parts + j, 1), :] for j in range(parts)], axis=1)

    twin = lax.rem(me.t + 2, 4)

    def first_norm_back():
        d_normed = full[...] + dtwo[...]
        unit, inv = normalize(dres[...])
        d_one = norm_back(d_normed, gains[0:1, :], unit, inv)
        dres[...] = d_one
        v0[...] = vec[...]
        v0[0:1, :] = row_sum(d_normed * unit)
        v0[3:4, :] = row_sum(d_one)
        v0[4:5, :] = row_sum(d_normed)
        low = d_one.astype(LOW)
        x[count:count + total, :] = low
        dctx[...] = dot(low, wal[3 * heads:, :], 1, 1).astype(LOW)

    def attend_back(q, k, v, dc, probs, pick_s):
        dqs, dks, dvs = [], [], []
        for h in range(n_heads):
            col = slice(h * HD, (h + 1) * HD)
            prob = probs(h)
            d_prob = dot(dc[:, col], v[:, col], 1, 1)
            dvs.append(dot(prob.astype(LOW), dc[:, col], 0, 0))
            ds = (prob * (d_prob - jnp.sum(prob * d_prob, axis=-1, keepdims=True))).astype(LOW)
            dqs.append(dot(ds, k[:, col], 1, 0) * scale)
            dks.append(dot(ds, q[:, col], 0, 0))
        dq = jnp.concatenate(dqs, axis=1)
        dv = jnp.concatenate(dvs, axis=1)
        spread = dot(pick_s, dq.astype(LOW), 0, 0).astype(LOW)
        return jnp.concatenate([spread, jnp.concatenate(dks, axis=1).astype(LOW), dv.astype(LOW)], axis=1), dq, dv

    def own_back(s):
        here = slice(s * rows, (s + 1) * rows)
        low, dq, dv = attend_back(
            qm[here, :], ko.at[at(s)], vo.at[at(s)], dctx[here, :], lambda h: pm[s * n_heads + h], pick[s]
        )
        dproj[at(s), 0:3 * heads] = low
        dproj[at(s), 3 * heads:] = jnp.zeros((length, heads), LOW)
        sums = jnp.concatenate([row_sum(dq), row_sum(dv)], axis=1)
        v0[2:3, 0:2 * heads] = sums if s == 0 else v0[2:3, 0:2 * heads] + sums

    def weight_grads(j):
        if j == 0:
            dproj[count:count + total, 0:3 * heads] = jnp.zeros((total, 3 * heads), LOW)
            dproj[count:count + total, 3 * heads:] = cm[...]
        col = slice(j * 256, (j + 1) * 256)
        ga[:, :, col] = dot(x[...], dproj[:, col], 0, 0).reshape(2 * n_u, shard, 256)

    def twin_rows():
        dctx[...] = dot(x[count:count + total, :], wpl[3 * heads:, :], 1, 1).astype(LOW)

    def pick_bias(row):
        out = jnp.zeros((1, heads), F32)
        for slot in range(4):
            out = jnp.where(twin == slot, biases[row:row + 1, slot * heads:(slot + 1) * heads], out)
        return out

    scale = 1.0 / math.sqrt(HD)
    position = lax.broadcasted_iota(jnp.int32, (1, length), 1)
    my_half = pl.ds(pl.multiple_of(me.c * half, 8), half)
    its_half = pl.ds(pl.multiple_of((1 - me.c) * half, 8), half)
    my_quarter = pl.ds(pl.multiple_of(me.p * quarter, 8), quarter)
    its_quarter = pl.ds(pl.multiple_of((1 - me.p) * quarter, 8), quarter)

    def at(s, start=0, size=None):
        return pl.ds(pl.multiple_of(s * length + start, 8), size or length)

    def key_bias(s):
        return jnp.where(position < lens[s], 0.0, -1000000000.0)

    def project(s):
        xs = x[at(s), :]
        qp[...] = ((dot(xs, wpl[0:heads, :], 1, 1) + pick_bias(0)) * scale).astype(LOW)
        kp[...] = dot(xs, wpl[heads:2 * heads, :], 1, 1).astype(LOW)
        vp[...] = (dot(xs, wpl[2 * heads:3 * heads, :], 1, 1) + pick_bias(1)).astype(LOW)

    def attend_one(s, h):
        col = slice(h * HD, (h + 1) * HD)
        e = dot(qp[:, col], kp[:, col], 1, 1) + key_bias(s)
        e = jnp.exp(e - jnp.max(e, axis=-1, keepdims=True))
        prob = (e / jnp.sum(e, axis=-1, keepdims=True)).astype(LOW)
        ctxp[:, col] = dot(prob, vp[:, col], 1, 0).astype(LOW)

    def mix_copy(s):
        return remote(sbuf.at[s], rbuf.at[s], sd_s.at[s], sd_r.at[s], me.core)

    def mix(s):
        for where, into in ((its_half, sbuf), (my_half, nrm)):
            base = at(s, where.start, half)
            into[s] = dot(ctx[base, :], wal[3 * heads:, :], 1, 0) + dot(ctxp[where, :], wpl[3 * heads:, :], 1, 0)
        mix_copy(s).start()

    def down_copy(s):
        return remote(dsc.at[s, its_quarter], rdn.at[s], sd_s.at[seqs + s], sd_r.at[seqs + s], me.y)

    def feed_start(s):
        mix_copy(s).wait()
        base = at(s, me.c * half, half)
        unit, _ = normalize(x[base, :].astype(F32) + (nrm[s] + rbuf[s]) + biases[2:3, :])
        nrm[s] = unit * gains[0:1, :] + biases[3:4, :]

    def feed(s, part):
        w_in, w_back, slot = ((wil, wbl, me.t), (pil, pbl, me.t + 1 - 2 * me.c))[part]
        low = nrm[s].astype(LOW)
        bias = hidden_bias(slot)
        total = dsc[s] if part else jnp.zeros((half, width), F32)
        for j in range(0, hidden, 256):
            col = slice(j, j + 256)
            pre = dot(low, w_in[:, col], 1, 0) + bias[:, col]
            act_low = pre * (0.5 * (1.0 + lax.erf(pre * (1.0 / math.sqrt(2.0)))))
            total = total + dot(act_low.astype(LOW), w_back[:, col], 1, 1)
        dsc[s] = total
        if part:
            down_copy(s).start()

    def out_rows(s, p):
        return at(s, me.c * half + p * quarter, quarter)

    def out_copy(s, k, p, peer):
        src = fin.at[s] if k < 2 else out_h.at[out_rows(s, p)]
        return remote(src, out_h.at[out_rows(s, me.p if k < 2 else p)], sd_s.at[(2 + k) * seqs + s], sd_r.at[(2 + k) * seqs + s], peer)

    def finish(s):
        down_copy(s).wait()
        res = nrm[s, my_quarter] + (dsc[s, my_quarter] + rdn[s]) + biases[4:5, :]
        unit, _ = normalize(res)
        fin[s] = (unit * gains[1:2, :] + biases[5:6, :]).astype(LOW).astype(F32)
        fetch("out", fin.at[s], out_h.at[out_rows(s, me.p)])
        out_copy(s, 0, me.p, me.y).start()
        out_copy(s, 1, me.p, me.core).start()

    def relay(s):
        out_copy(s, 0, me.p, me.y).wait()
        out_copy(s, 2, 1 - me.p, me.core).start()

    def relay_end(s):
        out_copy(s, 1, me.p, me.core).wait()
        out_copy(s, 2, 1 - me.p, me.core).wait()

    def back(s):
        here = slice(s * rows, (s + 1) * rows)
        q = dot(pick[s], qp[...], 1, 0).astype(LOW)
        dc = dctx[here, :]

        def probs(h):
            col = slice(h * HD, (h + 1) * HD)
            scores = dot(q[:, col], kp[:, col], 1, 1) + key_bias(s)
            e = jnp.exp(scores - jnp.max(scores, axis=-1, keepdims=True))
            return e / jnp.sum(e, axis=-1, keepdims=True)

        dpp[...] = attend_back(q, kp, vp, dc, probs, pick[s])[0]

    def entry_copy(s):
        return remote(sbuf.at[s], rig.at[s], sd_s.at[5 * seqs + s], sd_r.at[5 * seqs + s], me.core)

    def entry(s):
        for where, into in ((its_half, sbuf), (my_half, rbuf)):
            base = at(s, where.start, half)
            product = lambda a, w: dot(a, w[0:3 * heads, :], 1, 0)

            def add(low, high, s=s, into=into):
                into[s] = product(*low) + product(*high)

            own_part = lambda base=base: (dproj[base, 0:3 * heads], wal)
            twin_part = lambda where=where: (dpp[where, :], wpl)
            pl.when(me.p == 0)(lambda add=add, a=own_part, b=twin_part: add(a(), b()))
            pl.when(me.p == 1)(lambda add=add, a=own_part, b=twin_part: add(b(), a()))
        entry_copy(s).start()

    def grad_rows(s):
        return at(s, me.c * half, half)

    def grad_copy(s):
        return remote(rbuf.at[s], grad_h.at[grad_rows(s)], sd_s.at[6 * seqs + s], sd_r.at[6 * seqs + s], me.core)

    def entry_end(s):
        entry_copy(s).wait()
        d_one = dres[pl.ds(s * rows, rows), :]
        high = d_one.astype(LOW)
        rest = (d_one - high.astype(F32)).astype(LOW)
        some = pick[s, :, pl.ds(pl.multiple_of(me.c * half, lanes), half)]
        rbuf[s] = (rbuf[s] + rig[s]) + (dot(some, high, 0, 0) + dot(some, rest, 0, 0))
        fetch("out", rbuf.at[s], grad_h.at[grad_rows(s)])
        grad_copy(s).start()

    def turn_weights():
        for j in range(0, width, lanes):
            flip[...] = turned[j:j + lanes, :].T
            wrow_a[:, j:j + lanes] = flip[mine, :]

    def begin():
        for k in range(2):
            first_third(k).start()
        ready("gi", "gb")
        load_second()

    def own_start():
        ready("small", "one", "wal")
        first_norm_back()
        ready("att")
        load_third()

    def moments_in():
        ready("mi", "mb", "ma")
        turn_weights()

    def twin_start():
        ready("wpl", "ctx", "low")
        for k in range(2):
            first_third(k).wait()
            wpl[k * 3 * third:k * 3 * third + third, :] = wp[k].astype(LOW)
        twin_rows()

    work = [(0.0, begin), (4.4, own_start)]
    work += [(5.4 + s, lambda s=s: own_back(s)) for s in range(seqs)]
    work += [(8.4, lambda: ready("x"))] + [(8.5 + 0.7 * j, lambda j=j: weight_grads(j)) for j in range(width // 256)]
    work += [(10.7, lambda: vec_x().start()), (14.0, moments_in), (20.0, vectors_one), (28.0, vectors_two)]
    first_twin = 24.0
    for s in range(seqs):
        t = first_twin + 20.0 * s
        work += [(t, lambda s=s: (twin_start() if s == 0 else None, project(s)) and None)]
        work += [(t + 1.5 + h, lambda s=s, h=h: attend_one(s, h)) for h in range(n_heads)]
        work += [(t + 5.0, lambda s=s: mix(s)), (t + 5.5, lambda s=s: back(s)), (t + 7.5, lambda s=s: feed_start(s))]
        work += [(t + 8.0, lambda s=s: feed(s, 0)), (t + 9.5, lambda s=s: feed(s, 1)), (t + 11.0, lambda s=s: entry(s))]
        work += [(t + 24.0, lambda s=s: finish(s)), (t + 40.0, lambda s=s: relay(s)), (t + 20.0, lambda s=s: entry_end(s))]
    work += [(40.0, vectors_three)]
    for when, do in sorted(work, key=lambda one: one[0]):
        chain_until(when)
        do()
    for when in range(80, 120, 2):
        chain_until(float(when))
    chain_until(1e9)
    for s in range(seqs):
        relay_end(s)
        grad_copy(s).wait()
    for ref, out in ((mi, nmi_h), (mb, nmb_h), (mq, nmq_h), (mo, nmo_h)):
        fetch("out", ref, out)
    chain_end()
    ready("out")


def k2_call(lens, step, warmup, horizon, gains, biases, bias_in, k1, x, weights, moments):
    wqkv, wout, win, wback = weights
    count, width = x.shape
    seqs = lens.shape[0]
    heads, hidden = wout.shape[0], win.shape[1]
    length = count // seqs
    half, quarter = length // 2, length // 4
    shard = moments[1].shape[1]
    slots = width // shard
    n_u = slots // 2
    total = seqs * SPAN_ROWS
    units = seqs * (heads // HD)
    any_ = pl.BlockSpec(memory_space=pl.ANY)
    vm = pl.BlockSpec(memory_space=pltpu.VMEM)
    sm = pl.BlockSpec(memory_space=pltpu.SMEM)
    sds = lambda *shape: jax.ShapeDtypeStruct(shape, F32)
    V = lambda *shape: pltpu.VMEM(shape, F32)
    B = lambda *shape: pltpu.VMEM(shape, LOW)
    D = pltpu.SemaphoreType.DMA
    out_shape = (
        sds(count, width), sds(count, width), sds(slots, shard, hidden), sds(slots, shard, hidden), sds(slots, shard, width),
        sds(*moments[0].shape), sds(*moments[1].shape), sds(*moments[2].shape), sds(*moments[3].shape), sds(4, 16, width),
    )
    scratch = [
        V(*gains.shape), V(*biases.shape), V(*bias_in.shape), V(16, width), V(4, 16, width), V(2, heads // 2, width),
        B(count + total, width), V(slots, shard, width), V(n_u, shard, hidden), V(n_u, shard, hidden),
        B(count + total, width), B(count, heads), B(seqs, SPAN_ROWS, length), V(total, width),
        V(total, width), V(total, width), V(units, SPAN_ROWS, length), B(total, heads), B(count, heads), B(count, heads), B(total, heads), B(total, heads),
        B(width, width), B(width, width), B(width, hidden), B(width, hidden), B(width, hidden), B(width, hidden),
        V(shard, hidden), V(shard, hidden), V(shard, width),
        V(*moments[0].shape), V(*moments[1].shape), V(*moments[2].shape), V(*moments[3].shape), V(width, width), V(width, 128),
        B(length, heads), B(length, heads), B(length, heads), B(length, heads), B(length, 3 * heads),
        V(seqs, half, width), V(seqs, half, width), V(seqs, half, width), V(seqs, half, width),
        V(seqs, quarter, width), V(seqs, quarter, width), V(seqs, half, width),
        V(3, 2, n_u - 1, shard, width), V(n_u, shard, width), V(3, shard, width),
        V(16, width), V(16, width), V(16, width), V(n_u, 16, width),
        D((64,)), D((12 * n_u,)), D((12 * n_u,)), D((24 * n_u,)), D((24 * n_u,)), D((6 * n_u,)), D((6 * n_u,)),
        D((2 * n_u,)), D((2 * n_u,)), D((n_u + 3,)), D((n_u + 3,)), D((7 * seqs,)), D((7 * seqs,)), D((6,)), D((2, 2)),
    ]
    return pl.pallas_call(
        k2_kernel, out_shape=out_shape,
        in_specs=[sm] * 4 + [any_] * 31,
        out_specs=(any_,) * 10,
        scratch_shapes=scratch,
        compiler_params=pltpu.CompilerParams(collective_id=2, has_side_effects=True, vmem_limit_bytes=63 * 2**20),
    )(
        lens, step, warmup, horizon, gains, biases, bias_in, k1[-1], x, *k1[:-1], wqkv, wout, win, wback, *moments,
    )


def rates(step, warmup, horizon):
    clock = jnp.full((1, 128), step[0].astype(F32))
    warm = jnp.full((1, 128), warmup[0].astype(F32))
    far = jnp.full((1, 128), horizon[0].astype(F32))
    ratio = jnp.minimum(clock / warm, (far - clock) / (far - warm))[:, 0:1]
    return ratio, (1.0 - jnp.exp(clock * math.log(0.9)))[:, 0:1], (1.0 - jnp.exp(clock * math.log(0.999)))[:, 0:1]


def k3_kernel(step, warmup, horizon, *refs):
    n_big, n_small = 9, 7
    (out_h, grad_h, ci_h, cb_h, ca_h, *moms_h), refs = refs[:n_big], refs[n_big:]
    small_h, refs = refs[:n_small], refs[n_small:]
    (normed_o, grad_o, ci_o, cb_o, cq_o, co_o, *moms_o), refs = refs[:n_big + 1], refs[n_big + 1:]
    small_o, refs = refs[:6], refs[6:]
    (wide, low, turned, grad, ci, cb, ca, *moms), refs = refs[:n_big + 2], refs[n_big + 2:]
    (gains, biases, bias_in, mom_g, mom_b, mom_h, vt), refs = refs[:n_small], refs[n_small:]
    (ch_g, ch_b, ch_h, nm_g, nm_b, nm_h), (rsem, wsem) = refs[:6], refs[6:]
    chunks, size = wide.shape[:2]
    reads, copies = [], []

    def read(src, dst):
        copy = pltpu.make_async_copy(src, dst, rsem.at[len(reads)])
        copy.start()
        reads.append(copy)
        return copy

    def write(src, dst):
        copy = pltpu.make_async_copy(src, dst, wsem.at[len(copies)])
        copy.start()
        copies.append(copy)

    rows = [pl.ds(j * size, size) for j in range(chunks)]

    def pieces(src, buf, dst, n):
        step = src.shape[0] // n
        cuts = [pl.ds(j * step, step) for j in range(n)]
        return [(read(src.at[cut], buf.at[cut]), buf.at[cut], dst.at[cut]) for cut in cuts]

    first = pieces(grad_h, grad, grad_o, 4)
    got_ca = read(ca_h, ca)
    second = pieces(ci_h, ci, ci_o, 2) + pieces(cb_h, cb, cb_o, 2)
    got = [read(out_h.at[row], wide.at[j]) for j, row in enumerate(rows)]
    got_small = [read(src, dst) for src, dst in zip(small_h, (gains, biases, bias_in, mom_g, mom_b, mom_h, vt))]
    last = [(read(src, buf), buf, dst) for src, buf, dst in zip(moms_h, moms, moms_o)]
    for copy, buf, dst in first:
        copy.wait()
        write(buf, dst)
    got_ca.wait()
    width = turned.shape[1]
    lanes = 128
    for j in range(0, width, lanes):
        turned[j:j + lanes, :] = ca[:, :, j:j + lanes].reshape(width, lanes).T
    split = cq_o.shape[0]
    write(turned.at[pl.ds(0, split)], cq_o)
    write(turned.at[pl.ds(split, width - split)], co_o)
    for copy, buf, dst in second:
        copy.wait()
        write(buf, dst)
    for j, row in enumerate(rows):
        got[j].wait()
        low[j] = wide[j].astype(LOW)
        write(low.at[j], normed_o.at[row])
    for copy in got_small:
        copy.wait()
    put = (*rates(step, warmup, horizon), 0.0)
    heads = gains.shape[1] // 4
    hidden = vt.shape[2]
    common = vt[0]
    ch_g[...], nm_g[0], nm_g[1] = adam(gains[...], common[0:2], mom_g[0], mom_g[1], *put)
    query = jnp.concatenate([vt[k][2:3, 0:heads] for k in range(4)], axis=1)
    value = jnp.concatenate([vt[k][2:3, heads:2 * heads] for k in range(4)], axis=1)
    for row in range(6):
        grad_row = query if row == 0 else value if row == 1 else common[row + 1:row + 2]
        change, first, second = adam(biases[row:row + 1, :], grad_row, mom_b[row, 0:1], mom_b[row, 1:2], *put)
        ch_b[row:row + 1, :] = change
        nm_b[row, 0:1] = first
        nm_b[row, 1:2] = second
    parts = hidden // lanes
    for k in range(4):
        col = slice(k * hidden, (k + 1) * hidden)
        bias = jnp.concatenate([bias_in[k * parts + j:k * parts + j + 1, :] for j in range(parts)], axis=1)
        change, first, second = adam(bias, vt[k][8:9, :], mom_h[0:1, col], mom_h[1:2, col], *put)
        nm_h[0:1, col] = first
        nm_h[1:2, col] = second
        for j in range(parts):
            ch_h[k * parts + j:k * parts + j + 1, :] = change[:, j * lanes:(j + 1) * lanes]
    for src, dst in zip((ch_g, ch_b, ch_h, nm_g, nm_b, nm_h), small_o):
        write(src, dst)
    for copy, buf, dst in last:
        copy.wait()
        write(buf, dst)
    for copy in copies:
        copy.wait()


def k3_call(step, warmup, horizon, gains, biases, bias_in, mom_g, mom_b, mom_h, vt, big, heads):
    any_ = pl.BlockSpec(memory_space=pl.ANY)
    sm = pl.BlockSpec(memory_space=pltpu.SMEM)
    of = lambda a: jax.ShapeDtypeStruct(a.shape, a.dtype)
    held = lambda a: pltpu.VMEM(a.shape, F32)
    count, width = big[0].shape
    chunks = 6
    small = (gains, biases, bias_in, mom_g, mom_b, mom_h)
    sds = lambda *shape: jax.ShapeDtypeStruct(shape, F32)
    out_shape = (
        jax.ShapeDtypeStruct((count, width), LOW), *map(of, big[1:4]), sds(3 * heads, width), sds(heads, width),
        *map(of, big[5:]), *map(of, small),
    )
    return pl.pallas_call(
        k3_kernel,
        out_shape=out_shape,
        in_specs=[sm] * 3 + [any_] * (len(big) + 7),
        out_specs=(any_,) * len(out_shape),
        scratch_shapes=[
            pltpu.VMEM((chunks, count // chunks, width), F32), pltpu.VMEM((chunks, count // chunks, width), LOW),
            pltpu.VMEM((width, width), F32), *map(held, big[1:]), *map(held, small), held(vt), *map(held, small),
            pltpu.SemaphoreType.DMA((32,)), pltpu.SemaphoreType.DMA((32,)),
        ],
        compiler_params=pltpu.CompilerParams(vmem_limit_bytes=62 * 2**20),
    )(step, warmup, horizon, *big, *small, vt)


def fast(tokens_in, cotangent, span_mask, lengths, step, warmup, total, w_qkv, w_out, w_in, w_back, gains, biases, bias_in,
         mom_qkv, mom_out, mom_in, mom_back, mom_gains, mom_biases, mom_bias_in):
    width = tokens_in.shape[1]
    heads, hidden = w_out.shape[1], w_in.shape[1]
    wqkv_t = jnp.transpose(w_qkv, (1, 2, 0)).reshape(3 * heads, width)
    wout_t = w_out.T
    bias_tiles = bias_in.reshape(-1, 128)
    k1 = k1_call(
        tokens_in, cotangent, span_mask.reshape(-1, 128), lengths, wqkv_t, wout_t, w_in, w_back, gains, biases, bias_tiles,
        width // mom_out.shape[1]
    )
    *big, vt = k2_call(
        lengths, step, warmup, total, gains, biases, bias_tiles, k1, tokens_in, (wqkv_t, wout_t, w_in, w_back),
        (jnp.transpose(mom_qkv, (0, 2, 1, 3)), mom_out, mom_in, mom_back)
    )
    (
        out, grad, ci, cb, cq, co, nmq, nmo, nmi, nmb, ch_g, ch_b, ch_h, nm_g, nm_b, nm_h
    ) = k3_call(
        step, warmup, total, gains, biases, bias_tiles, mom_gains, jnp.transpose(mom_biases, (1, 0, 2)), mom_bias_in, vt, big, heads
    )
    return (
        out, grad, jnp.transpose(cq.reshape(3, heads, width), (2, 0, 1)), co.T,
        ci.reshape(width, hidden), cb.reshape(width, hidden), ch_g, ch_b, ch_h.reshape(-1),
        jnp.transpose(nmq, (0, 2, 1, 3)), nmo, nmi, nmb, nm_g, jnp.transpose(nm_b, (1, 0, 2)), nm_h,
    )


def layer_norm(values, gain, shift):
    center = values - jnp.mean(values, axis=-1, keepdims=True)
    spread = jnp.mean(center * center, axis=-1, keepdims=True)
    return center * lax.rsqrt(spread + NORM_EPS) * gain + shift


def exact_gelu(values):
    return jax.nn.gelu(values, approximate=False)


def outer_sum(left, right):
    return jnp.einsum("ta,tb->ab", left, right, preferred_element_type=jnp.float32)


def adam_step(weight, grad, moments, ratio, corr_one, corr_two, decay):
    first = BETA_ONE * moments[0] + (1.0 - BETA_ONE) * grad
    second = BETA_TWO * moments[1] + (1.0 - BETA_TWO) * grad * grad
    update = first / corr_one / (jnp.sqrt(second / corr_two) + ADAM_EPS) + decay * weight
    return (-ratio * update, jnp.stack([first, second]))


def on_device(
    tokens_in,
    cotangent,
    span_mask,
    lengths,
    step,
    warmup,
    total,
    w_qkv,
    w_out,
    w_in,
    w_back,
    gains,
    biases,
    bias_in,
    mom_qkv,
    mom_out,
    mom_in,
    mom_back,
    mom_gains,
    mom_biases,
    mom_bias_in,
):
    row_count, model_width = tokens_in.shape
    if mom_out.shape[1] % 8 == 0:
        return fast(
            tokens_in, cotangent, span_mask, lengths, step, warmup, total, w_qkv, w_out, w_in, w_back, gains, biases,
            bias_in, mom_qkv, mom_out, mom_in, mom_back, mom_gains, mom_biases, mom_bias_in
        )
    seq_count = lengths.shape[0]
    seq_length = row_count // seq_count
    head_cols = w_qkv.shape[2]
    hidden_cols = w_in.shape[1]
    head_size = HD
    local_heads = head_cols // head_size
    query_scale = 1.0 / math.sqrt(head_size)
    tensor_slot = lax.axis_index("tensor")
    bias_query = lax.dynamic_slice_in_dim(biases[0], tensor_slot * head_cols, head_cols)
    bias_value = lax.dynamic_slice_in_dim(biases[1], tensor_slot * head_cols, head_cols)
    bias_hidden = lax.dynamic_slice_in_dim(bias_in, tensor_slot * hidden_cols, hidden_cols)
    qkv_low = w_qkv.astype(jnp.bfloat16).reshape(model_width, 3 * head_cols)
    out_low = w_out.astype(jnp.bfloat16)
    in_low = w_in.astype(jnp.bfloat16)
    down_low = w_back.astype(jnp.bfloat16)
    projected = jnp.dot(tokens_in, qkv_low, preferred_element_type=jnp.float32).reshape(
        row_count, 3, head_cols
    )
    attn_shape = (seq_count, seq_length, local_heads, head_size)
    queries = (
        ((projected[:, 0] + bias_query) * query_scale).astype(jnp.bfloat16).reshape(attn_shape)
    )
    keys = projected[:, 1].astype(jnp.bfloat16).reshape(attn_shape)
    values = (projected[:, 2] + bias_value).astype(jnp.bfloat16).reshape(attn_shape)
    positions = jnp.arange(seq_length, dtype=jnp.int32)
    inside = positions[None, :] < lengths[:, None]
    key_bias = jnp.where(inside, 0.0, -1000000000.0).astype(jnp.float32)

    def score_block():
        raw = jnp.einsum("sqhd,skhd->shqk", queries, keys, preferred_element_type=jnp.float32)
        return raw + key_bias[:, None, None, :]

    scores = score_block()
    peak = jnp.max(scores, axis=-1, keepdims=True)
    log_total = peak + jnp.log(jnp.sum(jnp.exp(scores - peak), axis=-1, keepdims=True))
    probs_low = jnp.exp(scores - log_total).astype(jnp.bfloat16)
    context_low = (
        jnp.einsum("shqk,skhd->sqhd", probs_low, values, preferred_element_type=jnp.float32)
        .reshape(row_count, head_cols)
        .astype(jnp.bfloat16)
    )
    attn_part = jnp.einsum("tc,dc->td", context_low, out_low, preferred_element_type=jnp.float32)
    attn_sum = lax.psum(attn_part, "tensor")
    residual_one = tokens_in.astype(jnp.float32) + attn_sum + biases[2]
    normed = layer_norm(residual_one, gains[0], biases[3])
    normed_low = normed.astype(jnp.bfloat16)
    pre_act = jnp.dot(normed_low, in_low, preferred_element_type=jnp.float32) + bias_hidden
    act_low = exact_gelu(pre_act).astype(jnp.bfloat16)
    down_part = jnp.einsum("tf,df->td", act_low, down_low, preferred_element_type=jnp.float32)
    down_sum = lax.psum(down_part, "tensor")
    residual_two = normed + down_sum + biases[4]
    live = (inside.astype(jnp.int32) * span_mask.reshape(seq_count, seq_length)) > 0
    upto = (positions[:, None] <= positions[None, :]).astype(jnp.float32)
    rank = jnp.dot(live.astype(jnp.float32), upto).astype(jnp.int32) - 1
    slots = jnp.arange(SPAN_ROWS, dtype=jnp.int32)
    pick = (live[:, None, :] & (rank[:, None, :] == slots[None, :, None])).astype(jnp.float32)
    pick_low = pick.astype(jnp.bfloat16)

    def rows_of(values):
        width = values.shape[-1]
        return jnp.einsum(
            "srt,std->srd",
            pick,
            values.reshape(seq_count, seq_length, width),
            precision=lax.Precision.HIGHEST,
        ).reshape(seq_count * SPAN_ROWS, width)

    def low_rows_of(values):
        width = values.shape[-1]
        return jnp.einsum(
            "srt,std->srd",
            pick_low,
            values.reshape(seq_count, seq_length, width),
            preferred_element_type=jnp.bfloat16,
        ).reshape(seq_count * SPAN_ROWS, width)

    result = layer_norm(residual_two, gains[1], biases[5])
    normed_out = result.astype(jnp.bfloat16)
    residual_one_rows = rows_of(residual_one)
    residual_two_rows = rows_of(residual_two)
    grad_result = low_rows_of(cotangent).astype(jnp.float32)
    _, norm_two_back = jax.vjp(layer_norm, residual_two_rows, gains[1], biases[5])
    d_res_two, d_gain_two, d_shift_two = norm_two_back(grad_result)
    d_res_two_low = d_res_two.astype(jnp.bfloat16)
    normed_low_rows = low_rows_of(normed_low)
    pre_rows = jnp.dot(normed_low_rows, in_low, preferred_element_type=jnp.float32) + bias_hidden
    act_rows, gelu_back = jax.vjp(exact_gelu, pre_rows)
    grad_back = outer_sum(d_res_two_low, act_rows.astype(jnp.bfloat16))
    d_act = jnp.dot(d_res_two_low, down_low, preferred_element_type=jnp.float32)
    d_pre = gelu_back(d_act)[0]
    d_pre_low = d_pre.astype(jnp.bfloat16)
    grad_in = outer_sum(normed_low_rows, d_pre_low)
    d_normed_part = jnp.einsum("tf,df->td", d_pre_low, in_low, preferred_element_type=jnp.float32)
    d_normed = lax.psum(d_normed_part, "tensor") + d_res_two
    _, norm_one_back = jax.vjp(layer_norm, residual_one_rows, gains[0], biases[3])
    d_res_one, d_gain_one, d_shift_one = norm_one_back(d_normed)
    d_res_one_low = d_res_one.astype(jnp.bfloat16)
    grad_out_proj = outer_sum(d_res_one_low, low_rows_of(context_low))
    row_shape = (seq_count, SPAN_ROWS, local_heads, head_size)
    d_context = (
        jnp.dot(d_res_one_low, out_low, preferred_element_type=jnp.float32)
        .astype(jnp.bfloat16)
        .reshape(row_shape)
    )
    query_rows = low_rows_of(queries.reshape(row_count, head_cols)).reshape(row_shape)
    raw = jnp.einsum("sqhd,skhd->shqk", query_rows, keys, preferred_element_type=jnp.float32)
    probs = jax.nn.softmax(raw + key_bias[:, None, None, :], axis=-1)
    probs_again = probs.astype(jnp.bfloat16)
    d_probs = jnp.einsum("sqhd,skhd->shqk", d_context, values, preferred_element_type=jnp.float32)
    d_values = jnp.einsum(
        "shqk,sqhd->skhd", probs_again, d_context, preferred_element_type=jnp.float32
    ).reshape(row_count, head_cols)
    d_scores = (probs * (d_probs - jnp.sum(probs * d_probs, axis=-1, keepdims=True))).astype(
        jnp.bfloat16
    )
    d_queries = (
        jnp.einsum("shqk,skhd->sqhd", d_scores, keys, preferred_element_type=jnp.float32).reshape(
            seq_count * SPAN_ROWS, head_cols
        )
        * query_scale
    )
    d_keys = jnp.einsum(
        "shqk,sqhd->skhd", d_scores, query_rows, preferred_element_type=jnp.float32
    ).reshape(row_count, head_cols)

    def spread(row_values):
        width = row_values.shape[-1]
        return jnp.einsum(
            "srt,srd->std",
            pick,
            row_values.reshape(seq_count, SPAN_ROWS, width),
            precision=lax.Precision.HIGHEST,
        ).reshape(row_count, width)

    d_proj_low = (
        jnp.stack([spread(d_queries), d_keys, d_values], axis=1)
        .astype(jnp.bfloat16)
        .reshape(row_count, 3 * head_cols)
    )
    grad_qkv = outer_sum(tokens_in, d_proj_low).reshape(model_width, 3, head_cols)
    d_entry_part = jnp.einsum("tc,dc->td", d_proj_low, qkv_low, preferred_element_type=jnp.float32)
    input_grad = lax.psum(d_entry_part, "tensor") + spread(d_res_one)
    first_rank = (tensor_slot == 0).astype(jnp.float32)
    width_zero = jnp.zeros((model_width,), jnp.float32)

    def place_heads(partial_sum):
        return lax.dynamic_update_slice_in_dim(width_zero, partial_sum, tensor_slot * head_cols, 0)

    grad_gains = jnp.stack([d_gain_one, d_gain_two]) * first_rank
    grad_biases = jnp.stack(
        [
            place_heads(jnp.sum(d_queries, axis=0)),
            place_heads(jnp.sum(d_values, axis=0)),
            jnp.sum(d_res_one, axis=0) * first_rank,
            d_shift_one * first_rank,
            jnp.sum(d_res_two, axis=0) * first_rank,
            d_shift_two * first_rank,
        ]
    )
    grad_bias_in = lax.dynamic_update_slice_in_dim(
        jnp.zeros(bias_in.shape, jnp.float32), jnp.sum(d_pre, axis=0), tensor_slot * hidden_cols, 0
    )
    grad_gains, grad_biases, grad_bias_in = lax.psum(
        (grad_gains, grad_biases, grad_bias_in), ("dp", "tensor")
    )
    data_slot = lax.axis_index("dp")
    shard_rows = model_width // lax.axis_size("dp")
    owned = tuple(
        lax.psum_scatter(part, "dp", scatter_dimension=0, tiled=True)
        for part in (grad_qkv, grad_out_proj, grad_in, grad_back)
    )
    clock = step[0].astype(jnp.float32)
    warm = warmup[0].astype(jnp.float32)
    horizon = total[0].astype(jnp.float32)
    ratio = jnp.minimum(clock / warm, (horizon - clock) / (horizon - warm))
    corr_one = 1.0 - jnp.power(BETA_ONE, clock)
    corr_two = 1.0 - jnp.power(BETA_TWO, clock)
    change_rows = []
    fresh_moments = []
    for weight, grad_rows, moment in zip(
        (w_qkv, w_out, w_in, w_back), owned, (mom_qkv, mom_out, mom_in, mom_back)
    ):
        weight_rows = lax.dynamic_slice_in_dim(weight, data_slot * shard_rows, shard_rows, 0)
        row_change, new_moment = adam_step(
            weight_rows, grad_rows, moment, ratio, corr_one, corr_two, WEIGHT_DECAY
        )
        change_rows.append(row_change)
        fresh_moments.append(new_moment)
    change_qkv, change_out_proj, change_in_proj, change_back_proj = (
        lax.all_gather(change_rows[0], "dp", axis=0, tiled=True),
        lax.all_gather(change_rows[1], "dp", axis=0, tiled=True),
        lax.all_gather(change_rows[2], "dp", axis=0, tiled=True),
        lax.all_gather(change_rows[3], "dp", axis=0, tiled=True),
    )
    change_gains, new_mom_gains = adam_step(
        gains, grad_gains, mom_gains, ratio, corr_one, corr_two, 0.0
    )
    change_biases, new_mom_biases = adam_step(
        biases, grad_biases, mom_biases, ratio, corr_one, corr_two, 0.0
    )
    change_bias_in, new_mom_bias_in = adam_step(
        bias_in, grad_bias_in, mom_bias_in, ratio, corr_one, corr_two, 0.0
    )
    return (
        normed_out,
        input_grad,
        change_qkv,
        change_out_proj,
        change_in_proj,
        change_back_proj,
        change_gains,
        change_biases,
        change_bias_in,
        fresh_moments[0],
        fresh_moments[1],
        fresh_moments[2],
        fresh_moments[3],
        new_mom_gains,
        new_mom_biases,
        new_mom_bias_in,
    )


def solution(mesh):
    in_specs = (
        P("dp", None),
        P("dp", None),
        P("dp"),
        P("dp"),
        P(),
        P(),
        P(),
        P(None, None, "tensor"),
        P(None, "tensor"),
        P(None, "tensor"),
        P(None, "tensor"),
        P(),
        P(),
        P(),
        P(None, "dp", None, "tensor"),
        P(None, "dp", "tensor"),
        P(None, "dp", "tensor"),
        P(None, "dp", "tensor"),
        P(),
        P(),
        P(),
    )
    out_specs = (
        P("dp", None),
        P("dp", None),
        P(None, None, "tensor"),
        P(None, "tensor"),
        P(None, "tensor"),
        P(None, "tensor"),
        P(),
        P(),
        P(),
        P(None, "dp", None, "tensor"),
        P(None, "dp", "tensor"),
        P(None, "dp", "tensor"),
        P(None, "dp", "tensor"),
        P(),
        P(),
        P(),
    )
    return jax.shard_map(
        on_device, mesh=mesh, in_specs=in_specs, out_specs=out_specs, check_vma=False
    )
```
